32 devices in a mesh: seq: 16 (over z, y, core), head: 2 (over x).
Axes of the slice: x: 2, y: 2, z: 4, core: 2. Of those that a mesh axis runs over, the one named last changes fastest.
Arguments:
- tokens: bfloat16 [16, 1024, 1024], P('seq'), may hold values from -6 to 6
- segment_ids: int32 [16, 1024], P('seq'), may hold values from 0 to 7, as said below
- context_flags: int32 [16, 1024], P('seq'), may hold values from 0 to 1, as said below
- ln1_gain: bfloat16 [1024], replicated, may hold values from 0.25 to 1.75
- ln1_bias: bfloat16 [1024], replicated, may hold values from -4 to 4
- qkv_weight: bfloat16 [3, 1024, 1024], P(None, None, 'head'), may hold values from -0.1875 to 0.1875
- qv_bias: bfloat16 [2, 1024], P(None, 'head'), may hold values from -6 to 6
- out_weight: bfloat16 [1024, 1024], P('head'), may hold values from -1.5 to 1.5
- out_bias: bfloat16 [1024], replicated, may hold values from -4 to 4
- ln2_gain: bfloat16 [1024], replicated, may hold values from 0.25 to 1.75
- ln2_bias: bfloat16 [1024], replicated, may hold values from -4 to 4
- up_weight: bfloat16 [1024, 4096], P('seq', 'head'), may hold values from -0.1875 to 0.1875
- up_bias: bfloat16 [4096], P('head'), may hold values from -6 to 6
- down_weight: bfloat16 [4096, 1024], P('head', 'seq'), may hold values from -0.09375 to 0.09375
- down_bias: bfloat16 [1024], replicated, may hold values from -4 to 4
- cotangent: bfloat16 [16, 1024, 1024], P('seq'), may hold values from -6 to 6
Outputs:
- output: bfloat16 [16, 1024, 1024], P('seq')
- tokens_grad: bfloat16 [16, 1024, 1024], P('seq')
- ln1_gain_grad: float32 [1024], replicated
- ln1_bias_grad: float32 [1024], replicated
- qkv_weight_grad: float32 [3, 1024, 1024], P(None, 'seq', 'head')
- qv_bias_grad: float32 [2, 1024], P(None, 'head')
- out_weight_grad: float32 [1024, 1024], P('head', 'seq')
- out_bias_grad: float32 [1024], replicated
- ln2_gain_grad: float32 [1024], replicated
- ln2_bias_grad: float32 [1024], replicated
- up_weight_grad: float32 [1024, 4096], P('seq', 'head')
- up_bias_grad: float32 [4096], P('head')
- down_weight_grad: float32 [4096, 1024], P('head', 'seq')
- down_bias_grad: float32 [1024], replicated
The draws below stay inside these ranges and needn't reach their ends.
Inputs may be any that keep to these rules, and one draw needn't show every extreme that they name: `segment_ids`: every sequence holds exactly 8 tables, numbered 0 to 7 in order: the table number starts at 0 at the first row and never falls. `context_flags`: the first row of every table is a context row.
All inputs are finite; a program needn't handle non-finite values.
Results may differ from the reference program's by a relative error of at most 0.015.
Values may be sent and summed in bfloat16 or wider, within the bound.
A program may use at most 192 MiB of HBM per device.

```python
import math
import jax
import jax.numpy as jnp
from jax import lax

D = 1024
HEADS = 16
HEAD_DIM = 64
FF = 4096
LENGTH = 1024
SEQS = 16


table_count = 8


def table_layout(key):
    row_keys = jax.random.split(key, SEQS)
    picks = jax.vmap(lambda one_key: jax.random.permutation(one_key, LENGTH - 1))(row_keys)[:, :table_count - 1] + 1
    seq_index = jnp.arange(SEQS, dtype=jnp.int32)[:, None]
    starts = jnp.zeros((SEQS, LENGTH), jnp.int32).at[seq_index, picks].set(1)
    starts = starts.at[:, 0].set(1)
    segments = jnp.cumsum(starts, axis=1) - 1
    return (starts, segments.astype(jnp.int32))


def draw_segment_ids(key, part):
    starts, segments = table_layout(key)
    return segments


def draw_context_flags(key, part):
    starts, segments = table_layout(key)
    key = jax.random.fold_in(key, 7)
    picked = (jax.random.randint(key, (SEQS, LENGTH), 0, 10) < 7).astype(jnp.int32)
    return jnp.maximum(picked, starts).astype(jnp.int32)


def block_levels(rng, dims, shards, smallest, high):
    def one(axis_at, shards_of):
        draws = jax.random.uniform(jax.random.fold_in(jax.random.fold_in(rng, 6), axis_at), (shards_of,), jnp.float32, smallest / len(shards), high / len(shards))
        return jnp.repeat(jnp.exp(draws), dims[axis_at] // shards_of).reshape((-1,) + (1,) * (len(dims) - axis_at - 1))

    level = one(*shards[0])
    for cut in shards[1:]:
        level = level * one(*cut)
    return level


def bell_draw(stream_key, extent, scale, most, cuts=(), held_as=jnp.bfloat16):
    entries = scale * jax.random.normal(stream_key, extent, jnp.float32)
    if cuts:
        entries = entries * block_levels(stream_key, extent, cuts, -0.22, 0.18)
    return jnp.clip(entries, -most, most).astype(held_as)


def setup_inputs(seed: int = 0) -> dict:
    keys = jax.random.split(jax.random.key(seed), 17)
    return {
        "tokens": bell_draw(keys[0], (SEQS, LENGTH, D), 1.0, 6.0, ((0, 16),)),
        "segment_ids": draw_segment_ids(jax.random.fold_in(keys[16], 71), 0),
        "context_flags": draw_context_flags(jax.random.fold_in(keys[16], 71), 0),
        "ln1_gain": jnp.clip(1.0 + 0.15 * jax.random.normal(keys[3], (D,), jnp.float32), 0.25, 1.75).astype(jnp.bfloat16),
        "ln1_bias": bell_draw(keys[4], (D,), 0.3, 4.0),
        "qkv_weight": bell_draw(keys[5], (3, D, D), D ** -0.5, 0.1875, ((2, 2),)),
        "qv_bias": bell_draw(keys[6], (2, D), 0.5, 6.0, ((1, 2),)),
        "out_weight": bell_draw(keys[7], (D, D), (max(D // 64, 1)) ** -0.5, 1.5, ((0, 2),)),
        "out_bias": bell_draw(keys[8], (D,), 0.3, 4.0),
        "ln2_gain": jnp.clip(1.0 + 0.15 * jax.random.normal(keys[9], (D,), jnp.float32), 0.25, 1.75).astype(jnp.bfloat16),
        "ln2_bias": bell_draw(keys[10], (D,), 0.3, 4.0),
        "up_weight": bell_draw(keys[11], (D, FF), D ** -0.5, 0.1875, ((0, 16), (1, 2))),
        "up_bias": bell_draw(keys[12], (FF,), 0.5, 6.0, ((0, 2),)),
        "down_weight": bell_draw(keys[13], (FF, D), FF ** -0.5, 0.09375, ((0, 2), (1, 16))),
        "down_bias": bell_draw(keys[14], (D,), 0.3, 4.0),
        "cotangent": bell_draw(keys[15], (SEQS, LENGTH, D), 1.0, 6.0, ((0, 16),)),
    }


@jax.custom_vjp
def low(v):
    return lax.optimization_barrier(v.astype(jnp.bfloat16)).astype(jnp.float32)

@jax.custom_vjp
def low_back(v):
    return v

def low_keep(v):
    return (low(v), None)

def low_pass(kept, grad):
    return (grad,)

def back_keep(v):
    return (v, None)

def back_low(kept, grad):
    return (low(grad),)
low.defvjp(low_keep, low_pass)
low_back.defvjp(back_keep, back_low)
highest = lax.Precision.HIGHEST

def layer_norm(values_in, scaling, offset):
    middle = lax.optimization_barrier(jnp.mean(values_in, axis=-1, keepdims=True))
    centred = values_in - middle
    spread = lax.optimization_barrier(jnp.mean(centred * centred, axis=-1, keepdims=True))
    return centred * lax.rsqrt(spread + 1e-05) * scaling + offset

def gelu_exact(values_in):
    return 0.5 * values_in * (1.0 + jax.scipy.special.erf(values_in * 0.7071067811865476))

def forward(tokens, segments, context, params):
    gain_one, offset_one, qkv_weight, qv_bias, out_weight, out_bias, gain_two, offset_two, up_weight, up_bias, down_weight, down_bias = params
    length = tokens.shape[0]
    normed = low(layer_norm(tokens, gain_one, offset_one))
    queries = low(low_back(jnp.dot(normed, qkv_weight[0], precision=highest) + qv_bias[0]))
    key_rows = low(low_back(jnp.dot(normed, qkv_weight[1], precision=highest)))
    value_rows = low(low_back(jnp.dot(normed, qkv_weight[2], precision=highest) + qv_bias[1]))
    queries = queries.reshape(length, HEADS, HEAD_DIM)
    key_rows = key_rows.reshape(length, HEADS, HEAD_DIM)
    value_rows = value_rows.reshape(length, HEADS, HEAD_DIM)
    scores = jnp.einsum('qhd,khd->hqk', queries, key_rows, precision=highest) * (1.0 / math.sqrt(HEAD_DIM))
    scores = low_back(scores)
    allowed = (segments[:, None] == segments[None, :]) & (context[None, :] == 1)
    scores = jnp.where(allowed[None], scores, -1e+30)
    row_top = lax.optimization_barrier(jnp.max(scores, axis=-1, keepdims=True))
    exponent = jnp.exp(scores - row_top)
    soft_weights = exponent / lax.optimization_barrier(jnp.sum(exponent, axis=-1, keepdims=True))
    mixture = jnp.einsum('hqk,khd->qhd', low(soft_weights), value_rows, precision=highest).reshape(length, D)
    mixture = low(low_back(mixture))
    attended = low_back(jnp.dot(mixture, out_weight, precision=highest) + out_bias)
    middle_state = tokens + attended
    normed_two = low(layer_norm(middle_state, gain_two, offset_two))
    before = low_back(jnp.dot(normed_two, up_weight, precision=highest) + up_bias)
    active = low(gelu_exact(before))
    return middle_state + jnp.dot(active, down_weight, precision=highest) + down_bias

def reference(tokens, segment_ids, context_flags, ln1_gain, ln1_bias, qkv_weight, qv_bias, out_weight, out_bias, ln2_gain, ln2_bias, up_weight, up_bias, down_weight, down_bias, cotangent):
    params = tuple((member.astype(jnp.float32) for member in (ln1_gain, ln1_bias, qkv_weight, qv_bias, out_weight, out_bias, ln2_gain, ln2_bias, up_weight, up_bias, down_weight, down_bias)))
    per_step = math.gcd(SEQS, max(1, 2048 // LENGTH))
    step_count = SEQS // per_step

    def regroup(array):
        return array.reshape((step_count, per_step) + array.shape[1:])

    def one_group(totals, member):
        group_tokens, group_segments, group_context, group_cotangent = member

        def run_layer(batch, *weights):
            return jax.vmap(lambda row_block, seg_block, ctx_block: forward(row_block, seg_block, ctx_block, weights))(batch, group_segments, group_context)
        result, pull_back = jax.vjp(run_layer, group_tokens.astype(jnp.float32), *params)
        gradients = pull_back(group_cotangent.astype(jnp.float32))
        totals = tuple((total + grad for total, grad in zip(totals, gradients[1:])))
        return (totals, (result.astype(jnp.bfloat16), gradients[0].astype(jnp.bfloat16)))
    initial = tuple((jnp.zeros_like(member) for member in params))
    totals, (outputs, token_grads) = lax.scan(one_group, initial, (regroup(tokens), regroup(segment_ids), regroup(context_flags), regroup(cotangent)))
    outputs = outputs.reshape(tokens.shape)
    token_grads = token_grads.reshape(tokens.shape)
    return (outputs, token_grads, totals[0], totals[1], totals[2], totals[3], totals[4], totals[5], totals[6], totals[7], totals[8], totals[9], totals[10], totals[11])
```

```python
import math

import jax
import jax.numpy as jnp
from jax import lax
from jax.experimental import pallas as pl
from jax.experimental.pallas import tpu as pltpu
from jax.sharding import PartitionSpec as P

HEAD_DIM = 64


def layer_norm(values_in, scaling, offset):
    middle = jnp.mean(values_in, axis=-1, keepdims=True)
    centred = values_in - middle
    spread = jnp.mean(centred * centred, axis=-1, keepdims=True)
    return centred * lax.rsqrt(spread + 1e-05) * scaling + offset


def gelu_exact(values_in):
    return 0.5 * values_in * (1.0 + jax.scipy.special.erf(values_in * 0.7071067811865476))


def dot_rows(left, right):
    return lax.dot_general(
        left, right, (((1,), (1,)), ((), ())), preferred_element_type=jnp.float32
    )


def dot_cols(left, right):
    return lax.dot_general(
        left, right, (((0,), (0,)), ((), ())), preferred_element_type=jnp.float32
    )


def masked_scores(block_query, seq_keys, block_segments, seq_segments, seq_context, factor):
    raw_scores = (
        jnp.einsum("qhd,khd->hqk", block_query, seq_keys, preferred_element_type=jnp.float32)
        * factor
    )
    allowed = (block_segments[:, None] == seq_segments[None, :]) & (seq_context[None, :] == 1)
    return jnp.where(allowed[None], raw_scores, -1e30)


def generic_body(
    tokens,
    segment_ids,
    context_flags,
    ln1_gain,
    ln1_bias,
    qkv_weight,
    qv_bias,
    out_weight,
    out_bias,
    ln2_gain,
    ln2_bias,
    up_weight,
    up_bias,
    down_weight,
    down_bias,
    cotangent,
):
    seq_count, length, width = tokens.shape
    row_count = seq_count * length
    local_cols = qkv_weight.shape[2]
    head_count = local_cols // HEAD_DIM
    factor = 1.0 / math.sqrt(HEAD_DIM)
    block = min(512, length)
    blocks = length // block
    gain_one = ln1_gain.astype(jnp.float32)
    offset_one = ln1_bias.astype(jnp.float32)
    gain_two = ln2_gain.astype(jnp.float32)
    offset_two = ln2_bias.astype(jnp.float32)
    flat_in = tokens.astype(jnp.float32).reshape(row_count, width)
    normed_f, norm_one_pull = jax.vjp(layer_norm, flat_in, gain_one, offset_one)
    normed = normed_f.astype(jnp.bfloat16)
    queries = (
        jnp.dot(normed, qkv_weight[0], preferred_element_type=jnp.float32)
        + qv_bias[0].astype(jnp.float32)
    ).astype(jnp.bfloat16)
    key_rows = jnp.dot(normed, qkv_weight[1], preferred_element_type=jnp.float32).astype(
        jnp.bfloat16
    )
    value_rows = (
        jnp.dot(normed, qkv_weight[2], preferred_element_type=jnp.float32)
        + qv_bias[1].astype(jnp.float32)
    ).astype(jnp.bfloat16)

    def per_sequence(array):
        return array.reshape(seq_count, length, head_count, HEAD_DIM)

    def attend_sequence(member):
        seq_query, seq_keys, seq_values, seq_segments, seq_context = member

        def attend_block(portion):
            block_query, block_segments = portion
            scores = masked_scores(
                block_query, seq_keys, block_segments, seq_segments, seq_context, factor
            )
            row_top = jnp.max(scores, axis=-1, keepdims=True)
            exponent = jnp.exp(scores - row_top)
            row_total = jnp.sum(exponent, axis=-1, keepdims=True)
            soft_weights = (exponent / row_total).astype(jnp.bfloat16)
            block_mix = jnp.einsum(
                "hqk,khd->qhd", soft_weights, seq_values, preferred_element_type=jnp.float32
            )
            return (block_mix.astype(jnp.bfloat16), row_top + jnp.log(row_total))

        return lax.map(
            attend_block,
            (
                seq_query.reshape(blocks, block, head_count, HEAD_DIM),
                seq_segments.reshape(blocks, block),
            ),
        )

    mixture, log_totals = lax.map(
        attend_sequence,
        (
            per_sequence(queries),
            per_sequence(key_rows),
            per_sequence(value_rows),
            segment_ids,
            context_flags,
        ),
    )
    mixture = mixture.reshape(row_count, local_cols)
    partial_out = jnp.dot(mixture, out_weight, preferred_element_type=jnp.float32)
    grad_rows_all = cotangent.reshape(row_count, width)
    grad_float_all = grad_rows_all.astype(jnp.float32)
    grad_down_bias = jnp.sum(grad_float_all, axis=0)
    attended = lax.psum(partial_out, "head") + out_bias.astype(jnp.float32)
    middle_state = flat_in + attended
    normed_two_f, norm_two_pull = jax.vjp(layer_norm, middle_state, gain_two, offset_two)
    normed_two = normed_two_f.astype(jnp.bfloat16)
    up_part, down_part, up_shift = (
        lax.all_gather(up_weight, "head", axis=1, tiled=True),
        lax.all_gather(down_weight, "head", axis=0, tiled=True),
        lax.all_gather(up_bias, "head", axis=0, tiled=True),
    )
    up_full, down_full = (
        lax.all_gather(up_part, "seq", axis=0, tiled=True),
        lax.all_gather(down_part, "seq", axis=1, tiled=True),
    )
    before = jnp.dot(normed_two, up_full, preferred_element_type=jnp.float32) + up_shift.astype(
        jnp.float32
    )
    active_f, gelu_pull = jax.vjp(gelu_exact, before)
    active = active_f.astype(jnp.bfloat16)
    branch_out = jnp.dot(active, down_full, preferred_element_type=jnp.float32)
    final_rows = (middle_state + branch_out + down_bias.astype(jnp.float32)).astype(jnp.bfloat16)
    output = final_rows.reshape(tokens.shape)
    grad_float = grad_rows_all.astype(jnp.float32)
    grad_down = dot_cols(active, grad_rows_all)
    grad_active = dot_rows(grad_rows_all, down_full)
    (grad_before_f,) = gelu_pull(grad_active)
    grad_before = grad_before_f.astype(jnp.bfloat16)
    grad_up = dot_cols(normed_two, grad_before)
    grad_up_bias = jnp.sum(grad_before.astype(jnp.float32), axis=0)
    grad_normed_two = dot_rows(grad_before, up_full)
    grad_middle_norm, grad_gain_two, grad_offset_two = norm_two_pull(grad_normed_two)
    grad_middle = grad_float + grad_middle_norm
    ff_part = up_weight.shape[1]
    start_col = lax.axis_index("head") * ff_part
    grad_up = lax.dynamic_slice_in_dim(grad_up, start_col, ff_part, 1)
    grad_down = lax.dynamic_slice_in_dim(grad_down, start_col, ff_part, 0)
    grad_up_bias = lax.dynamic_slice_in_dim(grad_up_bias, start_col, ff_part, 0)
    grad_attended = grad_middle.astype(jnp.bfloat16)
    grad_out_bias = jnp.sum(grad_attended.astype(jnp.float32), axis=0)
    grad_out = dot_cols(mixture, grad_attended)
    grad_mixture = dot_rows(grad_attended, out_weight).astype(jnp.bfloat16)

    def back_sequence(member):
        seq_query, seq_keys, seq_values, seq_grad, seq_logs, seq_segments, seq_context = member

        def back_block(carry, portion):
            key_acc, value_acc = carry
            block_query, block_grad, block_logs, block_segments = portion
            scores = masked_scores(
                block_query, seq_keys, block_segments, seq_segments, seq_context, factor
            )
            soft_weights = jnp.exp(scores - block_logs)
            value_acc = value_acc + jnp.einsum(
                "hqk,qhd->khd",
                soft_weights.astype(jnp.bfloat16),
                block_grad,
                preferred_element_type=jnp.float32,
            )
            grad_soft = jnp.einsum(
                "qhd,khd->hqk", block_grad, seq_values, preferred_element_type=jnp.float32
            )
            row_inner = jnp.sum(soft_weights * grad_soft, axis=-1, keepdims=True)
            grad_scores = (soft_weights * (grad_soft - row_inner)).astype(jnp.bfloat16)
            grad_query = (
                jnp.einsum(
                    "hqk,khd->qhd", grad_scores, seq_keys, preferred_element_type=jnp.float32
                )
                * factor
            )
            key_acc = (
                key_acc
                + jnp.einsum(
                    "hqk,qhd->khd", grad_scores, block_query, preferred_element_type=jnp.float32
                )
                * factor
            )
            return ((key_acc, value_acc), grad_query)

        empty = jnp.zeros((length, head_count, HEAD_DIM), jnp.float32)
        (key_acc, value_acc), grad_query = lax.scan(
            back_block,
            (empty, empty),
            (
                seq_query.reshape(blocks, block, head_count, HEAD_DIM),
                seq_grad.reshape(blocks, block, head_count, HEAD_DIM),
                seq_logs,
                seq_segments.reshape(blocks, block),
            ),
        )
        return (grad_query, key_acc, value_acc)

    grad_queries, grad_keys, grad_values = lax.map(
        back_sequence,
        (
            per_sequence(queries),
            per_sequence(key_rows),
            per_sequence(value_rows),
            per_sequence(grad_mixture),
            log_totals,
            segment_ids,
            context_flags,
        ),
    )
    grad_queries = grad_queries.reshape(row_count, local_cols).astype(jnp.bfloat16)
    grad_keys = grad_keys.reshape(row_count, local_cols).astype(jnp.bfloat16)
    grad_values = grad_values.reshape(row_count, local_cols).astype(jnp.bfloat16)
    grad_qv_bias = jnp.stack(
        [
            jnp.sum(grad_queries.astype(jnp.float32), axis=0),
            jnp.sum(grad_values.astype(jnp.float32), axis=0),
        ]
    )
    grad_qkv = jnp.stack(
        [dot_cols(normed, grad_queries), dot_cols(normed, grad_keys), dot_cols(normed, grad_values)]
    )
    grad_normed = (
        dot_rows(grad_queries, qkv_weight[0])
        + dot_rows(grad_keys, qkv_weight[1])
        + dot_rows(grad_values, qkv_weight[2])
    )
    grad_normed = lax.psum(grad_normed, "head")
    grad_input_norm, grad_gain_one, grad_offset_one = norm_one_pull(grad_normed)
    tokens_grad = (grad_middle + grad_input_norm).astype(jnp.bfloat16).reshape(tokens.shape)
    summed_qkv, summed_out, summed_up, summed_down = (
        lax.psum_scatter(
            grad_qkv.astype(jnp.bfloat16), "seq", scatter_dimension=1, tiled=True
        ).astype(jnp.float32),
        lax.psum_scatter(
            grad_out.astype(jnp.bfloat16), "seq", scatter_dimension=1, tiled=True
        ).astype(jnp.float32),
        lax.psum_scatter(
            grad_up.astype(jnp.bfloat16), "seq", scatter_dimension=0, tiled=True
        ).astype(jnp.float32),
        lax.psum_scatter(
            grad_down.astype(jnp.bfloat16), "seq", scatter_dimension=1, tiled=True
        ).astype(jnp.float32),
    )
    smalls = lax.psum(
        (
            grad_gain_one,
            grad_offset_one,
            grad_qv_bias,
            grad_out_bias,
            grad_gain_two,
            grad_offset_two,
            grad_up_bias,
            grad_down_bias,
        ),
        "seq",
    )
    return (
        output,
        tokens_grad,
        smalls[0],
        smalls[1],
        summed_qkv,
        smalls[2],
        summed_out,
        smalls[3],
        smalls[4],
        smalls[5],
        summed_up,
        smalls[6],
        summed_down,
        smalls[7],
    )


MESH = pl.DeviceIdType.MESH
BF = jnp.bfloat16
F32 = jnp.float32
BLOCK = 256
PAIR = 2 * HEAD_DIM
Z_SIZE, Y_SIZE, CORES = 4, 2, 2
SEQ_SIZE = Z_SIZE * Y_SIZE * CORES


def nn(left, right):
    return jnp.dot(left, right, preferred_element_type=F32)


def place():
    me = lax.axis_index("seq")
    head = lax.axis_index("head")
    core = me % 2
    y = (me // 2) % 2
    across = {"seq": me, "head": 1 - head}
    core_mate = {"seq": me + 1 - 2 * core, "head": head}
    y_mate = {"seq": me + 2 - 4 * y, "head": head}
    z_mates = [{"seq": (me + 4 * d) % SEQ_SIZE, "head": head} for d in (1, 2, 3)]
    return me, head, core, y, across, core_mate, y_mate, z_mates


def greet(others):
    barrier = pltpu.get_barrier_semaphore()
    for other in others:
        pl.semaphore_signal(barrier, inc=1, device_id=other, device_id_type=MESH)
    pl.semaphore_wait(barrier, len(others))


def remote(src, dst, send_sem, recv_sem, other):
    return pltpu.make_async_remote_copy(
        src_ref=src, dst_ref=dst, send_sem=send_sem, recv_sem=recv_sem,
        device_id=other, device_id_type=MESH,
    )


def norm_stats(rows):
    middle = jnp.mean(rows, axis=-1, keepdims=True)
    centred = rows - middle
    spread = jnp.mean(centred * centred, axis=-1, keepdims=True)
    return centred, lax.rsqrt(spread + 1e-05)


def fwd_kernel(
    x_ref, seg_col, key_row, gain, offset, wqkv, qv_bias, wout, out_bias, shard,
    q_ref, k_ref, v_ref, mix_ref, mid_ref, wff,
    normed, bias, wout_x, mix_x,
    zs, zr, ys, yr, cs, cr, xs, xr, local,
):
    length, width = x_ref.shape
    blocks = length // BLOCK
    pairs = q_ref.shape[0]
    me, head, core, y, across, core_mate, y_mate, z_mates = place()
    greet([across, core_mate, y_mate, *z_mates])

    out_copy = remote(wout, wout_x, xs.at[0], xr.at[0], across)
    out_copy.start()
    own = [pltpu.make_async_copy(shard.at[u], wff.at[u, me], local.at[u]) for u in range(2)]
    from_y = me + 2 - 4 * y
    z_own = [[me] + [(me - 4 * d) % SEQ_SIZE for d in (1, 2, 3)] for _ in range(2)][0]
    z_mate = [from_y] + [(from_y - 4 * d) % SEQ_SIZE for d in (1, 2, 3)]
    mine = z_own + z_mate
    from_core = me + 1 - 2 * core
    theirs = [from_core] + [(from_core - 4 * d) % SEQ_SIZE for d in (1, 2, 3)]
    far = from_core + 2 - 4 * y
    theirs = theirs + [far] + [(far - 4 * d) % SEQ_SIZE for d in (1, 2, 3)]

    def z_copy(u, d):
        n = u * 3 + d - 1
        return remote(shard.at[u], wff.at[u, me], zs.at[n], zr.at[n], z_mates[d - 1])

    def z_arrival(u, d):
        n = u * 3 + d - 1
        slot = wff.at[u, z_own[d]]
        return remote(slot, slot, zs.at[n], zr.at[n], z_mates[d - 1])

    def y_copy(u, d):
        n = u * 4 + d
        src = shard.at[u] if d == 0 else wff.at[u, z_own[d]]
        return remote(src, wff.at[u, z_own[d]], ys.at[n], yr.at[n], y_mate)

    def y_arrival(u, d):
        n = u * 4 + d
        slot = wff.at[u, z_mate[d]]
        return remote(slot, slot, ys.at[n], yr.at[n], y_mate)

    def c_copy(u, e):
        n = u * 8 + e
        src = shard.at[u] if e == 0 else wff.at[u, mine[e]]
        return remote(src, wff.at[u, mine[e]], cs.at[n], cr.at[n], core_mate)

    def c_arrival(u, e):
        n = u * 8 + e
        slot = wff.at[u, theirs[e]]
        return remote(slot, slot, cs.at[n], cr.at[n], core_mate)

    for u in range(2):
        for d in (1, 2, 3):
            z_copy(u, d).start()
        y_copy(u, 0).start()
        c_copy(u, 0).start()
        own[u].start()

    def z_event(u, d):
        z_arrival(u, d).wait_recv()
        y_copy(u, d).start()
        c_copy(u, d).start()

    def y_event(u, d):
        y_arrival(u, d).wait_recv()
        c_copy(u, 4 + d).start()

    plan = {
        1: [(z_event, 0, 1), (y_event, 0, 0)], 2: [(z_event, 0, 2)], 4: [(z_event, 0, 3)],
        5: [(y_event, 0, 1)], 6: [(z_event, 1, 1), (y_event, 1, 0)], 7: [(y_event, 0, 2)],
        8: [(z_event, 1, 2)], 9: [(y_event, 0, 3)], 11: [(z_event, 1, 3)], 12: [(y_event, 1, 1)],
        14: [(y_event, 1, 2)],
    }
    last = [(y_event, 1, 3)]

    gains, offsets = gain[...], offset[...]

    def project(b, _):
        rows = pl.ds(pl.multiple_of(b * BLOCK, BLOCK), BLOCK)
        centred, scale = norm_stats(x_ref[rows, :].astype(F32))
        block = (centred * scale * gains + offsets).astype(BF)
        normed[rows, :] = block
        queries = ((nn(block, wqkv[0]) + qv_bias[0:1, :]).astype(BF) * 0.125).astype(BF)
        keys = nn(block, wqkv[1]).astype(BF)
        values = (nn(block, wqkv[2]) + qv_bias[1:2, :]).astype(BF)
        for p in range(pairs):
            cols = slice(p * PAIR, (p + 1) * PAIR)
            q_ref[p, rows, :] = queries[:, cols]
            k_ref[p, rows, :] = keys[:, cols]
            v_ref[p, rows, :] = values[:, cols]
        return 0

    lax.fori_loop(0, blocks, project, 0)

    low_lanes = lax.broadcasted_iota(jnp.int32, (1, PAIR), 1) < HEAD_DIM
    zero = jnp.zeros((1, PAIR), BF)

    def mix_copy(b):
        rows = pl.ds(pl.multiple_of(b * BLOCK, BLOCK), BLOCK)
        return rows

    def attend(t, _):
        b, p = t // pairs, t % pairs
        rows = pl.ds(pl.multiple_of(b * BLOCK, BLOCK), BLOCK)

        @pl.when(p == 0)
        def _():
            seen = seg_col[rows, :] == key_row[...]
            bias[...] = jnp.where(seen, 0.0, -1e30)

        queries, keys, values = q_ref[p, rows, :], k_ref[p], v_ref[p]
        parts = []
        for low in (True, False):
            own_lanes = low_lanes if low else jnp.logical_not(low_lanes)
            scores = dot_rows(jnp.where(own_lanes, queries, zero), keys) + bias[...]
            top = jnp.max(scores, axis=-1, keepdims=True)
            exponent = jnp.exp(scores - top)
            total = jnp.sum(exponent, axis=-1, keepdims=True)
            parts.append(nn(exponent.astype(BF), values) / total)
        mix_ref[p, rows, :] = jnp.where(low_lanes, parts[0], parts[1]).astype(BF)
        for step, events in plan.items():
            @pl.when(t == step)
            def _(events=events):
                for event, u, d in events:
                    event(u, d)
        for b_done in range(blocks):
            @pl.when(t == (b_done + 1) * pairs - 1)
            def _(b_done=b_done):
                mixture_copy(b_done).start()
        return 0

    def mixture_copy(b):
        part = pl.ds(b * BLOCK, BLOCK)
        return remote(
            mix_ref.at[:, part, :], mix_x.at[:, part, :], xs.at[1 + b], xr.at[1 + b], across
        )

    lax.fori_loop(0, blocks * pairs, attend, 0)
    for event, u, d in last:
        event(u, d)
    out_copy.wait_recv()
    for b in range(blocks):
        mixture_copy(b).wait_recv()
        rows = pl.ds(b * BLOCK, BLOCK)
        ours = jnp.concatenate([mix_ref[p, rows, :] for p in range(pairs)], axis=-1)
        other = jnp.concatenate([mix_x[p, rows, :] for p in range(pairs)], axis=-1)
        attended = nn(ours, wout[...]) + nn(other, wout_x[...]) + out_bias[...]
        mid_ref[rows, :] = x_ref[rows, :].astype(F32) + attended

    for u in range(2):
        for e in range(8):
            c_arrival(u, e).wait_recv()
    out_copy.wait_send()
    for b in range(blocks):
        mixture_copy(b).wait_send()
    for u in range(2):
        own[u].wait()
        for d in (1, 2, 3):
            z_copy(u, d).wait_send()
        for d in range(4):
            y_copy(u, d).wait_send()
        for e in range(8):
            c_copy(u, e).wait_send()


VMEM_SPEC = pl.BlockSpec(memory_space=pltpu.VMEM)
ANY_SPEC = pl.BlockSpec(memory_space=pl.ANY)


def run_fwd(x, seg_col, key_row, gain, offset, wqkv, qv_bias, wout, out_bias, shard):
    length, width = x.shape
    cols = wqkv.shape[2]
    pairs = cols // PAIR
    blocks = length // BLOCK
    hidden = shard.shape[2]
    lanes = jax.ShapeDtypeStruct((pairs, length, PAIR), BF)
    dma = pltpu.SemaphoreType.DMA
    return pl.pallas_call(
        fwd_kernel,
        out_shape=[
            lanes, lanes, lanes, lanes,
            jax.ShapeDtypeStruct((length, width), F32),
            jax.ShapeDtypeStruct((2, SEQ_SIZE, shard.shape[1], hidden), BF),
        ],
        in_specs=[VMEM_SPEC] * 9 + [ANY_SPEC],
        out_specs=[VMEM_SPEC] * 5 + [ANY_SPEC],
        scratch_shapes=[
            pltpu.VMEM((length, width), BF),
            pltpu.VMEM((BLOCK, length), F32),
            pltpu.VMEM(wout.shape, BF),
            pltpu.VMEM((pairs, length, PAIR), BF),
            dma((6,)), dma((6,)), dma((8,)), dma((8,)), dma((16,)), dma((16,)),
            dma((1 + blocks,)), dma((1 + blocks,)), dma((2,)),
        ],
        compiler_params=pltpu.CompilerParams(
            collective_id=0, has_side_effects=True, vmem_limit_bytes=56 * 2**20
        ),
    )(x, seg_col, key_row, gain, offset, wqkv, qv_bias, wout, out_bias, shard)


def pair_sum(partial):
    sent = partial.astype(BF)
    got = lax.ppermute(sent, "head", [(0, 1), (1, 0)])
    return sent.astype(F32) + got.astype(F32)


def fast_body(
    tokens, segment_ids, context_flags, ln1_gain, ln1_bias, qkv_weight, qv_bias, out_weight,
    out_bias, ln2_gain, ln2_bias, up_weight, up_bias, down_weight, down_bias, cotangent,
):
    _, length, width = tokens.shape
    hidden = up_weight.shape[1]
    cols = qkv_weight.shape[2]
    heads = cols // HEAD_DIM
    row = lambda v: v.astype(F32).reshape(1, -1)
    x, dy = tokens[0], cotangent[0]
    segments, context = segment_ids[0], context_flags[0]
    key_row = jnp.where(context == 1, segments, -1).reshape(1, length)
    seg_col = segments.reshape(length, 1)
    shard = jnp.stack([up_weight, down_weight.T])
    queries, key_rows, value_rows, mixture, middle_state, wff = run_fwd(
        x, seg_col, key_row, row(ln1_gain), row(ln1_bias), qkv_weight, qv_bias.astype(F32),
        out_weight, row(out_bias), shard,
    )
    up_full = wff[0].reshape(width, hidden)
    down_t = wff[1].reshape(width, hidden)
    flat = lambda v: v.transpose(1, 0, 2).reshape(length, cols)
    mix_flat = flat(mixture)

    gain_one, offset_one = ln1_gain.astype(F32), ln1_bias.astype(F32)
    gain_two, offset_two = ln2_gain.astype(F32), ln2_bias.astype(F32)
    normed_f, norm_one_pull = jax.vjp(layer_norm, x.astype(F32), gain_one, offset_one)
    normed = normed_f.astype(BF)
    grad_float = dy.astype(F32)
    grad_down_bias = jnp.sum(grad_float, axis=0)
    normed_two_f, norm_two_pull = jax.vjp(layer_norm, middle_state, gain_two, offset_two)
    normed_two = normed_two_f.astype(BF)
    before = nn(normed_two, up_full) + up_bias.astype(F32)
    active_f, gelu_pull = jax.vjp(gelu_exact, before)
    active = active_f.astype(BF)
    grad_active = nn(dy, down_t)
    (grad_before_f,) = gelu_pull(grad_active)
    grad_before = grad_before_f.astype(BF)
    grad_normed_two = pair_sum(dot_rows(grad_before, up_full))
    grad_down_t = dot_cols(dy, active)
    grad_up = dot_cols(normed_two, grad_before)
    grad_up_bias = jnp.sum(grad_before.astype(F32), axis=0)
    branch = pair_sum(dot_rows(active, down_t))
    output = (middle_state + branch + down_bias.astype(F32)).astype(BF)[None]
    grad_middle_norm, grad_gain_two, grad_offset_two = norm_two_pull(grad_normed_two)
    grad_middle = grad_float + grad_middle_norm
    grad_attended = grad_middle.astype(BF)
    grad_out_bias = jnp.sum(grad_attended.astype(F32), axis=0)
    grad_out_t = dot_cols(grad_attended, mix_flat)
    grad_mixture = dot_rows(grad_attended, out_weight).astype(BF)

    by_head = lambda v: v.reshape(length, heads, HEAD_DIM)
    q3, k3, v3 = (by_head(flat(m)) for m in (queries, key_rows, value_rows))
    gm3 = by_head(grad_mixture)
    allowed = segments[:, None] == key_row
    block = 512

    def back_block(carry, portion):
        key_acc, value_acc = carry
        block_query, block_grad, block_allowed = portion
        scores = jnp.einsum("qhd,khd->hqk", block_query, k3, preferred_element_type=F32)
        scores = jnp.where(block_allowed[None], scores, -1e30)
        soft = jax.nn.softmax(scores, axis=-1)
        value_acc = value_acc + jnp.einsum(
            "hqk,qhd->khd", soft.astype(BF), block_grad, preferred_element_type=F32
        )
        grad_soft = jnp.einsum("qhd,khd->hqk", block_grad, v3, preferred_element_type=F32)
        inner = jnp.sum(soft * grad_soft, axis=-1, keepdims=True)
        grad_scores = (soft * (grad_soft - inner)).astype(BF)
        grad_query = jnp.einsum("hqk,khd->qhd", grad_scores, k3, preferred_element_type=F32)
        key_acc = key_acc + jnp.einsum(
            "hqk,qhd->khd", grad_scores, block_query, preferred_element_type=F32
        )
        return (key_acc, value_acc), grad_query * 0.125

    empty = jnp.zeros((length, heads, HEAD_DIM), F32)
    (grad_keys, grad_values), grad_queries = lax.scan(
        back_block, (empty, empty),
        tuple(v.reshape((length // block, block) + v.shape[1:]) for v in (q3, gm3, allowed)),
    )
    grad_queries, grad_keys, grad_values = (
        g.reshape(length, cols).astype(BF) for g in (grad_queries, grad_keys, grad_values)
    )
    grad_qv_bias = jnp.stack(
        [jnp.sum(g.astype(F32), axis=0) for g in (grad_queries, grad_values)]
    )
    grad_qkv = jnp.stack([dot_cols(normed, g) for g in (grad_queries, grad_keys, grad_values)])
    grad_normed = pair_sum(
        dot_rows(grad_queries, qkv_weight[0])
        + dot_rows(grad_keys, qkv_weight[1])
        + dot_rows(grad_values, qkv_weight[2])
    )
    grad_input_norm, grad_gain_one, grad_offset_one = norm_one_pull(grad_normed)
    tokens_grad = (grad_middle + grad_input_norm).astype(BF)[None]

    def scatter(grad, dim):
        return lax.psum_scatter(
            grad.astype(BF), "seq", scatter_dimension=dim, tiled=True
        ).astype(F32)

    summed_up, summed_down = scatter(grad_up, 0), scatter(grad_down_t, 0).T
    summed_qkv, summed_out = scatter(grad_qkv, 1), scatter(grad_out_t, 0).T
    smalls = lax.psum(
        (
            grad_gain_one, grad_offset_one, grad_qv_bias, grad_out_bias,
            grad_gain_two, grad_offset_two, grad_up_bias, grad_down_bias,
        ),
        "seq",
    )
    return (
        output, tokens_grad, smalls[0], smalls[1], summed_qkv, smalls[2], summed_out, smalls[3],
        smalls[4], smalls[5], summed_up, smalls[6], summed_down, smalls[7],
    )


def solution(mesh):
    chosen = generic_body
    if mesh.shape["head"] == 2 and mesh.shape["seq"] == SEQ_SIZE:
        chosen = fast_body
    return jax.shard_map(
        chosen,
        mesh=mesh,
        in_specs=(
            P("seq", None, None),
            P("seq", None),
            P("seq", None),
            P(),
            P(),
            P(None, None, "head"),
            P(None, "head"),
            P("head", None),
            P(),
            P(),
            P(),
            P("seq", "head"),
            P("head"),
            P("head", "seq"),
            P(),
            P("seq", None, None),
        ),
        out_specs=(
            P("seq", None, None),
            P("seq", None, None),
            P(),
            P(),
            P(None, "seq", "head"),
            P(None, "head"),
            P("head", "seq"),
            P(),
            P(),
            P(),
            P("seq", "head"),
            P("head"),
            P("head", "seq"),
            P(),
        ),
        check_vma=False,
    )
```

```python
import math

import jax
import jax.numpy as jnp
from jax import lax
from jax.experimental import pallas as pl
from jax.experimental.pallas import tpu as pltpu
from jax.sharding import PartitionSpec as P

HEAD_DIM = 64


def layer_norm(values_in, scaling, offset):
    middle = jnp.mean(values_in, axis=-1, keepdims=True)
    centred = values_in - middle
    spread = jnp.mean(centred * centred, axis=-1, keepdims=True)
    return centred * lax.rsqrt(spread + 1e-05) * scaling + offset


def gelu_exact(values_in):
    return 0.5 * values_in * (1.0 + jax.scipy.special.erf(values_in * 0.7071067811865476))


def dot_rows(left, right):
    return lax.dot_general(
        left, right, (((1,), (1,)), ((), ())), preferred_element_type=jnp.float32
    )


def dot_cols(left, right):
    return lax.dot_general(
        left, right, (((0,), (0,)), ((), ())), preferred_element_type=jnp.float32
    )


def masked_scores(block_query, seq_keys, block_segments, seq_segments, seq_context, factor):
    raw_scores = (
        jnp.einsum("qhd,khd->hqk", block_query, seq_keys, preferred_element_type=jnp.float32)
        * factor
    )
    allowed = (block_segments[:, None] == seq_segments[None, :]) & (seq_context[None, :] == 1)
    return jnp.where(allowed[None], raw_scores, -1e30)


def generic_body(
    tokens,
    segment_ids,
    context_flags,
    ln1_gain,
    ln1_bias,
    qkv_weight,
    qv_bias,
    out_weight,
    out_bias,
    ln2_gain,
    ln2_bias,
    up_weight,
    up_bias,
    down_weight,
    down_bias,
    cotangent,
):
    seq_count, length, width = tokens.shape
    row_count = seq_count * length
    local_cols = qkv_weight.shape[2]
    head_count = local_cols // HEAD_DIM
    factor = 1.0 / math.sqrt(HEAD_DIM)
    block = min(512, length)
    blocks = length // block
    gain_one = ln1_gain.astype(jnp.float32)
    offset_one = ln1_bias.astype(jnp.float32)
    gain_two = ln2_gain.astype(jnp.float32)
    offset_two = ln2_bias.astype(jnp.float32)
    flat_in = tokens.astype(jnp.float32).reshape(row_count, width)
    normed_f, norm_one_pull = jax.vjp(layer_norm, flat_in, gain_one, offset_one)
    normed = normed_f.astype(jnp.bfloat16)
    queries = (
        jnp.dot(normed, qkv_weight[0], preferred_element_type=jnp.float32)
        + qv_bias[0].astype(jnp.float32)
    ).astype(jnp.bfloat16)
    key_rows = jnp.dot(normed, qkv_weight[1], preferred_element_type=jnp.float32).astype(
        jnp.bfloat16
    )
    value_rows = (
        jnp.dot(normed, qkv_weight[2], preferred_element_type=jnp.float32)
        + qv_bias[1].astype(jnp.float32)
    ).astype(jnp.bfloat16)

    def per_sequence(array):
        return array.reshape(seq_count, length, head_count, HEAD_DIM)

    def attend_sequence(member):
        seq_query, seq_keys, seq_values, seq_segments, seq_context = member

        def attend_block(portion):
            block_query, block_segments = portion
            scores = masked_scores(
                block_query, seq_keys, block_segments, seq_segments, seq_context, factor
            )
            row_top = jnp.max(scores, axis=-1, keepdims=True)
            exponent = jnp.exp(scores - row_top)
            row_total = jnp.sum(exponent, axis=-1, keepdims=True)
            soft_weights = (exponent / row_total).astype(jnp.bfloat16)
            block_mix = jnp.einsum(
                "hqk,khd->qhd", soft_weights, seq_values, preferred_element_type=jnp.float32
            )
            return (block_mix.astype(jnp.bfloat16), row_top + jnp.log(row_total))

        return lax.map(
            attend_block,
            (
                seq_query.reshape(blocks, block, head_count, HEAD_DIM),
                seq_segments.reshape(blocks, block),
            ),
        )

    mixture, log_totals = lax.map(
        attend_sequence,
        (
            per_sequence(queries),
            per_sequence(key_rows),
            per_sequence(value_rows),
            segment_ids,
            context_flags,
        ),
    )
    mixture = mixture.reshape(row_count, local_cols)
    partial_out = jnp.dot(mixture, out_weight, preferred_element_type=jnp.float32)
    grad_rows_all = cotangent.reshape(row_count, width)
    grad_float_all = grad_rows_all.astype(jnp.float32)
    grad_down_bias = jnp.sum(grad_float_all, axis=0)
    attended = lax.psum(partial_out, "head") + out_bias.astype(jnp.float32)
    middle_state = flat_in + attended
    normed_two_f, norm_two_pull = jax.vjp(layer_norm, middle_state, gain_two, offset_two)
    normed_two = normed_two_f.astype(jnp.bfloat16)
    up_part, down_part, up_shift = (
        lax.all_gather(up_weight, "head", axis=1, tiled=True),
        lax.all_gather(down_weight, "head", axis=0, tiled=True),
        lax.all_gather(up_bias, "head", axis=0, tiled=True),
    )
    up_full, down_full = (
        lax.all_gather(up_part, "seq", axis=0, tiled=True),
        lax.all_gather(down_part, "seq", axis=1, tiled=True),
    )
    before = jnp.dot(normed_two, up_full, preferred_element_type=jnp.float32) + up_shift.astype(
        jnp.float32
    )
    active_f, gelu_pull = jax.vjp(gelu_exact, before)
    active = active_f.astype(jnp.bfloat16)
    branch_out = jnp.dot(active, down_full, preferred_element_type=jnp.float32)
    final_rows = (middle_state + branch_out + down_bias.astype(jnp.float32)).astype(jnp.bfloat16)
    output = final_rows.reshape(tokens.shape)
    grad_float = grad_rows_all.astype(jnp.float32)
    grad_down = dot_cols(active, grad_rows_all)
    grad_active = dot_rows(grad_rows_all, down_full)
    (grad_before_f,) = gelu_pull(grad_active)
    grad_before = grad_before_f.astype(jnp.bfloat16)
    grad_up = dot_cols(normed_two, grad_before)
    grad_up_bias = jnp.sum(grad_before.astype(jnp.float32), axis=0)
    grad_normed_two = dot_rows(grad_before, up_full)
    grad_middle_norm, grad_gain_two, grad_offset_two = norm_two_pull(grad_normed_two)
    grad_middle = grad_float + grad_middle_norm
    ff_part = up_weight.shape[1]
    start_col = lax.axis_index("head") * ff_part
    grad_up = lax.dynamic_slice_in_dim(grad_up, start_col, ff_part, 1)
    grad_down = lax.dynamic_slice_in_dim(grad_down, start_col, ff_part, 0)
    grad_up_bias = lax.dynamic_slice_in_dim(grad_up_bias, start_col, ff_part, 0)
    grad_attended = grad_middle.astype(jnp.bfloat16)
    grad_out_bias = jnp.sum(grad_attended.astype(jnp.float32), axis=0)
    grad_out = dot_cols(mixture, grad_attended)
    grad_mixture = dot_rows(grad_attended, out_weight).astype(jnp.bfloat16)

    def back_sequence(member):
        seq_query, seq_keys, seq_values, seq_grad, seq_logs, seq_segments, seq_context = member

        def back_block(carry, portion):
            key_acc, value_acc = carry
            block_query, block_grad, block_logs, block_segments = portion
            scores = masked_scores(
                block_query, seq_keys, block_segments, seq_segments, seq_context, factor
            )
            soft_weights = jnp.exp(scores - block_logs)
            value_acc = value_acc + jnp.einsum(
                "hqk,qhd->khd",
                soft_weights.astype(jnp.bfloat16),
                block_grad,
                preferred_element_type=jnp.float32,
            )
            grad_soft = jnp.einsum(
                "qhd,khd->hqk", block_grad, seq_values, preferred_element_type=jnp.float32
            )
            row_inner = jnp.sum(soft_weights * grad_soft, axis=-1, keepdims=True)
            grad_scores = (soft_weights * (grad_soft - row_inner)).astype(jnp.bfloat16)
            grad_query = (
                jnp.einsum(
                    "hqk,khd->qhd", grad_scores, seq_keys, preferred_element_type=jnp.float32
                )
                * factor
            )
            key_acc = (
                key_acc
                + jnp.einsum(
                    "hqk,qhd->khd", grad_scores, block_query, preferred_element_type=jnp.float32
                )
                * factor
            )
            return ((key_acc, value_acc), grad_query)

        empty = jnp.zeros((length, head_count, HEAD_DIM), jnp.float32)
        (key_acc, value_acc), grad_query = lax.scan(
            back_block,
            (empty, empty),
            (
                seq_query.reshape(blocks, block, head_count, HEAD_DIM),
                seq_grad.reshape(blocks, block, head_count, HEAD_DIM),
                seq_logs,
                seq_segments.reshape(blocks, block),
            ),
        )
        return (grad_query, key_acc, value_acc)

    grad_queries, grad_keys, grad_values = lax.map(
        back_sequence,
        (
            per_sequence(queries),
            per_sequence(key_rows),
            per_sequence(value_rows),
            per_sequence(grad_mixture),
            log_totals,
            segment_ids,
            context_flags,
        ),
    )
    grad_queries = grad_queries.reshape(row_count, local_cols).astype(jnp.bfloat16)
    grad_keys = grad_keys.reshape(row_count, local_cols).astype(jnp.bfloat16)
    grad_values = grad_values.reshape(row_count, local_cols).astype(jnp.bfloat16)
    grad_qv_bias = jnp.stack(
        [
            jnp.sum(grad_queries.astype(jnp.float32), axis=0),
            jnp.sum(grad_values.astype(jnp.float32), axis=0),
        ]
    )
    grad_qkv = jnp.stack(
        [dot_cols(normed, grad_queries), dot_cols(normed, grad_keys), dot_cols(normed, grad_values)]
    )
    grad_normed = (
        dot_rows(grad_queries, qkv_weight[0])
        + dot_rows(grad_keys, qkv_weight[1])
        + dot_rows(grad_values, qkv_weight[2])
    )
    grad_normed = lax.psum(grad_normed, "head")
    grad_input_norm, grad_gain_one, grad_offset_one = norm_one_pull(grad_normed)
    tokens_grad = (grad_middle + grad_input_norm).astype(jnp.bfloat16).reshape(tokens.shape)
    summed_qkv, summed_out, summed_up, summed_down = (
        lax.psum_scatter(
            grad_qkv.astype(jnp.bfloat16), "seq", scatter_dimension=1, tiled=True
        ).astype(jnp.float32),
        lax.psum_scatter(
            grad_out.astype(jnp.bfloat16), "seq", scatter_dimension=1, tiled=True
        ).astype(jnp.float32),
        lax.psum_scatter(
            grad_up.astype(jnp.bfloat16), "seq", scatter_dimension=0, tiled=True
        ).astype(jnp.float32),
        lax.psum_scatter(
            grad_down.astype(jnp.bfloat16), "seq", scatter_dimension=1, tiled=True
        ).astype(jnp.float32),
    )
    smalls = lax.psum(
        (
            grad_gain_one,
            grad_offset_one,
            grad_qv_bias,
            grad_out_bias,
            grad_gain_two,
            grad_offset_two,
            grad_up_bias,
            grad_down_bias,
        ),
        "seq",
    )
    return (
        output,
        tokens_grad,
        smalls[0],
        smalls[1],
        summed_qkv,
        smalls[2],
        summed_out,
        smalls[3],
        smalls[4],
        smalls[5],
        summed_up,
        smalls[6],
        summed_down,
        smalls[7],
    )


MESH = pl.DeviceIdType.MESH
BF = jnp.bfloat16
F32 = jnp.float32
BLOCK = 256
STRIP = 128
GROUP = 2
PAIR = 2 * HEAD_DIM
Z_SIZE, Y_SIZE, CORES = 4, 2, 2
SEQ_SIZE = Z_SIZE * Y_SIZE * CORES


def nn(left, right):
    return jnp.dot(left, right, preferred_element_type=F32)


def place():
    me = lax.axis_index("seq")
    head = lax.axis_index("head")
    core = me % 2
    y = (me // 2) % 2
    across = {"seq": me, "head": 1 - head}
    core_mate = {"seq": me + 1 - 2 * core, "head": head}
    y_mate = {"seq": me + 2 - 4 * y, "head": head}
    z_mates = [{"seq": (me + 4 * d) % SEQ_SIZE, "head": head} for d in (1, 2, 3)]
    return me, head, core, y, across, core_mate, y_mate, z_mates


def greet(others):
    barrier = pltpu.get_barrier_semaphore()
    for other in others:
        pl.semaphore_signal(barrier, inc=1, device_id=other, device_id_type=MESH)
    pl.semaphore_wait(barrier, len(others))


def remote(src, dst, send_sem, recv_sem, other):
    return pltpu.make_async_remote_copy(
        src_ref=src, dst_ref=dst, send_sem=send_sem, recv_sem=recv_sem,
        device_id=other, device_id_type=MESH,
    )


def norm_stats(rows):
    middle = jnp.mean(rows, axis=-1, keepdims=True)
    centred = rows - middle
    spread = jnp.mean(centred * centred, axis=-1, keepdims=True)
    return centred, lax.rsqrt(spread + 1e-05)


def turn(block):
    return jnp.transpose(block)


def norm_back(inner, unit, scale):
    return scale * (
        inner
        - jnp.mean(inner, axis=-1, keepdims=True)
        - unit * jnp.mean(inner * unit, axis=-1, keepdims=True)
    )


def sum_rows(block):
    return jnp.sum(block, axis=0, keepdims=True)


def fwd_kernel(
    x_ref, seg_col, key_row, gain, offset, wqkv, qv_bias, wout, out_bias, shard,
    q_ref, k_ref, v_ref, mix_ref, mid_ref, normed_t, wff,
    bias, wout_x, mix_x,
    zs, zr, ys, yr, cs, cr, xs, xr, local,
):
    length, width = x_ref.shape
    blocks = length // BLOCK
    pairs = q_ref.shape[0]
    half = shard.shape[0] // 2
    me, head, core, y, across, core_mate, y_mate, z_mates = place()
    greet([across, core_mate, y_mate, *z_mates])

    out_copy = remote(wout, wout_x, xs.at[0], xr.at[0], across)
    out_copy.start()
    part = [pl.ds(u * half, half) for u in range(2)]
    own = [
        pltpu.make_async_copy(shard.at[part[u]], wff.at[part[u], me], local.at[u])
        for u in range(2)
    ]

    def column(first):
        return [first] + [(first + SEQ_SIZE - 4 * d) % SEQ_SIZE for d in (1, 2, 3)]

    from_core = me + 1 - 2 * core
    z_own, z_mate = column(me), column(me + 2 - 4 * y)
    mine = z_own + z_mate
    theirs = column(from_core) + column(from_core + 2 - 4 * y)

    def z_copy(u, d):
        n = u * 3 + d - 1
        return remote(
            shard.at[part[u]], wff.at[part[u], me], zs.at[n], zr.at[n], z_mates[d - 1]
        )

    def z_arrival(u, d):
        n = u * 3 + d - 1
        slot = wff.at[part[u], z_own[d]]
        return remote(slot, slot, zs.at[n], zr.at[n], z_mates[d - 1])

    def y_copy(u, d):
        n = u * 4 + d
        src = shard.at[part[u]] if d == 0 else wff.at[part[u], z_own[d]]
        return remote(src, wff.at[part[u], z_own[d]], ys.at[n], yr.at[n], y_mate)

    def y_arrival(u, d):
        n = u * 4 + d
        slot = wff.at[part[u], z_mate[d]]
        return remote(slot, slot, ys.at[n], yr.at[n], y_mate)

    def c_copy(u, e):
        n = u * 8 + e
        src = shard.at[part[u]] if e == 0 else wff.at[part[u], mine[e]]
        return remote(src, wff.at[part[u], mine[e]], cs.at[n], cr.at[n], core_mate)

    def c_arrival(u, e):
        n = u * 8 + e
        slot = wff.at[part[u], theirs[e]]
        return remote(slot, slot, cs.at[n], cr.at[n], core_mate)

    for u in range(2):
        for d in (1, 2, 3):
            z_copy(u, d).start()
        y_copy(u, 0).start()
        c_copy(u, 0).start()
        own[u].start()

    def z_event(u, d):
        z_arrival(u, d).wait_recv()
        y_copy(u, d).start()
        c_copy(u, d).start()

    def y_event(u, d):
        y_arrival(u, d).wait_recv()
        c_copy(u, 4 + d).start()

    plan = {
        1: [(z_event, 0, 1), (y_event, 0, 0)], 2: [(z_event, 0, 2)], 4: [(z_event, 0, 3)],
        5: [(y_event, 0, 1)], 6: [(z_event, 1, 1), (y_event, 1, 0)], 7: [(y_event, 0, 2)],
        8: [(z_event, 1, 2)], 9: [(y_event, 0, 3)], 11: [(z_event, 1, 3)], 12: [(y_event, 1, 1)],
        14: [(y_event, 1, 2)],
    }
    last = [(y_event, 1, 3)]

    gains, offsets = gain[...], offset[...]

    def project(b, _):
        rows = pl.ds(pl.multiple_of(b * BLOCK, BLOCK), BLOCK)
        centred, scale = norm_stats(x_ref[rows, :].astype(F32))
        block = (centred * scale * gains + offsets).astype(BF)
        normed_t[b] = turn(block)
        queries = ((nn(block, wqkv[0]) + qv_bias[0:1, :]).astype(BF) * 0.125).astype(BF)
        keys = nn(block, wqkv[1]).astype(BF)
        values = (nn(block, wqkv[2]) + qv_bias[1:2, :]).astype(BF)
        for p in range(pairs):
            cols = slice(p * PAIR, (p + 1) * PAIR)
            q_ref[p, rows, :] = queries[:, cols]
            k_ref[p, rows, :] = keys[:, cols]
            v_ref[p, rows, :] = values[:, cols]
        return 0

    lax.fori_loop(0, blocks, project, 0)

    low_lanes = lax.broadcasted_iota(jnp.int32, (1, PAIR), 1) < HEAD_DIM
    zero = jnp.zeros((1, PAIR), BF)

    def mixture_copy(b):
        rows = pl.ds(b * BLOCK, BLOCK)
        return remote(
            mix_ref.at[:, rows, :], mix_x.at[:, rows, :], xs.at[1 + b], xr.at[1 + b], across
        )

    def attend(t, _):
        b, p = t // pairs, t % pairs
        rows = pl.ds(pl.multiple_of(b * BLOCK, BLOCK), BLOCK)

        @pl.when(p == 0)
        def _():
            seen = seg_col[rows, :] == key_row[...]
            bias[...] = jnp.where(seen, 0.0, -1e30)

        queries, keys, values = q_ref[p, rows, :], k_ref[p], v_ref[p]
        parts = []
        for low in (True, False):
            own_lanes = low_lanes if low else jnp.logical_not(low_lanes)
            scores = dot_rows(jnp.where(own_lanes, queries, zero), keys) + bias[...]
            top = jnp.max(scores, axis=-1, keepdims=True)
            exponent = jnp.exp(scores - top)
            total = jnp.sum(exponent, axis=-1, keepdims=True)
            parts.append(nn(exponent.astype(BF), values) / total)
        mix_ref[p, rows, :] = jnp.where(low_lanes, parts[0], parts[1]).astype(BF)
        for step, events in plan.items():
            @pl.when(t == step)
            def _(events=events):
                for event, u, d in events:
                    event(u, d)
        for b_done in range(blocks):
            @pl.when(t == (b_done + 1) * pairs - 1)
            def _(b_done=b_done):
                mixture_copy(b_done).start()
        return 0

    lax.fori_loop(0, blocks * pairs, attend, 0)
    for event, u, d in last:
        event(u, d)
    out_copy.wait_recv()
    for b in range(blocks):
        mixture_copy(b).wait_recv()
        rows = pl.ds(b * BLOCK, BLOCK)
        ours = jnp.concatenate([mix_ref[p, rows, :] for p in range(pairs)], axis=-1)
        other = jnp.concatenate([mix_x[p, rows, :] for p in range(pairs)], axis=-1)
        attended = nn(ours, wout[...]) + nn(other, wout_x[...]) + out_bias[...]
        mid_ref[rows, :] = x_ref[rows, :].astype(F32) + attended

    for u in range(2):
        for e in range(8):
            c_arrival(u, e).wait_recv()
    out_copy.wait_send()
    for b in range(blocks):
        mixture_copy(b).wait_send()
    for u in range(2):
        own[u].wait()
        for d in (1, 2, 3):
            z_copy(u, d).wait_send()
        for d in range(4):
            y_copy(u, d).wait_send()
        for e in range(8):
            c_copy(u, e).wait_send()


VMEM_SPEC = pl.BlockSpec(memory_space=pltpu.VMEM)
ANY_SPEC = pl.BlockSpec(memory_space=pl.ANY)
VMEM_LIMIT = 62 * 2**20


def shape_of(dims, dtype):
    return jax.ShapeDtypeStruct(tuple(dims), dtype)


def run_fwd(x, seg_col, key_row, gain, offset, wqkv, qv_bias, wout, out_bias, shard):
    length, width = x.shape
    pairs = wqkv.shape[2] // PAIR
    blocks = length // BLOCK
    chunks, depth, chunk = shard.shape
    lanes = shape_of((pairs, length, PAIR), BF)
    dma = pltpu.SemaphoreType.DMA
    return pl.pallas_call(
        fwd_kernel,
        out_shape=[
            lanes, lanes, lanes, lanes,
            shape_of((length, width), F32),
            shape_of((blocks, width, BLOCK), BF),
            shape_of((chunks, SEQ_SIZE, depth, chunk), BF),
        ],
        in_specs=[VMEM_SPEC] * 9 + [ANY_SPEC],
        out_specs=[VMEM_SPEC] * 6 + [ANY_SPEC],
        scratch_shapes=[
            pltpu.VMEM((BLOCK, length), F32),
            pltpu.VMEM(wout.shape, BF),
            pltpu.VMEM((pairs, length, PAIR), BF),
            dma((6,)), dma((6,)), dma((8,)), dma((8,)), dma((16,)), dma((16,)),
            dma((1 + blocks,)), dma((1 + blocks,)), dma((2,)),
        ],
        compiler_params=pltpu.CompilerParams(
            collective_id=0, has_side_effects=True, vmem_limit_bytes=VMEM_LIMIT
        ),
    )(x, seg_col, key_row, gain, offset, wqkv, qv_bias, wout, out_bias, shard)


CHUNK = 512
INV_ROOT_TWO = 0.7071067811865476
INV_ROOT_TWO_PI = 0.3989422804014327


def ff_kernel(
    mid_hbm, dy_ref, wff, up_bias, gain, offset, wout,
    branch_ref, gmid_hbm, ga_t, gm_ref, summed, small_ref,
    normed, normed_t, dy_t, active, before_grad, gnt_acc, gnt_own, gnt_x, whole, from_mate,
    held, ready,
    xs, xr, cs, cr, ls, ws, ss,
):
    length, width = dy_ref.shape
    blocks = length // BLOCK
    chunks = wff.shape[0]
    half = chunks // 2
    pairs = gm_ref.shape[0]
    me, head, core, y, across, core_mate, y_mate, z_mates = place()
    greet([across, core_mate])
    gains, offsets = gain[...], offset[...]
    small_ref[...] = jnp.zeros_like(small_ref)

    def load(n):
        rows = pl.ds(n % blocks * BLOCK, BLOCK)
        return pltpu.make_async_copy(mid_hbm.at[rows, :], held.at[n % 2], ls.at[n % 2])

    def store(b):
        rows = pl.ds(b * BLOCK, BLOCK)
        return pltpu.make_async_copy(ready.at[b % 2], gmid_hbm.at[rows, :], ws.at[b % 2])

    load(0).start()
    load(1).start()

    def gnt_copy(b):
        return remote(gnt_own.at[b], gnt_x.at[b], xs.at[b], xr.at[b], across)

    def core_copy(n):
        return remote(
            whole.at[n, :, :, 1 - core], from_mate.at[n], cs.at[n], cr.at[n], core_mate
        )

    def forward(t, _):
        b, n = t // half, t % half
        rows = pl.ds(pl.multiple_of(b * BLOCK, BLOCK), BLOCK)

        for b_next in range(blocks):
            @pl.when(t == b_next * half)
            def _(b_next=b_next):
                load(b_next).wait()

        @pl.when(n == 0)
        def _():
            centred, scale = norm_stats(held[b % 2])
            block = (centred * scale * gains + offsets).astype(BF)
            normed[...] = block
            normed_t[b] = turn(block)
            dy_t[b] = turn(dy_ref[rows, :])
            small_ref[3:4, :] += sum_rows(dy_ref[rows, :].astype(F32))

        up = wff[n]
        before = nn(normed[...], up) + up_bias[n]
        spread = 0.5 * (1.0 + lax.erf(before * INV_ROOT_TWO))
        active[n, rows, :] = (before * spread).astype(BF)
        slope = spread + before * (INV_ROOT_TWO_PI * jnp.exp(before * before * -0.5))
        grad = (nn(dy_ref[rows, :], wff[half + n]) * slope).astype(BF)
        before_grad[n, rows, :] = grad
        small_ref[pl.ds(8 + n, 1), 0:CHUNK] += sum_rows(grad.astype(F32))
        back = dot_rows(grad, up)

        @pl.when(n == 0)
        def _():
            gnt_acc[...] = back

        @pl.when(n > 0)
        def _():
            gnt_acc[...] += back

        for b_done in range(blocks):
            @pl.when(t == (b_done + 1) * half - 1)
            def _(b_done=b_done):
                load(b_done + 2).start()
                gnt_own[b_done] = gnt_acc[...].astype(BF)
                gnt_copy(b_done).start()
        return 0

    lax.fori_loop(0, blocks * half, forward, 0)

    def weight_grads(left_t, right, first):
        top, planes = width // 2, Z_SIZE // 2

        def one(t, _):
            n, side = t // 2, t % 2
            cut = pl.ds(pl.multiple_of(side * top, top), top)
            total = nn(left_t[0, cut, :], right[n, pl.ds(0, BLOCK), :])
            for b in range(1, blocks):
                total += nn(left_t[b, cut, :], right[n, pl.ds(b * BLOCK, BLOCK), :])
            piece = total.astype(BF).reshape((planes,) + whole.shape[2:])
            whole[first + n, pl.ds(side * planes, planes)] = piece

            @pl.when(side == 1)
            def _():
                core_copy(first + n).start()

            return 0

        lax.fori_loop(0, 2 * half, one, 0)

    weight_grads(dy_t, active, half)
    weight_grads(normed_t, before_grad, 0)

    def branch(b, _):
        rows = pl.ds(pl.multiple_of(b * BLOCK, BLOCK), BLOCK)
        total = dot_rows(active[0, rows, :], wff[half])
        for n in range(1, half):
            total += dot_rows(active[n, rows, :], wff[half + n])
        branch_ref[rows, :] = total.astype(BF)
        return 0

    lax.fori_loop(0, blocks, branch, 0)

    def add_mate(n, _):
        core_copy(n).wait()
        both = whole[n, :, :, core].astype(F32) + from_mate[n].astype(F32)
        from_mate[n] = both.astype(BF)
        return 0

    lax.fori_loop(half, chunks, add_mate, 0)
    lax.fori_loop(0, half, add_mate, 0)
    keep = pltpu.make_async_copy(from_mate, summed, ss.at[0])
    keep.start()

    strips = BLOCK // STRIP
    for b in range(blocks):
        gnt_copy(b).wait()
        load(blocks + b).wait()
        if b >= 2:
            store(b - 2).wait()

        def through_norm(n, _, b=b):
            rows = pl.ds(pl.multiple_of(n * STRIP, STRIP), STRIP)
            full = pl.ds(pl.multiple_of(b * BLOCK + n * STRIP, STRIP), STRIP)
            grad = gnt_own[b, rows, :].astype(F32) + gnt_x[b, rows, :].astype(F32)
            centred, scale = norm_stats(held[b % 2, rows, :])
            unit = centred * scale
            small_ref[0:1, :] += sum_rows(grad * unit)
            small_ref[1:2, :] += sum_rows(grad)
            total = dy_ref[full, :].astype(F32) + norm_back(grad * gains, unit, scale)
            ready[b % 2, rows, :] = total
            low = total.astype(BF)
            small_ref[2:3, :] += sum_rows(low.astype(F32))
            ga_t[b, :, rows] = turn(low)
            mixed = dot_rows(low, wout[...]).astype(BF)
            for p in range(pairs):
                gm_ref[p, full, :] = mixed[:, p * PAIR:(p + 1) * PAIR]
            return 0

        lax.fori_loop(0, strips, through_norm, 0)
        store(b).start()
        if b + 2 < blocks:
            load(blocks + b + 2).start()
    store(blocks - 2).wait()
    store(blocks - 1).wait()
    keep.wait()


def run_ff(middle, dy, wff, up_bias, gain, offset, wout):
    length, width = middle.shape
    chunks = wff.shape[0]
    half = chunks // 2
    blocks = length // BLOCK
    pairs = wout.shape[0] // PAIR
    depth = width // SEQ_SIZE
    dma = pltpu.SemaphoreType.DMA
    turned = pltpu.VMEM((blocks, width, BLOCK), BF)
    rows = pltpu.VMEM((blocks, BLOCK, width), BF)
    hidden = pltpu.VMEM((half, length, CHUNK), BF)
    return pl.pallas_call(
        ff_kernel,
        out_shape=[
            shape_of((length, width), BF),
            shape_of((length, width), F32),
            shape_of((blocks, width, BLOCK), BF),
            shape_of((pairs, length, PAIR), BF),
            shape_of((chunks, Z_SIZE, Y_SIZE, depth, CHUNK), BF),
            shape_of((16, width), F32),
        ],
        in_specs=[ANY_SPEC] + [VMEM_SPEC] * 6,
        out_specs=[VMEM_SPEC, ANY_SPEC, VMEM_SPEC, VMEM_SPEC, ANY_SPEC, VMEM_SPEC],
        scratch_shapes=[
            pltpu.VMEM((BLOCK, width), BF), turned, turned, hidden, hidden,
            pltpu.VMEM((BLOCK, width), F32), rows, rows,
            pltpu.VMEM((chunks, Z_SIZE, Y_SIZE, CORES, depth, CHUNK), BF),
            pltpu.VMEM((chunks, Z_SIZE, Y_SIZE, depth, CHUNK), BF),
            pltpu.VMEM((2, BLOCK, width), F32), pltpu.VMEM((2, BLOCK, width), F32),
            dma((blocks,)), dma((blocks,)), dma((chunks,)), dma((chunks,)),
            dma((2,)), dma((2,)), dma((1,)),
        ],
        compiler_params=pltpu.CompilerParams(
            collective_id=1, has_side_effects=True, vmem_limit_bytes=VMEM_LIMIT
        ),
    )(middle, dy, wff, up_bias, gain, offset, wout)


def back_kernel(
    q_ref, k_ref, v_ref, mix_ref, gm_ref, ga_t, normed_t, wqkv, x_ref,
    seg_rows, key_col, gain, down_bias, small_in, mid_hbm, gmid_hbm, ff_part, branch,
    out_ref, tokens_ref, ff_sum, at_sum, small_out,
    key_acc, value_acc, dq, dk, dv, whole, mate, at_y, at_z, ff_y, ff_z, gn_own, gn_x,
    branch_x, branch_own, ff_own, held, small_own, small_z, small_y, small_c,
    bs, br, fys, fyr, fzs, fzr, acs, acr, ays, ayr, azs, azr, gs, gr, ls, ms, mr, os, hs,
):
    length, width = x_ref.shape
    blocks = length // BLOCK
    strips = length // STRIP
    pairs = q_ref.shape[0]
    chunks = ff_part.shape[0]
    groups = chunks // GROUP
    me, head, core, y, across, core_mate, y_mate, z_mates = place()
    z = me // (Y_SIZE * CORES)
    greet([across, core_mate, y_mate, *z_mates])

    def part(b):
        return pl.ds(b * BLOCK, BLOCK)

    def branch_copy(b):
        return remote(branch.at[part(b), :], branch_x.at[part(b), :], bs.at[b], br.at[b], across)

    def load(n):
        source = mid_hbm if n < blocks else gmid_hbm
        return pltpu.make_async_copy(
            source.at[part(n % blocks), :], held.at[n % 2], ls.at[n % 2]
        )

    def taken(n):
        if n + 2 < 2 * blocks:
            load(n + 2).start()

    def group(g):
        return pl.ds(g * GROUP, GROUP)

    def ff_y_copy(g):
        return remote(
            ff_part.at[group(g), :, 1 - y], ff_y.at[group(g)], fys.at[g], fyr.at[g], y_mate
        )

    def ff_z_copy(g, d):
        n = g * 3 + d - 1
        return remote(
            ff_y.at[group(g), (z + d) % Z_SIZE], ff_z.at[d - 1, group(g)],
            fzs.at[n], fzr.at[n], z_mates[d - 1],
        )

    def branch_load(b):
        return pltpu.make_async_copy(branch.at[part(b), :], branch_own.at[b % 2], hs.at[b % 2])

    def ff_load(g):
        return pltpu.make_async_copy(
            ff_part.at[group(g), :, y], ff_own.at[g % 2], os.at[g % 2]
        )

    def ff_y_event(g):
        ff_y_copy(g).wait_recv()
        ff_load(g).wait()
        for n in range(g * GROUP, (g + 1) * GROUP):
            own = ff_own[g % 2, n % GROUP]
            ff_y[n] = (ff_y[n].astype(F32) + own.astype(F32)).astype(BF)
        if g + 2 < groups:
            ff_load(g + 2).start()
        for d in (1, 2, 3):
            ff_z_copy(g, d).start()

    def ff_z_event(g):
        for d in (1, 2, 3):
            ff_z_copy(g, d).wait_recv()
        for n in range(g * GROUP, (g + 1) * GROUP):
            total = ff_y[n, z].astype(F32)
            for d in (1, 2, 3):
                total += ff_z[d - 1, n].astype(F32)
            ff_sum[n] = total

    def at_c_copy(p):
        return remote(whole.at[p, :, :, 1 - core], mate.at[p], acs.at[p], acr.at[p], core_mate)

    def at_y_copy(p):
        return remote(mate.at[p, :, 1 - y], at_y.at[p], ays.at[p], ayr.at[p], y_mate)

    def at_z_copy(p, d):
        n = p * 3 + d - 1
        return remote(
            at_y.at[p, (z + d) % Z_SIZE], at_z.at[d - 1, p], azs.at[n], azr.at[n], z_mates[d - 1]
        )

    def at_c_event(p):
        at_c_copy(p).wait_recv()
        mate[p] = (mate[p].astype(F32) + whole[p, :, :, core].astype(F32)).astype(BF)
        at_y_copy(p).start()

    def at_y_event(p):
        at_y_copy(p).wait_recv()
        at_y[p] = (at_y[p].astype(F32) + mate[p, :, y].astype(F32)).astype(BF)
        for d in (1, 2, 3):
            at_z_copy(p, d).start()

    def at_z_event(p):
        for d in (1, 2, 3):
            at_z_copy(p, d).wait_recv()
        total = at_y[p, z].astype(F32)
        for d in (1, 2, 3):
            total += at_z[d - 1, p].astype(F32)
        at_sum[p] = total

    def branch_event(b):
        branch_copy(b).wait_recv()
        load(b).wait()
        branch_load(b).wait()
        both = branch_own[b % 2].astype(F32) + branch_x[part(b), :].astype(F32)
        out_ref[part(b), :] = (held[b % 2] + both + down_bias[...]).astype(BF)
        taken(b)
        if b + 2 < blocks:
            branch_load(b + 2).start()

    for b in range(blocks):
        branch_copy(b).start()
    for n in range(2):
        load(n).start()
        branch_load(n).start()
        ff_load(n).start()
    for g in range(groups):
        ff_y_copy(g).start()

    plan = {
        9: [(ff_y_event, 0), (at_c_event, 0)], 11: [(branch_event, 0)], 15: [(ff_y_event, 1)],
        17: [(at_c_event, 1)], 19: [(branch_event, 1)], 21: [(ff_z_event, 0), (ff_y_event, 2)],
        25: [(at_c_event, 2)], 27: [(branch_event, 2)], 29: [(ff_y_event, 3), (ff_z_event, 1)],
    }

    low_lanes = lax.broadcasted_iota(jnp.int32, (1, PAIR), 1) < HEAD_DIM
    zero = jnp.zeros((1, PAIR), BF)

    def stacked(strip):
        return jnp.concatenate(
            [jnp.where(low_lanes, strip, zero), jnp.where(low_lanes, zero, strip)], axis=0
        )

    def attend(t, _):
        p, b = t // strips, t % strips
        rows = pl.ds(pl.multiple_of(b * STRIP, STRIP), STRIP)
        keys, values = k_ref[p], v_ref[p]
        queries, grads = stacked(q_ref[p, rows, :]), stacked(gm_ref[p, rows, :])
        seen = key_col[...] == jnp.concatenate([seg_rows[b], seg_rows[b]], axis=1)
        scores = jnp.where(seen, dot_rows(keys, queries), -1e30)
        exponent = jnp.exp(scores - jnp.max(scores, axis=0, keepdims=True))
        weights = exponent * (1.0 / sum_rows(exponent))
        grad_weights = dot_rows(values, grads)
        inner = sum_rows(weights * grad_weights)
        grad_scores = (weights * (grad_weights - inner)).astype(BF)
        to_values = nn(weights.astype(BF), grads)
        to_keys = nn(grad_scores, queries)
        to_queries = dot_cols(grad_scores, keys)
        dq[p, rows, :] = (
            jnp.where(low_lanes, to_queries[:STRIP], to_queries[STRIP:]) * 0.125
        ).astype(BF)

        @pl.when(b == 0)
        def _():
            key_acc[...] = to_keys
            value_acc[...] = to_values

        @pl.when(b > 0)
        def _():
            key_acc[...] += to_keys
            value_acc[...] += to_values

        @pl.when(b == strips - 1)
        def _():
            dk[p] = key_acc[...].astype(BF)
            dv[p] = value_acc[...].astype(BF)
            total = jnp.zeros((width, 3 * PAIR), F32)
            out_total = jnp.zeros((width, PAIR), F32)
            for n in range(blocks):
                right = jnp.concatenate(
                    [dq[p, part(n), :], dk[p, part(n), :], dv[p, part(n), :]], axis=1
                )
                total += nn(normed_t[n], right)
                out_total += nn(ga_t[n], mix_ref[p, part(n), :])
            both = jnp.concatenate([total, out_total], axis=1).astype(BF)
            whole[p] = both.reshape(whole.shape[1:])

        for p_done in range(pairs):
            @pl.when(t == (p_done + 1) * strips - 1)
            def _(p_done=p_done):
                at_c_copy(p_done).start()

        for step, events in plan.items():
            @pl.when(t == step)
            def _(events=events):
                for event, n in events:
                    event(n)
        return 0

    lax.fori_loop(0, pairs * strips, attend, 0)

    def gn_copy(b):
        return remote(gn_own.at[b], gn_x.at[b], gs.at[b], gr.at[b], across)

    for b in range(blocks):
        total = jnp.zeros((BLOCK, width), F32)
        for n, grad in enumerate((dq, dk, dv)):
            left = jnp.concatenate([grad[p, part(b), :] for p in range(pairs)], axis=1)
            total += dot_rows(left, wqkv[n])
        gn_own[b] = total.astype(BF)
        gn_copy(b).start()

    at_c_event(3)
    branch_event(3)
    small_own[...] = small_in[...]
    for p in range(pairs):
        first, second = p * PAIR, (pairs + p) * PAIR
        small_own[6:7, first:first + PAIR] = sum_rows(dq[p].astype(F32))
        small_own[6:7, second:second + PAIR] = sum_rows(dv[p].astype(F32))
    at_y_event(0)
    at_y_event(1)
    ff_z_event(2)
    gains = gain[...]
    for b in range(blocks):
        gn_copy(b).wait()
        load(blocks + b).wait()
        grad = gn_own[b].astype(F32) + gn_x[b].astype(F32)
        centred, scale = norm_stats(x_ref[part(b), :].astype(F32))
        unit = centred * scale
        small_own[4:5, :] += sum_rows(grad * unit)
        small_own[5:6, :] += sum_rows(grad)
        tokens_ref[part(b), :] = (
            held[b % 2] + norm_back(grad * gains, unit, scale)
        ).astype(BF)
        taken(blocks + b)
        if b == 0:
            at_y_event(2)
            at_y_event(3)
        if b == 1:
            ff_z_event(3)
            at_z_event(0)

    def small_z_copy(d):
        return remote(small_own, small_z.at[z], ms.at[d - 1], mr.at[d - 1], z_mates[d - 1])

    def small_z_arrival(d):
        slot = small_z.at[(z + Z_SIZE - d) % Z_SIZE]
        return remote(slot, slot, ms.at[d - 1], mr.at[d - 1], z_mates[d - 1])

    for d in (1, 2, 3):
        small_z_copy(d).start()
    small_z[z] = small_own[...]
    for p in (1, 2, 3):
        at_z_event(p)
    for d in (1, 2, 3):
        small_z_arrival(d).wait_recv()
    small_y[0] = small_z[0] + small_z[1] + small_z[2] + small_z[3]
    y_sum = remote(small_y.at[0], small_y.at[1], ms.at[3], mr.at[3], y_mate)
    y_sum.start()
    y_sum.wait()
    small_c[0] = small_y[0] + small_y[1]
    c_sum = remote(small_c.at[0], small_c.at[1], ms.at[4], mr.at[4], core_mate)
    c_sum.start()
    c_sum.wait()
    small_out[...] = small_c[0] + small_c[1]

    for d in (1, 2, 3):
        small_z_copy(d).wait_send()
    for b in range(blocks):
        branch_copy(b).wait_send()
    for g in range(groups):
        ff_y_copy(g).wait_send()
        for d in (1, 2, 3):
            ff_z_copy(g, d).wait_send()
    for p in range(pairs):
        at_c_copy(p).wait_send()
        at_y_copy(p).wait_send()
        for d in (1, 2, 3):
            at_z_copy(p, d).wait_send()


def run_back(
    queries, keys, values, mixture, grad_mixture, ga_t, normed_t, wqkv, x,
    seg_rows, key_col, gain, down_bias, small, middle, grad_middle, ff_part, branch,
):
    length, width = x.shape
    pairs = queries.shape[0]
    chunks, depth = ff_part.shape[0], ff_part.shape[3]
    groups = chunks // GROUP
    blocks = length // BLOCK
    dma = pltpu.SemaphoreType.DMA
    rows = pltpu.VMEM((blocks, BLOCK, width), BF)
    lanes = pltpu.VMEM((pairs, length, PAIR), BF)
    return pl.pallas_call(
        back_kernel,
        out_shape=[
            shape_of((length, width), BF),
            shape_of((length, width), BF),
            shape_of((chunks, depth, CHUNK), F32),
            shape_of((pairs, depth, CHUNK), F32),
            shape_of(small.shape, F32),
        ],
        in_specs=[VMEM_SPEC] * 14 + [ANY_SPEC] * 4,
        out_specs=[VMEM_SPEC] * 5,
        scratch_shapes=[
            pltpu.VMEM((length, PAIR), F32), pltpu.VMEM((length, PAIR), F32),
            lanes, lanes, lanes,
            pltpu.VMEM((pairs, Z_SIZE, Y_SIZE, CORES, depth, CHUNK), BF),
            pltpu.VMEM((pairs, Z_SIZE, Y_SIZE, depth, CHUNK), BF),
            pltpu.VMEM((pairs, Z_SIZE, depth, CHUNK), BF),
            pltpu.VMEM((3, pairs, depth, CHUNK), BF),
            pltpu.VMEM((chunks, Z_SIZE, depth, CHUNK), BF),
            pltpu.VMEM((3, chunks, depth, CHUNK), BF),
            rows, rows,
            pltpu.VMEM((length, width), BF),
            pltpu.VMEM((2, BLOCK, width), BF),
            pltpu.VMEM((2, GROUP, Z_SIZE, depth, CHUNK), BF),
            pltpu.VMEM((2, BLOCK, width), F32),
            pltpu.VMEM(small.shape, F32),
            pltpu.VMEM((Z_SIZE,) + small.shape, F32),
            pltpu.VMEM((2,) + small.shape, F32),
            pltpu.VMEM((2,) + small.shape, F32),
            dma((blocks,)), dma((blocks,)), dma((groups,)), dma((groups,)),
            dma((3 * groups,)), dma((3 * groups,)), dma((pairs,)), dma((pairs,)),
            dma((pairs,)), dma((pairs,)), dma((3 * pairs,)), dma((3 * pairs,)),
            dma((blocks,)), dma((blocks,)), dma((2,)), dma((5,)), dma((5,)), dma((2,)), dma((2,)),
        ],
        compiler_params=pltpu.CompilerParams(
            collective_id=2, has_side_effects=True, vmem_limit_bytes=VMEM_LIMIT
        ),
    )(
        queries, keys, values, mixture, grad_mixture, ga_t, normed_t, wqkv, x,
        seg_rows, key_col, gain, down_bias, small, middle, grad_middle, ff_part, branch,
    )


def fast_body(
    tokens, segment_ids, context_flags, ln1_gain, ln1_bias, qkv_weight, qv_bias, out_weight,
    out_bias, ln2_gain, ln2_bias, up_weight, up_bias, down_weight, down_bias, cotangent,
):
    _, length, width = tokens.shape
    hidden = up_weight.shape[1]
    depth = up_weight.shape[0]
    cols = qkv_weight.shape[2]
    pairs = cols // PAIR
    half = hidden // CHUNK
    row = lambda v: v.astype(F32).reshape(1, -1)
    x, dy = tokens[0], cotangent[0]
    segments = segment_ids[0]
    visible = jnp.where(context_flags[0] == 1, segments, -1)
    shard = jnp.concatenate([up_weight, down_weight.T], axis=1)
    shard = shard.reshape(depth, 2 * half, CHUNK).transpose(1, 0, 2)
    queries, keys, values, mixture, middle, normed_t, wff = run_fwd(
        x, segments.reshape(length, 1), visible.reshape(1, length), row(ln1_gain),
        row(ln1_bias), qkv_weight, qv_bias.astype(F32), out_weight, row(out_bias), shard,
    )
    branch, grad_middle, ga_t, grad_mixture, ff_part, small = run_ff(
        middle, dy, wff.reshape(2 * half, width, CHUNK),
        up_bias.astype(F32).reshape(half, 1, CHUNK), row(ln2_gain), row(ln2_bias), out_weight,
    )
    output, tokens_grad, ff_sum, at_sum, small = run_back(
        queries, keys, values, mixture, grad_mixture, ga_t, normed_t, qkv_weight, x,
        segments.reshape(length // STRIP, 1, STRIP), visible.reshape(length, 1),
        row(ln1_gain), row(down_bias), small, middle, grad_middle, ff_part, branch,
    )
    spread = ff_sum.transpose(1, 0, 2).reshape(depth, 2 * hidden)
    by_kind = at_sum.reshape(pairs, depth, 4, PAIR).transpose(2, 1, 0, 3).reshape(4, depth, cols)
    up_bias_grad = small[8:8 + half, :CHUNK].reshape(hidden)
    return (
        output[None], tokens_grad[None], small[4], small[5], by_kind[:3],
        small[6].reshape(2, cols), by_kind[3].T, small[2], small[0], small[1],
        spread[:, :hidden], up_bias_grad, spread[:, hidden:].T, small[3],
    )


def solution(mesh):
    chosen = generic_body
    if mesh.shape["head"] == 2 and mesh.shape["seq"] == SEQ_SIZE:
        chosen = fast_body
    return jax.shard_map(
        chosen,
        mesh=mesh,
        in_specs=(
            P("seq", None, None),
            P("seq", None),
            P("seq", None),
            P(),
            P(),
            P(None, None, "head"),
            P(None, "head"),
            P("head", None),
            P(),
            P(),
            P(),
            P("seq", "head"),
            P("head"),
            P("head", "seq"),
            P(),
            P("seq", None, None),
        ),
        out_specs=(
            P("seq", None, None),
            P("seq", None, None),
            P(),
            P(),
            P(None, "seq", "head"),
            P(None, "head"),
            P("head", "seq"),
            P(),
            P(),
            P(),
            P("seq", "head"),
            P("head"),
            P("head", "seq"),
            P(),
        ),
        check_vma=False,
    )
```

```python
import math

import jax
import jax.numpy as jnp
from jax import lax
from jax.experimental import pallas as pl
from jax.experimental.pallas import tpu as pltpu
from jax.sharding import PartitionSpec as P

HEAD_DIM = 64


def layer_norm(values_in, scaling, offset):
    middle = jnp.mean(values_in, axis=-1, keepdims=True)
    centred = values_in - middle
    spread = jnp.mean(centred * centred, axis=-1, keepdims=True)
    return centred * lax.rsqrt(spread + 1e-05) * scaling + offset


def gelu_exact(values_in):
    return 0.5 * values_in * (1.0 + jax.scipy.special.erf(values_in * 0.7071067811865476))


def dot_rows(left, right):
    return lax.dot_general(
        left, right, (((1,), (1,)), ((), ())), preferred_element_type=jnp.float32
    )


def dot_cols(left, right):
    return lax.dot_general(
        left, right, (((0,), (0,)), ((), ())), preferred_element_type=jnp.float32
    )


def masked_scores(block_query, seq_keys, block_segments, seq_segments, seq_context, factor):
    raw_scores = (
        jnp.einsum("qhd,khd->hqk", block_query, seq_keys, preferred_element_type=jnp.float32)
        * factor
    )
    allowed = (block_segments[:, None] == seq_segments[None, :]) & (seq_context[None, :] == 1)
    return jnp.where(allowed[None], raw_scores, -1e30)


def generic_body(
    tokens,
    segment_ids,
    context_flags,
    ln1_gain,
    ln1_bias,
    qkv_weight,
    qv_bias,
    out_weight,
    out_bias,
    ln2_gain,
    ln2_bias,
    up_weight,
    up_bias,
    down_weight,
    down_bias,
    cotangent,
):
    seq_count, length, width = tokens.shape
    row_count = seq_count * length
    local_cols = qkv_weight.shape[2]
    head_count = local_cols // HEAD_DIM
    factor = 1.0 / math.sqrt(HEAD_DIM)
    block = min(512, length)
    blocks = length // block
    gain_one = ln1_gain.astype(jnp.float32)
    offset_one = ln1_bias.astype(jnp.float32)
    gain_two = ln2_gain.astype(jnp.float32)
    offset_two = ln2_bias.astype(jnp.float32)
    flat_in = tokens.astype(jnp.float32).reshape(row_count, width)
    normed_f, norm_one_pull = jax.vjp(layer_norm, flat_in, gain_one, offset_one)
    normed = normed_f.astype(jnp.bfloat16)
    queries = (
        jnp.dot(normed, qkv_weight[0], preferred_element_type=jnp.float32)
        + qv_bias[0].astype(jnp.float32)
    ).astype(jnp.bfloat16)
    key_rows = jnp.dot(normed, qkv_weight[1], preferred_element_type=jnp.float32).astype(
        jnp.bfloat16
    )
    value_rows = (
        jnp.dot(normed, qkv_weight[2], preferred_element_type=jnp.float32)
        + qv_bias[1].astype(jnp.float32)
    ).astype(jnp.bfloat16)

    def per_sequence(array):
        return array.reshape(seq_count, length, head_count, HEAD_DIM)

    def attend_sequence(member):
        seq_query, seq_keys, seq_values, seq_segments, seq_context = member

        def attend_block(portion):
            block_query, block_segments = portion
            scores = masked_scores(
                block_query, seq_keys, block_segments, seq_segments, seq_context, factor
            )
            row_top = jnp.max(scores, axis=-1, keepdims=True)
            exponent = jnp.exp(scores - row_top)
            row_total = jnp.sum(exponent, axis=-1, keepdims=True)
            soft_weights = (exponent / row_total).astype(jnp.bfloat16)
            block_mix = jnp.einsum(
                "hqk,khd->qhd", soft_weights, seq_values, preferred_element_type=jnp.float32
            )
            return (block_mix.astype(jnp.bfloat16), row_top + jnp.log(row_total))

        return lax.map(
            attend_block,
            (
                seq_query.reshape(blocks, block, head_count, HEAD_DIM),
                seq_segments.reshape(blocks, block),
            ),
        )

    mixture, log_totals = lax.map(
        attend_sequence,
        (
            per_sequence(queries),
            per_sequence(key_rows),
            per_sequence(value_rows),
            segment_ids,
            context_flags,
        ),
    )
    mixture = mixture.reshape(row_count, local_cols)
    partial_out = jnp.dot(mixture, out_weight, preferred_element_type=jnp.float32)
    grad_rows_all = cotangent.reshape(row_count, width)
    grad_float_all = grad_rows_all.astype(jnp.float32)
    grad_down_bias = jnp.sum(grad_float_all, axis=0)
    attended = lax.psum(partial_out, "head") + out_bias.astype(jnp.float32)
    middle_state = flat_in + attended
    normed_two_f, norm_two_pull = jax.vjp(layer_norm, middle_state, gain_two, offset_two)
    normed_two = normed_two_f.astype(jnp.bfloat16)
    up_part, down_part, up_shift = (
        lax.all_gather(up_weight, "head", axis=1, tiled=True),
        lax.all_gather(down_weight, "head", axis=0, tiled=True),
        lax.all_gather(up_bias, "head", axis=0, tiled=True),
    )
    up_full, down_full = (
        lax.all_gather(up_part, "seq", axis=0, tiled=True),
        lax.all_gather(down_part, "seq", axis=1, tiled=True),
    )
    before = jnp.dot(normed_two, up_full, preferred_element_type=jnp.float32) + up_shift.astype(
        jnp.float32
    )
    active_f, gelu_pull = jax.vjp(gelu_exact, before)
    active = active_f.astype(jnp.bfloat16)
    branch_out = jnp.dot(active, down_full, preferred_element_type=jnp.float32)
    final_rows = (middle_state + branch_out + down_bias.astype(jnp.float32)).astype(jnp.bfloat16)
    output = final_rows.reshape(tokens.shape)
    grad_float = grad_rows_all.astype(jnp.float32)
    grad_down = dot_cols(active, grad_rows_all)
    grad_active = dot_rows(grad_rows_all, down_full)
    (grad_before_f,) = gelu_pull(grad_active)
    grad_before = grad_before_f.astype(jnp.bfloat16)
    grad_up = dot_cols(normed_two, grad_before)
    grad_up_bias = jnp.sum(grad_before.astype(jnp.float32), axis=0)
    grad_normed_two = dot_rows(grad_before, up_full)
    grad_middle_norm, grad_gain_two, grad_offset_two = norm_two_pull(grad_normed_two)
    grad_middle = grad_float + grad_middle_norm
    ff_part = up_weight.shape[1]
    start_col = lax.axis_index("head") * ff_part
    grad_up = lax.dynamic_slice_in_dim(grad_up, start_col, ff_part, 1)
    grad_down = lax.dynamic_slice_in_dim(grad_down, start_col, ff_part, 0)
    grad_up_bias = lax.dynamic_slice_in_dim(grad_up_bias, start_col, ff_part, 0)
    grad_attended = grad_middle.astype(jnp.bfloat16)
    grad_out_bias = jnp.sum(grad_attended.astype(jnp.float32), axis=0)
    grad_out = dot_cols(mixture, grad_attended)
    grad_mixture = dot_rows(grad_attended, out_weight).astype(jnp.bfloat16)

    def back_sequence(member):
        seq_query, seq_keys, seq_values, seq_grad, seq_logs, seq_segments, seq_context = member

        def back_block(carry, portion):
            key_acc, value_acc = carry
            block_query, block_grad, block_logs, block_segments = portion
            scores = masked_scores(
                block_query, seq_keys, block_segments, seq_segments, seq_context, factor
            )
            soft_weights = jnp.exp(scores - block_logs)
            value_acc = value_acc + jnp.einsum(
                "hqk,qhd->khd",
                soft_weights.astype(jnp.bfloat16),
                block_grad,
                preferred_element_type=jnp.float32,
            )
            grad_soft = jnp.einsum(
                "qhd,khd->hqk", block_grad, seq_values, preferred_element_type=jnp.float32
            )
            row_inner = jnp.sum(soft_weights * grad_soft, axis=-1, keepdims=True)
            grad_scores = (soft_weights * (grad_soft - row_inner)).astype(jnp.bfloat16)
            grad_query = (
                jnp.einsum(
                    "hqk,khd->qhd", grad_scores, seq_keys, preferred_element_type=jnp.float32
                )
                * factor
            )
            key_acc = (
                key_acc
                + jnp.einsum(
                    "hqk,qhd->khd", grad_scores, block_query, preferred_element_type=jnp.float32
                )
                * factor
            )
            return ((key_acc, value_acc), grad_query)

        empty = jnp.zeros((length, head_count, HEAD_DIM), jnp.float32)
        (key_acc, value_acc), grad_query = lax.scan(
            back_block,
            (empty, empty),
            (
                seq_query.reshape(blocks, block, head_count, HEAD_DIM),
                seq_grad.reshape(blocks, block, head_count, HEAD_DIM),
                seq_logs,
                seq_segments.reshape(blocks, block),
            ),
        )
        return (grad_query, key_acc, value_acc)

    grad_queries, grad_keys, grad_values = lax.map(
        back_sequence,
        (
            per_sequence(queries),
            per_sequence(key_rows),
            per_sequence(value_rows),
            per_sequence(grad_mixture),
            log_totals,
            segment_ids,
            context_flags,
        ),
    )
    grad_queries = grad_queries.reshape(row_count, local_cols).astype(jnp.bfloat16)
    grad_keys = grad_keys.reshape(row_count, local_cols).astype(jnp.bfloat16)
    grad_values = grad_values.reshape(row_count, local_cols).astype(jnp.bfloat16)
    grad_qv_bias = jnp.stack(
        [
            jnp.sum(grad_queries.astype(jnp.float32), axis=0),
            jnp.sum(grad_values.astype(jnp.float32), axis=0),
        ]
    )
    grad_qkv = jnp.stack(
        [dot_cols(normed, grad_queries), dot_cols(normed, grad_keys), dot_cols(normed, grad_values)]
    )
    grad_normed = (
        dot_rows(grad_queries, qkv_weight[0])
        + dot_rows(grad_keys, qkv_weight[1])
        + dot_rows(grad_values, qkv_weight[2])
    )
    grad_normed = lax.psum(grad_normed, "head")
    grad_input_norm, grad_gain_one, grad_offset_one = norm_one_pull(grad_normed)
    tokens_grad = (grad_middle + grad_input_norm).astype(jnp.bfloat16).reshape(tokens.shape)
    summed_qkv, summed_out, summed_up, summed_down = (
        lax.psum_scatter(
            grad_qkv.astype(jnp.bfloat16), "seq", scatter_dimension=1, tiled=True
        ).astype(jnp.float32),
        lax.psum_scatter(
            grad_out.astype(jnp.bfloat16), "seq", scatter_dimension=1, tiled=True
        ).astype(jnp.float32),
        lax.psum_scatter(
            grad_up.astype(jnp.bfloat16), "seq", scatter_dimension=0, tiled=True
        ).astype(jnp.float32),
        lax.psum_scatter(
            grad_down.astype(jnp.bfloat16), "seq", scatter_dimension=1, tiled=True
        ).astype(jnp.float32),
    )
    smalls = lax.psum(
        (
            grad_gain_one,
            grad_offset_one,
            grad_qv_bias,
            grad_out_bias,
            grad_gain_two,
            grad_offset_two,
            grad_up_bias,
            grad_down_bias,
        ),
        "seq",
    )
    return (
        output,
        tokens_grad,
        smalls[0],
        smalls[1],
        summed_qkv,
        smalls[2],
        summed_out,
        smalls[3],
        smalls[4],
        smalls[5],
        summed_up,
        smalls[6],
        summed_down,
        smalls[7],
    )


MESH = pl.DeviceIdType.MESH
BF = jnp.bfloat16
F32 = jnp.float32
BLOCK = 256
STRIP = 128
GROUP = 2
CHUNK = 512
PAIR = 2 * HEAD_DIM
Z_SIZE, Y_SIZE, CORES = 4, 2, 2
SEQ_SIZE = Z_SIZE * Y_SIZE * CORES
HOP = Y_SIZE * CORES
TABLES = 8
FAR = -1e30
VMEM_LIMIT = 62 * 2**20
INV_ROOT_TWO = 0.7071067811865476
INV_ROOT_TWO_PI = 0.3989422804014327
LN1_GAIN, LN1_BIAS, QV_BIAS, OUT_BIAS, LN2_GAIN, LN2_BIAS, UP_BIAS, DOWN_BIAS = 0, 1, 2, 3, 4, 5, 6, 8
SMALL_ROWS = 16
VMEM_SPEC = pl.BlockSpec(memory_space=pltpu.VMEM)
ANY_SPEC = pl.BlockSpec(memory_space=pl.ANY)


def shape_of(dims, dtype):
    return jax.ShapeDtypeStruct(tuple(dims), dtype)


def nn(left, right):
    return jnp.dot(left, right, preferred_element_type=F32)


def turn(block):
    return jnp.transpose(block)


def sum_rows(block):
    return jnp.sum(block, axis=0, keepdims=True)


def place():
    me = lax.axis_index("seq")
    head = lax.axis_index("head")
    core = me % 2
    y = (me // 2) % 2
    across = {"seq": me, "head": 1 - head}
    core_mate = {"seq": me + 1 - 2 * core, "head": head}
    y_mate = {"seq": me + 2 - 4 * y, "head": head}
    z_mates = [{"seq": (me + HOP * d) % SEQ_SIZE, "head": head} for d in (1, 2, 3)]
    return me, head, core, y, across, core_mate, y_mate, z_mates


def greet(others):
    barrier = pltpu.get_barrier_semaphore()
    for other in others:
        pl.semaphore_signal(barrier, inc=1, device_id=other, device_id_type=MESH)
    pl.semaphore_wait(barrier, len(others))


def remote(src, dst, send_sem, recv_sem, other):
    return pltpu.make_async_remote_copy(
        src_ref=src, dst_ref=dst, send_sem=send_sem, recv_sem=recv_sem,
        device_id=other, device_id_type=MESH,
    )


def norm_stats(rows):
    middle = jnp.mean(rows, axis=-1, keepdims=True)
    centred = rows - middle
    spread = jnp.mean(centred * centred, axis=-1, keepdims=True)
    return centred, lax.rsqrt(spread + 1e-05)


def norm_back(inner, unit, scale):
    return scale * (
        inner
        - jnp.mean(inner, axis=-1, keepdims=True)
        - unit * jnp.mean(inner * unit, axis=-1, keepdims=True)
    )


def lanes():
    return lax.broadcasted_iota(jnp.int32, (1, PAIR), 1)


def in_pieces(column, first, rest):
    high = column.astype(BF).astype(F32)
    mid = (column - high).astype(BF).astype(F32)
    low = column - high - mid
    at = lanes()
    return jnp.where(
        at == first, high, jnp.where(at == first + 1, mid, jnp.where(at == first + 2, low, rest))
    ).astype(BF)


def one_lanes(length):
    return jnp.broadcast_to(jnp.where(lanes() < 3, 1.0, 0.0).astype(BF), (length, PAIR))


def fwd_kernel(
    x_ref, seg_ref, context, params, wqkv, wout, up_shard, down_shard,
    q_ref, k_ref, v_ref, mix_ref, mid_ref, normed_t, wff, key_more, query_more,
    mask_more, down_t, wout_x, mix_x,
    zs, zr, ys, yr, cs, cr, xs, xr, local,
):
    length, width = x_ref.shape
    blocks = length // BLOCK
    pairs = q_ref.shape[0]
    cols = pairs * PAIR
    me, head, core, y, across, core_mate, y_mate, _ = place()
    z = me // HOP
    above = {"seq": (me + HOP) % SEQ_SIZE, "head": head}
    below = {"seq": (me + SEQ_SIZE - HOP) % SEQ_SIZE, "head": head}
    down_t[...] = turn(down_shard[...])
    greet([across, core_mate, y_mate, above, below])

    out_copy = remote(wout, wout_x, xs.at[0], xr.at[0], across)
    out_copy.start()
    shards = (up_shard, down_t)
    own = [pltpu.make_async_copy(shards[u], wff.at[u, me], local.at[u]) for u in range(2)]

    flows = [(0, 0)] + [(way, s) for s in (1, 2, 3) for way in (0, 1)]

    def there(way, s):
        return (z >= s) if way == 0 else (z + s < Z_SIZE)

    def source(base, way, s):
        away = SEQ_SIZE - HOP * s if way == 0 else HOP * s
        return (base + away) % SEQ_SIZE

    def z_copy(u, way, s):
        n = (u * 2 + way) * 3 + s - 1
        j = source(me, way, s - 1)
        src = shards[u] if s == 1 else wff.at[u, j]
        return remote(src, wff.at[u, j], zs.at[n], zr.at[n], above if way == 0 else below)

    def z_arrival(u, way, s):
        n = (u * 2 + way) * 3 + s - 1
        slot = wff.at[u, source(me, way, s)]
        return remote(slot, slot, zs.at[n], zr.at[n], above)

    def z_goes_on(way):
        return (z < Z_SIZE - 1) if way == 0 else (z > 0)

    def y_copy(u, f):
        n = u * 7 + f
        j = source(me, *flows[f])
        src = shards[u] if f == 0 else wff.at[u, j]
        return remote(src, wff.at[u, j], ys.at[n], yr.at[n], y_mate)

    def y_arrival(u, f):
        n = u * 7 + f
        slot = wff.at[u, source(me + 2 - 4 * y, *flows[f])]
        return remote(slot, slot, ys.at[n], yr.at[n], y_mate)

    def c_copy(u, f, from_y):
        n = (u * 2 + from_y) * 7 + f
        j = source(me + from_y * (2 - 4 * y), *flows[f])
        src = shards[u] if f == 0 and from_y == 0 else wff.at[u, j]
        return remote(src, wff.at[u, j], cs.at[n], cr.at[n], core_mate)

    def c_arrival(u, f, from_y):
        n = (u * 2 + from_y) * 7 + f
        slot = wff.at[u, source(me + 1 - 2 * core + from_y * (2 - 4 * y), *flows[f])]
        return remote(slot, slot, cs.at[n], cr.at[n], core_mate)

    def for_flow(f, do):
        if f == 0:
            do()
        else:
            pl.when(there(*flows[f]))(do)

    def for_step(s, do):
        for f, (way, step) in enumerate(flows):
            if step == s:
                for_flow(f, lambda f=f, way=way: do(f, way))

    def z_event(u, s):
        def one(f, way):
            z_arrival(u, way, s).wait_recv()
            if s < 3:
                pl.when(z_goes_on(way))(lambda: z_copy(u, way, s + 1).start())
            y_copy(u, f).start()
            c_copy(u, f, 0).start()
        for_step(s, one)

    def y_event(u, s):
        def one(f, way):
            y_arrival(u, f).wait_recv()
            c_copy(u, f, 1).start()
        for_step(s, one)

    for u in range(2):
        for way in (0, 1):
            pl.when(z_goes_on(way))(lambda u=u, way=way: z_copy(u, way, 1).start())
        y_copy(u, 0).start()
        c_copy(u, 0, 0).start()
        own[u].start()

    plan = {
        1: [(z_event, 0, 1), (y_event, 0, 0)], 3: [(z_event, 1, 1), (y_event, 1, 0)],
        5: [(z_event, 0, 2)], 7: [(z_event, 1, 2)], 9: [(y_event, 0, 1)], 11: [(z_event, 0, 3)],
        12: [(y_event, 1, 1)], 14: [(z_event, 1, 3)], 16: [(y_event, 0, 2)], 18: [(y_event, 1, 2)],
    }
    last = [(y_event, 0, 3), (y_event, 1, 3)]

    def tick(t):
        for step, events in plan.items():
            @pl.when(t == step)
            def _(events=events):
                for event, u, s in events:
                    event(u, s)

    at = lax.broadcasted_iota(jnp.int32, (PAIR, length), 0)
    same = at == seg_ref[...]
    hidden = context[...] != 1
    ones = jnp.logical_and(at > TABLES, at < TABLES + 4)
    key_side = jnp.logical_or(
        jnp.logical_and(at < TABLES, same),
        jnp.logical_or(jnp.logical_and(at == TABLES, hidden), ones),
    )
    query_side = jnp.logical_and(at <= TABLES, jnp.logical_not(same))
    key_more[...] = turn(jnp.where(key_side, 1.0, 0.0)).astype(BF)
    mask_more[...] = turn(jnp.where(query_side, FAR, 0.0)).astype(BF)

    gains, offsets = params[LN1_GAIN:LN1_GAIN + 1, :], params[LN1_BIAS:LN1_BIAS + 1, :]
    query_bias = params[QV_BIAS:QV_BIAS + 1, 0:cols]
    value_bias = params[QV_BIAS:QV_BIAS + 1, cols:2 * cols]

    def project(b, _):
        rows = pl.ds(pl.multiple_of(b * BLOCK, BLOCK), BLOCK)
        centred, scale = norm_stats(x_ref[rows, :].astype(F32))
        block = (centred * scale * gains + offsets).astype(BF)
        normed_t[b] = turn(block)
        queries = ((nn(block, wqkv[0]) + query_bias).astype(BF) * 0.125).astype(BF)
        keys = nn(block, wqkv[1]).astype(BF)
        values = (nn(block, wqkv[2]) + value_bias).astype(BF)
        for p in range(pairs):
            part = slice(p * PAIR, (p + 1) * PAIR)
            q_ref[p, rows, :] = queries[:, part]
            k_ref[p, rows, :] = keys[:, part]
            v_ref[p, rows, :] = values[:, part]
        tick(b)
        return 0

    lax.fori_loop(0, blocks, project, 0)

    low_lanes = lanes() < HEAD_DIM
    zero = jnp.zeros((1, PAIR), BF)

    def mixture_copy(b):
        rows = pl.ds(b * BLOCK, BLOCK)
        return remote(
            mix_ref.at[:, rows, :], mix_x.at[:, rows, :], xs.at[1 + b], xr.at[1 + b], across
        )

    def attend(t, _):
        b, p = t // pairs, t % pairs
        rows = pl.ds(pl.multiple_of(b * BLOCK, BLOCK), BLOCK)
        queries, more = q_ref[p, rows, :], mask_more[rows, :]
        keys = jnp.concatenate([k_ref[p], key_more[...]], axis=1)
        values = jnp.concatenate([v_ref[p], one_lanes(length)], axis=1)
        parts = []
        for low in (0, 1):
            own_lanes = jnp.logical_not(low_lanes) if low else low_lanes
            left = jnp.concatenate([jnp.where(own_lanes, queries, zero), more], axis=1)
            scores = dot_rows(left, keys)
            top = jnp.max(scores, axis=-1, keepdims=True)
            mixed = nn(jnp.exp(scores - top).astype(BF), values)
            total = mixed[:, PAIR:PAIR + 1]
            parts.append(mixed[:, :PAIR] / total)
            query_more[2 * p + low, rows, :] = in_pieces(
                -(top + jnp.log(total)), TABLES + 1, more.astype(F32)
            )
        mix_ref[p, rows, :] = jnp.where(low_lanes, parts[0], parts[1]).astype(BF)
        tick(t + blocks)
        for b_done in range(blocks):
            @pl.when(t == (b_done + 1) * pairs - 1)
            def _(b_done=b_done):
                mixture_copy(b_done).start()
        return 0

    lax.fori_loop(0, blocks * pairs, attend, 0)
    out_copy.wait_recv()
    for b in range(blocks):
        if b == blocks - 1:
            for event, u, s in last:
                event(u, s)
        mixture_copy(b).wait_recv()
        rows = pl.ds(b * BLOCK, BLOCK)
        ours = jnp.concatenate([mix_ref[p, rows, :] for p in range(pairs)], axis=-1)
        other = jnp.concatenate([mix_x[p, rows, :] for p in range(pairs)], axis=-1)
        attended = nn(ours, wout[...]) + nn(other, wout_x[...])
        mid_ref[rows, :] = (
            x_ref[rows, :].astype(F32) + (attended + params[OUT_BIAS:OUT_BIAS + 1, :])
        )

    out_copy.wait_send()
    for b in range(blocks):
        mixture_copy(b).wait_send()
    for u in range(2):
        own[u].wait()
        for way in (0, 1):
            pl.when(z_goes_on(way))(lambda u=u, way=way: z_copy(u, way, 1).wait_send())
        for f, (way, s) in enumerate(flows):
            def finish(u=u, f=f, way=way, s=s):
                if f and s < 3:
                    pl.when(z_goes_on(way))(lambda: z_copy(u, way, s + 1).wait_send())
                y_copy(u, f).wait_send()
                for from_y in (0, 1):
                    c_copy(u, f, from_y).wait_send()
                    c_arrival(u, f, from_y).wait_recv()
            for_flow(f, finish)


def run_fwd(x, seg, context, params, wqkv, wout, up_weight, down_weight):
    length, width = x.shape
    pairs = wqkv.shape[2] // PAIR
    blocks = length // BLOCK
    depth, hidden = up_weight.shape
    by_pair = shape_of((pairs, length, PAIR), BF)
    dma = pltpu.SemaphoreType.DMA
    return pl.pallas_call(
        fwd_kernel,
        out_shape=[
            by_pair, by_pair, by_pair, by_pair,
            shape_of((length, width), F32),
            shape_of((blocks, width, BLOCK), BF),
            shape_of((2, SEQ_SIZE, depth, hidden), BF),
            shape_of((length, PAIR), BF),
            shape_of((2 * pairs, length, PAIR), BF),
        ],
        in_specs=[VMEM_SPEC] * 6 + [ANY_SPEC, VMEM_SPEC],
        out_specs=[VMEM_SPEC] * 6 + [ANY_SPEC] + [VMEM_SPEC] * 2,
        scratch_shapes=[
            pltpu.VMEM((length, PAIR), BF),
            pltpu.VMEM((depth, hidden), BF),
            pltpu.VMEM(wout.shape, BF),
            pltpu.VMEM((pairs, length, PAIR), BF),
            dma((12,)), dma((12,)), dma((14,)), dma((14,)), dma((28,)), dma((28,)),
            dma((1 + blocks,)), dma((1 + blocks,)), dma((2,)),
        ],
        compiler_params=pltpu.CompilerParams(
            collective_id=0, has_side_effects=True, vmem_limit_bytes=VMEM_LIMIT
        ),
    )(x, seg, context, params, wqkv, wout, up_weight, down_weight)


def ff_kernel(
    mid_hbm, dy_ref, wff, params, wout,
    branch_ref, gmid_hbm, ga_t, gm_ref, summed, small_ref,
    normed, normed_t, dy_t, active, before_grad, gnt_acc, gnt_own, gnt_x, whole, from_mate,
    held, ready,
    xs, xr, cs, cr, ls, ws, ss,
):
    length, width = dy_ref.shape
    blocks = length // BLOCK
    hidden = wff.shape[3]
    half = hidden // CHUNK
    chunks = 2 * half
    pairs = gm_ref.shape[0]
    me, head, core, y, across, core_mate, y_mate, z_mates = place()
    greet([across, core_mate])
    gains, offsets = params[LN2_GAIN:LN2_GAIN + 1, :], params[LN2_BIAS:LN2_BIAS + 1, :]
    per_row = width // CHUNK

    def weight(kind, n):
        cut = pl.ds(pl.multiple_of(n * CHUNK, CHUNK), CHUNK)
        return wff[kind, :, :, cut].reshape(width, CHUNK)

    small_ref[...] = jnp.zeros_like(small_ref)

    def load(n):
        rows = pl.ds(n % blocks * BLOCK, BLOCK)
        return pltpu.make_async_copy(mid_hbm.at[rows, :], held.at[n % 2], ls.at[n % 2])

    def store(b):
        rows = pl.ds(b * BLOCK, BLOCK)
        return pltpu.make_async_copy(ready.at[b % 2], gmid_hbm.at[rows, :], ws.at[b % 2])

    load(0).start()
    load(1).start()

    def gnt_copy(b):
        return remote(gnt_own.at[b], gnt_x.at[b], xs.at[b], xr.at[b], across)

    def core_copy(n):
        return remote(
            whole.at[n, :, :, 1 - core], from_mate.at[n], cs.at[n], cr.at[n], core_mate
        )

    def forward(t, _):
        b, n = t // half, t % half
        rows = pl.ds(pl.multiple_of(b * BLOCK, BLOCK), BLOCK)

        for b_next in range(blocks):
            @pl.when(t == b_next * half)
            def _(b_next=b_next):
                load(b_next).wait()

        @pl.when(n == 0)
        def _():
            centred, scale = norm_stats(held[b % 2])
            block = (centred * scale * gains + offsets).astype(BF)
            normed[...] = block
            normed_t[b] = turn(block)
            dy_t[b] = turn(dy_ref[rows, :])
            small_ref[DOWN_BIAS:DOWN_BIAS + 1, :] += sum_rows(dy_ref[rows, :].astype(F32))

        up = weight(0, n)
        bias_row = pl.ds(UP_BIAS + n // per_row, 1)
        bias_cut = pl.ds(pl.multiple_of(n % per_row * CHUNK, CHUNK), CHUNK)
        before = nn(normed[...], up) + params[bias_row, bias_cut]
        spread = 0.5 * (1.0 + lax.erf(before * INV_ROOT_TWO))
        active[n, rows, :] = (before * spread).astype(BF)
        slope = spread + before * (INV_ROOT_TWO_PI * jnp.exp(before * before * -0.5))
        grad = (nn(dy_ref[rows, :], weight(1, n)) * slope).astype(BF)
        before_grad[n, rows, :] = grad
        small_ref[bias_row, bias_cut] += sum_rows(grad.astype(F32))
        back = dot_rows(grad, up)

        @pl.when(n == 0)
        def _():
            gnt_acc[...] = back

        @pl.when(n > 0)
        def _():
            gnt_acc[...] += back

        for b_done in range(blocks):
            @pl.when(t == (b_done + 1) * half - 1)
            def _(b_done=b_done):
                load(b_done + 2).start()
                gnt_own[b_done] = gnt_acc[...].astype(BF)
                gnt_copy(b_done).start()
        return 0

    lax.fori_loop(0, blocks * half, forward, 0)

    def weight_grads(left_t, right, first):
        top, planes = width // 2, Z_SIZE // 2

        def one(t, _):
            n, side = t // 2, t % 2
            cut = pl.ds(pl.multiple_of(side * top, top), top)
            total = nn(left_t[0, cut, :], right[n, pl.ds(0, BLOCK), :])
            for b in range(1, blocks):
                total += nn(left_t[b, cut, :], right[n, pl.ds(b * BLOCK, BLOCK), :])
            piece = total.astype(BF).reshape((planes,) + whole.shape[2:])
            whole[first + n, pl.ds(side * planes, planes)] = piece

            @pl.when(side == 1)
            def _():
                core_copy(first + n).start()

            return 0

        lax.fori_loop(0, 2 * half, one, 0)

    weight_grads(dy_t, active, half)
    weight_grads(normed_t, before_grad, 0)

    def branch(b, _):
        rows = pl.ds(pl.multiple_of(b * BLOCK, BLOCK), BLOCK)
        total = dot_rows(active[0, rows, :], weight(1, 0))
        for n in range(1, half):
            total += dot_rows(active[n, rows, :], weight(1, n))
        branch_ref[rows, :] = total.astype(BF)
        return 0

    lax.fori_loop(0, blocks, branch, 0)

    def add_mate(n, _):
        core_copy(n).wait()
        both = whole[n, :, :, core].astype(F32) + from_mate[n].astype(F32)
        from_mate[n] = both.astype(BF)
        return 0

    lax.fori_loop(half, chunks, add_mate, 0)
    lax.fori_loop(0, half, add_mate, 0)
    keep = pltpu.make_async_copy(from_mate, summed, ss.at[0])
    keep.start()

    strips = BLOCK // STRIP
    for b in range(blocks):
        gnt_copy(b).wait()
        load(blocks + b).wait()
        if b >= 2:
            store(b - 2).wait()

        def through_norm(n, _, b=b):
            rows = pl.ds(pl.multiple_of(n * STRIP, STRIP), STRIP)
            full = pl.ds(pl.multiple_of(b * BLOCK + n * STRIP, STRIP), STRIP)
            grad = gnt_own[b, rows, :].astype(F32) + gnt_x[b, rows, :].astype(F32)
            centred, scale = norm_stats(held[b % 2, rows, :])
            unit = centred * scale
            small_ref[LN2_GAIN:LN2_GAIN + 1, :] += sum_rows(grad * unit)
            small_ref[LN2_BIAS:LN2_BIAS + 1, :] += sum_rows(grad)
            total = dy_ref[full, :].astype(F32) + norm_back(grad * gains, unit, scale)
            ready[b % 2, rows, :] = total
            low = total.astype(BF)
            small_ref[OUT_BIAS:OUT_BIAS + 1, :] += sum_rows(low.astype(F32))
            ga_t[b, :, rows] = turn(low)
            mixed = dot_rows(low, wout[...]).astype(BF)
            for p in range(pairs):
                gm_ref[p, full, :] = mixed[:, p * PAIR:(p + 1) * PAIR]
            return 0

        lax.fori_loop(0, strips, through_norm, 0)
        store(b).start()
        if b + 2 < blocks:
            load(blocks + b + 2).start()
    store(blocks - 2).wait()
    store(blocks - 1).wait()
    keep.wait()


def run_ff(middle, dy, wff, params, wout):
    length, width = middle.shape
    half = wff.shape[3] // CHUNK
    chunks = 2 * half
    blocks = length // BLOCK
    pairs = wout.shape[0] // PAIR
    depth = width // SEQ_SIZE
    dma = pltpu.SemaphoreType.DMA
    turned = pltpu.VMEM((blocks, width, BLOCK), BF)
    rows = pltpu.VMEM((blocks, BLOCK, width), BF)
    hidden = pltpu.VMEM((half, length, CHUNK), BF)
    return pl.pallas_call(
        ff_kernel,
        out_shape=[
            shape_of((length, width), BF),
            shape_of((length, width), F32),
            shape_of((blocks, width, BLOCK), BF),
            shape_of((pairs, length, PAIR), BF),
            shape_of((chunks, Z_SIZE, Y_SIZE, depth, CHUNK), BF),
            shape_of((SMALL_ROWS, width), F32),
        ],
        in_specs=[ANY_SPEC] + [VMEM_SPEC] * 4,
        out_specs=[VMEM_SPEC, ANY_SPEC, VMEM_SPEC, VMEM_SPEC, ANY_SPEC, VMEM_SPEC],
        scratch_shapes=[
            pltpu.VMEM((BLOCK, width), BF), turned, turned, hidden, hidden,
            pltpu.VMEM((BLOCK, width), F32), rows, rows,
            pltpu.VMEM((chunks, Z_SIZE, Y_SIZE, CORES, depth, CHUNK), BF),
            pltpu.VMEM((chunks, Z_SIZE, Y_SIZE, depth, CHUNK), BF),
            pltpu.VMEM((2, BLOCK, width), F32), pltpu.VMEM((2, BLOCK, width), F32),
            dma((blocks,)), dma((blocks,)), dma((chunks,)), dma((chunks,)),
            dma((2,)), dma((2,)), dma((1,)),
        ],
        compiler_params=pltpu.CompilerParams(
            collective_id=1, has_side_effects=True, vmem_limit_bytes=VMEM_LIMIT
        ),
    )(middle, dy, wff, params, wout)


def back_kernel(
    q_ref, k_ref, v_ref, mix_ref, gm_ref, ga_t, normed_t, wqkv, x_ref,
    key_more, query_more, params, small_in, mid_hbm, gmid_hbm, ff_part, branch,
    out_ref, tokens_ref, qkv_sum, out_sum, up_sum, down_sum, small_out,
    key_acc, value_acc, dq, dk, dv, whole, mate, at_y, at_z, ff_y, ff_z, gn_own, gn_x,
    branch_x, branch_own, ff_own, held, small_own, small_z, small_y, small_c,
    bs, br, fys, fyr, fzs, fzr, acs, acr, ays, ayr, azs, azr, gs, gr, ls, ms, mr, os, hs,
):
    length, width = x_ref.shape
    blocks = length // BLOCK
    strips = length // STRIP
    pairs = q_ref.shape[0]
    chunks = ff_part.shape[0]
    half = chunks // 2
    groups = chunks // GROUP
    me, head, core, y, across, core_mate, y_mate, z_mates = place()
    z = me // (Y_SIZE * CORES)
    greet([across, core_mate, y_mate, *z_mates])

    def part(b):
        return pl.ds(b * BLOCK, BLOCK)

    def branch_copy(b):
        return remote(branch.at[part(b), :], branch_x.at[part(b), :], bs.at[b], br.at[b], across)

    def load(n):
        source = mid_hbm if n < blocks else gmid_hbm
        return pltpu.make_async_copy(
            source.at[part(n % blocks), :], held.at[n % 2], ls.at[n % 2]
        )

    def taken(n):
        if n + 2 < 2 * blocks:
            load(n + 2).start()

    def group(g):
        return pl.ds(g * GROUP, GROUP)

    def ff_y_copy(g):
        return remote(
            ff_part.at[group(g), :, 1 - y], ff_y.at[group(g)], fys.at[g], fyr.at[g], y_mate
        )

    def ff_z_copy(g, d):
        n = g * 3 + d - 1
        return remote(
            ff_y.at[group(g), (z + d) % Z_SIZE], ff_z.at[d - 1, group(g)],
            fzs.at[n], fzr.at[n], z_mates[d - 1],
        )

    def branch_load(b):
        return pltpu.make_async_copy(branch.at[part(b), :], branch_own.at[b % 2], hs.at[b % 2])

    def ff_load(g):
        return pltpu.make_async_copy(
            ff_part.at[group(g), :, y], ff_own.at[g % 2], os.at[g % 2]
        )

    def ff_y_event(g):
        ff_y_copy(g).wait_recv()
        ff_load(g).wait()
        for n in range(g * GROUP, (g + 1) * GROUP):
            own = ff_own[g % 2, n % GROUP]
            ff_y[n] = (ff_y[n].astype(F32) + own.astype(F32)).astype(BF)
        if g + 2 < groups:
            ff_load(g + 2).start()
            ff_y_copy(g + 2).start()
        for d in (1, 2, 3):
            ff_z_copy(g, d).start()

    def ff_z_event(g):
        for d in (1, 2, 3):
            ff_z_copy(g, d).wait_recv()
        for n in range(g * GROUP, (g + 1) * GROUP):
            total = ff_y[n, z].astype(F32)
            for d in (1, 2, 3):
                total += ff_z[d - 1, n].astype(F32)
            if n < half:
                up_sum[:, n * CHUNK:(n + 1) * CHUNK] = total
            else:
                down_sum[(n - half) * CHUNK:(n - half + 1) * CHUNK, :] = turn(total)

    def at_c_copy(p):
        return remote(whole.at[p, :, :, 1 - core], mate.at[p], acs.at[p], acr.at[p], core_mate)

    def at_y_copy(p):
        return remote(mate.at[p, :, 1 - y], at_y.at[p], ays.at[p], ayr.at[p], y_mate)

    def at_z_copy(p, d):
        n = p * 3 + d - 1
        return remote(
            at_y.at[p, (z + d) % Z_SIZE], at_z.at[d - 1, p], azs.at[n], azr.at[n], z_mates[d - 1]
        )

    def at_c_event(p):
        at_c_copy(p).wait_recv()
        mate[p] = (mate[p].astype(F32) + whole[p, :, :, core].astype(F32)).astype(BF)
        at_y_copy(p).start()

    def at_y_event(p):
        at_y_copy(p).wait_recv()
        at_y[p] = (at_y[p].astype(F32) + mate[p, :, y].astype(F32)).astype(BF)
        for d in (1, 2, 3):
            at_z_copy(p, d).start()

    def at_z_event(p):
        for d in (1, 2, 3):
            at_z_copy(p, d).wait_recv()
        total = at_y[p, z].astype(F32)
        for d in (1, 2, 3):
            total += at_z[d - 1, p].astype(F32)
        cut = slice(p * PAIR, (p + 1) * PAIR)
        for kind in range(3):
            qkv_sum[kind, :, cut] = total[:, kind * PAIR:(kind + 1) * PAIR]
        out_sum[cut, :] = turn(total[:, 3 * PAIR:])

    def branch_event(b):
        branch_copy(b).wait_recv()
        load(b).wait()
        branch_load(b).wait()
        both = branch_own[b % 2].astype(F32) + branch_x[part(b), :].astype(F32)
        out_ref[part(b), :] = (
            held[b % 2] + both + params[DOWN_BIAS:DOWN_BIAS + 1, :]
        ).astype(BF)
        taken(b)
        if b + 2 < blocks:
            branch_load(b + 2).start()

    for b in range(blocks):
        branch_copy(b).start()
    for n in range(2):
        load(n).start()
        branch_load(n).start()
        ff_load(n).start()
        ff_y_copy(n).start()

    plan = {
        10: [(at_c_event, 0)], 13: [(ff_y_event, 0), (branch_event, 0)], 18: [(at_c_event, 1)],
        26: [(at_c_event, 2), (ff_y_event, 1), (branch_event, 1)],
    }

    low_lanes = lanes() < HEAD_DIM
    zero = jnp.zeros((1, PAIR), BF)

    def stacked(strip):
        return jnp.concatenate(
            [jnp.where(low_lanes, strip, zero), jnp.where(low_lanes, zero, strip)], axis=0
        )

    def attend(t, _):
        p, b = t // strips, t % strips
        rows = pl.ds(pl.multiple_of(b * STRIP, STRIP), STRIP)
        keys = k_ref[p]
        queries, grads = stacked(q_ref[p, rows, :]), stacked(gm_ref[p, rows, :])
        more = jnp.concatenate(
            [query_more[2 * p, rows, :], query_more[2 * p + 1, rows, :]], axis=0
        )
        weights = jnp.exp(
            dot_rows(
                jnp.concatenate([keys, key_more[...]], axis=1),
                jnp.concatenate([queries, more], axis=1),
            )
        )
        mixture = mix_ref[p, rows, :]
        product = grads.astype(F32) * jnp.concatenate([mixture, mixture], axis=0).astype(F32)
        inner = -jnp.sum(product, axis=-1, keepdims=True)
        less = dot_rows(
            jnp.concatenate([v_ref[p], one_lanes(length)], axis=1),
            jnp.concatenate([grads, in_pieces(inner, 0, 0.0)], axis=1),
        )
        grad_scores = (weights * less).astype(BF)
        to_values = nn(weights.astype(BF), grads)
        to_keys = nn(grad_scores, queries)
        to_queries = dot_cols(grad_scores, keys)
        dq[p, rows, :] = (
            jnp.where(low_lanes, to_queries[:STRIP], to_queries[STRIP:]) * 0.125
        ).astype(BF)

        @pl.when(b == 0)
        def _():
            key_acc[...] = to_keys
            value_acc[...] = to_values

        @pl.when(b > 0)
        def _():
            key_acc[...] += to_keys
            value_acc[...] += to_values

        @pl.when(b == strips - 1)
        def _():
            dk[p] = key_acc[...].astype(BF)
            dv[p] = value_acc[...].astype(BF)
            total = jnp.zeros((width, 3 * PAIR), F32)
            out_total = jnp.zeros((width, PAIR), F32)
            for n in range(blocks):
                right = jnp.concatenate(
                    [dq[p, part(n), :], dk[p, part(n), :], dv[p, part(n), :]], axis=1
                )
                total += nn(normed_t[n], right)
                out_total += nn(ga_t[n], mix_ref[p, part(n), :])
            both = jnp.concatenate([total, out_total], axis=1).astype(BF)
            whole[p] = both.reshape(whole.shape[1:])

        for p_done in range(pairs):
            @pl.when(t == (p_done + 1) * strips - 1)
            def _(p_done=p_done):
                at_c_copy(p_done).start()

        for step, events in plan.items():
            @pl.when(t == step)
            def _(events=events):
                for event, n in events:
                    event(n)
        return 0

    lax.fori_loop(0, pairs * strips, attend, 0)

    def gn_copy(b):
        return remote(gn_own.at[b], gn_x.at[b], gs.at[b], gr.at[b], across)

    for b in range(blocks):
        total = jnp.zeros((BLOCK, width), F32)
        for n, grad in enumerate((dq, dk, dv)):
            left = jnp.concatenate([grad[p, part(b), :] for p in range(pairs)], axis=1)
            total += dot_rows(left, wqkv[n])
        gn_own[b] = total.astype(BF)
        gn_copy(b).start()

    at_c_event(3)
    small_own[...] = small_in[...]
    for p in range(pairs):
        first, second = p * PAIR, (pairs + p) * PAIR
        small_own[QV_BIAS:QV_BIAS + 1, first:first + PAIR] = sum_rows(dq[p].astype(F32))
        small_own[QV_BIAS:QV_BIAS + 1, second:second + PAIR] = sum_rows(dv[p].astype(F32))
    branch_event(2)
    ff_y_event(2)
    branch_event(3)
    ff_z_event(0)
    ff_y_event(3)
    at_y_event(0)
    ff_z_event(1)
    gains = params[LN1_GAIN:LN1_GAIN + 1, :]
    for b in range(blocks):
        gn_copy(b).wait()
        load(blocks + b).wait()
        grad = gn_own[b].astype(F32) + gn_x[b].astype(F32)
        centred, scale = norm_stats(x_ref[part(b), :].astype(F32))
        unit = centred * scale
        small_own[LN1_GAIN:LN1_GAIN + 1, :] += sum_rows(grad * unit)
        small_own[LN1_BIAS:LN1_BIAS + 1, :] += sum_rows(grad)
        tokens_ref[part(b), :] = (
            held[b % 2] + norm_back(grad * gains, unit, scale)
        ).astype(BF)
        taken(blocks + b)
        if b == 0:
            at_y_event(1)
            at_y_event(2)
            ff_z_event(2)
        if b == 1:
            at_y_event(3)
            ff_z_event(3)
        if b == 2:
            at_z_event(0)
            at_z_event(1)
            at_z_event(2)

    def small_z_copy(d):
        return remote(small_own, small_z.at[z], ms.at[d - 1], mr.at[d - 1], z_mates[d - 1])

    def small_z_arrival(d):
        slot = small_z.at[(z + Z_SIZE - d) % Z_SIZE]
        return remote(slot, slot, ms.at[d - 1], mr.at[d - 1], z_mates[d - 1])

    for d in (1, 2, 3):
        small_z_copy(d).start()
    small_z[z] = small_own[...]
    at_z_event(3)
    for d in (1, 2, 3):
        small_z_arrival(d).wait_recv()
    small_y[0] = small_z[0] + small_z[1] + small_z[2] + small_z[3]
    y_sum = remote(small_y.at[0], small_y.at[1], ms.at[3], mr.at[3], y_mate)
    y_sum.start()
    y_sum.wait()
    small_c[0] = small_y[0] + small_y[1]
    c_sum = remote(small_c.at[0], small_c.at[1], ms.at[4], mr.at[4], core_mate)
    c_sum.start()
    c_sum.wait()
    small_out[...] = small_c[0] + small_c[1]

    for d in (1, 2, 3):
        small_z_copy(d).wait_send()
    for b in range(blocks):
        branch_copy(b).wait_send()
    for g in range(groups):
        ff_y_copy(g).wait_send()
        for d in (1, 2, 3):
            ff_z_copy(g, d).wait_send()
    for p in range(pairs):
        at_c_copy(p).wait_send()
        at_y_copy(p).wait_send()
        for d in (1, 2, 3):
            at_z_copy(p, d).wait_send()


def run_back(
    queries, keys, values, mixture, grad_mixture, ga_t, normed_t, wqkv, x,
    key_more, query_more, params, small, middle, grad_middle, ff_part, branch,
):
    length, width = x.shape
    pairs = queries.shape[0]
    chunks, depth = ff_part.shape[0], ff_part.shape[3]
    groups = chunks // GROUP
    cols, hidden = pairs * PAIR, chunks // 2 * CHUNK
    blocks = length // BLOCK
    dma = pltpu.SemaphoreType.DMA
    rows = pltpu.VMEM((blocks, BLOCK, width), BF)
    lanes = pltpu.VMEM((pairs, length, PAIR), BF)
    return pl.pallas_call(
        back_kernel,
        out_shape=[
            shape_of((length, width), BF),
            shape_of((length, width), BF),
            shape_of((3, depth, cols), F32),
            shape_of((cols, depth), F32),
            shape_of((depth, hidden), F32),
            shape_of((hidden, depth), F32),
            shape_of(small.shape, F32),
        ],
        in_specs=[VMEM_SPEC] * 13 + [ANY_SPEC] * 4,
        out_specs=[VMEM_SPEC] * 7,
        scratch_shapes=[
            pltpu.VMEM((length, PAIR), F32), pltpu.VMEM((length, PAIR), F32),
            lanes, lanes, lanes,
            pltpu.VMEM((pairs, Z_SIZE, Y_SIZE, CORES, depth, CHUNK), BF),
            pltpu.VMEM((pairs, Z_SIZE, Y_SIZE, depth, CHUNK), BF),
            pltpu.VMEM((pairs, Z_SIZE, depth, CHUNK), BF),
            pltpu.VMEM((3, pairs, depth, CHUNK), BF),
            pltpu.VMEM((chunks, Z_SIZE, depth, CHUNK), BF),
            pltpu.VMEM((3, chunks, depth, CHUNK), BF),
            rows, rows,
            pltpu.VMEM((length, width), BF),
            pltpu.VMEM((2, BLOCK, width), BF),
            pltpu.VMEM((2, GROUP, Z_SIZE, depth, CHUNK), BF),
            pltpu.VMEM((2, BLOCK, width), F32),
            pltpu.VMEM(small.shape, F32),
            pltpu.VMEM((Z_SIZE,) + small.shape, F32),
            pltpu.VMEM((2,) + small.shape, F32),
            pltpu.VMEM((2,) + small.shape, F32),
            dma((blocks,)), dma((blocks,)), dma((groups,)), dma((groups,)),
            dma((3 * groups,)), dma((3 * groups,)), dma((pairs,)), dma((pairs,)),
            dma((pairs,)), dma((pairs,)), dma((3 * pairs,)), dma((3 * pairs,)),
            dma((blocks,)), dma((blocks,)), dma((2,)), dma((5,)), dma((5,)), dma((2,)), dma((2,)),
        ],
        compiler_params=pltpu.CompilerParams(
            collective_id=2, has_side_effects=True, vmem_limit_bytes=VMEM_LIMIT
        ),
    )(
        queries, keys, values, mixture, grad_mixture, ga_t, normed_t, wqkv, x,
        key_more, query_more, params, small, middle, grad_middle, ff_part, branch,
    )


def fast_body(
    tokens, segment_ids, context_flags, ln1_gain, ln1_bias, qkv_weight, qv_bias, out_weight,
    out_bias, ln2_gain, ln2_bias, up_weight, up_bias, down_weight, down_bias, cotangent,
):
    width = tokens.shape[2]
    hidden = up_weight.shape[1]
    cols = qkv_weight.shape[2]
    up_rows = hidden // width
    x, dy = tokens[0], cotangent[0]
    params = jnp.concatenate(
        [
            ln1_gain, ln1_bias, qv_bias.reshape(-1), out_bias, ln2_gain, ln2_bias, up_bias,
            down_bias, jnp.zeros(((SMALL_ROWS - 7 - up_rows) * width,), BF),
        ]
    ).astype(F32).reshape(SMALL_ROWS, width)
    queries, keys, values, mixture, middle, normed_t, wff, key_more, query_more = run_fwd(
        x, segment_ids, context_flags, params, qkv_weight, out_weight, up_weight, down_weight,
    )
    branch, grad_middle, ga_t, grad_mixture, ff_part, small = run_ff(
        middle, dy, wff, params, out_weight
    )
    output, tokens_grad, qkv_grad, out_grad, up_grad, down_grad, small = run_back(
        queries, keys, values, mixture, grad_mixture, ga_t, normed_t, qkv_weight, x,
        key_more, query_more, params, small, middle, grad_middle, ff_part, branch,
    )
    return (
        output[None], tokens_grad[None], small[LN1_GAIN], small[LN1_BIAS], qkv_grad,
        small[QV_BIAS].reshape(2, cols), out_grad, small[OUT_BIAS], small[LN2_GAIN],
        small[LN2_BIAS], up_grad, small[UP_BIAS:UP_BIAS + up_rows].reshape(hidden), down_grad,
        small[DOWN_BIAS],
    )


def solution(mesh):
    chosen = generic_body
    if mesh.shape["head"] == 2 and mesh.shape["seq"] == SEQ_SIZE:
        chosen = fast_body
    return jax.shard_map(
        chosen,
        mesh=mesh,
        in_specs=(
            P("seq", None, None),
            P("seq", None),
            P("seq", None),
            P(),
            P(),
            P(None, None, "head"),
            P(None, "head"),
            P("head", None),
            P(),
            P(),
            P(),
            P("seq", "head"),
            P("head"),
            P("head", "seq"),
            P(),
            P("seq", None, None),
        ),
        out_specs=(
            P("seq", None, None),
            P("seq", None, None),
            P(),
            P(),
            P(None, "seq", "head"),
            P(None, "head"),
            P("head", "seq"),
            P(),
            P(),
            P(),
            P("seq", "head"),
            P("head"),
            P("head", "seq"),
            P(),
        ),
        check_vma=False,
    )
```

```python
import math

import jax
import jax.numpy as jnp
from jax import lax
from jax.experimental import pallas as pl
from jax.experimental.pallas import tpu as pltpu
from jax.sharding import PartitionSpec as P

HEAD_DIM = 64


def layer_norm(values_in, scaling, offset):
    middle = jnp.mean(values_in, axis=-1, keepdims=True)
    centred = values_in - middle
    spread = jnp.mean(centred * centred, axis=-1, keepdims=True)
    return centred * lax.rsqrt(spread + 1e-05) * scaling + offset


def gelu_exact(values_in):
    return 0.5 * values_in * (1.0 + jax.scipy.special.erf(values_in * 0.7071067811865476))


def dot_rows(left, right):
    return lax.dot_general(
        left, right, (((1,), (1,)), ((), ())), preferred_element_type=jnp.float32
    )


def dot_cols(left, right):
    return lax.dot_general(
        left, right, (((0,), (0,)), ((), ())), preferred_element_type=jnp.float32
    )


def masked_scores(block_query, seq_keys, block_segments, seq_segments, seq_context, factor):
    raw_scores = (
        jnp.einsum("qhd,khd->hqk", block_query, seq_keys, preferred_element_type=jnp.float32)
        * factor
    )
    allowed = (block_segments[:, None] == seq_segments[None, :]) & (seq_context[None, :] == 1)
    return jnp.where(allowed[None], raw_scores, -1e30)


def generic_body(
    tokens,
    segment_ids,
    context_flags,
    ln1_gain,
    ln1_bias,
    qkv_weight,
    qv_bias,
    out_weight,
    out_bias,
    ln2_gain,
    ln2_bias,
    up_weight,
    up_bias,
    down_weight,
    down_bias,
    cotangent,
):
    seq_count, length, width = tokens.shape
    row_count = seq_count * length
    local_cols = qkv_weight.shape[2]
    head_count = local_cols // HEAD_DIM
    factor = 1.0 / math.sqrt(HEAD_DIM)
    block = min(512, length)
    blocks = length // block
    gain_one = ln1_gain.astype(jnp.float32)
    offset_one = ln1_bias.astype(jnp.float32)
    gain_two = ln2_gain.astype(jnp.float32)
    offset_two = ln2_bias.astype(jnp.float32)
    flat_in = tokens.astype(jnp.float32).reshape(row_count, width)
    normed_f, norm_one_pull = jax.vjp(layer_norm, flat_in, gain_one, offset_one)
    normed = normed_f.astype(jnp.bfloat16)
    queries = (
        jnp.dot(normed, qkv_weight[0], preferred_element_type=jnp.float32)
        + qv_bias[0].astype(jnp.float32)
    ).astype(jnp.bfloat16)
    key_rows = jnp.dot(normed, qkv_weight[1], preferred_element_type=jnp.float32).astype(
        jnp.bfloat16
    )
    value_rows = (
        jnp.dot(normed, qkv_weight[2], preferred_element_type=jnp.float32)
        + qv_bias[1].astype(jnp.float32)
    ).astype(jnp.bfloat16)

    def per_sequence(array):
        return array.reshape(seq_count, length, head_count, HEAD_DIM)

    def attend_sequence(member):
        seq_query, seq_keys, seq_values, seq_segments, seq_context = member

        def attend_block(portion):
            block_query, block_segments = portion
            scores = masked_scores(
                block_query, seq_keys, block_segments, seq_segments, seq_context, factor
            )
            row_top = jnp.max(scores, axis=-1, keepdims=True)
            exponent = jnp.exp(scores - row_top)
            row_total = jnp.sum(exponent, axis=-1, keepdims=True)
            soft_weights = (exponent / row_total).astype(jnp.bfloat16)
            block_mix = jnp.einsum(
                "hqk,khd->qhd", soft_weights, seq_values, preferred_element_type=jnp.float32
            )
            return (block_mix.astype(jnp.bfloat16), row_top + jnp.log(row_total))

        return lax.map(
            attend_block,
            (
                seq_query.reshape(blocks, block, head_count, HEAD_DIM),
                seq_segments.reshape(blocks, block),
            ),
        )

    mixture, log_totals = lax.map(
        attend_sequence,
        (
            per_sequence(queries),
            per_sequence(key_rows),
            per_sequence(value_rows),
            segment_ids,
            context_flags,
        ),
    )
    mixture = mixture.reshape(row_count, local_cols)
    partial_out = jnp.dot(mixture, out_weight, preferred_element_type=jnp.float32)
    grad_rows_all = cotangent.reshape(row_count, width)
    grad_float_all = grad_rows_all.astype(jnp.float32)
    grad_down_bias = jnp.sum(grad_float_all, axis=0)
    attended = lax.psum(partial_out, "head") + out_bias.astype(jnp.float32)
    middle_state = flat_in + attended
    normed_two_f, norm_two_pull = jax.vjp(layer_norm, middle_state, gain_two, offset_two)
    normed_two = normed_two_f.astype(jnp.bfloat16)
    up_part, down_part, up_shift = (
        lax.all_gather(up_weight, "head", axis=1, tiled=True),
        lax.all_gather(down_weight, "head", axis=0, tiled=True),
        lax.all_gather(up_bias, "head", axis=0, tiled=True),
    )
    up_full, down_full = (
        lax.all_gather(up_part, "seq", axis=0, tiled=True),
        lax.all_gather(down_part, "seq", axis=1, tiled=True),
    )
    before = jnp.dot(normed_two, up_full, preferred_element_type=jnp.float32) + up_shift.astype(
        jnp.float32
    )
    active_f, gelu_pull = jax.vjp(gelu_exact, before)
    active = active_f.astype(jnp.bfloat16)
    branch_out = jnp.dot(active, down_full, preferred_element_type=jnp.float32)
    final_rows = (middle_state + branch_out + down_bias.astype(jnp.float32)).astype(jnp.bfloat16)
    output = final_rows.reshape(tokens.shape)
    grad_float = grad_rows_all.astype(jnp.float32)
    grad_down = dot_cols(active, grad_rows_all)
    grad_active = dot_rows(grad_rows_all, down_full)
    (grad_before_f,) = gelu_pull(grad_active)
    grad_before = grad_before_f.astype(jnp.bfloat16)
    grad_up = dot_cols(normed_two, grad_before)
    grad_up_bias = jnp.sum(grad_before.astype(jnp.float32), axis=0)
    grad_normed_two = dot_rows(grad_before, up_full)
    grad_middle_norm, grad_gain_two, grad_offset_two = norm_two_pull(grad_normed_two)
    grad_middle = grad_float + grad_middle_norm
    ff_part = up_weight.shape[1]
    start_col = lax.axis_index("head") * ff_part
    grad_up = lax.dynamic_slice_in_dim(grad_up, start_col, ff_part, 1)
    grad_down = lax.dynamic_slice_in_dim(grad_down, start_col, ff_part, 0)
    grad_up_bias = lax.dynamic_slice_in_dim(grad_up_bias, start_col, ff_part, 0)
    grad_attended = grad_middle.astype(jnp.bfloat16)
    grad_out_bias = jnp.sum(grad_attended.astype(jnp.float32), axis=0)
    grad_out = dot_cols(mixture, grad_attended)
    grad_mixture = dot_rows(grad_attended, out_weight).astype(jnp.bfloat16)

    def back_sequence(member):
        seq_query, seq_keys, seq_values, seq_grad, seq_logs, seq_segments, seq_context = member

        def back_block(carry, portion):
            key_acc, value_acc = carry
            block_query, block_grad, block_logs, block_segments = portion
            scores = masked_scores(
                block_query, seq_keys, block_segments, seq_segments, seq_context, factor
            )
            soft_weights = jnp.exp(scores - block_logs)
            value_acc = value_acc + jnp.einsum(
                "hqk,qhd->khd",
                soft_weights.astype(jnp.bfloat16),
                block_grad,
                preferred_element_type=jnp.float32,
            )
            grad_soft = jnp.einsum(
                "qhd,khd->hqk", block_grad, seq_values, preferred_element_type=jnp.float32
            )
            row_inner = jnp.sum(soft_weights * grad_soft, axis=-1, keepdims=True)
            grad_scores = (soft_weights * (grad_soft - row_inner)).astype(jnp.bfloat16)
            grad_query = (
                jnp.einsum(
                    "hqk,khd->qhd", grad_scores, seq_keys, preferred_element_type=jnp.float32
                )
                * factor
            )
            key_acc = (
                key_acc
                + jnp.einsum(
                    "hqk,qhd->khd", grad_scores, block_query, preferred_element_type=jnp.float32
                )
                * factor
            )
            return ((key_acc, value_acc), grad_query)

        empty = jnp.zeros((length, head_count, HEAD_DIM), jnp.float32)
        (key_acc, value_acc), grad_query = lax.scan(
            back_block,
            (empty, empty),
            (
                seq_query.reshape(blocks, block, head_count, HEAD_DIM),
                seq_grad.reshape(blocks, block, head_count, HEAD_DIM),
                seq_logs,
                seq_segments.reshape(blocks, block),
            ),
        )
        return (grad_query, key_acc, value_acc)

    grad_queries, grad_keys, grad_values = lax.map(
        back_sequence,
        (
            per_sequence(queries),
            per_sequence(key_rows),
            per_sequence(value_rows),
            per_sequence(grad_mixture),
            log_totals,
            segment_ids,
            context_flags,
        ),
    )
    grad_queries = grad_queries.reshape(row_count, local_cols).astype(jnp.bfloat16)
    grad_keys = grad_keys.reshape(row_count, local_cols).astype(jnp.bfloat16)
    grad_values = grad_values.reshape(row_count, local_cols).astype(jnp.bfloat16)
    grad_qv_bias = jnp.stack(
        [
            jnp.sum(grad_queries.astype(jnp.float32), axis=0),
            jnp.sum(grad_values.astype(jnp.float32), axis=0),
        ]
    )
    grad_qkv = jnp.stack(
        [dot_cols(normed, grad_queries), dot_cols(normed, grad_keys), dot_cols(normed, grad_values)]
    )
    grad_normed = (
        dot_rows(grad_queries, qkv_weight[0])
        + dot_rows(grad_keys, qkv_weight[1])
        + dot_rows(grad_values, qkv_weight[2])
    )
    grad_normed = lax.psum(grad_normed, "head")
    grad_input_norm, grad_gain_one, grad_offset_one = norm_one_pull(grad_normed)
    tokens_grad = (grad_middle + grad_input_norm).astype(jnp.bfloat16).reshape(tokens.shape)
    summed_qkv, summed_out, summed_up, summed_down = (
        lax.psum_scatter(
            grad_qkv.astype(jnp.bfloat16), "seq", scatter_dimension=1, tiled=True
        ).astype(jnp.float32),
        lax.psum_scatter(
            grad_out.astype(jnp.bfloat16), "seq", scatter_dimension=1, tiled=True
        ).astype(jnp.float32),
        lax.psum_scatter(
            grad_up.astype(jnp.bfloat16), "seq", scatter_dimension=0, tiled=True
        ).astype(jnp.float32),
        lax.psum_scatter(
            grad_down.astype(jnp.bfloat16), "seq", scatter_dimension=1, tiled=True
        ).astype(jnp.float32),
    )
    smalls = lax.psum(
        (
            grad_gain_one,
            grad_offset_one,
            grad_qv_bias,
            grad_out_bias,
            grad_gain_two,
            grad_offset_two,
            grad_up_bias,
            grad_down_bias,
        ),
        "seq",
    )
    return (
        output,
        tokens_grad,
        smalls[0],
        smalls[1],
        summed_qkv,
        smalls[2],
        summed_out,
        smalls[3],
        smalls[4],
        smalls[5],
        summed_up,
        smalls[6],
        summed_down,
        smalls[7],
    )


MESH = pl.DeviceIdType.MESH
BF = jnp.bfloat16
F32 = jnp.float32
BLOCK = 256
STRIP = 128
GROUP = 2
CHUNK = 512
PAIR = 2 * HEAD_DIM
Z_SIZE, Y_SIZE, CORES = 4, 2, 2
SEQ_SIZE = Z_SIZE * Y_SIZE * CORES
HOP = Y_SIZE * CORES
TABLES = 8
FAR = -1e30
VMEM_LIMIT = 62 * 2**20
INV_ROOT_TWO = 0.7071067811865476
INV_ROOT_TWO_PI = 0.3989422804014327
LN1_GAIN, LN1_BIAS, QV_BIAS, OUT_BIAS, LN2_GAIN, LN2_BIAS, UP_BIAS, DOWN_BIAS = 0, 1, 2, 3, 4, 5, 6, 8
SMALL_ROWS = 16
VMEM_SPEC = pl.BlockSpec(memory_space=pltpu.VMEM)
ANY_SPEC = pl.BlockSpec(memory_space=pl.ANY)


def shape_of(dims, dtype):
    return jax.ShapeDtypeStruct(tuple(dims), dtype)


def nn(left, right):
    return jnp.dot(left, right, preferred_element_type=F32)


def turn(block):
    return jnp.transpose(block)


def sum_rows(block):
    return jnp.sum(block, axis=0, keepdims=True)


def place():
    me = lax.axis_index("seq")
    head = lax.axis_index("head")
    core = me % 2
    y = (me // 2) % 2
    across = {"seq": me, "head": 1 - head}
    core_mate = {"seq": me + 1 - 2 * core, "head": head}
    y_mate = {"seq": me + 2 - 4 * y, "head": head}
    z_mates = [{"seq": (me + HOP * d) % SEQ_SIZE, "head": head} for d in (1, 2, 3)]
    return me, head, core, y, across, core_mate, y_mate, z_mates


def greet(others):
    barrier = pltpu.get_barrier_semaphore()
    for other in others:
        pl.semaphore_signal(barrier, inc=1, device_id=other, device_id_type=MESH)
    pl.semaphore_wait(barrier, len(others))


def remote(src, dst, send_sem, recv_sem, other):
    return pltpu.make_async_remote_copy(
        src_ref=src, dst_ref=dst, send_sem=send_sem, recv_sem=recv_sem,
        device_id=other, device_id_type=MESH,
    )


def norm_stats(rows):
    middle = jnp.mean(rows, axis=-1, keepdims=True)
    centred = rows - middle
    spread = jnp.mean(centred * centred, axis=-1, keepdims=True)
    return centred, lax.rsqrt(spread + 1e-05)


def norm_back(inner, unit, scale):
    return scale * (
        inner
        - jnp.mean(inner, axis=-1, keepdims=True)
        - unit * jnp.mean(inner * unit, axis=-1, keepdims=True)
    )


def as_row(vector):
    return vector[...].astype(F32).reshape(1, -1)


def lanes():
    return lax.broadcasted_iota(jnp.int32, (1, PAIR), 1)


def in_pieces(column, first, rest):
    high = column.astype(BF).astype(F32)
    mid = (column - high).astype(BF).astype(F32)
    low = column - high - mid
    at = lanes()
    return jnp.where(
        at == first, high, jnp.where(at == first + 1, mid, jnp.where(at == first + 2, low, rest))
    ).astype(BF)


def one_lanes(length):
    return jnp.broadcast_to(jnp.where(lanes() < 3, 1.0, 0.0).astype(BF), (length, PAIR))


def fwd_kernel(
    x_ref, seg_ref, context, gain, offset, qv_bias, out_bias, wqkv, wout, up_shard, down_shard,
    q_out, k_out, v_out, mix_out, mid_out, normed_out, wff, key_out, query_out,
    q_ref, k_ref, v_ref, mix_ref, mid_ref, normed_t, key_more, query_more,
    mask_more, wout_x, mix_x,
    zs, zr, ys, yr, cs, cr, xs, xr, local, outs,
):
    length, width = x_ref.shape
    blocks = length // BLOCK
    pairs = q_ref.shape[0]
    cols = pairs * PAIR
    me, head, core, y, across, core_mate, y_mate, _ = place()
    z = me // HOP
    above = {"seq": (me + HOP) % SEQ_SIZE, "head": head}
    below = {"seq": (me + SEQ_SIZE - HOP) % SEQ_SIZE, "head": head}
    greet([across, core_mate, y_mate, above, below])

    out_copy = remote(wout, wout_x, xs.at[0], xr.at[0], across)
    out_copy.start()
    shards = (up_shard, down_shard)
    own = [pltpu.make_async_copy(shards[u], wff.at[u, me], local.at[u]) for u in range(2)]

    flows = [(0, 0)] + [(way, s) for s in (1, 2, 3) for way in (0, 1)]

    def there(way, s):
        return (z >= s) if way == 0 else (z + s < Z_SIZE)

    def source(base, way, s):
        away = SEQ_SIZE - HOP * s if way == 0 else HOP * s
        return (base + away) % SEQ_SIZE

    def z_copy(u, way, s):
        n = (u * 2 + way) * 3 + s - 1
        j = source(me, way, s - 1)
        src = shards[u] if s == 1 else wff.at[u, j]
        return remote(src, wff.at[u, j], zs.at[n], zr.at[n], above if way == 0 else below)

    def z_arrival(u, way, s):
        n = (u * 2 + way) * 3 + s - 1
        slot = wff.at[u, source(me, way, s)]
        return remote(slot, slot, zs.at[n], zr.at[n], above)

    def z_goes_on(way):
        return (z < Z_SIZE - 1) if way == 0 else (z > 0)

    def y_copy(u, f):
        n = u * 7 + f
        j = source(me, *flows[f])
        src = shards[u] if f == 0 else wff.at[u, j]
        return remote(src, wff.at[u, j], ys.at[n], yr.at[n], y_mate)

    def y_arrival(u, f):
        n = u * 7 + f
        slot = wff.at[u, source(me + 2 - 4 * y, *flows[f])]
        return remote(slot, slot, ys.at[n], yr.at[n], y_mate)

    def c_copy(u, f, from_y):
        n = (u * 2 + from_y) * 7 + f
        j = source(me + from_y * (2 - 4 * y), *flows[f])
        src = shards[u] if f == 0 and from_y == 0 else wff.at[u, j]
        return remote(src, wff.at[u, j], cs.at[n], cr.at[n], core_mate)

    def c_arrival(u, f, from_y):
        n = (u * 2 + from_y) * 7 + f
        slot = wff.at[u, source(me + 1 - 2 * core + from_y * (2 - 4 * y), *flows[f])]
        return remote(slot, slot, cs.at[n], cr.at[n], core_mate)

    def for_flow(f, do):
        if f == 0:
            do()
        else:
            pl.when(there(*flows[f]))(do)

    def for_step(s, do):
        for f, (way, step) in enumerate(flows):
            if step == s:
                for_flow(f, lambda f=f, way=way: do(f, way))

    def z_event(u, s):
        def one(f, way):
            z_arrival(u, way, s).wait_recv()
            if s < 3:
                pl.when(z_goes_on(way))(lambda: z_copy(u, way, s + 1).start())
            y_copy(u, f).start()
            c_copy(u, f, 0).start()
        for_step(s, one)

    def y_event(u, s):
        def one(f, way):
            y_arrival(u, f).wait_recv()
            c_copy(u, f, 1).start()
        for_step(s, one)

    for u in range(2):
        for way in (0, 1):
            pl.when(z_goes_on(way))(lambda u=u, way=way: z_copy(u, way, 1).start())
        y_copy(u, 0).start()
        c_copy(u, 0, 0).start()
        own[u].start()

    plan = {
        1: [(z_event, 0, 1), (y_event, 0, 0)], 3: [(z_event, 1, 1), (y_event, 1, 0)],
        5: [(z_event, 0, 2)], 7: [(z_event, 1, 2)], 9: [(y_event, 0, 1)], 11: [(z_event, 0, 3)],
        12: [(y_event, 1, 1)], 14: [(z_event, 1, 3)], 16: [(y_event, 0, 2)], 18: [(y_event, 1, 2)],
    }
    last = [(y_event, 0, 3), (y_event, 1, 3)]

    def tick(t):
        for step, events in plan.items():
            @pl.when(t == step)
            def _(events=events):
                for event, u, s in events:
                    event(u, s)

    at = lax.broadcasted_iota(jnp.int32, (PAIR, length), 0)
    same = at == seg_ref[...]
    hidden = context[...] != 1
    ones = jnp.logical_and(at > TABLES, at < TABLES + 4)
    key_side = jnp.logical_or(
        jnp.logical_and(at < TABLES, same),
        jnp.logical_or(jnp.logical_and(at == TABLES, hidden), ones),
    )
    query_side = jnp.logical_and(at <= TABLES, jnp.logical_not(same))
    key_more[...] = turn(jnp.where(key_side, 1.0, 0.0)).astype(BF)
    mask_more[...] = turn(jnp.where(query_side, FAR, 0.0)).astype(BF)

    keep = [
        pltpu.make_async_copy(here, there, outs.at[n])
        for n, (here, there) in enumerate(
            (
                (q_ref, q_out), (k_ref, k_out), (v_ref, v_out), (normed_t, normed_out),
                (key_more, key_out), (query_more, query_out), (mix_ref, mix_out),
            )
        )
    ]
    gains, offsets = as_row(gain), as_row(offset)
    query_bias = qv_bias[0:1, :].astype(F32)
    value_bias = qv_bias[1:2, :].astype(F32)

    def project(b, _):
        rows = pl.ds(pl.multiple_of(b * BLOCK, BLOCK), BLOCK)
        centred, scale = norm_stats(x_ref[rows, :].astype(F32))
        block = (centred * scale * gains + offsets).astype(BF)
        normed_t[b] = turn(block)
        queries = ((nn(block, wqkv[0]) + query_bias).astype(BF) * 0.125).astype(BF)
        keys = nn(block, wqkv[1]).astype(BF)
        values = (nn(block, wqkv[2]) + value_bias).astype(BF)
        for p in range(pairs):
            part = slice(p * PAIR, (p + 1) * PAIR)
            q_ref[p, rows, :] = queries[:, part]
            k_ref[p, rows, :] = keys[:, part]
            v_ref[p, rows, :] = values[:, part]
        tick(b)
        return 0

    lax.fori_loop(0, blocks, project, 0)
    for n in range(5):
        keep[n].start()

    low_lanes = lanes() < HEAD_DIM
    zero = jnp.zeros((1, PAIR), BF)

    def mixture_copy(b):
        rows = pl.ds(b * BLOCK, BLOCK)
        return remote(
            mix_ref.at[:, rows, :], mix_x.at[:, rows, :], xs.at[1 + b], xr.at[1 + b], across
        )

    def attend(t, _):
        b, p = t // pairs, t % pairs
        rows = pl.ds(pl.multiple_of(b * BLOCK, BLOCK), BLOCK)
        queries, more = q_ref[p, rows, :], mask_more[rows, :]
        keys = jnp.concatenate([k_ref[p], key_more[...]], axis=1)
        values = jnp.concatenate([v_ref[p], one_lanes(length)], axis=1)
        parts = []
        for low in (0, 1):
            own_lanes = jnp.logical_not(low_lanes) if low else low_lanes
            left = jnp.concatenate([jnp.where(own_lanes, queries, zero), more], axis=1)
            scores = dot_rows(left, keys)
            top = jnp.max(scores, axis=-1, keepdims=True)
            mixed = nn(jnp.exp(scores - top).astype(BF), values)
            total = mixed[:, PAIR:PAIR + 1]
            parts.append(mixed[:, :PAIR] / total)
            query_more[2 * p + low, rows, :] = in_pieces(
                -(top + jnp.log(total)), TABLES + 1, more.astype(F32)
            )
        mix_ref[p, rows, :] = jnp.where(low_lanes, parts[0], parts[1]).astype(BF)
        tick(t + blocks)
        for b_done in range(blocks):
            @pl.when(t == (b_done + 1) * pairs - 1)
            def _(b_done=b_done):
                mixture_copy(b_done).start()
        return 0

    lax.fori_loop(0, blocks * pairs, attend, 0)
    keep[5].start()
    keep[6].start()
    out_copy.wait_recv()
    out_row = as_row(out_bias)

    def mid_copy(b):
        rows = pl.ds(b * BLOCK, BLOCK)
        return pltpu.make_async_copy(mid_ref.at[rows, :], mid_out.at[rows, :], outs.at[7 + b])

    for b in range(blocks):
        if b == blocks - 1:
            for event, u, s in last:
                event(u, s)
        mixture_copy(b).wait_recv()
        rows = pl.ds(b * BLOCK, BLOCK)
        ours = jnp.concatenate([mix_ref[p, rows, :] for p in range(pairs)], axis=-1)
        other = jnp.concatenate([mix_x[p, rows, :] for p in range(pairs)], axis=-1)
        attended = nn(ours, wout[...]) + nn(other, wout_x[...])
        mid_ref[rows, :] = x_ref[rows, :].astype(F32) + (attended + out_row)
        mid_copy(b).start()

    out_copy.wait_send()
    for copy in keep:
        copy.wait()
    for b in range(blocks):
        mixture_copy(b).wait_send()
        mid_copy(b).wait()
    for u in range(2):
        own[u].wait()
        for way in (0, 1):
            pl.when(z_goes_on(way))(lambda u=u, way=way: z_copy(u, way, 1).wait_send())
        for f, (way, s) in enumerate(flows):
            def finish(u=u, f=f, way=way, s=s):
                if f and s < 3:
                    pl.when(z_goes_on(way))(lambda: z_copy(u, way, s + 1).wait_send())
                y_copy(u, f).wait_send()
                for from_y in (0, 1):
                    c_copy(u, f, from_y).wait_send()
                    c_arrival(u, f, from_y).wait_recv()
            for_flow(f, finish)


def run_fwd(x, seg, context, gain, offset, qv_bias, out_bias, wqkv, wout, up_weight, down_t):
    length, width = x.shape
    pairs = wqkv.shape[2] // PAIR
    blocks = length // BLOCK
    depth, hidden = up_weight.shape
    by_pair, by_head = (pairs, length, PAIR), (2 * pairs, length, PAIR)
    turned = (blocks, width, BLOCK)
    dma = pltpu.SemaphoreType.DMA
    return pl.pallas_call(
        fwd_kernel,
        out_shape=[shape_of(by_pair, BF)] * 4 + [
            shape_of((length, width), F32),
            shape_of(turned, BF),
            shape_of((2, SEQ_SIZE, depth, hidden), BF),
            shape_of((length, PAIR), BF),
            shape_of(by_head, BF),
        ],
        in_specs=[VMEM_SPEC] * 9 + [ANY_SPEC] * 2,
        out_specs=[ANY_SPEC] * 9,
        scratch_shapes=[pltpu.VMEM(by_pair, BF)] * 4 + [
            pltpu.VMEM((length, width), F32),
            pltpu.VMEM(turned, BF),
            pltpu.VMEM((length, PAIR), BF),
            pltpu.VMEM(by_head, BF),
            pltpu.VMEM((length, PAIR), BF),
            pltpu.VMEM(wout.shape, BF),
            pltpu.VMEM(by_pair, BF),
            dma((12,)), dma((12,)), dma((14,)), dma((14,)), dma((28,)), dma((28,)),
            dma((1 + blocks,)), dma((1 + blocks,)), dma((2,)), dma((7 + blocks,)),
        ],
        compiler_params=pltpu.CompilerParams(
            collective_id=0, has_side_effects=True, vmem_limit_bytes=VMEM_LIMIT
        ),
    )(x, seg, context, gain, offset, qv_bias, out_bias, wqkv, wout, up_weight, down_t)


def ff_kernel(
    mid_hbm, dy_hbm, wff_hbm, gain, offset, up_bias, wout_hbm,
    branch_out, gmid_hbm, ga_out, gm_out, summed, small_ref,
    dy_ref, wff, wout, bias_row, branch_ref, ga_t, gm_ref, normed, normed_t, dy_t, active, before_grad, gnt_acc, gnt_own, gnt_x, whole, from_mate,
    held, ready,
    xs, xr, cs, cr, ls, ws, ss, ins, outs,
):
    length, width = dy_ref.shape
    blocks = length // BLOCK
    hidden = wff.shape[3]
    half = hidden // CHUNK
    chunks = 2 * half
    pairs = gm_ref.shape[0]
    me, head, core, y, across, core_mate, y_mate, z_mates = place()
    dy_load = pltpu.make_async_copy(dy_hbm, dy_ref, ins.at[0])
    wout_load = pltpu.make_async_copy(wout_hbm, wout, ins.at[1])

    def wff_load(n):
        cut = pl.ds(n * CHUNK, CHUNK)
        return pltpu.make_async_copy(
            wff_hbm.at[:, :, :, cut], wff.at[:, :, :, cut], ins.at[2 + n]
        )

    dy_load.start()
    for n in range(half):
        wff_load(n).start()
    wout_load.start()
    greet([across, core_mate])
    gains, offsets = as_row(gain), as_row(offset)
    bias_row[...] = as_row(up_bias)
    per_row = width // CHUNK

    def weight(kind, n):
        cut = pl.ds(pl.multiple_of(n * CHUNK, CHUNK), CHUNK)
        return wff[kind, :, :, cut].reshape(width, CHUNK)

    small_ref[...] = jnp.zeros_like(small_ref)

    def load(n):
        rows = pl.ds(n % blocks * BLOCK, BLOCK)
        return pltpu.make_async_copy(mid_hbm.at[rows, :], held.at[n % 2], ls.at[n % 2])

    def store(b):
        rows = pl.ds(b * BLOCK, BLOCK)
        return pltpu.make_async_copy(ready.at[b % 2], gmid_hbm.at[rows, :], ws.at[b % 2])

    load(0).start()
    load(1).start()

    def gnt_copy(b):
        return remote(gnt_own.at[b], gnt_x.at[b], xs.at[b], xr.at[b], across)

    def core_copy(n):
        return remote(
            whole.at[n, :, :, 1 - core], from_mate.at[n], cs.at[n], cr.at[n], core_mate
        )

    def forward(t, _):
        b, n = t // half, t % half
        rows = pl.ds(pl.multiple_of(b * BLOCK, BLOCK), BLOCK)

        for b_next in range(blocks):
            @pl.when(t == b_next * half)
            def _(b_next=b_next):
                load(b_next).wait()
                if b_next == 0:
                    dy_load.wait()

        for n_first in range(half):
            @pl.when(t == n_first)
            def _(n_first=n_first):
                wff_load(n_first).wait()

        @pl.when(n == 0)
        def _():
            centred, scale = norm_stats(held[b % 2])
            block = (centred * scale * gains + offsets).astype(BF)
            normed[...] = block
            normed_t[b] = turn(block)
            dy_t[b] = turn(dy_ref[rows, :])
            small_ref[DOWN_BIAS:DOWN_BIAS + 1, :] += sum_rows(dy_ref[rows, :].astype(F32))

        up = weight(0, n)
        cut = pl.ds(pl.multiple_of(n * CHUNK, CHUNK), CHUNK)
        small_at = pl.ds(UP_BIAS + n // per_row, 1)
        small_cut = pl.ds(pl.multiple_of(n % per_row * CHUNK, CHUNK), CHUNK)
        before = nn(normed[...], up) + bias_row[:, cut]
        spread = 0.5 * (1.0 + lax.erf(before * INV_ROOT_TWO))
        active[n, rows, :] = (before * spread).astype(BF)
        slope = spread + before * (INV_ROOT_TWO_PI * jnp.exp(before * before * -0.5))
        grad = (nn(dy_ref[rows, :], weight(1, n)) * slope).astype(BF)
        before_grad[n, rows, :] = grad
        small_ref[small_at, small_cut] += sum_rows(grad.astype(F32))
        back = dot_rows(grad, up)

        @pl.when(n == 0)
        def _():
            gnt_acc[...] = back

        @pl.when(n > 0)
        def _():
            gnt_acc[...] += back

        for b_done in range(blocks):
            @pl.when(t == (b_done + 1) * half - 1)
            def _(b_done=b_done):
                load(b_done + 2).start()
                gnt_own[b_done] = gnt_acc[...].astype(BF)
                gnt_copy(b_done).start()
        return 0

    lax.fori_loop(0, blocks * half, forward, 0)

    def weight_grads(left_t, right, first):
        top, planes = width // 2, Z_SIZE // 2

        def one(t, _):
            n, side = t // 2, t % 2
            cut = pl.ds(pl.multiple_of(side * top, top), top)
            total = nn(left_t[0, cut, :], right[n, pl.ds(0, BLOCK), :])
            for b in range(1, blocks):
                total += nn(left_t[b, cut, :], right[n, pl.ds(b * BLOCK, BLOCK), :])
            piece = total.astype(BF).reshape((planes,) + whole.shape[2:])
            whole[first + n, pl.ds(side * planes, planes)] = piece

            @pl.when(side == 1)
            def _():
                core_copy(first + n).start()

            return 0

        lax.fori_loop(0, 2 * half, one, 0)

    weight_grads(dy_t, active, half)
    weight_grads(normed_t, before_grad, 0)

    def branch(b, _):
        rows = pl.ds(pl.multiple_of(b * BLOCK, BLOCK), BLOCK)
        total = dot_rows(active[0, rows, :], weight(1, 0))
        for n in range(1, half):
            total += dot_rows(active[n, rows, :], weight(1, n))
        branch_ref[rows, :] = total.astype(BF)
        return 0

    lax.fori_loop(0, blocks, branch, 0)
    branch_keep = pltpu.make_async_copy(branch_ref, branch_out, outs.at[0])
    branch_keep.start()
    wout_load.wait()

    def ga_copy(b):
        return pltpu.make_async_copy(ga_t.at[b], ga_out.at[b], outs.at[1 + b])

    def gm_copy(b):
        rows = pl.ds(b * BLOCK, BLOCK)
        return pltpu.make_async_copy(
            gm_ref.at[:, rows, :], gm_out.at[:, rows, :], outs.at[1 + blocks + b]
        )


    def add_mate(n, _):
        core_copy(n).wait()
        both = whole[n, :, :, core].astype(F32) + from_mate[n].astype(F32)
        from_mate[n] = both.astype(BF)
        return 0

    lax.fori_loop(half, chunks, add_mate, 0)
    lax.fori_loop(0, half, add_mate, 0)
    keep = pltpu.make_async_copy(from_mate, summed, ss.at[0])
    keep.start()

    strips = BLOCK // STRIP
    for b in range(blocks):
        gnt_copy(b).wait()
        load(blocks + b).wait()
        if b >= 2:
            store(b - 2).wait()

        def through_norm(n, _, b=b):
            rows = pl.ds(pl.multiple_of(n * STRIP, STRIP), STRIP)
            full = pl.ds(pl.multiple_of(b * BLOCK + n * STRIP, STRIP), STRIP)
            grad = gnt_own[b, rows, :].astype(F32) + gnt_x[b, rows, :].astype(F32)
            centred, scale = norm_stats(held[b % 2, rows, :])
            unit = centred * scale
            small_ref[LN2_GAIN:LN2_GAIN + 1, :] += sum_rows(grad * unit)
            small_ref[LN2_BIAS:LN2_BIAS + 1, :] += sum_rows(grad)
            total = dy_ref[full, :].astype(F32) + norm_back(grad * gains, unit, scale)
            ready[b % 2, rows, :] = total
            low = total.astype(BF)
            small_ref[OUT_BIAS:OUT_BIAS + 1, :] += sum_rows(low.astype(F32))
            ga_t[b, :, rows] = turn(low)
            mixed = dot_rows(low, wout[...]).astype(BF)
            for p in range(pairs):
                gm_ref[p, full, :] = mixed[:, p * PAIR:(p + 1) * PAIR]
            return 0

        lax.fori_loop(0, strips, through_norm, 0)
        store(b).start()
        ga_copy(b).start()
        gm_copy(b).start()
        if b + 2 < blocks:
            load(blocks + b + 2).start()
    store(blocks - 2).wait()
    store(blocks - 1).wait()
    for b in range(blocks):
        ga_copy(b).wait()
        gm_copy(b).wait()
    branch_keep.wait()
    keep.wait()


def run_ff(middle, dy, wff, gain, offset, up_bias, wout):
    length, width = middle.shape
    half = wff.shape[3] // CHUNK
    chunks = 2 * half
    blocks = length // BLOCK
    pairs = wout.shape[0] // PAIR
    depth = width // SEQ_SIZE
    dma = pltpu.SemaphoreType.DMA
    turned = pltpu.VMEM((blocks, width, BLOCK), BF)
    rows = pltpu.VMEM((blocks, BLOCK, width), BF)
    hidden = pltpu.VMEM((half, length, CHUNK), BF)
    return pl.pallas_call(
        ff_kernel,
        out_shape=[
            shape_of((length, width), BF),
            shape_of((length, width), F32),
            shape_of((blocks, width, BLOCK), BF),
            shape_of((pairs, length, PAIR), BF),
            shape_of((chunks, Z_SIZE, Y_SIZE, depth, CHUNK), BF),
            shape_of((SMALL_ROWS, width), F32),
        ],
        in_specs=[ANY_SPEC] * 3 + [VMEM_SPEC] * 3 + [ANY_SPEC],
        out_specs=[ANY_SPEC] * 5 + [VMEM_SPEC],
        scratch_shapes=[
            pltpu.VMEM((length, width), BF), pltpu.VMEM(wff.shape, BF),
            pltpu.VMEM(wout.shape, BF), pltpu.VMEM((1, half * CHUNK), F32),
            pltpu.VMEM((length, width), BF), turned, pltpu.VMEM((pairs, length, PAIR), BF),
            pltpu.VMEM((BLOCK, width), BF), turned, turned, hidden, hidden,
            pltpu.VMEM((BLOCK, width), F32), rows, rows,
            pltpu.VMEM((chunks, Z_SIZE, Y_SIZE, CORES, depth, CHUNK), BF),
            pltpu.VMEM((chunks, Z_SIZE, Y_SIZE, depth, CHUNK), BF),
            pltpu.VMEM((2, BLOCK, width), F32), pltpu.VMEM((2, BLOCK, width), F32),
            dma((blocks,)), dma((blocks,)), dma((chunks,)), dma((chunks,)),
            dma((2,)), dma((2,)), dma((1,)), dma((2 + half,)), dma((1 + 2 * blocks,)),
        ],
        compiler_params=pltpu.CompilerParams(
            collective_id=1, has_side_effects=True, vmem_limit_bytes=VMEM_LIMIT
        ),
    )(middle, dy, wff, gain, offset, up_bias, wout)


def back_kernel(
    q_hbm, k_hbm, v_hbm, mix_hbm, gm_hbm, query_hbm, ga_hbm, normed_hbm, wqkv_hbm, x_hbm,
    key_more, gain, down_bias, small_in, mid_hbm, gmid_hbm, ff_part, branch,
    out_hbm, tokens_hbm, qkv_sum, out_sum, up_sum, down_sum,
    gain_one, offset_one, qv_small, out_small, gain_two, offset_two, up_small, down_small,
    q_ref, k_ref, v_ref, mix_ref, gm_ref, query_more, ga_t, normed_t, wqkv, x_ref,
    out_ref, tokens_ref, key_t, key_acc, value_acc, dq, dk, dv, whole, mate, at_y, at_z, ff_y, ff_z, gn_own, gn_x,
    branch_x, branch_own, ff_own, held, small_own, small_z, small_y, small_c,
    bs, br, fys, fyr, fzs, fzr, acs, acr, ays, ayr, azs, azr, gs, gr, ls, ms, mr, os, hs, ins, more_ins, outs,
):
    length, width = x_ref.shape
    blocks = length // BLOCK
    strips = length // STRIP
    pairs = q_ref.shape[0]
    chunks = ff_part.shape[0]
    half = chunks // 2
    groups = chunks // GROUP
    me, head, core, y, across, core_mate, y_mate, z_mates = place()
    z = me // (Y_SIZE * CORES)
    by_pair = (
        (q_hbm, q_ref), (k_hbm, k_ref), (v_hbm, v_ref), (mix_hbm, mix_ref), (gm_hbm, gm_ref),
    )

    def pair_loads(p):
        both = pl.ds(2 * p, 2)
        first = p * (len(by_pair) + 1)
        return [
            pltpu.make_async_copy(src.at[p], dst.at[p], ins.at[first + n])
            for n, (src, dst) in enumerate(by_pair)
        ] + [
            pltpu.make_async_copy(
                query_hbm.at[both], query_more.at[both], ins.at[first + len(by_pair)]
            )
        ]

    late_loads = [
        pltpu.make_async_copy(src, dst, more_ins.at[n])
        for n, (src, dst) in enumerate(
            ((ga_hbm, ga_t), (normed_hbm, normed_t), (wqkv_hbm, wqkv), (x_hbm, x_ref))
        )
    ]
    for p in range(pairs):
        for copy in pair_loads(p):
            copy.start()
        if p == 0:
            late_loads[0].start()
            late_loads[1].start()
    late_loads[2].start()
    late_loads[3].start()
    greet([across, core_mate, y_mate, *z_mates])

    def part(b):
        return pl.ds(b * BLOCK, BLOCK)

    def branch_copy(b):
        return remote(branch.at[part(b), :], branch_x.at[part(b), :], bs.at[b], br.at[b], across)

    def load(n):
        source = mid_hbm if n < blocks else gmid_hbm
        return pltpu.make_async_copy(
            source.at[part(n % blocks), :], held.at[n % 2], ls.at[n % 2]
        )

    def taken(n):
        if n + 2 < 2 * blocks:
            load(n + 2).start()

    def group(g):
        return pl.ds(g * GROUP, GROUP)

    def ff_y_copy(g):
        return remote(
            ff_part.at[group(g), :, 1 - y], ff_y.at[group(g)], fys.at[g], fyr.at[g], y_mate
        )

    def ff_z_copy(g, d):
        n = g * 3 + d - 1
        return remote(
            ff_y.at[group(g), (z + d) % Z_SIZE], ff_z.at[d - 1, group(g)],
            fzs.at[n], fzr.at[n], z_mates[d - 1],
        )

    def branch_load(b):
        return pltpu.make_async_copy(branch.at[part(b), :], branch_own.at[b % 2], hs.at[b % 2])

    def ff_load(g):
        return pltpu.make_async_copy(
            ff_part.at[group(g), :, y], ff_own.at[g % 2], os.at[g % 2]
        )

    def ff_y_event(g):
        ff_y_copy(g).wait_recv()
        ff_load(g).wait()
        for n in range(g * GROUP, (g + 1) * GROUP):
            own = ff_own[g % 2, n % GROUP]
            ff_y[n] = (ff_y[n].astype(F32) + own.astype(F32)).astype(BF)
        if g + 2 < groups:
            ff_load(g + 2).start()
            ff_y_copy(g + 2).start()
        for d in (1, 2, 3):
            ff_z_copy(g, d).start()

    def ff_z_event(g):
        for d in (1, 2, 3):
            ff_z_copy(g, d).wait_recv()
        for n in range(g * GROUP, (g + 1) * GROUP):
            total = ff_y[n, z].astype(F32)
            for d in (1, 2, 3):
                total += ff_z[d - 1, n].astype(F32)
            if n < half:
                up_sum[:, n * CHUNK:(n + 1) * CHUNK] = total
            else:
                down_sum[:, (n - half) * CHUNK:(n - half + 1) * CHUNK] = total

    def at_c_copy(p):
        return remote(whole.at[p, :, :, 1 - core], mate.at[p], acs.at[p], acr.at[p], core_mate)

    def at_y_copy(p):
        return remote(mate.at[p, :, 1 - y], at_y.at[p], ays.at[p], ayr.at[p], y_mate)

    def at_z_copy(p, d):
        n = p * 3 + d - 1
        return remote(
            at_y.at[p, (z + d) % Z_SIZE], at_z.at[d - 1, p], azs.at[n], azr.at[n], z_mates[d - 1]
        )

    def at_c_event(p):
        at_c_copy(p).wait_recv()
        mate[p] = (mate[p].astype(F32) + whole[p, :, :, core].astype(F32)).astype(BF)
        at_y_copy(p).start()

    def at_y_event(p):
        at_y_copy(p).wait_recv()
        at_y[p] = (at_y[p].astype(F32) + mate[p, :, y].astype(F32)).astype(BF)
        for d in (1, 2, 3):
            at_z_copy(p, d).start()

    def at_z_event(p):
        for d in (1, 2, 3):
            at_z_copy(p, d).wait_recv()
        total = at_y[p, z].astype(F32)
        for d in (1, 2, 3):
            total += at_z[d - 1, p].astype(F32)
        cut = slice(p * PAIR, (p + 1) * PAIR)
        for kind in range(3):
            qkv_sum[kind, :, cut] = total[:, kind * PAIR:(kind + 1) * PAIR]
        out_sum[:, cut] = total[:, 3 * PAIR:]

    def out_copy(b):
        return pltpu.make_async_copy(out_ref.at[part(b), :], out_hbm.at[part(b), :], outs.at[b])

    def tokens_copy(b):
        return pltpu.make_async_copy(
            tokens_ref.at[part(b), :], tokens_hbm.at[part(b), :], outs.at[blocks + b]
        )

    def branch_event(b):
        branch_copy(b).wait_recv()
        load(b).wait()
        branch_load(b).wait()
        both = branch_own[b % 2].astype(F32) + branch_x[part(b), :].astype(F32)
        out_ref[part(b), :] = (held[b % 2] + both + as_row(down_bias)).astype(BF)
        out_copy(b).start()
        taken(b)
        if b + 2 < blocks:
            branch_load(b + 2).start()

    for b in range(blocks):
        branch_copy(b).start()
    for n in range(2):
        load(n).start()
        branch_load(n).start()
        ff_load(n).start()
        ff_y_copy(n).start()

    plan = {
        11: [(at_c_event, 0)], 15: [(ff_y_event, 0), (branch_event, 0)], 19: [(at_c_event, 1)],
        27: [(at_c_event, 2), (ff_y_event, 1), (branch_event, 1)],
    }

    low_lanes = lanes() < HEAD_DIM
    zero = jnp.zeros((1, PAIR), BF)

    def stacked(strip):
        return jnp.concatenate(
            [jnp.where(low_lanes, strip, zero), jnp.where(low_lanes, zero, strip)], axis=0
        )

    def attend(t, _):
        p, b = t // strips, t % strips
        rows = pl.ds(pl.multiple_of(b * STRIP, STRIP), STRIP)

        @pl.when(b == 0)
        def _():
            for p_now in range(pairs):
                @pl.when(p == p_now)
                def _(p_now=p_now):
                    for copy in pair_loads(p_now):
                        copy.wait()
            key_t[...] = turn(k_ref[p])
            key_acc[...] = jnp.zeros_like(key_acc)
            value_acc[...] = jnp.zeros_like(value_acc)

        queries, grads = stacked(q_ref[p, rows, :]), stacked(gm_ref[p, rows, :])
        more = jnp.concatenate(
            [query_more[2 * p, rows, :], query_more[2 * p + 1, rows, :]], axis=0
        )
        mixture = mix_ref[p, rows, :]
        product = grads.astype(F32) * jnp.concatenate([mixture, mixture], axis=0).astype(F32)
        inner = -jnp.sum(product, axis=-1, keepdims=True)
        query_side = jnp.concatenate([queries, more], axis=1)
        grad_side = jnp.concatenate([grads, in_pieces(inner, 0, 0.0)], axis=1)
        to_queries = jnp.zeros((PAIR, 2 * STRIP), F32)
        for n in range(blocks):
            keys = jnp.concatenate([k_ref[p, part(n), :], key_more[part(n), :]], axis=1)
            values = jnp.concatenate([v_ref[p, part(n), :], one_lanes(BLOCK)], axis=1)
            weights = jnp.exp(dot_rows(keys, query_side))
            grad_scores = (weights * dot_rows(values, grad_side)).astype(BF)
            value_acc[part(n), :] += nn(weights.astype(BF), grads)
            key_acc[part(n), :] += nn(grad_scores, queries)
            to_queries += nn(key_t[:, part(n)], grad_scores)
        own = jnp.concatenate(
            [to_queries[:HEAD_DIM, :STRIP], to_queries[HEAD_DIM:, STRIP:]], axis=0
        )
        dq[p, rows, :] = (turn(own) * 0.125).astype(BF)

        @pl.when(b == strips - 1)
        def _():
            @pl.when(p == 0)
            def _():
                late_loads[0].wait()
                late_loads[1].wait()

            dk[p] = key_acc[...].astype(BF)
            dv[p] = value_acc[...].astype(BF)
            total = jnp.zeros((width, 3 * PAIR), F32)
            out_total = jnp.zeros((width, PAIR), F32)
            for n in range(blocks):
                right = jnp.concatenate(
                    [dq[p, part(n), :], dk[p, part(n), :], dv[p, part(n), :]], axis=1
                )
                total += nn(normed_t[n], right)
                out_total += nn(ga_t[n], mix_ref[p, part(n), :])
            both = jnp.concatenate([total, out_total], axis=1).astype(BF)
            whole[p] = both.reshape(whole.shape[1:])
            at_c_copy(p).start()

        @pl.when(b % 4 == 3)
        def _():
            for step, events in plan.items():
                @pl.when(t == step)
                def _(events=events):
                    for event, n in events:
                        event(n)
        return 0

    lax.fori_loop(0, pairs * strips, attend, 0)
    late_loads[2].wait()
    late_loads[3].wait()

    def gn_copy(b):
        return remote(gn_own.at[b], gn_x.at[b], gs.at[b], gr.at[b], across)

    for b in range(blocks):
        total = jnp.zeros((BLOCK, width), F32)
        for n, grad in enumerate((dq, dk, dv)):
            left = jnp.concatenate([grad[p, part(b), :] for p in range(pairs)], axis=1)
            total += dot_rows(left, wqkv[n])
        gn_own[b] = total.astype(BF)
        gn_copy(b).start()

    at_c_event(3)
    small_own[...] = small_in[...]
    for p in range(pairs):
        first, second = p * PAIR, (pairs + p) * PAIR
        small_own[QV_BIAS:QV_BIAS + 1, first:first + PAIR] = sum_rows(dq[p].astype(F32))
        small_own[QV_BIAS:QV_BIAS + 1, second:second + PAIR] = sum_rows(dv[p].astype(F32))
    branch_event(2)
    ff_y_event(2)
    branch_event(3)
    ff_z_event(0)
    ff_y_event(3)
    at_y_event(0)
    ff_z_event(1)
    gains = as_row(gain)
    for b in range(blocks):
        gn_copy(b).wait()
        load(blocks + b).wait()
        grad = gn_own[b].astype(F32) + gn_x[b].astype(F32)
        centred, scale = norm_stats(x_ref[part(b), :].astype(F32))
        unit = centred * scale
        small_own[LN1_GAIN:LN1_GAIN + 1, :] += sum_rows(grad * unit)
        small_own[LN1_BIAS:LN1_BIAS + 1, :] += sum_rows(grad)
        tokens_ref[part(b), :] = (
            held[b % 2] + norm_back(grad * gains, unit, scale)
        ).astype(BF)
        tokens_copy(b).start()
        taken(blocks + b)
        if b == 0:
            at_y_event(1)
            at_y_event(2)
            ff_z_event(2)
        if b == 1:
            at_y_event(3)
            ff_z_event(3)
        if b == 2:
            at_z_event(0)
            at_z_event(1)
            at_z_event(2)

    def small_z_copy(d):
        return remote(small_own, small_z.at[z], ms.at[d - 1], mr.at[d - 1], z_mates[d - 1])

    def small_z_arrival(d):
        slot = small_z.at[(z + Z_SIZE - d) % Z_SIZE]
        return remote(slot, slot, ms.at[d - 1], mr.at[d - 1], z_mates[d - 1])

    for d in (1, 2, 3):
        small_z_copy(d).start()
    small_z[z] = small_own[...]
    at_z_event(3)
    for d in (1, 2, 3):
        small_z_arrival(d).wait_recv()
    small_y[0] = small_z[0] + small_z[1] + small_z[2] + small_z[3]
    y_sum = remote(small_y.at[0], small_y.at[1], ms.at[3], mr.at[3], y_mate)
    y_sum.start()
    y_sum.wait()
    small_c[0] = small_y[0] + small_y[1]
    c_sum = remote(small_c.at[0], small_c.at[1], ms.at[4], mr.at[4], core_mate)
    c_sum.start()
    c_sum.wait()
    small = small_c[0] + small_c[1]
    for kind, target in (
        (LN1_GAIN, gain_one), (LN1_BIAS, offset_one), (OUT_BIAS, out_small),
        (LN2_GAIN, gain_two), (LN2_BIAS, offset_two), (DOWN_BIAS, down_small),
    ):
        target[...] = small[kind:kind + 1, :].reshape(width)
    cols = pairs * PAIR
    qv_small[0:1, :] = small[QV_BIAS:QV_BIAS + 1, :cols]
    qv_small[1:2, :] = small[QV_BIAS:QV_BIAS + 1, cols:]
    for n in range(up_small.shape[0] // width):
        row = small[UP_BIAS + n:UP_BIAS + n + 1, :]
        up_small[n * width:(n + 1) * width] = row.reshape(width)

    for d in (1, 2, 3):
        small_z_copy(d).wait_send()
    for b in range(blocks):
        out_copy(b).wait()
        tokens_copy(b).wait()
        branch_copy(b).wait_send()
    for g in range(groups):
        ff_y_copy(g).wait_send()
        for d in (1, 2, 3):
            ff_z_copy(g, d).wait_send()
    for p in range(pairs):
        at_c_copy(p).wait_send()
        at_y_copy(p).wait_send()
        for d in (1, 2, 3):
            at_z_copy(p, d).wait_send()


def run_back(
    queries, keys, values, mixture, grad_mixture, query_more, ga_t, normed_t, wqkv, x,
    key_more, gain, down_bias, small, middle, grad_middle, ff_part, branch,
):
    length, width = x.shape
    pairs = queries.shape[0]
    chunks, depth = ff_part.shape[0], ff_part.shape[3]
    groups = chunks // GROUP
    cols, hidden = pairs * PAIR, chunks // 2 * CHUNK
    blocks = length // BLOCK
    dma = pltpu.SemaphoreType.DMA
    rows = pltpu.VMEM((blocks, BLOCK, width), BF)
    by_pair = pltpu.VMEM((pairs, length, PAIR), BF)
    whole_rows = pltpu.VMEM((length, width), BF)
    row = shape_of((width,), F32)
    loaded = (
        queries, keys, values, mixture, grad_mixture, query_more, ga_t, normed_t, wqkv, x
    )
    return pl.pallas_call(
        back_kernel,
        out_shape=[
            shape_of((length, width), BF),
            shape_of((length, width), BF),
            shape_of((3, depth, cols), F32),
            shape_of((depth, cols), F32),
            shape_of((depth, hidden), F32),
            shape_of((depth, hidden), F32),
            row, row, shape_of((2, cols), F32), row, row, row, shape_of((hidden,), F32), row,
        ],
        in_specs=[ANY_SPEC] * 10 + [VMEM_SPEC] * 4 + [ANY_SPEC] * 4,
        out_specs=[ANY_SPEC] * 2 + [VMEM_SPEC] * 12,
        scratch_shapes=[pltpu.VMEM(v.shape, BF) for v in loaded] + [
            whole_rows, whole_rows, pltpu.VMEM((PAIR, length), BF),
            pltpu.VMEM((length, PAIR), F32), pltpu.VMEM((length, PAIR), F32),
            by_pair, by_pair, by_pair,
            pltpu.VMEM((pairs, Z_SIZE, Y_SIZE, CORES, depth, CHUNK), BF),
            pltpu.VMEM((pairs, Z_SIZE, Y_SIZE, depth, CHUNK), BF),
            pltpu.VMEM((pairs, Z_SIZE, depth, CHUNK), BF),
            pltpu.VMEM((3, pairs, depth, CHUNK), BF),
            pltpu.VMEM((chunks, Z_SIZE, depth, CHUNK), BF),
            pltpu.VMEM((3, chunks, depth, CHUNK), BF),
            rows, rows, whole_rows,
            pltpu.VMEM((2, BLOCK, width), BF),
            pltpu.VMEM((2, GROUP, Z_SIZE, depth, CHUNK), BF),
            pltpu.VMEM((2, BLOCK, width), F32),
            pltpu.VMEM(small.shape, F32),
            pltpu.VMEM((Z_SIZE,) + small.shape, F32),
            pltpu.VMEM((2,) + small.shape, F32),
            pltpu.VMEM((2,) + small.shape, F32),
            dma((blocks,)), dma((blocks,)), dma((groups,)), dma((groups,)),
            dma((3 * groups,)), dma((3 * groups,)), dma((pairs,)), dma((pairs,)),
            dma((pairs,)), dma((pairs,)), dma((3 * pairs,)), dma((3 * pairs,)),
            dma((blocks,)), dma((blocks,)), dma((2,)), dma((5,)), dma((5,)), dma((2,)), dma((2,)),
            dma((6 * pairs,)), dma((4,)), dma((2 * blocks,)),
        ],
        compiler_params=pltpu.CompilerParams(
            collective_id=2, has_side_effects=True, vmem_limit_bytes=VMEM_LIMIT
        ),
    )(*loaded, key_more, gain, down_bias, small, middle, grad_middle, ff_part, branch)


def hand_over_kernel(*refs):
    count = len(refs) // 2
    sems = refs[-1]
    copies = [
        pltpu.make_async_copy(refs[n], refs[count + n], sems.at[n]) for n in range(count)
    ]
    for copy in copies:
        copy.start()
    for copy in copies:
        copy.wait()


def hand_over(results):
    return pl.pallas_call(
        hand_over_kernel,
        out_shape=[shape_of(v.shape, v.dtype) for v in results],
        in_specs=[ANY_SPEC] * len(results),
        out_specs=[ANY_SPEC] * len(results),
        scratch_shapes=[pltpu.SemaphoreType.DMA((len(results),))],
        compiler_params=pltpu.CompilerParams(vmem_limit_bytes=VMEM_LIMIT),
    )(*results)


def fast_body(
    tokens, segment_ids, context_flags, ln1_gain, ln1_bias, qkv_weight, qv_bias, out_weight,
    out_bias, ln2_gain, ln2_bias, up_weight, up_bias, down_weight, down_bias, cotangent,
):
    x, dy = tokens[0], cotangent[0]
    queries, keys, values, mixture, middle, normed_t, wff, key_more, query_more = run_fwd(
        x, segment_ids, context_flags, ln1_gain, ln1_bias, qv_bias, out_bias, qkv_weight,
        out_weight, up_weight, down_weight.T,
    )
    branch, grad_middle, ga_t, grad_mixture, ff_part, small = run_ff(
        middle, dy, wff, ln2_gain, ln2_bias, up_bias, out_weight
    )
    (
        output, tokens_grad, qkv_grad, out_grad, up_grad, down_grad, gain_one, offset_one,
        qv_grad, out_bias_grad, gain_two, offset_two, up_bias_grad, down_bias_grad,
    ) = hand_over(run_back(
        queries, keys, values, mixture, grad_mixture, query_more, ga_t, normed_t, qkv_weight, x,
        key_more, ln1_gain, down_bias, small, middle, grad_middle, ff_part, branch,
    ))
    return (
        output[None], tokens_grad[None], gain_one, offset_one, qkv_grad, qv_grad, out_grad.T,
        out_bias_grad, gain_two, offset_two, up_grad, up_bias_grad, down_grad.T, down_bias_grad,
    )


def solution(mesh):
    chosen = generic_body
    if mesh.shape["head"] == 2 and mesh.shape["seq"] == SEQ_SIZE:
        chosen = fast_body
    return jax.shard_map(
        chosen,
        mesh=mesh,
        in_specs=(
            P("seq", None, None),
            P("seq", None),
            P("seq", None),
            P(),
            P(),
            P(None, None, "head"),
            P(None, "head"),
            P("head", None),
            P(),
            P(),
            P(),
            P("seq", "head"),
            P("head"),
            P("head", "seq"),
            P(),
            P("seq", None, None),
        ),
        out_specs=(
            P("seq", None, None),
            P("seq", None, None),
            P(),
            P(),
            P(None, "seq", "head"),
            P(None, "head"),
            P("head", "seq"),
            P(),
            P(),
            P(),
            P("seq", "head"),
            P("head"),
            P("head", "seq"),
            P(),
        ),
        check_vma=False,
    )
```

```python
import math

import jax
import jax.numpy as jnp
from jax import lax
from jax.experimental import pallas as pl
from jax.experimental.pallas import tpu as pltpu
from jax.sharding import PartitionSpec as P

HEAD_DIM = 64


def layer_norm(values_in, scaling, offset):
    middle = jnp.mean(values_in, axis=-1, keepdims=True)
    centred = values_in - middle
    spread = jnp.mean(centred * centred, axis=-1, keepdims=True)
    return centred * lax.rsqrt(spread + 1e-05) * scaling + offset


def gelu_exact(values_in):
    return 0.5 * values_in * (1.0 + jax.scipy.special.erf(values_in * 0.7071067811865476))


def dot_rows(left, right):
    return lax.dot_general(
        left, right, (((1,), (1,)), ((), ())), preferred_element_type=jnp.float32
    )


def dot_cols(left, right):
    return lax.dot_general(
        left, right, (((0,), (0,)), ((), ())), preferred_element_type=jnp.float32
    )


def masked_scores(block_query, seq_keys, block_segments, seq_segments, seq_context, factor):
    raw_scores = (
        jnp.einsum("qhd,khd->hqk", block_query, seq_keys, preferred_element_type=jnp.float32)
        * factor
    )
    allowed = (block_segments[:, None] == seq_segments[None, :]) & (seq_context[None, :] == 1)
    return jnp.where(allowed[None], raw_scores, -1e30)


def generic_body(
    tokens,
    segment_ids,
    context_flags,
    ln1_gain,
    ln1_bias,
    qkv_weight,
    qv_bias,
    out_weight,
    out_bias,
    ln2_gain,
    ln2_bias,
    up_weight,
    up_bias,
    down_weight,
    down_bias,
    cotangent,
):
    seq_count, length, width = tokens.shape
    row_count = seq_count * length
    local_cols = qkv_weight.shape[2]
    head_count = local_cols // HEAD_DIM
    factor = 1.0 / math.sqrt(HEAD_DIM)
    block = min(512, length)
    blocks = length // block
    gain_one = ln1_gain.astype(jnp.float32)
    offset_one = ln1_bias.astype(jnp.float32)
    gain_two = ln2_gain.astype(jnp.float32)
    offset_two = ln2_bias.astype(jnp.float32)
    flat_in = tokens.astype(jnp.float32).reshape(row_count, width)
    normed_f, norm_one_pull = jax.vjp(layer_norm, flat_in, gain_one, offset_one)
    normed = normed_f.astype(jnp.bfloat16)
    queries = (
        jnp.dot(normed, qkv_weight[0], preferred_element_type=jnp.float32)
        + qv_bias[0].astype(jnp.float32)
    ).astype(jnp.bfloat16)
    key_rows = jnp.dot(normed, qkv_weight[1], preferred_element_type=jnp.float32).astype(
        jnp.bfloat16
    )
    value_rows = (
        jnp.dot(normed, qkv_weight[2], preferred_element_type=jnp.float32)
        + qv_bias[1].astype(jnp.float32)
    ).astype(jnp.bfloat16)

    def per_sequence(array):
        return array.reshape(seq_count, length, head_count, HEAD_DIM)

    def attend_sequence(member):
        seq_query, seq_keys, seq_values, seq_segments, seq_context = member

        def attend_block(portion):
            block_query, block_segments = portion
            scores = masked_scores(
                block_query, seq_keys, block_segments, seq_segments, seq_context, factor
            )
            row_top = jnp.max(scores, axis=-1, keepdims=True)
            exponent = jnp.exp(scores - row_top)
            row_total = jnp.sum(exponent, axis=-1, keepdims=True)
            soft_weights = (exponent / row_total).astype(jnp.bfloat16)
            block_mix = jnp.einsum(
                "hqk,khd->qhd", soft_weights, seq_values, preferred_element_type=jnp.float32
            )
            return (block_mix.astype(jnp.bfloat16), row_top + jnp.log(row_total))

        return lax.map(
            attend_block,
            (
                seq_query.reshape(blocks, block, head_count, HEAD_DIM),
                seq_segments.reshape(blocks, block),
            ),
        )

    mixture, log_totals = lax.map(
        attend_sequence,
        (
            per_sequence(queries),
            per_sequence(key_rows),
            per_sequence(value_rows),
            segment_ids,
            context_flags,
        ),
    )
    mixture = mixture.reshape(row_count, local_cols)
    partial_out = jnp.dot(mixture, out_weight, preferred_element_type=jnp.float32)
    grad_rows_all = cotangent.reshape(row_count, width)
    grad_float_all = grad_rows_all.astype(jnp.float32)
    grad_down_bias = jnp.sum(grad_float_all, axis=0)
    attended = lax.psum(partial_out, "head") + out_bias.astype(jnp.float32)
    middle_state = flat_in + attended
    normed_two_f, norm_two_pull = jax.vjp(layer_norm, middle_state, gain_two, offset_two)
    normed_two = normed_two_f.astype(jnp.bfloat16)
    up_part, down_part, up_shift = (
        lax.all_gather(up_weight, "head", axis=1, tiled=True),
        lax.all_gather(down_weight, "head", axis=0, tiled=True),
        lax.all_gather(up_bias, "head", axis=0, tiled=True),
    )
    up_full, down_full = (
        lax.all_gather(up_part, "seq", axis=0, tiled=True),
        lax.all_gather(down_part, "seq", axis=1, tiled=True),
    )
    before = jnp.dot(normed_two, up_full, preferred_element_type=jnp.float32) + up_shift.astype(
        jnp.float32
    )
    active_f, gelu_pull = jax.vjp(gelu_exact, before)
    active = active_f.astype(jnp.bfloat16)
    branch_out = jnp.dot(active, down_full, preferred_element_type=jnp.float32)
    final_rows = (middle_state + branch_out + down_bias.astype(jnp.float32)).astype(jnp.bfloat16)
    output = final_rows.reshape(tokens.shape)
    grad_float = grad_rows_all.astype(jnp.float32)
    grad_down = dot_cols(active, grad_rows_all)
    grad_active = dot_rows(grad_rows_all, down_full)
    (grad_before_f,) = gelu_pull(grad_active)
    grad_before = grad_before_f.astype(jnp.bfloat16)
    grad_up = dot_cols(normed_two, grad_before)
    grad_up_bias = jnp.sum(grad_before.astype(jnp.float32), axis=0)
    grad_normed_two = dot_rows(grad_before, up_full)
    grad_middle_norm, grad_gain_two, grad_offset_two = norm_two_pull(grad_normed_two)
    grad_middle = grad_float + grad_middle_norm
    ff_part = up_weight.shape[1]
    start_col = lax.axis_index("head") * ff_part
    grad_up = lax.dynamic_slice_in_dim(grad_up, start_col, ff_part, 1)
    grad_down = lax.dynamic_slice_in_dim(grad_down, start_col, ff_part, 0)
    grad_up_bias = lax.dynamic_slice_in_dim(grad_up_bias, start_col, ff_part, 0)
    grad_attended = grad_middle.astype(jnp.bfloat16)
    grad_out_bias = jnp.sum(grad_attended.astype(jnp.float32), axis=0)
    grad_out = dot_cols(mixture, grad_attended)
    grad_mixture = dot_rows(grad_attended, out_weight).astype(jnp.bfloat16)

    def back_sequence(member):
        seq_query, seq_keys, seq_values, seq_grad, seq_logs, seq_segments, seq_context = member

        def back_block(carry, portion):
            key_acc, value_acc = carry
            block_query, block_grad, block_logs, block_segments = portion
            scores = masked_scores(
                block_query, seq_keys, block_segments, seq_segments, seq_context, factor
            )
            soft_weights = jnp.exp(scores - block_logs)
            value_acc = value_acc + jnp.einsum(
                "hqk,qhd->khd",
                soft_weights.astype(jnp.bfloat16),
                block_grad,
                preferred_element_type=jnp.float32,
            )
            grad_soft = jnp.einsum(
                "qhd,khd->hqk", block_grad, seq_values, preferred_element_type=jnp.float32
            )
            row_inner = jnp.sum(soft_weights * grad_soft, axis=-1, keepdims=True)
            grad_scores = (soft_weights * (grad_soft - row_inner)).astype(jnp.bfloat16)
            grad_query = (
                jnp.einsum(
                    "hqk,khd->qhd", grad_scores, seq_keys, preferred_element_type=jnp.float32
                )
                * factor
            )
            key_acc = (
                key_acc
                + jnp.einsum(
                    "hqk,qhd->khd", grad_scores, block_query, preferred_element_type=jnp.float32
                )
                * factor
            )
            return ((key_acc, value_acc), grad_query)

        empty = jnp.zeros((length, head_count, HEAD_DIM), jnp.float32)
        (key_acc, value_acc), grad_query = lax.scan(
            back_block,
            (empty, empty),
            (
                seq_query.reshape(blocks, block, head_count, HEAD_DIM),
                seq_grad.reshape(blocks, block, head_count, HEAD_DIM),
                seq_logs,
                seq_segments.reshape(blocks, block),
            ),
        )
        return (grad_query, key_acc, value_acc)

    grad_queries, grad_keys, grad_values = lax.map(
        back_sequence,
        (
            per_sequence(queries),
            per_sequence(key_rows),
            per_sequence(value_rows),
            per_sequence(grad_mixture),
            log_totals,
            segment_ids,
            context_flags,
        ),
    )
    grad_queries = grad_queries.reshape(row_count, local_cols).astype(jnp.bfloat16)
    grad_keys = grad_keys.reshape(row_count, local_cols).astype(jnp.bfloat16)
    grad_values = grad_values.reshape(row_count, local_cols).astype(jnp.bfloat16)
    grad_qv_bias = jnp.stack(
        [
            jnp.sum(grad_queries.astype(jnp.float32), axis=0),
            jnp.sum(grad_values.astype(jnp.float32), axis=0),
        ]
    )
    grad_qkv = jnp.stack(
        [dot_cols(normed, grad_queries), dot_cols(normed, grad_keys), dot_cols(normed, grad_values)]
    )
    grad_normed = (
        dot_rows(grad_queries, qkv_weight[0])
        + dot_rows(grad_keys, qkv_weight[1])
        + dot_rows(grad_values, qkv_weight[2])
    )
    grad_normed = lax.psum(grad_normed, "head")
    grad_input_norm, grad_gain_one, grad_offset_one = norm_one_pull(grad_normed)
    tokens_grad = (grad_middle + grad_input_norm).astype(jnp.bfloat16).reshape(tokens.shape)
    summed_qkv, summed_out, summed_up, summed_down = (
        lax.psum_scatter(
            grad_qkv.astype(jnp.bfloat16), "seq", scatter_dimension=1, tiled=True
        ).astype(jnp.float32),
        lax.psum_scatter(
            grad_out.astype(jnp.bfloat16), "seq", scatter_dimension=1, tiled=True
        ).astype(jnp.float32),
        lax.psum_scatter(
            grad_up.astype(jnp.bfloat16), "seq", scatter_dimension=0, tiled=True
        ).astype(jnp.float32),
        lax.psum_scatter(
            grad_down.astype(jnp.bfloat16), "seq", scatter_dimension=1, tiled=True
        ).astype(jnp.float32),
    )
    smalls = lax.psum(
        (
            grad_gain_one,
            grad_offset_one,
            grad_qv_bias,
            grad_out_bias,
            grad_gain_two,
            grad_offset_two,
            grad_up_bias,
            grad_down_bias,
        ),
        "seq",
    )
    return (
        output,
        tokens_grad,
        smalls[0],
        smalls[1],
        summed_qkv,
        smalls[2],
        summed_out,
        smalls[3],
        smalls[4],
        smalls[5],
        summed_up,
        smalls[6],
        summed_down,
        smalls[7],
    )


MESH = pl.DeviceIdType.MESH
BF = jnp.bfloat16
F32 = jnp.float32
BLOCK = 256
STRIP = 128
GROUP = 2
CHUNK = 512
PAIR = 2 * HEAD_DIM
Z_SIZE, Y_SIZE, CORES = 4, 2, 2
SEQ_SIZE = Z_SIZE * Y_SIZE * CORES
HOP = Y_SIZE * CORES
TABLES = 8
FAR = -1e30
VMEM_LIMIT = 62 * 2**20
INV_ROOT_TWO = 0.7071067811865476
INV_ROOT_TWO_PI = 0.3989422804014327
LN1_GAIN, LN1_BIAS, QV_BIAS, OUT_BIAS, LN2_GAIN, LN2_BIAS, UP_BIAS, DOWN_BIAS = 0, 1, 2, 3, 4, 5, 6, 8
SMALL_ROWS = 16
VMEM_SPEC = pl.BlockSpec(memory_space=pltpu.VMEM)
ANY_SPEC = pl.BlockSpec(memory_space=pl.ANY)


def shape_of(dims, dtype):
    return jax.ShapeDtypeStruct(tuple(dims), dtype)


def nn(left, right):
    return jnp.dot(left, right, preferred_element_type=F32)


def turn(block):
    return jnp.transpose(block)


def sum_rows(block):
    return jnp.sum(block, axis=0, keepdims=True)


def place():
    me = lax.axis_index("seq")
    head = lax.axis_index("head")
    core = me % 2
    y = (me // 2) % 2
    across = {"seq": me, "head": 1 - head}
    core_mate = {"seq": me + 1 - 2 * core, "head": head}
    y_mate = {"seq": me + 2 - 4 * y, "head": head}
    z_mates = [{"seq": (me + HOP * d) % SEQ_SIZE, "head": head} for d in (1, 2, 3)]
    return me, head, core, y, across, core_mate, y_mate, z_mates


def greet(others):
    barrier = pltpu.get_barrier_semaphore()
    for other in others:
        pl.semaphore_signal(barrier, inc=1, device_id=other, device_id_type=MESH)
    pl.semaphore_wait(barrier, len(others))


def remote(src, dst, send_sem, recv_sem, other):
    return pltpu.make_async_remote_copy(
        src_ref=src, dst_ref=dst, send_sem=send_sem, recv_sem=recv_sem,
        device_id=other, device_id_type=MESH,
    )


def norm_stats(rows):
    middle = jnp.mean(rows, axis=-1, keepdims=True)
    centred = rows - middle
    spread = jnp.mean(centred * centred, axis=-1, keepdims=True)
    return centred, lax.rsqrt(spread + 1e-05)


def norm_back(inner, unit, scale):
    return scale * (
        inner
        - jnp.mean(inner, axis=-1, keepdims=True)
        - unit * jnp.mean(inner * unit, axis=-1, keepdims=True)
    )


def as_row(vector):
    return vector[...].astype(F32).reshape(1, -1)


def lanes():
    return lax.broadcasted_iota(jnp.int32, (1, PAIR), 1)


def in_pieces(column, first, rest):
    high = column.astype(BF).astype(F32)
    mid = (column - high).astype(BF).astype(F32)
    low = column - high - mid
    at = lanes()
    return jnp.where(
        at == first, high, jnp.where(at == first + 1, mid, jnp.where(at == first + 2, low, rest))
    ).astype(BF)


def one_lanes(length):
    return jnp.broadcast_to(jnp.where(lanes() < 3, 1.0, 0.0).astype(BF), (length, PAIR))


def fwd_kernel(
    x_ref, seg_ref, context, gain, offset, qv_bias, out_bias, wqkv, wout, up_shard, down_shard,
    q_out, k_out, v_out, mix_out, mid_out, normed_out, wff_out, key_out, query_out,
    wff, q_ref, k_ref, v_ref, mix_ref, mid_ref, normed_t, key_more, query_more,
    mask_more, wout_x, mix_x,
    zs, zr, ys, yr, cs, cr, xs, xr, local, outs,
):
    length, width = x_ref.shape
    blocks = length // BLOCK
    pairs = q_ref.shape[0]
    cols = pairs * PAIR
    me, head, core, y, across, core_mate, y_mate, _ = place()
    z = me // HOP
    above = {"seq": (me + HOP) % SEQ_SIZE, "head": head}
    below = {"seq": (me + SEQ_SIZE - HOP) % SEQ_SIZE, "head": head}
    own = [
        pltpu.make_async_copy(shard, wff.at[u, me], local.at[u])
        for u, shard in enumerate((up_shard, down_shard))
    ]
    own[0].start()
    own[1].start()
    greet([across, core_mate, y_mate, above, below])

    out_copy = remote(wout, wout_x, xs.at[0], xr.at[0], across)
    out_copy.start()

    flows = [(0, 0)] + [(way, s) for s in (1, 2, 3) for way in (0, 1)]

    def there(way, s):
        return (z >= s) if way == 0 else (z + s < Z_SIZE)

    def source(base, way, s):
        away = SEQ_SIZE - HOP * s if way == 0 else HOP * s
        return (base + away) % SEQ_SIZE

    def z_copy(u, way, s):
        n = (u * 2 + way) * 3 + s - 1
        j = source(me, way, s - 1)
        return remote(wff.at[u, j], wff.at[u, j], zs.at[n], zr.at[n], above if way == 0 else below)

    def z_arrival(u, way, s):
        n = (u * 2 + way) * 3 + s - 1
        slot = wff.at[u, source(me, way, s)]
        return remote(slot, slot, zs.at[n], zr.at[n], above)

    def z_goes_on(way):
        return (z < Z_SIZE - 1) if way == 0 else (z > 0)

    def y_copy(u, f):
        n = u * 7 + f
        j = source(me, *flows[f])
        return remote(wff.at[u, j], wff.at[u, j], ys.at[n], yr.at[n], y_mate)

    def y_arrival(u, f):
        n = u * 7 + f
        slot = wff.at[u, source(me + 2 - 4 * y, *flows[f])]
        return remote(slot, slot, ys.at[n], yr.at[n], y_mate)

    def c_copy(u, f, from_y):
        n = (u * 2 + from_y) * 7 + f
        j = source(me + from_y * (2 - 4 * y), *flows[f])
        return remote(wff.at[u, j], wff.at[u, j], cs.at[n], cr.at[n], core_mate)

    def c_arrival(u, f, from_y):
        n = (u * 2 + from_y) * 7 + f
        slot = wff.at[u, source(me + 1 - 2 * core + from_y * (2 - 4 * y), *flows[f])]
        return remote(slot, slot, cs.at[n], cr.at[n], core_mate)

    def for_flow(f, do):
        if f == 0:
            do()
        else:
            pl.when(there(*flows[f]))(do)

    def for_step(s, do):
        for f, (way, step) in enumerate(flows):
            if step == s:
                for_flow(f, lambda f=f, way=way: do(f, way))

    def z_event(u, s):
        def one(f, way):
            z_arrival(u, way, s).wait_recv()
            if s < 3:
                pl.when(z_goes_on(way))(lambda: z_copy(u, way, s + 1).start())
            y_copy(u, f).start()
            c_copy(u, f, 0).start()
        for_step(s, one)

    def y_event(u, s):
        def one(f, way):
            y_arrival(u, f).wait_recv()
            c_copy(u, f, 1).start()
        for_step(s, one)

    for u in range(2):
        own[u].wait()
        for way in (0, 1):
            pl.when(z_goes_on(way))(lambda u=u, way=way: z_copy(u, way, 1).start())
        y_copy(u, 0).start()
        c_copy(u, 0, 0).start()

    plan = {
        1: [(z_event, 0, 1), (y_event, 0, 0)], 3: [(z_event, 1, 1), (y_event, 1, 0)],
        5: [(z_event, 0, 2)], 7: [(z_event, 1, 2)], 9: [(y_event, 0, 1)], 11: [(z_event, 0, 3)],
        12: [(y_event, 1, 1)], 14: [(z_event, 1, 3)], 16: [(y_event, 0, 2)], 18: [(y_event, 1, 2)],
    }
    last = [(y_event, 0, 3), (y_event, 1, 3)]

    def tick(t):
        for step, events in plan.items():
            @pl.when(t == step)
            def _(events=events):
                for event, u, s in events:
                    event(u, s)

    at = lax.broadcasted_iota(jnp.int32, (PAIR, length), 0)
    same = at == seg_ref[...]
    hidden = context[...] != 1
    ones = jnp.logical_and(at > TABLES, at < TABLES + 4)
    key_side = jnp.logical_or(
        jnp.logical_and(at < TABLES, same),
        jnp.logical_or(jnp.logical_and(at == TABLES, hidden), ones),
    )
    query_side = jnp.logical_and(at <= TABLES, jnp.logical_not(same))
    key_more[...] = turn(jnp.where(key_side, 1.0, 0.0)).astype(BF)
    mask_more[...] = turn(jnp.where(query_side, FAR, 0.0)).astype(BF)

    keep = [
        pltpu.make_async_copy(here, there, outs.at[n])
        for n, (here, there) in enumerate(
            (
                (q_ref, q_out), (k_ref, k_out), (v_ref, v_out), (normed_t, normed_out),
                (key_more, key_out), (query_more, query_out), (mix_ref, mix_out),
            )
        )
    ]
    gains, offsets = as_row(gain), as_row(offset)
    query_bias = qv_bias[0:1, :].astype(F32)
    value_bias = qv_bias[1:2, :].astype(F32)

    def project(b, _):
        rows = pl.ds(pl.multiple_of(b * BLOCK, BLOCK), BLOCK)
        centred, scale = norm_stats(x_ref[rows, :].astype(F32))
        block = (centred * scale * gains + offsets).astype(BF)
        normed_t[b] = turn(block)
        queries = ((nn(block, wqkv[0]) + query_bias).astype(BF) * 0.125).astype(BF)
        keys = nn(block, wqkv[1]).astype(BF)
        values = (nn(block, wqkv[2]) + value_bias).astype(BF)
        for p in range(pairs):
            part = slice(p * PAIR, (p + 1) * PAIR)
            q_ref[p, rows, :] = queries[:, part]
            k_ref[p, rows, :] = keys[:, part]
            v_ref[p, rows, :] = values[:, part]
        tick(b)
        return 0

    lax.fori_loop(0, blocks, project, 0)
    for n in range(5):
        keep[n].start()

    low_lanes = lanes() < HEAD_DIM
    zero = jnp.zeros((1, PAIR), BF)

    def mixture_copy(b):
        rows = pl.ds(b * BLOCK, BLOCK)
        return remote(
            mix_ref.at[:, rows, :], mix_x.at[:, rows, :], xs.at[1 + b], xr.at[1 + b], across
        )

    def attend(t, _):
        b, p = t // pairs, t % pairs
        rows = pl.ds(pl.multiple_of(b * BLOCK, BLOCK), BLOCK)
        queries, more = q_ref[p, rows, :], mask_more[rows, :]
        keys = jnp.concatenate([k_ref[p], key_more[...]], axis=1)
        values = jnp.concatenate([v_ref[p], one_lanes(length)], axis=1)
        parts = []
        for low in (0, 1):
            own_lanes = jnp.logical_not(low_lanes) if low else low_lanes
            left = jnp.concatenate([jnp.where(own_lanes, queries, zero), more], axis=1)
            scores = dot_rows(left, keys)
            top = jnp.max(scores, axis=-1, keepdims=True)
            mixed = nn(jnp.exp(scores - top).astype(BF), values)
            total = mixed[:, PAIR:PAIR + 1]
            parts.append(mixed[:, :PAIR] / total)
            query_more[2 * p + low, rows, :] = in_pieces(
                -(top + jnp.log(total)), TABLES + 1, more.astype(F32)
            )
        mix_ref[p, rows, :] = jnp.where(low_lanes, parts[0], parts[1]).astype(BF)
        tick(t + blocks)
        for b_done in range(blocks):
            @pl.when(t == (b_done + 1) * pairs - 1)
            def _(b_done=b_done):
                mixture_copy(b_done).start()
        return 0

    lax.fori_loop(0, blocks * pairs, attend, 0)
    keep[5].start()
    keep[6].start()
    out_copy.wait_recv()
    out_row = as_row(out_bias)

    def mid_copy(b):
        rows = pl.ds(b * BLOCK, BLOCK)
        return pltpu.make_async_copy(mid_ref.at[rows, :], mid_out.at[rows, :], outs.at[7 + b])

    for b in range(blocks):
        if b == blocks - 1:
            for event, u, s in last:
                event(u, s)
        mixture_copy(b).wait_recv()
        rows = pl.ds(b * BLOCK, BLOCK)
        ours = jnp.concatenate([mix_ref[p, rows, :] for p in range(pairs)], axis=-1)
        other = jnp.concatenate([mix_x[p, rows, :] for p in range(pairs)], axis=-1)
        attended = nn(ours, wout[...]) + nn(other, wout_x[...])
        mid_ref[rows, :] = x_ref[rows, :].astype(F32) + (attended + out_row)
        mid_copy(b).start()

    wff_keep = [pltpu.make_async_copy(wff.at[u], wff_out.at[u], local.at[u]) for u in range(2)]
    for u in range(2):
        for f in range(len(flows)):
            def arrive(u=u, f=f):
                for from_y in (0, 1):
                    c_arrival(u, f, from_y).wait_recv()
            for_flow(f, arrive)
        wff_keep[u].start()
    out_copy.wait_send()
    for copy in keep + wff_keep:
        copy.wait()
    for b in range(blocks):
        mixture_copy(b).wait_send()
        mid_copy(b).wait()
    for u in range(2):
        for way in (0, 1):
            pl.when(z_goes_on(way))(lambda u=u, way=way: z_copy(u, way, 1).wait_send())
        for f, (way, s) in enumerate(flows):
            def finish(u=u, f=f, way=way, s=s):
                if f and s < 3:
                    pl.when(z_goes_on(way))(lambda: z_copy(u, way, s + 1).wait_send())
                y_copy(u, f).wait_send()
                for from_y in (0, 1):
                    c_copy(u, f, from_y).wait_send()
            for_flow(f, finish)


def run_fwd(x, seg, context, gain, offset, qv_bias, out_bias, wqkv, wout, up_weight, down_t):
    length, width = x.shape
    pairs = wqkv.shape[2] // PAIR
    blocks = length // BLOCK
    depth, hidden = up_weight.shape
    by_pair, by_head = (pairs, length, PAIR), (2 * pairs, length, PAIR)
    turned = (blocks, width, BLOCK)
    dma = pltpu.SemaphoreType.DMA
    return pl.pallas_call(
        fwd_kernel,
        out_shape=[shape_of(by_pair, BF)] * 4 + [
            shape_of((length, width), F32),
            shape_of(turned, BF),
            shape_of((2, SEQ_SIZE, depth, hidden), BF),
            shape_of((length, PAIR), BF),
            shape_of(by_head, BF),
        ],
        in_specs=[VMEM_SPEC] * 9 + [ANY_SPEC] * 2,
        out_specs=[ANY_SPEC] * 9,
        scratch_shapes=[pltpu.VMEM((2, SEQ_SIZE, depth, hidden), BF)]
        + [pltpu.VMEM(by_pair, BF)] * 4 + [
            pltpu.VMEM((length, width), F32),
            pltpu.VMEM(turned, BF),
            pltpu.VMEM((length, PAIR), BF),
            pltpu.VMEM(by_head, BF),
            pltpu.VMEM((length, PAIR), BF),
            pltpu.VMEM(wout.shape, BF),
            pltpu.VMEM(by_pair, BF),
            dma((12,)), dma((12,)), dma((14,)), dma((14,)), dma((28,)), dma((28,)),
            dma((1 + blocks,)), dma((1 + blocks,)), dma((2,)), dma((7 + blocks,)),
        ],
        compiler_params=pltpu.CompilerParams(
            collective_id=0, has_side_effects=True, vmem_limit_bytes=VMEM_LIMIT
        ),
    )(x, seg, context, gain, offset, qv_bias, out_bias, wqkv, wout, up_weight, down_t)


def ff_kernel(
    mid_hbm, dy_hbm, wff_hbm, gain, offset, up_bias, wout_hbm,
    branch_out, gmid_hbm, ga_out, gm_out, summed, small_ref,
    dy_ref, wff, wout, bias_row, branch_ref, ga_t, gm_ref, normed, normed_t, dy_t, active, before_grad, gnt_acc, gnt_own, gnt_x, whole, from_mate,
    held, ready,
    xs, xr, cs, cr, ls, ws, ss, ins, outs,
):
    length, width = dy_ref.shape
    blocks = length // BLOCK
    hidden = wff.shape[3]
    half = hidden // CHUNK
    chunks = 2 * half
    pairs = gm_ref.shape[0]
    me, head, core, y, across, core_mate, y_mate, z_mates = place()
    dy_load = pltpu.make_async_copy(dy_hbm, dy_ref, ins.at[0])
    wout_load = pltpu.make_async_copy(wout_hbm, wout, ins.at[1])

    def wff_load(n):
        cut = pl.ds(n * CHUNK, CHUNK)
        return pltpu.make_async_copy(
            wff_hbm.at[:, :, :, cut], wff.at[:, :, :, cut], ins.at[2 + n]
        )

    dy_load.start()
    for n in range(half):
        wff_load(n).start()
    wout_load.start()
    greet([across, core_mate])
    gains, offsets = as_row(gain), as_row(offset)
    bias_row[...] = as_row(up_bias)
    per_row = width // CHUNK

    def weight(kind, n):
        cut = pl.ds(pl.multiple_of(n * CHUNK, CHUNK), CHUNK)
        return wff[kind, :, :, cut].reshape(width, CHUNK)

    small_ref[...] = jnp.zeros_like(small_ref)

    def load(n):
        rows = pl.ds(n % blocks * BLOCK, BLOCK)
        return pltpu.make_async_copy(mid_hbm.at[rows, :], held.at[n % 2], ls.at[n % 2])

    def store(b):
        rows = pl.ds(b * BLOCK, BLOCK)
        return pltpu.make_async_copy(ready.at[b % 2], gmid_hbm.at[rows, :], ws.at[b % 2])

    load(0).start()
    load(1).start()

    def gnt_copy(b):
        return remote(gnt_own.at[b], gnt_x.at[b], xs.at[b], xr.at[b], across)

    def core_copy(n):
        return remote(
            whole.at[n, :, :, 1 - core], from_mate.at[n], cs.at[n], cr.at[n], core_mate
        )

    def forward(t, _):
        b, n = t // half, t % half
        rows = pl.ds(pl.multiple_of(b * BLOCK, BLOCK), BLOCK)

        for b_next in range(blocks):
            @pl.when(t == b_next * half)
            def _(b_next=b_next):
                load(b_next).wait()
                if b_next == 0:
                    dy_load.wait()

        for n_first in range(half):
            @pl.when(t == n_first)
            def _(n_first=n_first):
                wff_load(n_first).wait()

        @pl.when(n == 0)
        def _():
            centred, scale = norm_stats(held[b % 2])
            block = (centred * scale * gains + offsets).astype(BF)
            normed[...] = block
            normed_t[b] = turn(block)
            dy_t[b] = turn(dy_ref[rows, :])
            small_ref[DOWN_BIAS:DOWN_BIAS + 1, :] += sum_rows(dy_ref[rows, :].astype(F32))

        up = weight(0, n)
        cut = pl.ds(pl.multiple_of(n * CHUNK, CHUNK), CHUNK)
        small_at = pl.ds(UP_BIAS + n // per_row, 1)
        small_cut = pl.ds(pl.multiple_of(n % per_row * CHUNK, CHUNK), CHUNK)
        before = nn(normed[...], up) + bias_row[:, cut]
        spread = 0.5 * (1.0 + lax.erf(before * INV_ROOT_TWO))
        active[n, rows, :] = (before * spread).astype(BF)
        slope = spread + before * (INV_ROOT_TWO_PI * jnp.exp(before * before * -0.5))
        grad = (nn(dy_ref[rows, :], weight(1, n)) * slope).astype(BF)
        before_grad[n, rows, :] = grad
        small_ref[small_at, small_cut] += sum_rows(grad.astype(F32))
        back = dot_rows(grad, up)

        @pl.when(n == 0)
        def _():
            gnt_acc[...] = back

        @pl.when(n > 0)
        def _():
            gnt_acc[...] += back

        for b_done in range(blocks):
            @pl.when(t == (b_done + 1) * half - 1)
            def _(b_done=b_done):
                load(b_done + 2).start()
                gnt_own[b_done] = gnt_acc[...].astype(BF)
                gnt_copy(b_done).start()
        return 0

    lax.fori_loop(0, blocks * half, forward, 0)

    def weight_grads(left_t, right, first):
        top, planes = width // 2, Z_SIZE // 2

        def one(t, _):
            n, side = t // 2, t % 2
            cut = pl.ds(pl.multiple_of(side * top, top), top)
            total = nn(left_t[0, cut, :], right[n, pl.ds(0, BLOCK), :])
            for b in range(1, blocks):
                total += nn(left_t[b, cut, :], right[n, pl.ds(b * BLOCK, BLOCK), :])
            piece = total.astype(BF).reshape((planes,) + whole.shape[2:])
            whole[first + n, pl.ds(side * planes, planes)] = piece

            @pl.when(side == 1)
            def _():
                core_copy(first + n).start()

            return 0

        lax.fori_loop(0, 2 * half, one, 0)

    weight_grads(dy_t, active, half)
    weight_grads(normed_t, before_grad, 0)

    def branch(b, _):
        rows = pl.ds(pl.multiple_of(b * BLOCK, BLOCK), BLOCK)
        total = dot_rows(active[0, rows, :], weight(1, 0))
        for n in range(1, half):
            total += dot_rows(active[n, rows, :], weight(1, n))
        branch_ref[rows, :] = total.astype(BF)
        return 0

    lax.fori_loop(0, blocks, branch, 0)
    branch_keep = pltpu.make_async_copy(branch_ref, branch_out, outs.at[0])
    branch_keep.start()
    wout_load.wait()

    def ga_copy(b):
        return pltpu.make_async_copy(ga_t.at[b], ga_out.at[b], outs.at[1 + b])

    def gm_copy(b):
        rows = pl.ds(b * BLOCK, BLOCK)
        return pltpu.make_async_copy(
            gm_ref.at[:, rows, :], gm_out.at[:, rows, :], outs.at[1 + blocks + b]
        )


    def add_mate(n, _):
        core_copy(n).wait()
        both = whole[n, :, :, core].astype(F32) + from_mate[n].astype(F32)
        from_mate[n] = both.astype(BF)
        return 0

    lax.fori_loop(half, chunks, add_mate, 0)
    lax.fori_loop(0, half, add_mate, 0)
    keep = pltpu.make_async_copy(from_mate, summed, ss.at[0])
    keep.start()

    strips = BLOCK // STRIP
    for b in range(blocks):
        gnt_copy(b).wait()
        load(blocks + b).wait()
        if b >= 2:
            store(b - 2).wait()

        def through_norm(n, _, b=b):
            rows = pl.ds(pl.multiple_of(n * STRIP, STRIP), STRIP)
            full = pl.ds(pl.multiple_of(b * BLOCK + n * STRIP, STRIP), STRIP)
            grad = gnt_own[b, rows, :].astype(F32) + gnt_x[b, rows, :].astype(F32)
            centred, scale = norm_stats(held[b % 2, rows, :])
            unit = centred * scale
            small_ref[LN2_GAIN:LN2_GAIN + 1, :] += sum_rows(grad * unit)
            small_ref[LN2_BIAS:LN2_BIAS + 1, :] += sum_rows(grad)
            total = dy_ref[full, :].astype(F32) + norm_back(grad * gains, unit, scale)
            ready[b % 2, rows, :] = total
            low = total.astype(BF)
            small_ref[OUT_BIAS:OUT_BIAS + 1, :] += sum_rows(low.astype(F32))
            ga_t[b, :, rows] = turn(low)
            mixed = dot_rows(low, wout[...]).astype(BF)
            for p in range(pairs):
                gm_ref[p, full, :] = mixed[:, p * PAIR:(p + 1) * PAIR]
            return 0

        lax.fori_loop(0, strips, through_norm, 0)
        store(b).start()
        ga_copy(b).start()
        gm_copy(b).start()
        if b + 2 < blocks:
            load(blocks + b + 2).start()
    store(blocks - 2).wait()
    store(blocks - 1).wait()
    for b in range(blocks):
        ga_copy(b).wait()
        gm_copy(b).wait()
    branch_keep.wait()
    keep.wait()


def run_ff(middle, dy, wff, gain, offset, up_bias, wout):
    length, width = middle.shape
    half = wff.shape[3] // CHUNK
    chunks = 2 * half
    blocks = length // BLOCK
    pairs = wout.shape[0] // PAIR
    depth = width // SEQ_SIZE
    dma = pltpu.SemaphoreType.DMA
    turned = pltpu.VMEM((blocks, width, BLOCK), BF)
    rows = pltpu.VMEM((blocks, BLOCK, width), BF)
    hidden = pltpu.VMEM((half, length, CHUNK), BF)
    return pl.pallas_call(
        ff_kernel,
        out_shape=[
            shape_of((length, width), BF),
            shape_of((length, width), F32),
            shape_of((blocks, width, BLOCK), BF),
            shape_of((pairs, length, PAIR), BF),
            shape_of((chunks, Z_SIZE, Y_SIZE, depth, CHUNK), BF),
            shape_of((SMALL_ROWS, width), F32),
        ],
        in_specs=[ANY_SPEC] * 3 + [VMEM_SPEC] * 3 + [ANY_SPEC],
        out_specs=[ANY_SPEC] * 5 + [VMEM_SPEC],
        scratch_shapes=[
            pltpu.VMEM((length, width), BF), pltpu.VMEM(wff.shape, BF),
            pltpu.VMEM(wout.shape, BF), pltpu.VMEM((1, half * CHUNK), F32),
            pltpu.VMEM((length, width), BF), turned, pltpu.VMEM((pairs, length, PAIR), BF),
            pltpu.VMEM((BLOCK, width), BF), turned, turned, hidden, hidden,
            pltpu.VMEM((BLOCK, width), F32), rows, rows,
            pltpu.VMEM((chunks, Z_SIZE, Y_SIZE, CORES, depth, CHUNK), BF),
            pltpu.VMEM((chunks, Z_SIZE, Y_SIZE, depth, CHUNK), BF),
            pltpu.VMEM((2, BLOCK, width), F32), pltpu.VMEM((2, BLOCK, width), F32),
            dma((blocks,)), dma((blocks,)), dma((chunks,)), dma((chunks,)),
            dma((2,)), dma((2,)), dma((1,)), dma((2 + half,)), dma((1 + 2 * blocks,)),
        ],
        compiler_params=pltpu.CompilerParams(
            collective_id=1, has_side_effects=True, vmem_limit_bytes=VMEM_LIMIT
        ),
    )(middle, dy, wff, gain, offset, up_bias, wout)


def back_kernel(
    q_hbm, k_hbm, v_hbm, mix_hbm, gm_hbm, query_hbm, ga_hbm, normed_hbm, wqkv_hbm, x_hbm,
    key_more, gain, down_bias, small_in, mid_hbm, gmid_hbm, ff_part, branch,
    out_hbm, tokens_hbm, qkv_sum, out_sum, up_sum, down_sum,
    gain_one, offset_one, qv_small, out_small, gain_two, offset_two, up_small, down_small,
    q_ref, k_ref, v_ref, mix_ref, gm_ref, query_more, ga_t, normed_t, wqkv, x_ref,
    out_ref, tokens_ref, key_t, key_acc, value_acc, dq, dk, dv, whole, mate, at_y, at_z, ff_y, ff_z, gn_own, gn_x,
    branch_x, branch_own, ff_own, held, small_own, small_z, small_y, small_c,
    bs, br, fys, fyr, fzs, fzr, acs, acr, ays, ayr, azs, azr, gs, gr, ls, ms, mr, os, hs, ins, more_ins, outs,
):
    length, width = x_ref.shape
    blocks = length // BLOCK
    strips = length // STRIP
    pairs = q_ref.shape[0]
    chunks = ff_part.shape[0]
    half = chunks // 2
    groups = chunks // GROUP
    me, head, core, y, across, core_mate, y_mate, z_mates = place()
    z = me // (Y_SIZE * CORES)
    by_pair = (
        (q_hbm, q_ref), (k_hbm, k_ref), (v_hbm, v_ref), (mix_hbm, mix_ref), (gm_hbm, gm_ref),
    )

    def pair_loads(p):
        both = pl.ds(2 * p, 2)
        first = p * (len(by_pair) + 1)
        return [
            pltpu.make_async_copy(src.at[p], dst.at[p], ins.at[first + n])
            for n, (src, dst) in enumerate(by_pair)
        ] + [
            pltpu.make_async_copy(
                query_hbm.at[both], query_more.at[both], ins.at[first + len(by_pair)]
            )
        ]

    late_loads = [
        pltpu.make_async_copy(src, dst, more_ins.at[n])
        for n, (src, dst) in enumerate(
            ((ga_hbm, ga_t), (normed_hbm, normed_t), (wqkv_hbm, wqkv), (x_hbm, x_ref))
        )
    ]
    for p in range(pairs):
        for copy in pair_loads(p):
            copy.start()
        if p == 0:
            late_loads[0].start()
            late_loads[1].start()
    late_loads[2].start()
    late_loads[3].start()
    greet([across, core_mate, y_mate, *z_mates])

    def part(b):
        return pl.ds(b * BLOCK, BLOCK)

    def branch_copy(b):
        return remote(branch.at[part(b), :], branch_x.at[part(b), :], bs.at[b], br.at[b], across)

    def load(n):
        source = mid_hbm if n < blocks else gmid_hbm
        return pltpu.make_async_copy(
            source.at[part(n % blocks), :], held.at[n % 2], ls.at[n % 2]
        )

    def taken(n):
        if n + 2 < 2 * blocks:
            load(n + 2).start()

    def group(g):
        return pl.ds(g * GROUP, GROUP)

    def ff_y_copy(g):
        return remote(
            ff_part.at[group(g), :, 1 - y], ff_y.at[group(g)], fys.at[g], fyr.at[g], y_mate
        )

    def ff_z_copy(g, d):
        n = g * 3 + d - 1
        return remote(
            ff_y.at[group(g), (z + d) % Z_SIZE], ff_z.at[d - 1, group(g)],
            fzs.at[n], fzr.at[n], z_mates[d - 1],
        )

    def branch_load(b):
        return pltpu.make_async_copy(branch.at[part(b), :], branch_own.at[b % 2], hs.at[b % 2])

    def ff_load(g):
        return pltpu.make_async_copy(
            ff_part.at[group(g), :, y], ff_own.at[g % 2], os.at[g % 2]
        )

    def ff_y_event(g):
        ff_y_copy(g).wait_recv()
        ff_load(g).wait()
        for n in range(g * GROUP, (g + 1) * GROUP):
            own = ff_own[g % 2, n % GROUP]
            ff_y[n] = (ff_y[n].astype(F32) + own.astype(F32)).astype(BF)
        if g + 2 < groups:
            ff_load(g + 2).start()
            ff_y_copy(g + 2).start()
        for d in (1, 2, 3):
            ff_z_copy(g, d).start()

    def ff_z_event(g):
        for d in (1, 2, 3):
            ff_z_copy(g, d).wait_recv()
        for n in range(g * GROUP, (g + 1) * GROUP):
            total = ff_y[n, z].astype(F32)
            for d in (1, 2, 3):
                total += ff_z[d - 1, n].astype(F32)
            if n < half:
                up_sum[:, n * CHUNK:(n + 1) * CHUNK] = total
            else:
                down_sum[:, (n - half) * CHUNK:(n - half + 1) * CHUNK] = total

    def at_c_copy(p):
        return remote(whole.at[p, :, :, 1 - core], mate.at[p], acs.at[p], acr.at[p], core_mate)

    def at_y_copy(p):
        return remote(mate.at[p, :, 1 - y], at_y.at[p], ays.at[p], ayr.at[p], y_mate)

    def at_z_copy(p, d):
        n = p * 3 + d - 1
        return remote(
            at_y.at[p, (z + d) % Z_SIZE], at_z.at[d - 1, p], azs.at[n], azr.at[n], z_mates[d - 1]
        )

    def at_c_event(p):
        at_c_copy(p).wait_recv()
        mate[p] = (mate[p].astype(F32) + whole[p, :, :, core].astype(F32)).astype(BF)
        at_y_copy(p).start()

    def at_y_event(p):
        at_y_copy(p).wait_recv()
        at_y[p] = (at_y[p].astype(F32) + mate[p, :, y].astype(F32)).astype(BF)
        for d in (1, 2, 3):
            at_z_copy(p, d).start()

    def at_z_event(p):
        for d in (1, 2, 3):
            at_z_copy(p, d).wait_recv()
        total = at_y[p, z].astype(F32)
        for d in (1, 2, 3):
            total += at_z[d - 1, p].astype(F32)
        cut = slice(p * PAIR, (p + 1) * PAIR)
        for kind in range(3):
            qkv_sum[kind, :, cut] = total[:, kind * PAIR:(kind + 1) * PAIR]
        out_sum[:, cut] = total[:, 3 * PAIR:]

    def out_copy(b):
        return pltpu.make_async_copy(out_ref.at[part(b), :], out_hbm.at[part(b), :], outs.at[b])

    def tokens_copy(b):
        return pltpu.make_async_copy(
            tokens_ref.at[part(b), :], tokens_hbm.at[part(b), :], outs.at[blocks + b]
        )

    def branch_event(b):
        branch_copy(b).wait_recv()
        load(b).wait()
        branch_load(b).wait()
        both = branch_own[b % 2].astype(F32) + branch_x[part(b), :].astype(F32)
        out_ref[part(b), :] = (held[b % 2] + both + as_row(down_bias)).astype(BF)
        out_copy(b).start()
        taken(b)
        if b + 2 < blocks:
            branch_load(b + 2).start()

    for b in range(blocks):
        branch_copy(b).start()
    for n in range(2):
        load(n).start()
        branch_load(n).start()
        ff_load(n).start()
        ff_y_copy(n).start()

    plan = {
        11: [(at_c_event, 0)], 15: [(ff_y_event, 0), (branch_event, 0)], 19: [(at_c_event, 1)],
        27: [(at_c_event, 2), (ff_y_event, 1), (branch_event, 1)],
    }

    low_lanes = lanes() < HEAD_DIM
    zero = jnp.zeros((1, PAIR), BF)

    def stacked(strip):
        return jnp.concatenate(
            [jnp.where(low_lanes, strip, zero), jnp.where(low_lanes, zero, strip)], axis=0
        )

    def attend(t, _):
        p, b = t // strips, t % strips
        rows = pl.ds(pl.multiple_of(b * STRIP, STRIP), STRIP)

        @pl.when(b == 0)
        def _():
            for p_now in range(pairs):
                @pl.when(p == p_now)
                def _(p_now=p_now):
                    for copy in pair_loads(p_now):
                        copy.wait()
            key_t[...] = turn(k_ref[p])
            key_acc[...] = jnp.zeros_like(key_acc)
            value_acc[...] = jnp.zeros_like(value_acc)

        queries, grads = stacked(q_ref[p, rows, :]), stacked(gm_ref[p, rows, :])
        more = jnp.concatenate(
            [query_more[2 * p, rows, :], query_more[2 * p + 1, rows, :]], axis=0
        )
        mixture = mix_ref[p, rows, :]
        product = grads.astype(F32) * jnp.concatenate([mixture, mixture], axis=0).astype(F32)
        inner = -jnp.sum(product, axis=-1, keepdims=True)
        query_side = jnp.concatenate([queries, more], axis=1)
        grad_side = jnp.concatenate([grads, in_pieces(inner, 0, 0.0)], axis=1)
        to_queries = jnp.zeros((PAIR, 2 * STRIP), F32)
        for n in range(blocks):
            keys = jnp.concatenate([k_ref[p, part(n), :], key_more[part(n), :]], axis=1)
            values = jnp.concatenate([v_ref[p, part(n), :], one_lanes(BLOCK)], axis=1)
            weights = jnp.exp(dot_rows(keys, query_side))
            grad_scores = (weights * dot_rows(values, grad_side)).astype(BF)
            value_acc[part(n), :] += nn(weights.astype(BF), grads)
            key_acc[part(n), :] += nn(grad_scores, queries)
            to_queries += nn(key_t[:, part(n)], grad_scores)
        own = jnp.concatenate(
            [to_queries[:HEAD_DIM, :STRIP], to_queries[HEAD_DIM:, STRIP:]], axis=0
        )
        dq[p, rows, :] = (turn(own) * 0.125).astype(BF)

        @pl.when(b == strips - 1)
        def _():
            @pl.when(p == 0)
            def _():
                late_loads[0].wait()
                late_loads[1].wait()

            dk[p] = key_acc[...].astype(BF)
            dv[p] = value_acc[...].astype(BF)
            total = jnp.zeros((width, 3 * PAIR), F32)
            out_total = jnp.zeros((width, PAIR), F32)
            for n in range(blocks):
                right = jnp.concatenate(
                    [dq[p, part(n), :], dk[p, part(n), :], dv[p, part(n), :]], axis=1
                )
                total += nn(normed_t[n], right)
                out_total += nn(ga_t[n], mix_ref[p, part(n), :])
            both = jnp.concatenate([total, out_total], axis=1).astype(BF)
            whole[p] = both.reshape(whole.shape[1:])
            at_c_copy(p).start()

        @pl.when(b % 4 == 3)
        def _():
            for step, events in plan.items():
                @pl.when(t == step)
                def _(events=events):
                    for event, n in events:
                        event(n)
        return 0

    lax.fori_loop(0, pairs * strips, attend, 0)
    late_loads[2].wait()
    late_loads[3].wait()

    def gn_copy(b):
        return remote(gn_own.at[b], gn_x.at[b], gs.at[b], gr.at[b], across)

    for b in range(blocks):
        total = jnp.zeros((BLOCK, width), F32)
        for n, grad in enumerate((dq, dk, dv)):
            left = jnp.concatenate([grad[p, part(b), :] for p in range(pairs)], axis=1)
            total += dot_rows(left, wqkv[n])
        gn_own[b] = total.astype(BF)
        gn_copy(b).start()

    at_c_event(3)
    small_own[...] = small_in[...]
    for p in range(pairs):
        first, second = p * PAIR, (pairs + p) * PAIR
        small_own[QV_BIAS:QV_BIAS + 1, first:first + PAIR] = sum_rows(dq[p].astype(F32))
        small_own[QV_BIAS:QV_BIAS + 1, second:second + PAIR] = sum_rows(dv[p].astype(F32))
    branch_event(2)
    ff_y_event(2)
    branch_event(3)
    ff_z_event(0)
    ff_y_event(3)
    at_y_event(0)
    ff_z_event(1)
    gains = as_row(gain)
    for b in range(blocks):
        gn_copy(b).wait()
        load(blocks + b).wait()
        grad = gn_own[b].astype(F32) + gn_x[b].astype(F32)
        centred, scale = norm_stats(x_ref[part(b), :].astype(F32))
        unit = centred * scale
        small_own[LN1_GAIN:LN1_GAIN + 1, :] += sum_rows(grad * unit)
        small_own[LN1_BIAS:LN1_BIAS + 1, :] += sum_rows(grad)
        tokens_ref[part(b), :] = (
            held[b % 2] + norm_back(grad * gains, unit, scale)
        ).astype(BF)
        tokens_copy(b).start()
        taken(blocks + b)
        if b == 0:
            at_y_event(1)
            at_y_event(2)
            ff_z_event(2)
        if b == 1:
            at_y_event(3)
            ff_z_event(3)
        if b == 2:
            at_z_event(0)
            at_z_event(1)
            at_z_event(2)

    def small_z_copy(d):
        return remote(small_own, small_z.at[z], ms.at[d - 1], mr.at[d - 1], z_mates[d - 1])

    def small_z_arrival(d):
        slot = small_z.at[(z + Z_SIZE - d) % Z_SIZE]
        return remote(slot, slot, ms.at[d - 1], mr.at[d - 1], z_mates[d - 1])

    for d in (1, 2, 3):
        small_z_copy(d).start()
    small_z[z] = small_own[...]
    at_z_event(3)
    for d in (1, 2, 3):
        small_z_arrival(d).wait_recv()
    small_y[0] = small_z[0] + small_z[1] + small_z[2] + small_z[3]
    y_sum = remote(small_y.at[0], small_y.at[1], ms.at[3], mr.at[3], y_mate)
    y_sum.start()
    y_sum.wait()
    small_c[0] = small_y[0] + small_y[1]
    c_sum = remote(small_c.at[0], small_c.at[1], ms.at[4], mr.at[4], core_mate)
    c_sum.start()
    c_sum.wait()
    small = small_c[0] + small_c[1]
    for kind, target in (
        (LN1_GAIN, gain_one), (LN1_BIAS, offset_one), (OUT_BIAS, out_small),
        (LN2_GAIN, gain_two), (LN2_BIAS, offset_two), (DOWN_BIAS, down_small),
    ):
        target[...] = small[kind:kind + 1, :].reshape(width)
    cols = pairs * PAIR
    qv_small[0:1, :] = small[QV_BIAS:QV_BIAS + 1, :cols]
    qv_small[1:2, :] = small[QV_BIAS:QV_BIAS + 1, cols:]
    for n in range(up_small.shape[0] // width):
        row = small[UP_BIAS + n:UP_BIAS + n + 1, :]
        up_small[n * width:(n + 1) * width] = row.reshape(width)

    for d in (1, 2, 3):
        small_z_copy(d).wait_send()
    for b in range(blocks):
        out_copy(b).wait()
        tokens_copy(b).wait()
        branch_copy(b).wait_send()
    for g in range(groups):
        ff_y_copy(g).wait_send()
        for d in (1, 2, 3):
            ff_z_copy(g, d).wait_send()
    for p in range(pairs):
        at_c_copy(p).wait_send()
        at_y_copy(p).wait_send()
        for d in (1, 2, 3):
            at_z_copy(p, d).wait_send()


def run_back(
    queries, keys, values, mixture, grad_mixture, query_more, ga_t, normed_t, wqkv, x,
    key_more, gain, down_bias, small, middle, grad_middle, ff_part, branch,
):
    length, width = x.shape
    pairs = queries.shape[0]
    chunks, depth = ff_part.shape[0], ff_part.shape[3]
    groups = chunks // GROUP
    cols, hidden = pairs * PAIR, chunks // 2 * CHUNK
    blocks = length // BLOCK
    dma = pltpu.SemaphoreType.DMA
    rows = pltpu.VMEM((blocks, BLOCK, width), BF)
    by_pair = pltpu.VMEM((pairs, length, PAIR), BF)
    whole_rows = pltpu.VMEM((length, width), BF)
    row = shape_of((width,), F32)
    loaded = (
        queries, keys, values, mixture, grad_mixture, query_more, ga_t, normed_t, wqkv, x
    )
    return pl.pallas_call(
        back_kernel,
        out_shape=[
            shape_of((length, width), BF),
            shape_of((length, width), BF),
            shape_of((3, depth, cols), F32),
            shape_of((depth, cols), F32),
            shape_of((depth, hidden), F32),
            shape_of((depth, hidden), F32),
            row, row, shape_of((2, cols), F32), row, row, row, shape_of((hidden,), F32), row,
        ],
        in_specs=[ANY_SPEC] * 10 + [VMEM_SPEC] * 4 + [ANY_SPEC] * 4,
        out_specs=[ANY_SPEC] * 2 + [VMEM_SPEC] * 12,
        scratch_shapes=[pltpu.VMEM(v.shape, BF) for v in loaded] + [
            whole_rows, whole_rows, pltpu.VMEM((PAIR, length), BF),
            pltpu.VMEM((length, PAIR), F32), pltpu.VMEM((length, PAIR), F32),
            by_pair, by_pair, by_pair,
            pltpu.VMEM((pairs, Z_SIZE, Y_SIZE, CORES, depth, CHUNK), BF),
            pltpu.VMEM((pairs, Z_SIZE, Y_SIZE, depth, CHUNK), BF),
            pltpu.VMEM((pairs, Z_SIZE, depth, CHUNK), BF),
            pltpu.VMEM((3, pairs, depth, CHUNK), BF),
            pltpu.VMEM((chunks, Z_SIZE, depth, CHUNK), BF),
            pltpu.VMEM((3, chunks, depth, CHUNK), BF),
            rows, rows, whole_rows,
            pltpu.VMEM((2, BLOCK, width), BF),
            pltpu.VMEM((2, GROUP, Z_SIZE, depth, CHUNK), BF),
            pltpu.VMEM((2, BLOCK, width), F32),
            pltpu.VMEM(small.shape, F32),
            pltpu.VMEM((Z_SIZE,) + small.shape, F32),
            pltpu.VMEM((2,) + small.shape, F32),
            pltpu.VMEM((2,) + small.shape, F32),
            dma((blocks,)), dma((blocks,)), dma((groups,)), dma((groups,)),
            dma((3 * groups,)), dma((3 * groups,)), dma((pairs,)), dma((pairs,)),
            dma((pairs,)), dma((pairs,)), dma((3 * pairs,)), dma((3 * pairs,)),
            dma((blocks,)), dma((blocks,)), dma((2,)), dma((5,)), dma((5,)), dma((2,)), dma((2,)),
            dma((6 * pairs,)), dma((4,)), dma((2 * blocks,)),
        ],
        compiler_params=pltpu.CompilerParams(
            collective_id=2, has_side_effects=True, vmem_limit_bytes=VMEM_LIMIT
        ),
    )(*loaded, key_more, gain, down_bias, small, middle, grad_middle, ff_part, branch)


def hand_over_kernel(*refs):
    *refs, sems = refs
    count = len(refs) // 3
    refs = refs[:count] + refs[2 * count:] + refs[count:2 * count]
    loads, stores = (
        [
            pltpu.make_async_copy(refs[a * count + n], refs[b * count + n], sems.at[a, n])
            for n in range(count)
        ]
        for a, b in ((0, 1), (1, 2))
    )
    for load in loads:
        load.start()
    for load, store in zip(loads, stores):
        load.wait()
        store.start()
    for store in stores:
        store.wait()


def hand_over(results):
    return pl.pallas_call(
        hand_over_kernel,
        out_shape=[shape_of(v.shape, v.dtype) for v in results],
        in_specs=[ANY_SPEC] * len(results),
        out_specs=[ANY_SPEC] * len(results),
        scratch_shapes=[pltpu.VMEM(v.shape, v.dtype) for v in results] + [
            pltpu.SemaphoreType.DMA((2, len(results)))
        ],
        compiler_params=pltpu.CompilerParams(vmem_limit_bytes=VMEM_LIMIT),
    )(*results)


def fast_body(
    tokens, segment_ids, context_flags, ln1_gain, ln1_bias, qkv_weight, qv_bias, out_weight,
    out_bias, ln2_gain, ln2_bias, up_weight, up_bias, down_weight, down_bias, cotangent,
):
    x, dy = tokens[0], cotangent[0]
    queries, keys, values, mixture, middle, normed_t, wff, key_more, query_more = run_fwd(
        x, segment_ids, context_flags, ln1_gain, ln1_bias, qv_bias, out_bias, qkv_weight,
        out_weight, up_weight, down_weight.T,
    )
    branch, grad_middle, ga_t, grad_mixture, ff_part, small = run_ff(
        middle, dy, wff, ln2_gain, ln2_bias, up_bias, out_weight
    )
    (
        output, tokens_grad, qkv_grad, out_grad, up_grad, down_grad, gain_one, offset_one,
        qv_grad, out_bias_grad, gain_two, offset_two, up_bias_grad, down_bias_grad,
    ) = hand_over(run_back(
        queries, keys, values, mixture, grad_mixture, query_more, ga_t, normed_t, qkv_weight, x,
        key_more, ln1_gain, down_bias, small, middle, grad_middle, ff_part, branch,
    ))
    return (
        output[None], tokens_grad[None], gain_one, offset_one, qkv_grad, qv_grad, out_grad.T,
        out_bias_grad, gain_two, offset_two, up_grad, up_bias_grad, down_grad.T, down_bias_grad,
    )


def solution(mesh):
    chosen = generic_body
    if mesh.shape["head"] == 2 and mesh.shape["seq"] == SEQ_SIZE:
        chosen = fast_body
    return jax.shard_map(
        chosen,
        mesh=mesh,
        in_specs=(
            P("seq", None, None),
            P("seq", None),
            P("seq", None),
            P(),
            P(),
            P(None, None, "head"),
            P(None, "head"),
            P("head", None),
            P(),
            P(),
            P(),
            P("seq", "head"),
            P("head"),
            P("head", "seq"),
            P(),
            P("seq", None, None),
        ),
        out_specs=(
            P("seq", None, None),
            P("seq", None, None),
            P(),
            P(),
            P(None, "seq", "head"),
            P(None, "head"),
            P("head", "seq"),
            P(),
            P(),
            P(),
            P("seq", "head"),
            P("head"),
            P("head", "seq"),
            P(),
        ),
        check_vma=False,
    )
```

```python
import math

import jax
import jax.numpy as jnp
from jax import lax
from jax.experimental import pallas as pl
from jax.experimental.pallas import tpu as pltpu
from jax.sharding import PartitionSpec as P

HEAD_DIM = 64


def layer_norm(values_in, scaling, offset):
    middle = jnp.mean(values_in, axis=-1, keepdims=True)
    centred = values_in - middle
    spread = jnp.mean(centred * centred, axis=-1, keepdims=True)
    return centred * lax.rsqrt(spread + 1e-05) * scaling + offset


def gelu_exact(values_in):
    return 0.5 * values_in * (1.0 + jax.scipy.special.erf(values_in * 0.7071067811865476))


def dot_rows(left, right):
    return lax.dot_general(
        left, right, (((1,), (1,)), ((), ())), preferred_element_type=jnp.float32
    )


def dot_cols(left, right):
    return lax.dot_general(
        left, right, (((0,), (0,)), ((), ())), preferred_element_type=jnp.float32
    )


def masked_scores(block_query, seq_keys, block_segments, seq_segments, seq_context, factor):
    raw_scores = (
        jnp.einsum("qhd,khd->hqk", block_query, seq_keys, preferred_element_type=jnp.float32)
        * factor
    )
    allowed = (block_segments[:, None] == seq_segments[None, :]) & (seq_context[None, :] == 1)
    return jnp.where(allowed[None], raw_scores, -1e30)


def generic_body(
    tokens,
    segment_ids,
    context_flags,
    ln1_gain,
    ln1_bias,
    qkv_weight,
    qv_bias,
    out_weight,
    out_bias,
    ln2_gain,
    ln2_bias,
    up_weight,
    up_bias,
    down_weight,
    down_bias,
    cotangent,
):
    seq_count, length, width = tokens.shape
    row_count = seq_count * length
    local_cols = qkv_weight.shape[2]
    head_count = local_cols // HEAD_DIM
    factor = 1.0 / math.sqrt(HEAD_DIM)
    block = min(512, length)
    blocks = length // block
    gain_one = ln1_gain.astype(jnp.float32)
    offset_one = ln1_bias.astype(jnp.float32)
    gain_two = ln2_gain.astype(jnp.float32)
    offset_two = ln2_bias.astype(jnp.float32)
    flat_in = tokens.astype(jnp.float32).reshape(row_count, width)
    normed_f, norm_one_pull = jax.vjp(layer_norm, flat_in, gain_one, offset_one)
    normed = normed_f.astype(jnp.bfloat16)
    queries = (
        jnp.dot(normed, qkv_weight[0], preferred_element_type=jnp.float32)
        + qv_bias[0].astype(jnp.float32)
    ).astype(jnp.bfloat16)
    key_rows = jnp.dot(normed, qkv_weight[1], preferred_element_type=jnp.float32).astype(
        jnp.bfloat16
    )
    value_rows = (
        jnp.dot(normed, qkv_weight[2], preferred_element_type=jnp.float32)
        + qv_bias[1].astype(jnp.float32)
    ).astype(jnp.bfloat16)

    def per_sequence(array):
        return array.reshape(seq_count, length, head_count, HEAD_DIM)

    def attend_sequence(member):
        seq_query, seq_keys, seq_values, seq_segments, seq_context = member

        def attend_block(portion):
            block_query, block_segments = portion
            scores = masked_scores(
                block_query, seq_keys, block_segments, seq_segments, seq_context, factor
            )
            row_top = jnp.max(scores, axis=-1, keepdims=True)
            exponent = jnp.exp(scores - row_top)
            row_total = jnp.sum(exponent, axis=-1, keepdims=True)
            soft_weights = (exponent / row_total).astype(jnp.bfloat16)
            block_mix = jnp.einsum(
                "hqk,khd->qhd", soft_weights, seq_values, preferred_element_type=jnp.float32
            )
            return (block_mix.astype(jnp.bfloat16), row_top + jnp.log(row_total))

        return lax.map(
            attend_block,
            (
                seq_query.reshape(blocks, block, head_count, HEAD_DIM),
                seq_segments.reshape(blocks, block),
            ),
        )

    mixture, log_totals = lax.map(
        attend_sequence,
        (
            per_sequence(queries),
            per_sequence(key_rows),
            per_sequence(value_rows),
            segment_ids,
            context_flags,
        ),
    )
    mixture = mixture.reshape(row_count, local_cols)
    partial_out = jnp.dot(mixture, out_weight, preferred_element_type=jnp.float32)
    grad_rows_all = cotangent.reshape(row_count, width)
    grad_float_all = grad_rows_all.astype(jnp.float32)
    grad_down_bias = jnp.sum(grad_float_all, axis=0)
    attended = lax.psum(partial_out, "head") + out_bias.astype(jnp.float32)
    middle_state = flat_in + attended
    normed_two_f, norm_two_pull = jax.vjp(layer_norm, middle_state, gain_two, offset_two)
    normed_two = normed_two_f.astype(jnp.bfloat16)
    up_part, down_part, up_shift = (
        lax.all_gather(up_weight, "head", axis=1, tiled=True),
        lax.all_gather(down_weight, "head", axis=0, tiled=True),
        lax.all_gather(up_bias, "head", axis=0, tiled=True),
    )
    up_full, down_full = (
        lax.all_gather(up_part, "seq", axis=0, tiled=True),
        lax.all_gather(down_part, "seq", axis=1, tiled=True),
    )
    before = jnp.dot(normed_two, up_full, preferred_element_type=jnp.float32) + up_shift.astype(
        jnp.float32
    )
    active_f, gelu_pull = jax.vjp(gelu_exact, before)
    active = active_f.astype(jnp.bfloat16)
    branch_out = jnp.dot(active, down_full, preferred_element_type=jnp.float32)
    final_rows = (middle_state + branch_out + down_bias.astype(jnp.float32)).astype(jnp.bfloat16)
    output = final_rows.reshape(tokens.shape)
    grad_float = grad_rows_all.astype(jnp.float32)
    grad_down = dot_cols(active, grad_rows_all)
    grad_active = dot_rows(grad_rows_all, down_full)
    (grad_before_f,) = gelu_pull(grad_active)
    grad_before = grad_before_f.astype(jnp.bfloat16)
    grad_up = dot_cols(normed_two, grad_before)
    grad_up_bias = jnp.sum(grad_before.astype(jnp.float32), axis=0)
    grad_normed_two = dot_rows(grad_before, up_full)
    grad_middle_norm, grad_gain_two, grad_offset_two = norm_two_pull(grad_normed_two)
    grad_middle = grad_float + grad_middle_norm
    ff_part = up_weight.shape[1]
    start_col = lax.axis_index("head") * ff_part
    grad_up = lax.dynamic_slice_in_dim(grad_up, start_col, ff_part, 1)
    grad_down = lax.dynamic_slice_in_dim(grad_down, start_col, ff_part, 0)
    grad_up_bias = lax.dynamic_slice_in_dim(grad_up_bias, start_col, ff_part, 0)
    grad_attended = grad_middle.astype(jnp.bfloat16)
    grad_out_bias = jnp.sum(grad_attended.astype(jnp.float32), axis=0)
    grad_out = dot_cols(mixture, grad_attended)
    grad_mixture = dot_rows(grad_attended, out_weight).astype(jnp.bfloat16)

    def back_sequence(member):
        seq_query, seq_keys, seq_values, seq_grad, seq_logs, seq_segments, seq_context = member

        def back_block(carry, portion):
            key_acc, value_acc = carry
            block_query, block_grad, block_logs, block_segments = portion
            scores = masked_scores(
                block_query, seq_keys, block_segments, seq_segments, seq_context, factor
            )
            soft_weights = jnp.exp(scores - block_logs)
            value_acc = value_acc + jnp.einsum(
                "hqk,qhd->khd",
                soft_weights.astype(jnp.bfloat16),
                block_grad,
                preferred_element_type=jnp.float32,
            )
            grad_soft = jnp.einsum(
                "qhd,khd->hqk", block_grad, seq_values, preferred_element_type=jnp.float32
            )
            row_inner = jnp.sum(soft_weights * grad_soft, axis=-1, keepdims=True)
            grad_scores = (soft_weights * (grad_soft - row_inner)).astype(jnp.bfloat16)
            grad_query = (
                jnp.einsum(
                    "hqk,khd->qhd", grad_scores, seq_keys, preferred_element_type=jnp.float32
                )
                * factor
            )
            key_acc = (
                key_acc
                + jnp.einsum(
                    "hqk,qhd->khd", grad_scores, block_query, preferred_element_type=jnp.float32
                )
                * factor
            )
            return ((key_acc, value_acc), grad_query)

        empty = jnp.zeros((length, head_count, HEAD_DIM), jnp.float32)
        (key_acc, value_acc), grad_query = lax.scan(
            back_block,
            (empty, empty),
            (
                seq_query.reshape(blocks, block, head_count, HEAD_DIM),
                seq_grad.reshape(blocks, block, head_count, HEAD_DIM),
                seq_logs,
                seq_segments.reshape(blocks, block),
            ),
        )
        return (grad_query, key_acc, value_acc)

    grad_queries, grad_keys, grad_values = lax.map(
        back_sequence,
        (
            per_sequence(queries),
            per_sequence(key_rows),
            per_sequence(value_rows),
            per_sequence(grad_mixture),
            log_totals,
            segment_ids,
            context_flags,
        ),
    )
    grad_queries = grad_queries.reshape(row_count, local_cols).astype(jnp.bfloat16)
    grad_keys = grad_keys.reshape(row_count, local_cols).astype(jnp.bfloat16)
    grad_values = grad_values.reshape(row_count, local_cols).astype(jnp.bfloat16)
    grad_qv_bias = jnp.stack(
        [
            jnp.sum(grad_queries.astype(jnp.float32), axis=0),
            jnp.sum(grad_values.astype(jnp.float32), axis=0),
        ]
    )
    grad_qkv = jnp.stack(
        [dot_cols(normed, grad_queries), dot_cols(normed, grad_keys), dot_cols(normed, grad_values)]
    )
    grad_normed = (
        dot_rows(grad_queries, qkv_weight[0])
        + dot_rows(grad_keys, qkv_weight[1])
        + dot_rows(grad_values, qkv_weight[2])
    )
    grad_normed = lax.psum(grad_normed, "head")
    grad_input_norm, grad_gain_one, grad_offset_one = norm_one_pull(grad_normed)
    tokens_grad = (grad_middle + grad_input_norm).astype(jnp.bfloat16).reshape(tokens.shape)
    summed_qkv, summed_out, summed_up, summed_down = (
        lax.psum_scatter(
            grad_qkv.astype(jnp.bfloat16), "seq", scatter_dimension=1, tiled=True
        ).astype(jnp.float32),
        lax.psum_scatter(
            grad_out.astype(jnp.bfloat16), "seq", scatter_dimension=1, tiled=True
        ).astype(jnp.float32),
        lax.psum_scatter(
            grad_up.astype(jnp.bfloat16), "seq", scatter_dimension=0, tiled=True
        ).astype(jnp.float32),
        lax.psum_scatter(
            grad_down.astype(jnp.bfloat16), "seq", scatter_dimension=1, tiled=True
        ).astype(jnp.float32),
    )
    smalls = lax.psum(
        (
            grad_gain_one,
            grad_offset_one,
            grad_qv_bias,
            grad_out_bias,
            grad_gain_two,
            grad_offset_two,
            grad_up_bias,
            grad_down_bias,
        ),
        "seq",
    )
    return (
        output,
        tokens_grad,
        smalls[0],
        smalls[1],
        summed_qkv,
        smalls[2],
        summed_out,
        smalls[3],
        smalls[4],
        smalls[5],
        summed_up,
        smalls[6],
        summed_down,
        smalls[7],
    )


MESH = pl.DeviceIdType.MESH
BF = jnp.bfloat16
F32 = jnp.float32
BLOCK = 256
STRIP = 512
PIECE = 128
WIDE = 1024
GROUP = 2
CHUNK = 512
PAIR = 2 * HEAD_DIM
Z_SIZE, Y_SIZE, CORES = 4, 2, 2
SEQ_SIZE = Z_SIZE * Y_SIZE * CORES
HOP = Y_SIZE * CORES
TABLES = 8
FAR = -1e30
VMEM_LIMIT = 62 * 2**20
INV_ROOT_TWO = 0.7071067811865476
INV_ROOT_TWO_PI = 0.3989422804014327
LN1_GAIN, LN1_BIAS, QV_BIAS, OUT_BIAS, LN2_GAIN, LN2_BIAS, UP_BIAS, DOWN_BIAS = 0, 1, 2, 3, 4, 5, 6, 8
SMALL_ROWS = 16
VMEM_SPEC = pl.BlockSpec(memory_space=pltpu.VMEM)
ANY_SPEC = pl.BlockSpec(memory_space=pl.ANY)


def shape_of(dims, dtype):
    return jax.ShapeDtypeStruct(tuple(dims), dtype)


def nn(left, right):
    return jnp.dot(left, right, preferred_element_type=F32)


def turn(block):
    return jnp.transpose(block)


def sum_rows(block):
    return jnp.sum(block, axis=0, keepdims=True)


def place():
    me = lax.axis_index("seq")
    head = lax.axis_index("head")
    core = me % 2
    y = (me // 2) % 2
    across = {"seq": me, "head": 1 - head}
    core_mate = {"seq": me + 1 - 2 * core, "head": head}
    y_mate = {"seq": me + 2 - 4 * y, "head": head}
    z_mates = [{"seq": (me + HOP * d) % SEQ_SIZE, "head": head} for d in (1, 2, 3)]
    return me, head, core, y, across, core_mate, y_mate, z_mates


def greet(others):
    barrier = pltpu.get_barrier_semaphore()
    for other in others:
        pl.semaphore_signal(barrier, inc=1, device_id=other, device_id_type=MESH)
    pl.semaphore_wait(barrier, len(others))


def remote(src, dst, send_sem, recv_sem, other):
    return pltpu.make_async_remote_copy(
        src_ref=src, dst_ref=dst, send_sem=send_sem, recv_sem=recv_sem,
        device_id=other, device_id_type=MESH,
    )


def norm_stats(rows):
    middle = jnp.mean(rows, axis=-1, keepdims=True)
    centred = rows - middle
    spread = jnp.mean(centred * centred, axis=-1, keepdims=True)
    return centred, lax.rsqrt(spread + 1e-05)


def norm_back(inner, unit, scale):
    return scale * (
        inner
        - jnp.mean(inner, axis=-1, keepdims=True)
        - unit * jnp.mean(inner * unit, axis=-1, keepdims=True)
    )


def as_row(vector):
    return vector[...].astype(F32).reshape(1, -1)


def lanes():
    return lax.broadcasted_iota(jnp.int32, (1, PAIR), 1)


def in_pieces(column, first, rest):
    high = column.astype(BF).astype(F32)
    mid = (column - high).astype(BF).astype(F32)
    low = column - high - mid
    at = lanes()
    return jnp.where(
        at == first, high, jnp.where(at == first + 1, mid, jnp.where(at == first + 2, low, rest))
    ).astype(BF)


def one_lanes(length):
    return jnp.broadcast_to(jnp.where(lanes() < 3, 1.0, 0.0).astype(BF), (length, PAIR))


def fwd_kernel(
    x_ref, seg_ref, context, gain, offset, qv_bias, out_bias, wqkv, wout, up_shard, down_shard,
    q_out, k_out, v_out, mix_out, mid_out, normed_out, wff_out, key_out, query_out,
    wff, q_ref, k_ref, v_ref, mix_ref, mid_ref, normed_t, key_more, query_more,
    mask_more, wout_x, mix_x,
    zs, zr, ys, yr, cs, cr, xs, xr, local, outs,
):
    length, width = x_ref.shape
    blocks = length // BLOCK
    pairs = q_ref.shape[0]
    cols = pairs * PAIR
    me, head, core, y, across, core_mate, y_mate, _ = place()
    z = me // HOP
    above = {"seq": (me + HOP) % SEQ_SIZE, "head": head}
    below = {"seq": (me + SEQ_SIZE - HOP) % SEQ_SIZE, "head": head}
    own = [
        pltpu.make_async_copy(shard, wff.at[u, me], local.at[u])
        for u, shard in enumerate((up_shard, down_shard))
    ]
    own[0].start()
    own[1].start()
    greet([across, core_mate, y_mate, above, below])

    out_copy = remote(wout, wout_x, xs.at[0], xr.at[0], across)
    out_copy.start()

    flows = [(0, 0)] + [(way, s) for s in (1, 2, 3) for way in (0, 1)]

    def there(way, s):
        return (z >= s) if way == 0 else (z + s < Z_SIZE)

    def source(base, way, s):
        away = SEQ_SIZE - HOP * s if way == 0 else HOP * s
        return (base + away) % SEQ_SIZE

    def z_copy(u, way, s):
        n = (u * 2 + way) * 3 + s - 1
        j = source(me, way, s - 1)
        return remote(wff.at[u, j], wff.at[u, j], zs.at[n], zr.at[n], above if way == 0 else below)

    def z_arrival(u, way, s):
        n = (u * 2 + way) * 3 + s - 1
        slot = wff.at[u, source(me, way, s)]
        return remote(slot, slot, zs.at[n], zr.at[n], above)

    def z_goes_on(way):
        return (z < Z_SIZE - 1) if way == 0 else (z > 0)

    def y_copy(u, f):
        n = u * 7 + f
        j = source(me, *flows[f])
        return remote(wff.at[u, j], wff.at[u, j], ys.at[n], yr.at[n], y_mate)

    def y_arrival(u, f):
        n = u * 7 + f
        slot = wff.at[u, source(me + 2 - 4 * y, *flows[f])]
        return remote(slot, slot, ys.at[n], yr.at[n], y_mate)

    def c_copy(u, f, from_y):
        n = (u * 2 + from_y) * 7 + f
        j = source(me + from_y * (2 - 4 * y), *flows[f])
        return remote(wff.at[u, j], wff.at[u, j], cs.at[n], cr.at[n], core_mate)

    def c_arrival(u, f, from_y):
        n = (u * 2 + from_y) * 7 + f
        slot = wff.at[u, source(me + 1 - 2 * core + from_y * (2 - 4 * y), *flows[f])]
        return remote(slot, slot, cs.at[n], cr.at[n], core_mate)

    def for_flow(f, do):
        if f == 0:
            do()
        else:
            pl.when(there(*flows[f]))(do)

    def for_step(s, do):
        for f, (way, step) in enumerate(flows):
            if step == s:
                for_flow(f, lambda f=f, way=way: do(f, way))

    def z_event(u, s):
        def one(f, way):
            z_arrival(u, way, s).wait_recv()
            if s < 3:
                pl.when(z_goes_on(way))(lambda: z_copy(u, way, s + 1).start())
            y_copy(u, f).start()
            c_copy(u, f, 0).start()
        for_step(s, one)

    def y_event(u, s):
        def one(f, way):
            y_arrival(u, f).wait_recv()
            c_copy(u, f, 1).start()
        for_step(s, one)

    for u in range(2):
        own[u].wait()
        for way in (0, 1):
            pl.when(z_goes_on(way))(lambda u=u, way=way: z_copy(u, way, 1).start())
        y_copy(u, 0).start()
        c_copy(u, 0, 0).start()

    plan = {
        3: [(z_event, 0, 1), (y_event, 0, 0)], 5: [(z_event, 1, 1), (y_event, 1, 0)],
        7: [(z_event, 0, 2)], 9: [(z_event, 1, 2), (y_event, 0, 1)], 10: [(y_event, 1, 1)],
        11: [(z_event, 0, 3)],
    }
    last = [
        (z_event, 1, 3), (y_event, 0, 2), (y_event, 1, 2), (y_event, 0, 3), (y_event, 1, 3)
    ]

    def tick(t):
        for step, events in plan.items():
            @pl.when(t == step)
            def _(events=events):
                for event, u, s in events:
                    event(u, s)

    at = lax.broadcasted_iota(jnp.int32, (PAIR, length), 0)
    same = at == seg_ref[...]
    hidden = context[...] != 1
    ones = jnp.logical_and(at > TABLES, at < TABLES + 4)
    key_side = jnp.logical_or(
        jnp.logical_and(at < TABLES, same),
        jnp.logical_or(jnp.logical_and(at == TABLES, hidden), ones),
    )
    query_side = jnp.logical_and(at <= TABLES, jnp.logical_not(same))
    key_more[...] = turn(jnp.where(key_side, 1.0, 0.0)).astype(BF)
    mask_more[...] = turn(jnp.where(query_side, FAR, 0.0)).astype(BF)

    keep = [
        pltpu.make_async_copy(here, there, outs.at[n])
        for n, (here, there) in enumerate(
            (
                (q_ref, q_out), (k_ref, k_out), (v_ref, v_out), (normed_t, normed_out),
                (key_more, key_out), (query_more, query_out), (mix_ref, mix_out),
            )
        )
    ]
    gains, offsets = as_row(gain), as_row(offset)
    query_bias = qv_bias[0:1, :].astype(F32)
    value_bias = qv_bias[1:2, :].astype(F32)

    def project(b, _):
        rows = pl.ds(pl.multiple_of(b * BLOCK, BLOCK), BLOCK)
        centred, scale = norm_stats(x_ref[rows, :].astype(F32))
        block = (centred * scale * gains + offsets).astype(BF)
        normed_t[b] = turn(block)
        queries = ((nn(block, wqkv[0]) + query_bias).astype(BF) * 0.125).astype(BF)
        keys = nn(block, wqkv[1]).astype(BF)
        values = (nn(block, wqkv[2]) + value_bias).astype(BF)
        for p in range(pairs):
            part = slice(p * PAIR, (p + 1) * PAIR)
            q_ref[p, rows, :] = queries[:, part]
            k_ref[p, rows, :] = keys[:, part]
            v_ref[p, rows, :] = values[:, part]
        tick(b)
        return 0

    lax.fori_loop(0, blocks, project, 0)
    for n in range(5):
        keep[n].start()

    low_lanes = lanes() < HEAD_DIM
    zero = jnp.zeros((1, PAIR), BF)

    def mixture_copy(b):
        rows = pl.ds(pl.multiple_of(b * BLOCK, BLOCK), BLOCK)
        return remote(
            mix_ref.at[:, rows, :], mix_x.at[:, rows, :], xs.at[1 + b], xr.at[1 + b], across
        )

    per_step = STRIP // BLOCK

    def attend(t, _):
        b, p = t // pairs, t % pairs
        keys = jnp.concatenate([k_ref[p], key_more[...]], axis=1)
        values = jnp.concatenate([v_ref[p], one_lanes(length)], axis=1)
        chains = []
        for n in range(per_step):
            rows = pl.ds(pl.multiple_of(b * STRIP + n * BLOCK, BLOCK), BLOCK)
            queries, more = q_ref[p, rows, :], mask_more[rows, :]
            for low in (0, 1):
                own_lanes = jnp.logical_not(low_lanes) if low else low_lanes
                left = jnp.concatenate([jnp.where(own_lanes, queries, zero), more], axis=1)
                chains.append((rows, low, more, dot_rows(left, keys)))
        parts = []
        for rows, low, more, scores in chains:
            top = jnp.max(scores, axis=-1, keepdims=True)
            mixed = nn(jnp.exp(scores - top).astype(BF), values)
            total = mixed[:, PAIR:PAIR + 1]
            parts.append(mixed[:, :PAIR] / total)
            query_more[2 * p + low, rows, :] = in_pieces(
                -(top + jnp.log(total)), TABLES + 1, more.astype(F32)
            )
            if low:
                mix_ref[p, rows, :] = jnp.where(low_lanes, *parts[-2:]).astype(BF)
        tick(t + blocks)

        @pl.when(p == pairs - 1)
        def _():
            for n in range(per_step):
                mixture_copy(b * per_step + n).start()

        return 0

    lax.fori_loop(0, length // STRIP * pairs, attend, 0)
    keep[5].start()
    keep[6].start()
    out_copy.wait_recv()
    out_row = as_row(out_bias)

    def mid_copy(b):
        rows = pl.ds(b * BLOCK, BLOCK)
        return pltpu.make_async_copy(mid_ref.at[rows, :], mid_out.at[rows, :], outs.at[7 + b])

    for b in range(blocks):
        if b < 3:
            for event, u, s in last[b:b + 1]:
                event(u, s)
        else:
            for event, u, s in last[3:]:
                event(u, s)
        mixture_copy(b).wait_recv()
        rows = pl.ds(b * BLOCK, BLOCK)
        ours = jnp.concatenate([mix_ref[p, rows, :] for p in range(pairs)], axis=-1)
        other = jnp.concatenate([mix_x[p, rows, :] for p in range(pairs)], axis=-1)
        attended = nn(ours, wout[...]) + nn(other, wout_x[...])
        mid_ref[rows, :] = x_ref[rows, :].astype(F32) + (attended + out_row)
        mid_copy(b).start()

    wff_keep = [pltpu.make_async_copy(wff.at[u], wff_out.at[u], local.at[u]) for u in range(2)]
    for u in range(2):
        for f in range(len(flows)):
            def arrive(u=u, f=f):
                for from_y in (0, 1):
                    c_arrival(u, f, from_y).wait_recv()
            for_flow(f, arrive)
        wff_keep[u].start()
    out_copy.wait_send()
    for copy in keep + wff_keep:
        copy.wait()
    for b in range(blocks):
        mixture_copy(b).wait_send()
        mid_copy(b).wait()
    for u in range(2):
        for way in (0, 1):
            pl.when(z_goes_on(way))(lambda u=u, way=way: z_copy(u, way, 1).wait_send())
        for f, (way, s) in enumerate(flows):
            def finish(u=u, f=f, way=way, s=s):
                if f and s < 3:
                    pl.when(z_goes_on(way))(lambda: z_copy(u, way, s + 1).wait_send())
                y_copy(u, f).wait_send()
                for from_y in (0, 1):
                    c_copy(u, f, from_y).wait_send()
            for_flow(f, finish)


def run_fwd(x, seg, context, gain, offset, qv_bias, out_bias, wqkv, wout, up_weight, down_t):
    length, width = x.shape
    pairs = wqkv.shape[2] // PAIR
    blocks = length // BLOCK
    depth, hidden = up_weight.shape
    by_pair, by_head = (pairs, length, PAIR), (2 * pairs, length, PAIR)
    turned = (blocks, width, BLOCK)
    dma = pltpu.SemaphoreType.DMA
    return pl.pallas_call(
        fwd_kernel,
        out_shape=[shape_of(by_pair, BF)] * 4 + [
            shape_of((length, width), F32),
            shape_of(turned, BF),
            shape_of((2, SEQ_SIZE, depth, hidden), BF),
            shape_of((length, PAIR), BF),
            shape_of(by_head, BF),
        ],
        in_specs=[VMEM_SPEC] * 9 + [ANY_SPEC] * 2,
        out_specs=[ANY_SPEC] * 9,
        scratch_shapes=[pltpu.VMEM((2, SEQ_SIZE, depth, hidden), BF)]
        + [pltpu.VMEM(by_pair, BF)] * 4 + [
            pltpu.VMEM((length, width), F32),
            pltpu.VMEM(turned, BF),
            pltpu.VMEM((length, PAIR), BF),
            pltpu.VMEM(by_head, BF),
            pltpu.VMEM((length, PAIR), BF),
            pltpu.VMEM(wout.shape, BF),
            pltpu.VMEM(by_pair, BF),
            dma((12,)), dma((12,)), dma((14,)), dma((14,)), dma((28,)), dma((28,)),
            dma((1 + blocks,)), dma((1 + blocks,)), dma((2,)), dma((7 + blocks,)),
        ],
        compiler_params=pltpu.CompilerParams(
            collective_id=0, has_side_effects=True, vmem_limit_bytes=VMEM_LIMIT
        ),
    )(x, seg, context, gain, offset, qv_bias, out_bias, wqkv, wout, up_weight, down_t)


def ff_kernel(
    mid_hbm, dy_hbm, wff_hbm, gain, offset, up_bias, wout_hbm,
    branch_out, gmid_hbm, ga_out, gm_out, summed, small_ref,
    dy_ref, wff, wout, bias_row, branch_ref, ga_t, gm_ref, normed, normed_t, dy_t, active, before_grad, gnt_acc, gnt_own, gnt_x, whole, from_mate,
    held, ready,
    xs, xr, cs, cr, ls, ws, ss, ins, outs,
):
    length, width = dy_ref.shape
    blocks = length // BLOCK
    hidden = wff.shape[3]
    half = hidden // WIDE
    chunks = 2 * hidden // CHUNK
    pairs = gm_ref.shape[0]
    me, head, core, y, across, core_mate, y_mate, z_mates = place()
    dy_load = pltpu.make_async_copy(dy_hbm, dy_ref, ins.at[0])
    wout_load = pltpu.make_async_copy(wout_hbm, wout, ins.at[1])

    def wff_load(n):
        cut = pl.ds(n * WIDE, WIDE)
        return pltpu.make_async_copy(
            wff_hbm.at[:, :, :, cut], wff.at[:, :, :, cut], ins.at[2 + n]
        )

    dy_load.start()
    for n in range(half):
        wff_load(n).start()
    wout_load.start()
    greet([across, core_mate])
    gains, offsets = as_row(gain), as_row(offset)
    bias_row[...] = as_row(up_bias)

    def weight(kind, n):
        cut = pl.ds(pl.multiple_of(n * WIDE, WIDE), WIDE)
        return wff[kind, :, :, cut].reshape(width, WIDE)

    small_ref[...] = jnp.zeros_like(small_ref)

    def load(n):
        rows = pl.ds(n % blocks * BLOCK, BLOCK)
        return pltpu.make_async_copy(mid_hbm.at[rows, :], held.at[n % 2], ls.at[n % 2])

    def store(b):
        rows = pl.ds(b * BLOCK, BLOCK)
        return pltpu.make_async_copy(ready.at[b % 2], gmid_hbm.at[rows, :], ws.at[b % 2])

    load(0).start()
    load(1).start()

    def gnt_copy(b):
        return remote(gnt_own.at[b], gnt_x.at[b], xs.at[b], xr.at[b], across)

    def core_copy(n):
        return remote(
            whole.at[n, :, :, 1 - core], from_mate.at[n], cs.at[n], cr.at[n], core_mate
        )

    def forward(t, _):
        b, n = t // half, t % half
        rows = pl.ds(pl.multiple_of(b * BLOCK, BLOCK), BLOCK)

        for b_next in range(blocks):
            @pl.when(t == b_next * half)
            def _(b_next=b_next):
                load(b_next).wait()
                if b_next == 0:
                    dy_load.wait()

        for n_first in range(half):
            @pl.when(t == n_first)
            def _(n_first=n_first):
                wff_load(n_first).wait()

        @pl.when(n == 0)
        def _():
            centred, scale = norm_stats(held[b % 2])
            block = (centred * scale * gains + offsets).astype(BF)
            normed[...] = block
            normed_t[:, rows] = turn(block)
            dy_t[:, rows] = turn(dy_ref[rows, :])
            small_ref[DOWN_BIAS:DOWN_BIAS + 1, :] += sum_rows(dy_ref[rows, :].astype(F32))

        up = weight(0, n)
        cut = pl.ds(pl.multiple_of(n * WIDE, WIDE), WIDE)
        before = nn(normed[...], up) + bias_row[:, cut]
        spread = 0.5 * (1.0 + lax.erf(before * INV_ROOT_TWO))
        active[n, rows, :] = (before * spread).astype(BF)
        slope = spread + before * (INV_ROOT_TWO_PI * jnp.exp(before * before * -0.5))
        grad = (nn(dy_ref[rows, :], weight(1, n)) * slope).astype(BF)
        before_grad[n, rows, :] = grad
        small_ref[pl.ds(UP_BIAS + n, 1), :] += sum_rows(grad.astype(F32))
        back = dot_rows(grad, up)

        @pl.when(n == 0)
        def _():
            gnt_acc[...] = back

        @pl.when(n > 0)
        def _():
            gnt_acc[...] += back

        for b_done in range(blocks):
            @pl.when(t == (b_done + 1) * half - 1)
            def _(b_done=b_done):
                load(b_done + 2).start()
                gnt_own[b_done] = gnt_acc[...].astype(BF)
                gnt_copy(b_done).start()
        return 0

    lax.fori_loop(0, blocks * half, forward, 0)

    def weight_grads(left_t, right, first):
        cut_rows = width // Z_SIZE
        per_wide = WIDE // CHUNK

        def one(t, _):
            n, plane = t // Z_SIZE, t % Z_SIZE
            cut = pl.ds(pl.multiple_of(plane * cut_rows, cut_rows), cut_rows)
            total = nn(left_t[cut, :], right[n]).astype(BF)
            for m in range(per_wide):
                piece = total[:, m * CHUNK:(m + 1) * CHUNK]
                whole[first + n * per_wide + m, plane] = piece.reshape(whole.shape[2:])

            @pl.when(plane == Z_SIZE - 1)
            def _():
                for m in range(per_wide):
                    core_copy(first + n * per_wide + m).start()

            return 0

        lax.fori_loop(0, Z_SIZE * half, one, 0)

    weight_grads(dy_t, active, chunks // 2)
    weight_grads(normed_t, before_grad, 0)

    def branch(b, _):
        rows = pl.ds(pl.multiple_of(b * BLOCK, BLOCK), BLOCK)
        total = dot_rows(active[0, rows, :], weight(1, 0))
        for n in range(1, half):
            total += dot_rows(active[n, rows, :], weight(1, n))
        branch_ref[rows, :] = total.astype(BF)
        return 0

    lax.fori_loop(0, blocks, branch, 0)
    branch_keep = pltpu.make_async_copy(branch_ref, branch_out, outs.at[0])
    branch_keep.start()
    wout_load.wait()

    def ga_copy(b):
        return pltpu.make_async_copy(ga_t.at[b], ga_out.at[b], outs.at[1 + b])

    def gm_copy(b):
        rows = pl.ds(b * BLOCK, BLOCK)
        return pltpu.make_async_copy(
            gm_ref.at[:, rows, :], gm_out.at[:, rows, :], outs.at[1 + blocks + b]
        )


    def add_mate(n, _):
        core_copy(n).wait()
        both = whole[n, :, :, core].astype(F32) + from_mate[n].astype(F32)
        from_mate[n] = both.astype(BF)
        return 0

    lax.fori_loop(chunks // 2, chunks, add_mate, 0)
    lax.fori_loop(0, chunks // 2, add_mate, 0)
    keep = pltpu.make_async_copy(from_mate, summed, ss.at[0])
    keep.start()

    strips = BLOCK // PIECE
    for b in range(blocks):
        gnt_copy(b).wait()
        load(blocks + b).wait()
        if b >= 2:
            store(b - 2).wait()

        def through_norm(n, _, b=b):
            rows = pl.ds(pl.multiple_of(n * PIECE, PIECE), PIECE)
            full = pl.ds(pl.multiple_of(b * BLOCK + n * PIECE, PIECE), PIECE)
            grad = gnt_own[b, rows, :].astype(F32) + gnt_x[b, rows, :].astype(F32)
            centred, scale = norm_stats(held[b % 2, rows, :])
            unit = centred * scale
            small_ref[LN2_GAIN:LN2_GAIN + 1, :] += sum_rows(grad * unit)
            small_ref[LN2_BIAS:LN2_BIAS + 1, :] += sum_rows(grad)
            total = dy_ref[full, :].astype(F32) + norm_back(grad * gains, unit, scale)
            ready[b % 2, rows, :] = total
            low = total.astype(BF)
            small_ref[OUT_BIAS:OUT_BIAS + 1, :] += sum_rows(low.astype(F32))
            ga_t[b, :, rows] = turn(low)
            mixed = dot_rows(low, wout[...]).astype(BF)
            for p in range(pairs):
                gm_ref[p, full, :] = mixed[:, p * PAIR:(p + 1) * PAIR]
            return 0

        lax.fori_loop(0, strips, through_norm, 0)
        store(b).start()
        ga_copy(b).start()
        gm_copy(b).start()
        if b + 2 < blocks:
            load(blocks + b + 2).start()
    store(blocks - 2).wait()
    store(blocks - 1).wait()
    for b in range(blocks):
        ga_copy(b).wait()
        gm_copy(b).wait()
    branch_keep.wait()
    keep.wait()


def run_ff(middle, dy, wff, gain, offset, up_bias, wout):
    length, width = middle.shape
    half = wff.shape[3] // WIDE
    chunks = 2 * wff.shape[3] // CHUNK
    blocks = length // BLOCK
    pairs = wout.shape[0] // PAIR
    depth = width // SEQ_SIZE
    dma = pltpu.SemaphoreType.DMA
    turned = pltpu.VMEM((blocks, width, BLOCK), BF)
    rows = pltpu.VMEM((blocks, BLOCK, width), BF)
    hidden = pltpu.VMEM((half, length, WIDE), BF)
    flat_t = pltpu.VMEM((width, length), BF)
    return pl.pallas_call(
        ff_kernel,
        out_shape=[
            shape_of((length, width), BF),
            shape_of((length, width), F32),
            shape_of((blocks, width, BLOCK), BF),
            shape_of((pairs, length, PAIR), BF),
            shape_of((chunks, Z_SIZE, Y_SIZE, depth, CHUNK), BF),
            shape_of((SMALL_ROWS, width), F32),
        ],
        in_specs=[ANY_SPEC] * 3 + [VMEM_SPEC] * 3 + [ANY_SPEC],
        out_specs=[ANY_SPEC] * 5 + [VMEM_SPEC],
        scratch_shapes=[
            pltpu.VMEM((length, width), BF), pltpu.VMEM(wff.shape, BF),
            pltpu.VMEM(wout.shape, BF), pltpu.VMEM((1, half * WIDE), F32),
            pltpu.VMEM((length, width), BF), turned, pltpu.VMEM((pairs, length, PAIR), BF),
            pltpu.VMEM((BLOCK, width), BF), flat_t, flat_t, hidden, hidden,
            pltpu.VMEM((BLOCK, width), F32), rows, rows,
            pltpu.VMEM((chunks, Z_SIZE, Y_SIZE, CORES, depth, CHUNK), BF),
            pltpu.VMEM((chunks, Z_SIZE, Y_SIZE, depth, CHUNK), BF),
            pltpu.VMEM((2, BLOCK, width), F32), pltpu.VMEM((2, BLOCK, width), F32),
            dma((blocks,)), dma((blocks,)), dma((chunks,)), dma((chunks,)),
            dma((2,)), dma((2,)), dma((1,)), dma((2 + half,)), dma((1 + 2 * blocks,)),
        ],
        compiler_params=pltpu.CompilerParams(
            collective_id=1, has_side_effects=True, vmem_limit_bytes=VMEM_LIMIT
        ),
    )(middle, dy, wff, gain, offset, up_bias, wout)


def back_kernel(
    q_hbm, k_hbm, v_hbm, mix_hbm, gm_hbm, query_hbm, ga_hbm, normed_hbm, wqkv_hbm, x_hbm,
    key_more, gain, down_bias, small_in, mid_hbm, gmid_hbm, ff_part, branch,
    out_hbm, tokens_hbm, qkv_sum, out_sum, up_sum, down_sum,
    gain_one, offset_one, qv_small, out_small, gain_two, offset_two, up_small, down_small,
    q_ref, k_ref, v_ref, mix_ref, gm_ref, query_more, ga_t, normed_t, wqkv, x_ref,
    out_ref, tokens_ref, key_t, key_acc, value_acc, dq, dk, dv, whole, mate, at_y, at_z, ff_y, ff_z, gn_own, gn_x,
    branch_x, branch_own, ff_own, held, small_own, small_z, small_y, small_c,
    bs, br, fys, fyr, fzs, fzr, acs, acr, ays, ayr, azs, azr, gs, gr, ls, ms, mr, os, hs, ins, more_ins, outs,
):
    length, width = x_ref.shape
    blocks = length // BLOCK
    strips = length // STRIP
    pairs = q_ref.shape[0]
    chunks = ff_part.shape[0]
    half = chunks // 2
    groups = chunks // GROUP
    me, head, core, y, across, core_mate, y_mate, z_mates = place()
    z = me // (Y_SIZE * CORES)
    by_pair = (
        (q_hbm, q_ref), (k_hbm, k_ref), (v_hbm, v_ref), (mix_hbm, mix_ref), (gm_hbm, gm_ref),
    )

    def pair_loads(p):
        both = pl.ds(2 * p, 2)
        first = p * (len(by_pair) + 1)
        return [
            pltpu.make_async_copy(src.at[p], dst.at[p], ins.at[first + n])
            for n, (src, dst) in enumerate(by_pair)
        ] + [
            pltpu.make_async_copy(
                query_hbm.at[both], query_more.at[both], ins.at[first + len(by_pair)]
            )
        ]

    late_loads = [
        pltpu.make_async_copy(src, dst, more_ins.at[n])
        for n, (src, dst) in enumerate(
            ((ga_hbm, ga_t), (normed_hbm, normed_t), (wqkv_hbm, wqkv), (x_hbm, x_ref))
        )
    ]
    for p in range(pairs):
        for copy in pair_loads(p):
            copy.start()
        if p == 0:
            late_loads[0].start()
            late_loads[1].start()
    late_loads[2].start()
    late_loads[3].start()
    greet([across, core_mate, y_mate, *z_mates])

    def part(b):
        return pl.ds(b * BLOCK, BLOCK)

    def branch_copy(b):
        return remote(branch.at[part(b), :], branch_x.at[part(b), :], bs.at[b], br.at[b], across)

    def load(n):
        source = mid_hbm if n < blocks else gmid_hbm
        return pltpu.make_async_copy(
            source.at[part(n % blocks), :], held.at[n % 2], ls.at[n % 2]
        )

    def taken(n):
        if n + 2 < 2 * blocks:
            load(n + 2).start()

    def group(g):
        return pl.ds(g * GROUP, GROUP)

    def ff_y_copy(g):
        return remote(
            ff_part.at[group(g), :, 1 - y], ff_y.at[group(g)], fys.at[g], fyr.at[g], y_mate
        )

    def ff_z_copy(g, d):
        n = g * 3 + d - 1
        return remote(
            ff_y.at[group(g), (z + d) % Z_SIZE], ff_z.at[d - 1, group(g)],
            fzs.at[n], fzr.at[n], z_mates[d - 1],
        )

    def branch_load(b):
        return pltpu.make_async_copy(branch.at[part(b), :], branch_own.at[b % 2], hs.at[b % 2])

    def ff_load(g):
        return pltpu.make_async_copy(
            ff_part.at[group(g), :, y], ff_own.at[g % 2], os.at[g % 2]
        )

    def ff_y_event(g):
        ff_y_copy(g).wait_recv()
        ff_load(g).wait()
        for n in range(g * GROUP, (g + 1) * GROUP):
            own = ff_own[g % 2, n % GROUP]
            ff_y[n] = (ff_y[n].astype(F32) + own.astype(F32)).astype(BF)
        if g + 2 < groups:
            ff_load(g + 2).start()
            ff_y_copy(g + 2).start()
        for d in (1, 2, 3):
            ff_z_copy(g, d).start()

    def ff_z_event(g):
        for d in (1, 2, 3):
            ff_z_copy(g, d).wait_recv()
        for n in range(g * GROUP, (g + 1) * GROUP):
            total = ff_y[n, z].astype(F32)
            for d in (1, 2, 3):
                total += ff_z[d - 1, n].astype(F32)
            if n < half:
                up_sum[:, n * CHUNK:(n + 1) * CHUNK] = total
            else:
                down_sum[:, (n - half) * CHUNK:(n - half + 1) * CHUNK] = total

    def at_c_copy(p):
        return remote(whole.at[p, :, :, 1 - core], mate.at[p], acs.at[p], acr.at[p], core_mate)

    def at_y_copy(p):
        return remote(mate.at[p, :, 1 - y], at_y.at[p], ays.at[p], ayr.at[p], y_mate)

    def at_z_copy(p, d):
        n = p * 3 + d - 1
        return remote(
            at_y.at[p, (z + d) % Z_SIZE], at_z.at[d - 1, p], azs.at[n], azr.at[n], z_mates[d - 1]
        )

    def at_c_event(p):
        at_c_copy(p).wait_recv()
        mate[p] = (mate[p].astype(F32) + whole[p, :, :, core].astype(F32)).astype(BF)
        at_y_copy(p).start()

    def at_y_event(p):
        at_y_copy(p).wait_recv()
        at_y[p] = (at_y[p].astype(F32) + mate[p, :, y].astype(F32)).astype(BF)
        for d in (1, 2, 3):
            at_z_copy(p, d).start()

    def at_z_event(p):
        for d in (1, 2, 3):
            at_z_copy(p, d).wait_recv()
        total = at_y[p, z].astype(F32)
        for d in (1, 2, 3):
            total += at_z[d - 1, p].astype(F32)
        cut = slice(p * PAIR, (p + 1) * PAIR)
        for kind in range(3):
            qkv_sum[kind, :, cut] = total[:, kind * PAIR:(kind + 1) * PAIR]
        out_sum[:, cut] = total[:, 3 * PAIR:]

    def out_copy(b):
        return pltpu.make_async_copy(out_ref.at[part(b), :], out_hbm.at[part(b), :], outs.at[b])

    def tokens_copy(b):
        return pltpu.make_async_copy(
            tokens_ref.at[part(b), :], tokens_hbm.at[part(b), :], outs.at[blocks + b]
        )

    def branch_event(b):
        branch_copy(b).wait_recv()
        load(b).wait()
        branch_load(b).wait()
        both = branch_own[b % 2].astype(F32) + branch_x[part(b), :].astype(F32)
        out_ref[part(b), :] = (held[b % 2] + both + as_row(down_bias)).astype(BF)
        out_copy(b).start()
        taken(b)
        if b + 2 < blocks:
            branch_load(b + 2).start()

    for b in range(blocks):
        branch_copy(b).start()
    for n in range(2):
        load(n).start()
        branch_load(n).start()
        ff_load(n).start()
        ff_y_copy(n).start()

    plan = {
        2: [(at_c_event, 0), (ff_y_event, 0), (branch_event, 0)], 4: [(at_c_event, 1)],
        5: [(ff_y_event, 1), (branch_event, 1)], 6: [(at_c_event, 2)],
    }

    low_lanes = lanes() < HEAD_DIM
    zero = jnp.zeros((1, PAIR), BF)

    def stacked(strip):
        return jnp.concatenate(
            [jnp.where(low_lanes, strip, zero), jnp.where(low_lanes, zero, strip)], axis=0
        )

    def attend(t, _):
        p, b = t // strips, t % strips
        rows = pl.ds(pl.multiple_of(b * STRIP, STRIP), STRIP)

        @pl.when(b == 0)
        def _():
            for p_now in range(pairs):
                @pl.when(p == p_now)
                def _(p_now=p_now):
                    for copy in pair_loads(p_now):
                        copy.wait()
            key_t[...] = turn(k_ref[p])
            key_acc[...] = jnp.zeros_like(key_acc)
            value_acc[...] = jnp.zeros_like(value_acc)

        queries, grads = stacked(q_ref[p, rows, :]), stacked(gm_ref[p, rows, :])
        more = jnp.concatenate(
            [query_more[2 * p, rows, :], query_more[2 * p + 1, rows, :]], axis=0
        )
        mixture = mix_ref[p, rows, :]
        product = grads.astype(F32) * jnp.concatenate([mixture, mixture], axis=0).astype(F32)
        inner = -jnp.sum(product, axis=-1, keepdims=True)
        query_side = jnp.concatenate([queries, more], axis=1)
        grad_side = jnp.concatenate([grads, in_pieces(inner, 0, 0.0)], axis=1)
        to_queries = jnp.zeros((PAIR, 2 * STRIP), F32)
        for n in range(blocks):
            keys = jnp.concatenate([k_ref[p, part(n), :], key_more[part(n), :]], axis=1)
            values = jnp.concatenate([v_ref[p, part(n), :], one_lanes(BLOCK)], axis=1)
            weights = jnp.exp(dot_rows(keys, query_side))
            grad_scores = (weights * dot_rows(values, grad_side)).astype(BF)
            value_acc[part(n), :] += nn(weights.astype(BF), grads)
            key_acc[part(n), :] += nn(grad_scores, queries)
            to_queries += nn(key_t[:, part(n)], grad_scores)
        own = jnp.concatenate(
            [to_queries[:HEAD_DIM, :STRIP], to_queries[HEAD_DIM:, STRIP:]], axis=0
        )
        dq[p, rows, :] = (turn(own) * 0.125).astype(BF)

        @pl.when(b == strips - 1)
        def _():
            @pl.when(p == 0)
            def _():
                late_loads[0].wait()
                late_loads[1].wait()

            dk[p] = key_acc[...].astype(BF)
            dv[p] = value_acc[...].astype(BF)
            total = jnp.zeros((width, 3 * PAIR), F32)
            out_total = jnp.zeros((width, PAIR), F32)
            for n in range(blocks):
                right = jnp.concatenate(
                    [dq[p, part(n), :], dk[p, part(n), :], dv[p, part(n), :]], axis=1
                )
                total += nn(normed_t[n], right)
                out_total += nn(ga_t[n], mix_ref[p, part(n), :])
            both = jnp.concatenate([total, out_total], axis=1).astype(BF)
            whole[p] = both.reshape(whole.shape[1:])
            at_c_copy(p).start()

        for step, events in plan.items():
            @pl.when(t == step)
            def _(events=events):
                for event, n in events:
                    event(n)
        return 0

    lax.fori_loop(0, pairs * strips, attend, 0)
    late_loads[2].wait()
    late_loads[3].wait()

    def gn_copy(b):
        return remote(gn_own.at[b], gn_x.at[b], gs.at[b], gr.at[b], across)

    for b in range(blocks):
        total = jnp.zeros((BLOCK, width), F32)
        for n, grad in enumerate((dq, dk, dv)):
            left = jnp.concatenate([grad[p, part(b), :] for p in range(pairs)], axis=1)
            total += dot_rows(left, wqkv[n])
        gn_own[b] = total.astype(BF)
        gn_copy(b).start()

    at_c_event(3)
    small_own[...] = small_in[...]
    for p in range(pairs):
        first, second = p * PAIR, (pairs + p) * PAIR
        small_own[QV_BIAS:QV_BIAS + 1, first:first + PAIR] = sum_rows(dq[p].astype(F32))
        small_own[QV_BIAS:QV_BIAS + 1, second:second + PAIR] = sum_rows(dv[p].astype(F32))
    branch_event(2)
    ff_y_event(2)
    branch_event(3)
    ff_z_event(0)
    ff_y_event(3)
    at_y_event(0)
    ff_z_event(1)
    gains = as_row(gain)
    for b in range(blocks):
        gn_copy(b).wait()
        load(blocks + b).wait()
        grad = gn_own[b].astype(F32) + gn_x[b].astype(F32)
        centred, scale = norm_stats(x_ref[part(b), :].astype(F32))
        unit = centred * scale
        small_own[LN1_GAIN:LN1_GAIN + 1, :] += sum_rows(grad * unit)
        small_own[LN1_BIAS:LN1_BIAS + 1, :] += sum_rows(grad)
        tokens_ref[part(b), :] = (
            held[b % 2] + norm_back(grad * gains, unit, scale)
        ).astype(BF)
        tokens_copy(b).start()
        taken(blocks + b)
        if b == 0:
            at_y_event(1)
            at_y_event(2)
            ff_z_event(2)
        if b == 1:
            at_y_event(3)
            ff_z_event(3)
        if b == 2:
            at_z_event(0)
            at_z_event(1)
            at_z_event(2)

    def small_z_copy(d):
        return remote(small_own, small_z.at[z], ms.at[d - 1], mr.at[d - 1], z_mates[d - 1])

    def small_z_arrival(d):
        slot = small_z.at[(z + Z_SIZE - d) % Z_SIZE]
        return remote(slot, slot, ms.at[d - 1], mr.at[d - 1], z_mates[d - 1])

    for d in (1, 2, 3):
        small_z_copy(d).start()
    small_z[z] = small_own[...]
    at_z_event(3)
    for d in (1, 2, 3):
        small_z_arrival(d).wait_recv()
    small_y[0] = small_z[0] + small_z[1] + small_z[2] + small_z[3]
    y_sum = remote(small_y.at[0], small_y.at[1], ms.at[3], mr.at[3], y_mate)
    y_sum.start()
    y_sum.wait()
    small_c[0] = small_y[0] + small_y[1]
    c_sum = remote(small_c.at[0], small_c.at[1], ms.at[4], mr.at[4], core_mate)
    c_sum.start()
    c_sum.wait()
    small = small_c[0] + small_c[1]
    for kind, target in (
        (LN1_GAIN, gain_one), (LN1_BIAS, offset_one), (OUT_BIAS, out_small),
        (LN2_GAIN, gain_two), (LN2_BIAS, offset_two), (DOWN_BIAS, down_small),
    ):
        target[...] = small[kind:kind + 1, :].reshape(width)
    cols = pairs * PAIR
    qv_small[0:1, :] = small[QV_BIAS:QV_BIAS + 1, :cols]
    qv_small[1:2, :] = small[QV_BIAS:QV_BIAS + 1, cols:]
    for n in range(up_small.shape[0] // width):
        row = small[UP_BIAS + n:UP_BIAS + n + 1, :]
        up_small[n * width:(n + 1) * width] = row.reshape(width)

    for d in (1, 2, 3):
        small_z_copy(d).wait_send()
    for b in range(blocks):
        out_copy(b).wait()
        tokens_copy(b).wait()
        branch_copy(b).wait_send()
    for g in range(groups):
        ff_y_copy(g).wait_send()
        for d in (1, 2, 3):
            ff_z_copy(g, d).wait_send()
    for p in range(pairs):
        at_c_copy(p).wait_send()
        at_y_copy(p).wait_send()
        for d in (1, 2, 3):
            at_z_copy(p, d).wait_send()


def run_back(
    queries, keys, values, mixture, grad_mixture, query_more, ga_t, normed_t, wqkv, x,
    key_more, gain, down_bias, small, middle, grad_middle, ff_part, branch,
):
    length, width = x.shape
    pairs = queries.shape[0]
    chunks, depth = ff_part.shape[0], ff_part.shape[3]
    groups = chunks // GROUP
    cols, hidden = pairs * PAIR, chunks // 2 * CHUNK
    blocks = length // BLOCK
    dma = pltpu.SemaphoreType.DMA
    rows = pltpu.VMEM((blocks, BLOCK, width), BF)
    by_pair = pltpu.VMEM((pairs, length, PAIR), BF)
    whole_rows = pltpu.VMEM((length, width), BF)
    row = shape_of((width,), F32)
    loaded = (
        queries, keys, values, mixture, grad_mixture, query_more, ga_t, normed_t, wqkv, x
    )
    return pl.pallas_call(
        back_kernel,
        out_shape=[
            shape_of((length, width), BF),
            shape_of((length, width), BF),
            shape_of((3, depth, cols), F32),
            shape_of((depth, cols), F32),
            shape_of((depth, hidden), F32),
            shape_of((depth, hidden), F32),
            row, row, shape_of((2, cols), F32), row, row, row, shape_of((hidden,), F32), row,
        ],
        in_specs=[ANY_SPEC] * 10 + [VMEM_SPEC] * 4 + [ANY_SPEC] * 4,
        out_specs=[ANY_SPEC] * 2 + [VMEM_SPEC] * 12,
        scratch_shapes=[pltpu.VMEM(v.shape, BF) for v in loaded] + [
            whole_rows, whole_rows, pltpu.VMEM((PAIR, length), BF),
            pltpu.VMEM((length, PAIR), F32), pltpu.VMEM((length, PAIR), F32),
            by_pair, by_pair, by_pair,
            pltpu.VMEM((pairs, Z_SIZE, Y_SIZE, CORES, depth, CHUNK), BF),
            pltpu.VMEM((pairs, Z_SIZE, Y_SIZE, depth, CHUNK), BF),
            pltpu.VMEM((pairs, Z_SIZE, depth, CHUNK), BF),
            pltpu.VMEM((3, pairs, depth, CHUNK), BF),
            pltpu.VMEM((chunks, Z_SIZE, depth, CHUNK), BF),
            pltpu.VMEM((3, chunks, depth, CHUNK), BF),
            rows, rows, whole_rows,
            pltpu.VMEM((2, BLOCK, width), BF),
            pltpu.VMEM((2, GROUP, Z_SIZE, depth, CHUNK), BF),
            pltpu.VMEM((2, BLOCK, width), F32),
            pltpu.VMEM(small.shape, F32),
            pltpu.VMEM((Z_SIZE,) + small.shape, F32),
            pltpu.VMEM((2,) + small.shape, F32),
            pltpu.VMEM((2,) + small.shape, F32),
            dma((blocks,)), dma((blocks,)), dma((groups,)), dma((groups,)),
            dma((3 * groups,)), dma((3 * groups,)), dma((pairs,)), dma((pairs,)),
            dma((pairs,)), dma((pairs,)), dma((3 * pairs,)), dma((3 * pairs,)),
            dma((blocks,)), dma((blocks,)), dma((2,)), dma((5,)), dma((5,)), dma((2,)), dma((2,)),
            dma((6 * pairs,)), dma((4,)), dma((2 * blocks,)),
        ],
        compiler_params=pltpu.CompilerParams(
            collective_id=2, has_side_effects=True, vmem_limit_bytes=VMEM_LIMIT
        ),
    )(*loaded, key_more, gain, down_bias, small, middle, grad_middle, ff_part, branch)


def hand_over_kernel(*refs):
    *refs, sems = refs
    count = len(refs) // 3
    refs = refs[:count] + refs[2 * count:] + refs[count:2 * count]
    loads, stores = (
        [
            pltpu.make_async_copy(refs[a * count + n], refs[b * count + n], sems.at[a, n])
            for n in range(count)
        ]
        for a, b in ((0, 1), (1, 2))
    )
    for load in loads:
        load.start()
    for load, store in zip(loads, stores):
        load.wait()
        store.start()
    for store in stores:
        store.wait()


def hand_over(results):
    return pl.pallas_call(
        hand_over_kernel,
        out_shape=[shape_of(v.shape, v.dtype) for v in results],
        in_specs=[ANY_SPEC] * len(results),
        out_specs=[ANY_SPEC] * len(results),
        scratch_shapes=[pltpu.VMEM(v.shape, v.dtype) for v in results] + [
            pltpu.SemaphoreType.DMA((2, len(results)))
        ],
        compiler_params=pltpu.CompilerParams(vmem_limit_bytes=VMEM_LIMIT),
    )(*results)


def fast_body(
    tokens, segment_ids, context_flags, ln1_gain, ln1_bias, qkv_weight, qv_bias, out_weight,
    out_bias, ln2_gain, ln2_bias, up_weight, up_bias, down_weight, down_bias, cotangent,
):
    x, dy = tokens[0], cotangent[0]
    queries, keys, values, mixture, middle, normed_t, wff, key_more, query_more = run_fwd(
        x, segment_ids, context_flags, ln1_gain, ln1_bias, qv_bias, out_bias, qkv_weight,
        out_weight, up_weight, down_weight.T,
    )
    branch, grad_middle, ga_t, grad_mixture, ff_part, small = run_ff(
        middle, dy, wff, ln2_gain, ln2_bias, up_bias, out_weight
    )
    (
        output, tokens_grad, qkv_grad, out_grad, up_grad, down_grad, gain_one, offset_one,
        qv_grad, out_bias_grad, gain_two, offset_two, up_bias_grad, down_bias_grad,
    ) = hand_over(run_back(
        queries, keys, values, mixture, grad_mixture, query_more, ga_t, normed_t, qkv_weight, x,
        key_more, ln1_gain, down_bias, small, middle, grad_middle, ff_part, branch,
    ))
    return (
        output[None], tokens_grad[None], gain_one, offset_one, qkv_grad, qv_grad, out_grad.T,
        out_bias_grad, gain_two, offset_two, up_grad, up_bias_grad, down_grad.T, down_bias_grad,
    )


def solution(mesh):
    chosen = generic_body
    if mesh.shape["head"] == 2 and mesh.shape["seq"] == SEQ_SIZE:
        chosen = fast_body
    return jax.shard_map(
        chosen,
        mesh=mesh,
        in_specs=(
            P("seq", None, None),
            P("seq", None),
            P("seq", None),
            P(),
            P(),
            P(None, None, "head"),
            P(None, "head"),
            P("head", None),
            P(),
            P(),
            P(),
            P("seq", "head"),
            P("head"),
            P("head", "seq"),
            P(),
            P("seq", None, None),
        ),
        out_specs=(
            P("seq", None, None),
            P("seq", None, None),
            P(),
            P(),
            P(None, "seq", "head"),
            P(None, "head"),
            P("head", "seq"),
            P(),
            P(),
            P(),
            P("seq", "head"),
            P("head"),
            P("head", "seq"),
            P(),
        ),
        check_vma=False,
    )
```

```python
import math

import jax
import jax.numpy as jnp
from jax import lax
from jax.experimental import pallas as pl
from jax.experimental.pallas import tpu as pltpu
from jax.sharding import PartitionSpec as P

HEAD_DIM = 64


def layer_norm(values_in, scaling, offset):
    middle = jnp.mean(values_in, axis=-1, keepdims=True)
    centred = values_in - middle
    spread = jnp.mean(centred * centred, axis=-1, keepdims=True)
    return centred * lax.rsqrt(spread + 1e-05) * scaling + offset


def gelu_exact(values_in):
    return 0.5 * values_in * (1.0 + jax.scipy.special.erf(values_in * 0.7071067811865476))


def dot_rows(left, right):
    return lax.dot_general(
        left, right, (((1,), (1,)), ((), ())), preferred_element_type=jnp.float32
    )


def dot_cols(left, right):
    return lax.dot_general(
        left, right, (((0,), (0,)), ((), ())), preferred_element_type=jnp.float32
    )


def masked_scores(block_query, seq_keys, block_segments, seq_segments, seq_context, factor):
    raw_scores = (
        jnp.einsum("qhd,khd->hqk", block_query, seq_keys, preferred_element_type=jnp.float32)
        * factor
    )
    allowed = (block_segments[:, None] == seq_segments[None, :]) & (seq_context[None, :] == 1)
    return jnp.where(allowed[None], raw_scores, -1e30)


def generic_body(
    tokens,
    segment_ids,
    context_flags,
    ln1_gain,
    ln1_bias,
    qkv_weight,
    qv_bias,
    out_weight,
    out_bias,
    ln2_gain,
    ln2_bias,
    up_weight,
    up_bias,
    down_weight,
    down_bias,
    cotangent,
):
    seq_count, length, width = tokens.shape
    row_count = seq_count * length
    local_cols = qkv_weight.shape[2]
    head_count = local_cols // HEAD_DIM
    factor = 1.0 / math.sqrt(HEAD_DIM)
    block = min(512, length)
    blocks = length // block
    gain_one = ln1_gain.astype(jnp.float32)
    offset_one = ln1_bias.astype(jnp.float32)
    gain_two = ln2_gain.astype(jnp.float32)
    offset_two = ln2_bias.astype(jnp.float32)
    flat_in = tokens.astype(jnp.float32).reshape(row_count, width)
    normed_f, norm_one_pull = jax.vjp(layer_norm, flat_in, gain_one, offset_one)
    normed = normed_f.astype(jnp.bfloat16)
    queries = (
        jnp.dot(normed, qkv_weight[0], preferred_element_type=jnp.float32)
        + qv_bias[0].astype(jnp.float32)
    ).astype(jnp.bfloat16)
    key_rows = jnp.dot(normed, qkv_weight[1], preferred_element_type=jnp.float32).astype(
        jnp.bfloat16
    )
    value_rows = (
        jnp.dot(normed, qkv_weight[2], preferred_element_type=jnp.float32)
        + qv_bias[1].astype(jnp.float32)
    ).astype(jnp.bfloat16)

    def per_sequence(array):
        return array.reshape(seq_count, length, head_count, HEAD_DIM)

    def attend_sequence(member):
        seq_query, seq_keys, seq_values, seq_segments, seq_context = member

        def attend_block(portion):
            block_query, block_segments = portion
            scores = masked_scores(
                block_query, seq_keys, block_segments, seq_segments, seq_context, factor
            )
            row_top = jnp.max(scores, axis=-1, keepdims=True)
            exponent = jnp.exp(scores - row_top)
            row_total = jnp.sum(exponent, axis=-1, keepdims=True)
            soft_weights = (exponent / row_total).astype(jnp.bfloat16)
            block_mix = jnp.einsum(
                "hqk,khd->qhd", soft_weights, seq_values, preferred_element_type=jnp.float32
            )
            return (block_mix.astype(jnp.bfloat16), row_top + jnp.log(row_total))

        return lax.map(
            attend_block,
            (
                seq_query.reshape(blocks, block, head_count, HEAD_DIM),
                seq_segments.reshape(blocks, block),
            ),
        )

    mixture, log_totals = lax.map(
        attend_sequence,
        (
            per_sequence(queries),
            per_sequence(key_rows),
            per_sequence(value_rows),
            segment_ids,
            context_flags,
        ),
    )
    mixture = mixture.reshape(row_count, local_cols)
    partial_out = jnp.dot(mixture, out_weight, preferred_element_type=jnp.float32)
    grad_rows_all = cotangent.reshape(row_count, width)
    grad_float_all = grad_rows_all.astype(jnp.float32)
    grad_down_bias = jnp.sum(grad_float_all, axis=0)
    attended = lax.psum(partial_out, "head") + out_bias.astype(jnp.float32)
    middle_state = flat_in + attended
    normed_two_f, norm_two_pull = jax.vjp(layer_norm, middle_state, gain_two, offset_two)
    normed_two = normed_two_f.astype(jnp.bfloat16)
    up_part, down_part, up_shift = (
        lax.all_gather(up_weight, "head", axis=1, tiled=True),
        lax.all_gather(down_weight, "head", axis=0, tiled=True),
        lax.all_gather(up_bias, "head", axis=0, tiled=True),
    )
    up_full, down_full = (
        lax.all_gather(up_part, "seq", axis=0, tiled=True),
        lax.all_gather(down_part, "seq", axis=1, tiled=True),
    )
    before = jnp.dot(normed_two, up_full, preferred_element_type=jnp.float32) + up_shift.astype(
        jnp.float32
    )
    active_f, gelu_pull = jax.vjp(gelu_exact, before)
    active = active_f.astype(jnp.bfloat16)
    branch_out = jnp.dot(active, down_full, preferred_element_type=jnp.float32)
    final_rows = (middle_state + branch_out + down_bias.astype(jnp.float32)).astype(jnp.bfloat16)
    output = final_rows.reshape(tokens.shape)
    grad_float = grad_rows_all.astype(jnp.float32)
    grad_down = dot_cols(active, grad_rows_all)
    grad_active = dot_rows(grad_rows_all, down_full)
    (grad_before_f,) = gelu_pull(grad_active)
    grad_before = grad_before_f.astype(jnp.bfloat16)
    grad_up = dot_cols(normed_two, grad_before)
    grad_up_bias = jnp.sum(grad_before.astype(jnp.float32), axis=0)
    grad_normed_two = dot_rows(grad_before, up_full)
    grad_middle_norm, grad_gain_two, grad_offset_two = norm_two_pull(grad_normed_two)
    grad_middle = grad_float + grad_middle_norm
    ff_part = up_weight.shape[1]
    start_col = lax.axis_index("head") * ff_part
    grad_up = lax.dynamic_slice_in_dim(grad_up, start_col, ff_part, 1)
    grad_down = lax.dynamic_slice_in_dim(grad_down, start_col, ff_part, 0)
    grad_up_bias = lax.dynamic_slice_in_dim(grad_up_bias, start_col, ff_part, 0)
    grad_attended = grad_middle.astype(jnp.bfloat16)
    grad_out_bias = jnp.sum(grad_attended.astype(jnp.float32), axis=0)
    grad_out = dot_cols(mixture, grad_attended)
    grad_mixture = dot_rows(grad_attended, out_weight).astype(jnp.bfloat16)

    def back_sequence(member):
        seq_query, seq_keys, seq_values, seq_grad, seq_logs, seq_segments, seq_context = member

        def back_block(carry, portion):
            key_acc, value_acc = carry
            block_query, block_grad, block_logs, block_segments = portion
            scores = masked_scores(
                block_query, seq_keys, block_segments, seq_segments, seq_context, factor
            )
            soft_weights = jnp.exp(scores - block_logs)
            value_acc = value_acc + jnp.einsum(
                "hqk,qhd->khd",
                soft_weights.astype(jnp.bfloat16),
                block_grad,
                preferred_element_type=jnp.float32,
            )
            grad_soft = jnp.einsum(
                "qhd,khd->hqk", block_grad, seq_values, preferred_element_type=jnp.float32
            )
            row_inner = jnp.sum(soft_weights * grad_soft, axis=-1, keepdims=True)
            grad_scores = (soft_weights * (grad_soft - row_inner)).astype(jnp.bfloat16)
            grad_query = (
                jnp.einsum(
                    "hqk,khd->qhd", grad_scores, seq_keys, preferred_element_type=jnp.float32
                )
                * factor
            )
            key_acc = (
                key_acc
                + jnp.einsum(
                    "hqk,qhd->khd", grad_scores, block_query, preferred_element_type=jnp.float32
                )
                * factor
            )
            return ((key_acc, value_acc), grad_query)

        empty = jnp.zeros((length, head_count, HEAD_DIM), jnp.float32)
        (key_acc, value_acc), grad_query = lax.scan(
            back_block,
            (empty, empty),
            (
                seq_query.reshape(blocks, block, head_count, HEAD_DIM),
                seq_grad.reshape(blocks, block, head_count, HEAD_DIM),
                seq_logs,
                seq_segments.reshape(blocks, block),
            ),
        )
        return (grad_query, key_acc, value_acc)

    grad_queries, grad_keys, grad_values = lax.map(
        back_sequence,
        (
            per_sequence(queries),
            per_sequence(key_rows),
            per_sequence(value_rows),
            per_sequence(grad_mixture),
            log_totals,
            segment_ids,
            context_flags,
        ),
    )
    grad_queries = grad_queries.reshape(row_count, local_cols).astype(jnp.bfloat16)
    grad_keys = grad_keys.reshape(row_count, local_cols).astype(jnp.bfloat16)
    grad_values = grad_values.reshape(row_count, local_cols).astype(jnp.bfloat16)
    grad_qv_bias = jnp.stack(
        [
            jnp.sum(grad_queries.astype(jnp.float32), axis=0),
            jnp.sum(grad_values.astype(jnp.float32), axis=0),
        ]
    )
    grad_qkv = jnp.stack(
        [dot_cols(normed, grad_queries), dot_cols(normed, grad_keys), dot_cols(normed, grad_values)]
    )
    grad_normed = (
        dot_rows(grad_queries, qkv_weight[0])
        + dot_rows(grad_keys, qkv_weight[1])
        + dot_rows(grad_values, qkv_weight[2])
    )
    grad_normed = lax.psum(grad_normed, "head")
    grad_input_norm, grad_gain_one, grad_offset_one = norm_one_pull(grad_normed)
    tokens_grad = (grad_middle + grad_input_norm).astype(jnp.bfloat16).reshape(tokens.shape)
    summed_qkv, summed_out, summed_up, summed_down = (
        lax.psum_scatter(
            grad_qkv.astype(jnp.bfloat16), "seq", scatter_dimension=1, tiled=True
        ).astype(jnp.float32),
        lax.psum_scatter(
            grad_out.astype(jnp.bfloat16), "seq", scatter_dimension=1, tiled=True
        ).astype(jnp.float32),
        lax.psum_scatter(
            grad_up.astype(jnp.bfloat16), "seq", scatter_dimension=0, tiled=True
        ).astype(jnp.float32),
        lax.psum_scatter(
            grad_down.astype(jnp.bfloat16), "seq", scatter_dimension=1, tiled=True
        ).astype(jnp.float32),
    )
    smalls = lax.psum(
        (
            grad_gain_one,
            grad_offset_one,
            grad_qv_bias,
            grad_out_bias,
            grad_gain_two,
            grad_offset_two,
            grad_up_bias,
            grad_down_bias,
        ),
        "seq",
    )
    return (
        output,
        tokens_grad,
        smalls[0],
        smalls[1],
        summed_qkv,
        smalls[2],
        summed_out,
        smalls[3],
        smalls[4],
        smalls[5],
        summed_up,
        smalls[6],
        summed_down,
        smalls[7],
    )


MESH = pl.DeviceIdType.MESH
BF = jnp.bfloat16
F32 = jnp.float32
BLOCK = 256
STRIP = 512
PIECE = 128
WIDE = 1024
GROUP = 2
CHUNK = 512
PAIR = 2 * HEAD_DIM
Z_SIZE, Y_SIZE, CORES = 4, 2, 2
SEQ_SIZE = Z_SIZE * Y_SIZE * CORES
HOP = Y_SIZE * CORES
TABLES = 8
FAR = -1e30
VMEM_LIMIT = 62 * 2**20
INV_ROOT_TWO = 0.7071067811865476
INV_ROOT_TWO_PI = 0.3989422804014327
LN1_GAIN, LN1_BIAS, QV_BIAS, OUT_BIAS, LN2_GAIN, LN2_BIAS, UP_BIAS, DOWN_BIAS = 0, 1, 2, 3, 4, 5, 6, 8
SMALL_ROWS = 16
VMEM_SPEC = pl.BlockSpec(memory_space=pltpu.VMEM)
ANY_SPEC = pl.BlockSpec(memory_space=pl.ANY)


def shape_of(dims, dtype):
    return jax.ShapeDtypeStruct(tuple(dims), dtype)


def nn(left, right):
    return jnp.dot(left, right, preferred_element_type=F32)


def turn(block):
    return jnp.transpose(block)


def sum_rows(block):
    return jnp.sum(block, axis=0, keepdims=True)


def place():
    me = lax.axis_index("seq")
    head = lax.axis_index("head")
    core = me % 2
    y = (me // 2) % 2
    across = {"seq": me, "head": 1 - head}
    core_mate = {"seq": me + 1 - 2 * core, "head": head}
    y_mate = {"seq": me + 2 - 4 * y, "head": head}
    z_mates = [{"seq": (me + HOP * d) % SEQ_SIZE, "head": head} for d in (1, 2, 3)]
    return me, head, core, y, across, core_mate, y_mate, z_mates


def greet(others):
    barrier = pltpu.get_barrier_semaphore()
    for other in others:
        pl.semaphore_signal(barrier, inc=1, device_id=other, device_id_type=MESH)
    pl.semaphore_wait(barrier, len(others))


def remote(src, dst, send_sem, recv_sem, other):
    return pltpu.make_async_remote_copy(
        src_ref=src, dst_ref=dst, send_sem=send_sem, recv_sem=recv_sem,
        device_id=other, device_id_type=MESH,
    )


def norm_stats(rows):
    middle = jnp.mean(rows, axis=-1, keepdims=True)
    centred = rows - middle
    spread = jnp.mean(centred * centred, axis=-1, keepdims=True)
    return centred, lax.rsqrt(spread + 1e-05)


def norm_back(inner, unit, scale):
    return scale * (
        inner
        - jnp.mean(inner, axis=-1, keepdims=True)
        - unit * jnp.mean(inner * unit, axis=-1, keepdims=True)
    )


def as_row(vector):
    return vector[...].astype(F32).reshape(1, -1)


def lanes():
    return lax.broadcasted_iota(jnp.int32, (1, PAIR), 1)


def in_pieces(column, first, rest):
    high = column.astype(BF).astype(F32)
    mid = (column - high).astype(BF).astype(F32)
    low = column - high - mid
    at = lanes()
    return jnp.where(
        at == first, high, jnp.where(at == first + 1, mid, jnp.where(at == first + 2, low, rest))
    ).astype(BF)


def one_lanes(length):
    return jnp.broadcast_to(jnp.where(lanes() < 3, 1.0, 0.0).astype(BF), (length, PAIR))


def fwd_kernel(
    x_ref, seg_ref, context, gain, offset, qv_bias, out_bias, gain_two, offset_two, up_bias,
    wqkv, wout, up_shard, down_shard,
    q_out, k_out, v_out, mix_out, mid_out, normed_out, wff_out, key_out, query_out,
    normed_two_out, active_out, slope_out,
    wff, q_ref, k_ref, v_ref, mix_ref, mid_ref, normed_t, key_more, query_more,
    normed_two_t, active, slope, bias_row, mask_more, wout_x, mix_x,
    zs, zr, ys, yr, cs, cr, xs, xr, local, outs,
):
    length, width = x_ref.shape
    blocks = length // BLOCK
    pairs = q_ref.shape[0]
    cols = pairs * PAIR
    me, head, core, y, across, core_mate, y_mate, _ = place()
    z = me // HOP
    above = {"seq": (me + HOP) % SEQ_SIZE, "head": head}
    below = {"seq": (me + SEQ_SIZE - HOP) % SEQ_SIZE, "head": head}
    own = [
        pltpu.make_async_copy(shard, wff.at[u, me], local.at[u])
        for u, shard in enumerate((up_shard, down_shard))
    ]
    own[0].start()
    own[1].start()
    greet([across, core_mate, y_mate, above, below])

    out_copy = remote(wout, wout_x, xs.at[0], xr.at[0], across)
    out_copy.start()

    flows = [(0, 0)] + [(way, s) for s in (1, 2, 3) for way in (0, 1)]

    def there(way, s):
        return (z >= s) if way == 0 else (z + s < Z_SIZE)

    def source(base, way, s):
        away = SEQ_SIZE - HOP * s if way == 0 else HOP * s
        return (base + away) % SEQ_SIZE

    def z_copy(u, way, s):
        n = (u * 2 + way) * 3 + s - 1
        j = source(me, way, s - 1)
        return remote(wff.at[u, j], wff.at[u, j], zs.at[n], zr.at[n], above if way == 0 else below)

    def z_arrival(u, way, s):
        n = (u * 2 + way) * 3 + s - 1
        slot = wff.at[u, source(me, way, s)]
        return remote(slot, slot, zs.at[n], zr.at[n], above)

    def z_goes_on(way):
        return (z < Z_SIZE - 1) if way == 0 else (z > 0)

    def y_copy(u, f):
        n = u * 7 + f
        j = source(me, *flows[f])
        return remote(wff.at[u, j], wff.at[u, j], ys.at[n], yr.at[n], y_mate)

    def y_arrival(u, f):
        n = u * 7 + f
        slot = wff.at[u, source(me + 2 - 4 * y, *flows[f])]
        return remote(slot, slot, ys.at[n], yr.at[n], y_mate)

    def c_copy(u, f, from_y):
        n = (u * 2 + from_y) * 7 + f
        j = source(me + from_y * (2 - 4 * y), *flows[f])
        return remote(wff.at[u, j], wff.at[u, j], cs.at[n], cr.at[n], core_mate)

    def c_arrival(u, f, from_y):
        n = (u * 2 + from_y) * 7 + f
        slot = wff.at[u, source(me + 1 - 2 * core + from_y * (2 - 4 * y), *flows[f])]
        return remote(slot, slot, cs.at[n], cr.at[n], core_mate)

    def for_flow(f, do):
        if f == 0:
            do()
        else:
            pl.when(there(*flows[f]))(do)

    def for_step(s, do):
        for f, (way, step) in enumerate(flows):
            if step == s:
                for_flow(f, lambda f=f, way=way: do(f, way))

    def z_event(u, s):
        def one(f, way):
            z_arrival(u, way, s).wait_recv()
            if s < 3:
                pl.when(z_goes_on(way))(lambda: z_copy(u, way, s + 1).start())
            y_copy(u, f).start()
            c_copy(u, f, 0).start()
        for_step(s, one)
        if u == 0 and s == 1:
            start_z(1)
        if u == 0 and s == 2:
            y_copy(1, 0).start()
            c_copy(1, 0, 0).start()

    def y_event(u, s):
        def one(f, way):
            y_arrival(u, f).wait_recv()
            c_copy(u, f, 1).start()
        for_step(s, one)

    def start_z(u):
        for way in (0, 1):
            pl.when(z_goes_on(way))(lambda way=way: z_copy(u, way, 1).start())

    own[0].wait()
    start_z(0)
    y_copy(0, 0).start()
    c_copy(0, 0, 0).start()
    own[1].wait()

    plan = {
        2: [(z_event, 0, 1), (y_event, 0, 0)], 4: [(z_event, 0, 2)], 6: [(y_event, 0, 1)],
        7: [(z_event, 0, 3)], 8: [(z_event, 1, 1)], 9: [(y_event, 0, 2), (y_event, 1, 0)],
        10: [(z_event, 1, 2)], 11: [(y_event, 0, 3)],
    }

    def tick(t):
        for step, events in plan.items():
            @pl.when(t == step)
            def _(events=events):
                for event, u, s in events:
                    event(u, s)

    at = lax.broadcasted_iota(jnp.int32, (PAIR, length), 0)
    same = at == seg_ref[...]
    hidden = context[...] != 1
    ones = jnp.logical_and(at > TABLES, at < TABLES + 4)
    key_side = jnp.logical_or(
        jnp.logical_and(at < TABLES, same),
        jnp.logical_or(jnp.logical_and(at == TABLES, hidden), ones),
    )
    query_side = jnp.logical_and(at <= TABLES, jnp.logical_not(same))
    key_more[...] = turn(jnp.where(key_side, 1.0, 0.0)).astype(BF)
    mask_more[...] = turn(jnp.where(query_side, FAR, 0.0)).astype(BF)

    keep = [
        pltpu.make_async_copy(here, there, outs.at[n])
        for n, (here, there) in enumerate(
            (
                (q_ref, q_out), (k_ref, k_out), (v_ref, v_out), (normed_t, normed_out),
                (key_more, key_out), (query_more, query_out), (mix_ref, mix_out),
            )
        )
    ]
    gains, offsets = as_row(gain), as_row(offset)
    query_bias = qv_bias[0:1, :].astype(F32)
    value_bias = qv_bias[1:2, :].astype(F32)

    def project(b, _):
        rows = pl.ds(pl.multiple_of(b * BLOCK, BLOCK), BLOCK)
        centred, scale = norm_stats(x_ref[rows, :].astype(F32))
        block = (centred * scale * gains + offsets).astype(BF)
        normed_t[b] = turn(block)
        queries = ((nn(block, wqkv[0]) + query_bias).astype(BF) * 0.125).astype(BF)
        keys = nn(block, wqkv[1]).astype(BF)
        values = (nn(block, wqkv[2]) + value_bias).astype(BF)
        for p in range(pairs):
            part = slice(p * PAIR, (p + 1) * PAIR)
            q_ref[p, rows, :] = queries[:, part]
            k_ref[p, rows, :] = keys[:, part]
            v_ref[p, rows, :] = values[:, part]
        tick(b)
        return 0

    lax.fori_loop(0, blocks, project, 0)
    for n in range(5):
        keep[n].start()

    low_lanes = lanes() < HEAD_DIM
    zero = jnp.zeros((1, PAIR), BF)

    def mixture_copy(b):
        rows = pl.ds(pl.multiple_of(b * BLOCK, BLOCK), BLOCK)
        return remote(
            mix_ref.at[:, rows, :], mix_x.at[:, rows, :], xs.at[1 + b], xr.at[1 + b], across
        )

    per_step = STRIP // BLOCK

    def attend(t, _):
        b, p = t // pairs, t % pairs
        keys = jnp.concatenate([k_ref[p], key_more[...]], axis=1)
        values = jnp.concatenate([v_ref[p], one_lanes(length)], axis=1)
        chains = []
        for n in range(per_step):
            rows = pl.ds(pl.multiple_of(b * STRIP + n * BLOCK, BLOCK), BLOCK)
            queries, more = q_ref[p, rows, :], mask_more[rows, :]
            for low in (0, 1):
                own_lanes = jnp.logical_not(low_lanes) if low else low_lanes
                left = jnp.concatenate([jnp.where(own_lanes, queries, zero), more], axis=1)
                chains.append((rows, low, more, dot_rows(left, keys)))
        parts = []
        for rows, low, more, scores in chains:
            top = jnp.max(scores, axis=-1, keepdims=True)
            mixed = nn(jnp.exp(scores - top).astype(BF), values)
            total = mixed[:, PAIR:PAIR + 1]
            parts.append(mixed[:, :PAIR] / total)
            query_more[2 * p + low, rows, :] = in_pieces(
                -(top + jnp.log(total)), TABLES + 1, more.astype(F32)
            )
            if low:
                mix_ref[p, rows, :] = jnp.where(low_lanes, *parts[-2:]).astype(BF)
        tick(t + blocks)

        @pl.when(p == pairs - 1)
        def _():
            for n in range(per_step):
                mixture_copy(b * per_step + n).start()

        return 0

    lax.fori_loop(0, length // STRIP * pairs, attend, 0)
    keep[5].start()
    keep[6].start()
    out_copy.wait_recv()
    out_row = as_row(out_bias)

    def mid_copy(b):
        rows = pl.ds(b * BLOCK, BLOCK)
        return pltpu.make_async_copy(mid_ref.at[rows, :], mid_out.at[rows, :], outs.at[7 + b])

    gains_two, offsets_two = as_row(gain_two), as_row(offset_two)
    bias_row[...] = as_row(up_bias)

    def half_copies(b):
        rows = pl.ds(b * BLOCK, BLOCK)
        return [
            pltpu.make_async_copy(
                here.at[:, rows, :], there.at[:, rows, :], outs.at[7 + blocks + 2 * b + n]
            )
            for n, (here, there) in enumerate(((active, active_out), (slope, slope_out)))
        ]

    def up_half(b):
        rows = pl.ds(b * BLOCK, BLOCK)
        centred, scale = norm_stats(mid_ref[rows, :])
        block = (centred * scale * gains_two + offsets_two).astype(BF)
        normed_two_t[:, rows] = turn(block)

        def one(n, _):
            cut = pl.ds(pl.multiple_of(n * WIDE, WIDE), WIDE)
            before = nn(block, wff[0, :, :, cut].reshape(width, WIDE)) + bias_row[:, cut]
            spread = 0.5 * (1.0 + lax.erf(before * INV_ROOT_TWO))
            active[n, rows, :] = (before * spread).astype(BF)
            bell = INV_ROOT_TWO_PI * jnp.exp(before * before * -0.5)
            slope[n, rows, :] = (spread + before * bell).astype(BF)
            return 0

        lax.fori_loop(0, active.shape[0], one, 0)
        for copy in half_copies(b):
            copy.start()

    def arrive(u):
        for f in range(len(flows)):
            def one(f=f):
                for from_y in (0, 1):
                    c_arrival(u, f, from_y).wait_recv()
            for_flow(f, one)

    for b in range(blocks):
        mixture_copy(b).wait_recv()
        rows = pl.ds(b * BLOCK, BLOCK)
        ours = jnp.concatenate([mix_ref[p, rows, :] for p in range(pairs)], axis=-1)
        other = jnp.concatenate([mix_x[p, rows, :] for p in range(pairs)], axis=-1)
        attended = nn(ours, wout[...]) + nn(other, wout_x[...])
        mid_ref[rows, :] = x_ref[rows, :].astype(F32) + (attended + out_row)
        mid_copy(b).start()
        if b == 0:
            z_event(1, 3)
            arrive(0)
        up_half(b)
        if b < 3:
            y_event(1, b + 1)
    normed_two_keep = pltpu.make_async_copy(
        normed_two_t, normed_two_out, outs.at[7 + 3 * blocks]
    )
    normed_two_keep.start()
    wff_keep = [pltpu.make_async_copy(wff.at[u], wff_out.at[u], local.at[u]) for u in range(2)]
    wff_keep[0].start()
    arrive(1)
    wff_keep[1].start()
    out_copy.wait_send()
    for copy in keep + wff_keep + [normed_two_keep]:
        copy.wait()
    for b in range(blocks):
        for copy in half_copies(b):
            copy.wait()
    for b in range(blocks):
        mixture_copy(b).wait_send()
        mid_copy(b).wait()
    for u in range(2):
        for way in (0, 1):
            pl.when(z_goes_on(way))(lambda u=u, way=way: z_copy(u, way, 1).wait_send())
        for f, (way, s) in enumerate(flows):
            def finish(u=u, f=f, way=way, s=s):
                if f and s < 3:
                    pl.when(z_goes_on(way))(lambda: z_copy(u, way, s + 1).wait_send())
                y_copy(u, f).wait_send()
                for from_y in (0, 1):
                    c_copy(u, f, from_y).wait_send()
            for_flow(f, finish)


def run_fwd(
    x, seg, context, gain, offset, qv_bias, out_bias, gain_two, offset_two, up_bias, wqkv, wout,
    up_weight, down_t,
):
    length, width = x.shape
    pairs = wqkv.shape[2] // PAIR
    blocks = length // BLOCK
    depth, hidden = up_weight.shape
    by_pair, by_head = (pairs, length, PAIR), (2 * pairs, length, PAIR)
    turned = (blocks, width, BLOCK)
    halves = (hidden // WIDE, length, WIDE)
    dma = pltpu.SemaphoreType.DMA
    return pl.pallas_call(
        fwd_kernel,
        out_shape=[shape_of(by_pair, BF)] * 4 + [
            shape_of((length, width), F32),
            shape_of(turned, BF),
            shape_of((2, SEQ_SIZE, depth, hidden), BF),
            shape_of((length, PAIR), BF),
            shape_of(by_head, BF),
            shape_of((width, length), BF),
            shape_of(halves, BF),
            shape_of(halves, BF),
        ],
        in_specs=[VMEM_SPEC] * 12 + [ANY_SPEC] * 2,
        out_specs=[ANY_SPEC] * 12,
        scratch_shapes=[pltpu.VMEM((2, SEQ_SIZE, depth, hidden), BF)]
        + [pltpu.VMEM(by_pair, BF)] * 4 + [
            pltpu.VMEM((length, width), F32),
            pltpu.VMEM(turned, BF),
            pltpu.VMEM((length, PAIR), BF),
            pltpu.VMEM(by_head, BF),
            pltpu.VMEM((width, length), BF),
            pltpu.VMEM(halves, BF),
            pltpu.VMEM(halves, BF),
            pltpu.VMEM((1, hidden), F32),
            pltpu.VMEM((length, PAIR), BF),
            pltpu.VMEM(wout.shape, BF),
            pltpu.VMEM(by_pair, BF),
            dma((12,)), dma((12,)), dma((14,)), dma((14,)), dma((28,)), dma((28,)),
            dma((1 + blocks,)), dma((1 + blocks,)), dma((2,)), dma((8 + 3 * blocks,)),
        ],
        compiler_params=pltpu.CompilerParams(
            collective_id=0, has_side_effects=True, vmem_limit_bytes=VMEM_LIMIT
        ),
    )(
        x, seg, context, gain, offset, qv_bias, out_bias, gain_two, offset_two, up_bias, wqkv,
        wout, up_weight, down_t,
    )


def ff_kernel(
    mid_hbm, dy_hbm, wff_hbm, normed_two_hbm, active_hbm, slope_hbm, gain, wout_hbm,
    branch_out, gmid_hbm, ga_out, gm_out, summed, small_ref,
    dy_ref, wff, wout, branch_ref, ga_t, gm_ref, normed_t, dy_t, active, before_grad, gnt_acc, gnt_own, gnt_x, whole, from_mate,
    held, ready,
    xs, xr, cs, cr, ls, ws, ss, ins, outs,
):
    length, width = dy_ref.shape
    blocks = length // BLOCK
    hidden = wff.shape[3]
    half = hidden // WIDE
    chunks = 2 * hidden // CHUNK
    pairs = gm_ref.shape[0]
    me, head, core, y, across, core_mate, y_mate, z_mates = place()
    dy_load = pltpu.make_async_copy(dy_hbm, dy_ref, ins.at[0])
    wout_load = pltpu.make_async_copy(wout_hbm, wout, ins.at[1])

    def step_loads(n):
        cut = pl.ds(n * WIDE, WIDE)
        return [
            pltpu.make_async_copy(src, dst, ins.at[4 + 3 * n + m])
            for m, (src, dst) in enumerate(
                (
                    (wff_hbm.at[1, :, :, cut], wff.at[1, :, :, cut]),
                    (slope_hbm.at[n], before_grad.at[n]),
                    (wff_hbm.at[0, :, :, cut], wff.at[0, :, :, cut]),
                )
            )
        ]

    active_load = pltpu.make_async_copy(active_hbm, active, ins.at[2])
    normed_load = pltpu.make_async_copy(normed_two_hbm, normed_t, ins.at[3])
    dy_load.start()
    for n in range(half):
        for copy in step_loads(n):
            copy.start()
    active_load.start()
    normed_load.start()
    wout_load.start()
    greet([across, core_mate])
    gains = as_row(gain)

    def weight(kind, n):
        cut = pl.ds(pl.multiple_of(n * WIDE, WIDE), WIDE)
        return wff[kind, :, :, cut].reshape(width, WIDE)

    small_ref[...] = jnp.zeros_like(small_ref)

    def load(b):
        rows = pl.ds(b * BLOCK, BLOCK)
        return pltpu.make_async_copy(mid_hbm.at[rows, :], held.at[b % 2], ls.at[b % 2])

    def store(b):
        rows = pl.ds(b * BLOCK, BLOCK)
        return pltpu.make_async_copy(ready.at[b % 2], gmid_hbm.at[rows, :], ws.at[b % 2])

    load(0).start()
    load(1).start()

    def gnt_copy(b):
        return remote(gnt_own.at[b], gnt_x.at[b], xs.at[b], xr.at[b], across)

    def core_copy(n):
        return remote(
            whole.at[n, :, :, 1 - core], from_mate.at[n], cs.at[n], cr.at[n], core_mate
        )

    def forward(t, _):
        b, n = t // half, t % half
        rows = pl.ds(pl.multiple_of(b * BLOCK, BLOCK), BLOCK)

        for n_first in range(half):
            @pl.when(t == n_first)
            def _(n_first=n_first):
                if n_first == 0:
                    dy_load.wait()
                for copy in step_loads(n_first):
                    copy.wait()

        @pl.when(n == 0)
        def _():
            dy_t[:, rows] = turn(dy_ref[rows, :])
            small_ref[DOWN_BIAS:DOWN_BIAS + 1, :] += sum_rows(dy_ref[rows, :].astype(F32))

        up = weight(0, n)
        grad = nn(dy_ref[rows, :], weight(1, n)) * before_grad[n, rows, :].astype(F32)
        grad = grad.astype(BF)
        before_grad[n, rows, :] = grad
        small_ref[pl.ds(UP_BIAS + n, 1), :] += sum_rows(grad.astype(F32))
        back = dot_rows(grad, up)

        @pl.when(n == 0)
        def _():
            gnt_acc[...] = back

        @pl.when(n > 0)
        def _():
            gnt_acc[...] += back

        for b_done in range(blocks):
            @pl.when(t == (b_done + 1) * half - 1)
            def _(b_done=b_done):
                gnt_own[b_done] = gnt_acc[...].astype(BF)
                gnt_copy(b_done).start()
        return 0

    lax.fori_loop(0, blocks * half, forward, 0)

    def weight_grads(left_t, right, first):
        cut_rows = width // Z_SIZE
        per_wide = WIDE // CHUNK

        def one(t, _):
            n, plane = t // Z_SIZE, t % Z_SIZE
            cut = pl.ds(pl.multiple_of(plane * cut_rows, cut_rows), cut_rows)
            total = nn(left_t[cut, :], right[n]).astype(BF)
            for m in range(per_wide):
                piece = total[:, m * CHUNK:(m + 1) * CHUNK]
                whole[first + n * per_wide + m, plane] = piece.reshape(whole.shape[2:])

            @pl.when(plane == Z_SIZE - 1)
            def _():
                for m in range(per_wide):
                    core_copy(first + n * per_wide + m).start()

            return 0

        lax.fori_loop(0, Z_SIZE * half, one, 0)

    active_load.wait()
    normed_load.wait()
    weight_grads(dy_t, active, chunks // 2)
    weight_grads(normed_t, before_grad, 0)

    def branch(b, _):
        rows = pl.ds(pl.multiple_of(b * BLOCK, BLOCK), BLOCK)
        total = dot_rows(active[0, rows, :], weight(1, 0))
        for n in range(1, half):
            total += dot_rows(active[n, rows, :], weight(1, n))
        branch_ref[rows, :] = total.astype(BF)
        return 0

    lax.fori_loop(0, blocks, branch, 0)
    branch_keep = pltpu.make_async_copy(branch_ref, branch_out, outs.at[0])
    branch_keep.start()
    wout_load.wait()

    def ga_copy(b):
        return pltpu.make_async_copy(ga_t.at[b], ga_out.at[b], outs.at[1 + b])

    def gm_copy(b):
        rows = pl.ds(b * BLOCK, BLOCK)
        return pltpu.make_async_copy(
            gm_ref.at[:, rows, :], gm_out.at[:, rows, :], outs.at[1 + blocks + b]
        )


    def add_mate(n, _):
        core_copy(n).wait()
        both = whole[n, :, :, core].astype(F32) + from_mate[n].astype(F32)
        from_mate[n] = both.astype(BF)
        return 0

    lax.fori_loop(chunks // 2, chunks, add_mate, 0)
    lax.fori_loop(0, chunks // 2, add_mate, 0)
    keep = pltpu.make_async_copy(from_mate, summed, ss.at[0])
    keep.start()

    strips = BLOCK // PIECE
    for b in range(blocks):
        gnt_copy(b).wait()
        load(b).wait()
        if b >= 2:
            store(b - 2).wait()

        def through_norm(n, _, b=b):
            rows = pl.ds(pl.multiple_of(n * PIECE, PIECE), PIECE)
            full = pl.ds(pl.multiple_of(b * BLOCK + n * PIECE, PIECE), PIECE)
            grad = gnt_own[b, rows, :].astype(F32) + gnt_x[b, rows, :].astype(F32)
            centred, scale = norm_stats(held[b % 2, rows, :])
            unit = centred * scale
            small_ref[LN2_GAIN:LN2_GAIN + 1, :] += sum_rows(grad * unit)
            small_ref[LN2_BIAS:LN2_BIAS + 1, :] += sum_rows(grad)
            total = dy_ref[full, :].astype(F32) + norm_back(grad * gains, unit, scale)
            ready[b % 2, rows, :] = total
            low = total.astype(BF)
            small_ref[OUT_BIAS:OUT_BIAS + 1, :] += sum_rows(low.astype(F32))
            ga_t[b, :, rows] = turn(low)
            mixed = dot_rows(low, wout[...]).astype(BF)
            for p in range(pairs):
                gm_ref[p, full, :] = mixed[:, p * PAIR:(p + 1) * PAIR]
            return 0

        lax.fori_loop(0, strips, through_norm, 0)
        store(b).start()
        ga_copy(b).start()
        gm_copy(b).start()
        if b + 2 < blocks:
            load(b + 2).start()
    store(blocks - 2).wait()
    store(blocks - 1).wait()
    for b in range(blocks):
        ga_copy(b).wait()
        gm_copy(b).wait()
    branch_keep.wait()
    keep.wait()


def run_ff(middle, dy, wff, normed_two_t, active, slope, gain, wout):
    length, width = middle.shape
    half = wff.shape[3] // WIDE
    chunks = 2 * wff.shape[3] // CHUNK
    blocks = length // BLOCK
    pairs = wout.shape[0] // PAIR
    depth = width // SEQ_SIZE
    dma = pltpu.SemaphoreType.DMA
    turned = pltpu.VMEM((blocks, width, BLOCK), BF)
    rows = pltpu.VMEM((blocks, BLOCK, width), BF)
    hidden = pltpu.VMEM((half, length, WIDE), BF)
    flat_t = pltpu.VMEM((width, length), BF)
    return pl.pallas_call(
        ff_kernel,
        out_shape=[
            shape_of((length, width), BF),
            shape_of((length, width), F32),
            shape_of((blocks, width, BLOCK), BF),
            shape_of((pairs, length, PAIR), BF),
            shape_of((chunks, Z_SIZE, Y_SIZE, depth, CHUNK), BF),
            shape_of((SMALL_ROWS, width), F32),
        ],
        in_specs=[ANY_SPEC] * 6 + [VMEM_SPEC, ANY_SPEC],
        out_specs=[ANY_SPEC] * 5 + [VMEM_SPEC],
        scratch_shapes=[
            pltpu.VMEM((length, width), BF), pltpu.VMEM(wff.shape, BF),
            pltpu.VMEM(wout.shape, BF),
            pltpu.VMEM((length, width), BF), turned, pltpu.VMEM((pairs, length, PAIR), BF),
            flat_t, flat_t, hidden, hidden,
            pltpu.VMEM((BLOCK, width), F32), rows, rows,
            pltpu.VMEM((chunks, Z_SIZE, Y_SIZE, CORES, depth, CHUNK), BF),
            pltpu.VMEM((chunks, Z_SIZE, Y_SIZE, depth, CHUNK), BF),
            pltpu.VMEM((2, BLOCK, width), F32), pltpu.VMEM((2, BLOCK, width), F32),
            dma((blocks,)), dma((blocks,)), dma((chunks,)), dma((chunks,)),
            dma((2,)), dma((2,)), dma((1,)), dma((4 + 3 * half,)), dma((1 + 2 * blocks,)),
        ],
        compiler_params=pltpu.CompilerParams(
            collective_id=1, has_side_effects=True, vmem_limit_bytes=VMEM_LIMIT
        ),
    )(middle, dy, wff, normed_two_t, active, slope, gain, wout)


def back_kernel(
    q_hbm, k_hbm, v_hbm, mix_hbm, gm_hbm, query_hbm, ga_hbm, normed_hbm, wqkv_hbm, x_hbm,
    key_more, gain, down_bias, small_in, mid_hbm, gmid_hbm, ff_part, branch,
    out_hbm, tokens_hbm, qkv_sum, out_sum, up_sum, down_sum,
    gain_one, offset_one, qv_small, out_small, gain_two, offset_two, up_small, down_small,
    q_ref, k_ref, v_ref, mix_ref, gm_ref, query_more, ga_t, normed_t, wqkv, x_ref,
    out_ref, tokens_ref, key_t, key_acc, value_acc, dq, dk, dv, whole, mate, at_y, at_z, ff_y, ff_z, gn_own, gn_x,
    branch_x, branch_own, ff_own, held, small_own, small_z, small_y, small_c,
    bs, br, fys, fyr, fzs, fzr, acs, acr, ays, ayr, azs, azr, gs, gr, ls, ms, mr, os, hs, ins, more_ins, outs,
):
    length, width = x_ref.shape
    blocks = length // BLOCK
    strips = length // STRIP
    pairs = q_ref.shape[0]
    chunks = ff_part.shape[0]
    half = chunks // 2
    groups = chunks // GROUP
    me, head, core, y, across, core_mate, y_mate, z_mates = place()
    z = me // (Y_SIZE * CORES)
    by_pair = (
        (q_hbm, q_ref), (k_hbm, k_ref), (v_hbm, v_ref), (mix_hbm, mix_ref), (gm_hbm, gm_ref),
    )

    def pair_loads(p):
        both = pl.ds(2 * p, 2)
        first = p * (len(by_pair) + 1)
        return [
            pltpu.make_async_copy(src.at[p], dst.at[p], ins.at[first + n])
            for n, (src, dst) in enumerate(by_pair)
        ] + [
            pltpu.make_async_copy(
                query_hbm.at[both], query_more.at[both], ins.at[first + len(by_pair)]
            )
        ]

    late_loads = [
        pltpu.make_async_copy(src, dst, more_ins.at[n])
        for n, (src, dst) in enumerate(
            ((ga_hbm, ga_t), (normed_hbm, normed_t), (wqkv_hbm, wqkv), (x_hbm, x_ref))
        )
    ]
    for p in range(pairs):
        for copy in pair_loads(p):
            copy.start()
        if p == 0:
            late_loads[0].start()
            late_loads[1].start()
    late_loads[2].start()
    late_loads[3].start()
    greet([across, core_mate, y_mate, *z_mates])

    def part(b):
        return pl.ds(b * BLOCK, BLOCK)

    def branch_copy(b):
        return remote(branch.at[part(b), :], branch_x.at[part(b), :], bs.at[b], br.at[b], across)

    def load(n):
        source = mid_hbm if n < blocks else gmid_hbm
        return pltpu.make_async_copy(
            source.at[part(n % blocks), :], held.at[n % 2], ls.at[n % 2]
        )

    def taken(n):
        if n + 2 < 2 * blocks:
            load(n + 2).start()

    def group(g):
        return pl.ds(g * GROUP, GROUP)

    def ff_y_copy(g):
        return remote(
            ff_part.at[group(g), :, 1 - y], ff_y.at[group(g)], fys.at[g], fyr.at[g], y_mate
        )

    def ff_z_copy(g, d):
        n = g * 3 + d - 1
        return remote(
            ff_y.at[group(g), (z + d) % Z_SIZE], ff_z.at[d - 1, group(g)],
            fzs.at[n], fzr.at[n], z_mates[d - 1],
        )

    def branch_load(b):
        return pltpu.make_async_copy(branch.at[part(b), :], branch_own.at[b % 2], hs.at[b % 2])

    def ff_load(g):
        return pltpu.make_async_copy(
            ff_part.at[group(g), :, y], ff_own.at[g % 2], os.at[g % 2]
        )

    def ff_y_event(g):
        ff_y_copy(g).wait_recv()
        ff_load(g).wait()
        for n in range(g * GROUP, (g + 1) * GROUP):
            own = ff_own[g % 2, n % GROUP]
            ff_y[n] = (ff_y[n].astype(F32) + own.astype(F32)).astype(BF)
        if g + 2 < groups:
            ff_load(g + 2).start()
            ff_y_copy(g + 2).start()
        for d in (1, 2, 3):
            ff_z_copy(g, d).start()

    def ff_z_event(g):
        for d in (1, 2, 3):
            ff_z_copy(g, d).wait_recv()
        for n in range(g * GROUP, (g + 1) * GROUP):
            total = ff_y[n, z].astype(F32)
            for d in (1, 2, 3):
                total += ff_z[d - 1, n].astype(F32)
            if n < half:
                up_sum[:, n * CHUNK:(n + 1) * CHUNK] = total
            else:
                down_sum[:, (n - half) * CHUNK:(n - half + 1) * CHUNK] = total

    def at_c_copy(p):
        return remote(whole.at[p, :, :, 1 - core], mate.at[p], acs.at[p], acr.at[p], core_mate)

    def at_y_copy(p):
        return remote(mate.at[p, :, 1 - y], at_y.at[p], ays.at[p], ayr.at[p], y_mate)

    def at_z_copy(p, d):
        n = p * 3 + d - 1
        return remote(
            at_y.at[p, (z + d) % Z_SIZE], at_z.at[d - 1, p], azs.at[n], azr.at[n], z_mates[d - 1]
        )

    def at_c_event(p):
        at_c_copy(p).wait_recv()
        mate[p] = (mate[p].astype(F32) + whole[p, :, :, core].astype(F32)).astype(BF)
        at_y_copy(p).start()

    def at_y_event(p):
        at_y_copy(p).wait_recv()
        at_y[p] = (at_y[p].astype(F32) + mate[p, :, y].astype(F32)).astype(BF)
        for d in (1, 2, 3):
            at_z_copy(p, d).start()

    def at_z_event(p):
        for d in (1, 2, 3):
            at_z_copy(p, d).wait_recv()
        total = at_y[p, z].astype(F32)
        for d in (1, 2, 3):
            total += at_z[d - 1, p].astype(F32)
        cut = slice(p * PAIR, (p + 1) * PAIR)
        for kind in range(3):
            qkv_sum[kind, :, cut] = total[:, kind * PAIR:(kind + 1) * PAIR]
        out_sum[:, cut] = total[:, 3 * PAIR:]

    def out_copy(b):
        return pltpu.make_async_copy(out_ref.at[part(b), :], out_hbm.at[part(b), :], outs.at[b])

    def tokens_copy(b):
        return pltpu.make_async_copy(
            tokens_ref.at[part(b), :], tokens_hbm.at[part(b), :], outs.at[blocks + b]
        )

    def branch_event(b):
        branch_copy(b).wait_recv()
        load(b).wait()
        branch_load(b).wait()
        both = branch_own[b % 2].astype(F32) + branch_x[part(b), :].astype(F32)
        out_ref[part(b), :] = (held[b % 2] + both + as_row(down_bias)).astype(BF)
        out_copy(b).start()
        taken(b)
        if b + 2 < blocks:
            branch_load(b + 2).start()

    for b in range(blocks):
        branch_copy(b).start()
    for n in range(2):
        load(n).start()
        branch_load(n).start()
        ff_load(n).start()
        ff_y_copy(n).start()

    plan = {
        2: [(at_c_event, 0), (ff_y_event, 0), (branch_event, 0)], 4: [(at_c_event, 1)],
        5: [(ff_y_event, 1), (branch_event, 1)], 6: [(at_c_event, 2)],
    }

    low_lanes = lanes() < HEAD_DIM
    zero = jnp.zeros((1, PAIR), BF)

    def stacked(strip):
        return jnp.concatenate(
            [jnp.where(low_lanes, strip, zero), jnp.where(low_lanes, zero, strip)], axis=0
        )

    def attend(t, _):
        p, b = t // strips, t % strips
        rows = pl.ds(pl.multiple_of(b * STRIP, STRIP), STRIP)

        @pl.when(b == 0)
        def _():
            for p_now in range(pairs):
                @pl.when(p == p_now)
                def _(p_now=p_now):
                    for copy in pair_loads(p_now):
                        copy.wait()
            key_t[...] = turn(k_ref[p])
            key_acc[...] = jnp.zeros_like(key_acc)
            value_acc[...] = jnp.zeros_like(value_acc)

        queries, grads = stacked(q_ref[p, rows, :]), stacked(gm_ref[p, rows, :])
        more = jnp.concatenate(
            [query_more[2 * p, rows, :], query_more[2 * p + 1, rows, :]], axis=0
        )
        mixture = mix_ref[p, rows, :]
        product = grads.astype(F32) * jnp.concatenate([mixture, mixture], axis=0).astype(F32)
        inner = -jnp.sum(product, axis=-1, keepdims=True)
        query_side = jnp.concatenate([queries, more], axis=1)
        grad_side = jnp.concatenate([grads, in_pieces(inner, 0, 0.0)], axis=1)
        to_queries = jnp.zeros((PAIR, 2 * STRIP), F32)
        for n in range(blocks):
            keys = jnp.concatenate([k_ref[p, part(n), :], key_more[part(n), :]], axis=1)
            values = jnp.concatenate([v_ref[p, part(n), :], one_lanes(BLOCK)], axis=1)
            weights = jnp.exp(dot_rows(keys, query_side)).astype(BF)
            grad_scores = weights * dot_rows(values, grad_side).astype(BF)
            value_acc[part(n), :] += nn(weights, grads)
            key_acc[part(n), :] += nn(grad_scores, queries)
            to_queries += nn(key_t[:, part(n)], grad_scores)
        own = jnp.concatenate(
            [to_queries[:HEAD_DIM, :STRIP], to_queries[HEAD_DIM:, STRIP:]], axis=0
        )
        dq[p, rows, :] = (turn(own) * 0.125).astype(BF)

        @pl.when(b == strips - 1)
        def _():
            @pl.when(p == 0)
            def _():
                late_loads[0].wait()
                late_loads[1].wait()

            dk[p] = key_acc[...].astype(BF)
            dv[p] = value_acc[...].astype(BF)
            total = jnp.zeros((width, 3 * PAIR), F32)
            out_total = jnp.zeros((width, PAIR), F32)
            for n in range(blocks):
                right = jnp.concatenate(
                    [dq[p, part(n), :], dk[p, part(n), :], dv[p, part(n), :]], axis=1
                )
                total += nn(normed_t[n], right)
                out_total += nn(ga_t[n], mix_ref[p, part(n), :])
            both = jnp.concatenate([total, out_total], axis=1).astype(BF)
            whole[p] = both.reshape(whole.shape[1:])
            at_c_copy(p).start()

        for step, events in plan.items():
            @pl.when(t == step)
            def _(events=events):
                for event, n in events:
                    event(n)
        return 0

    lax.fori_loop(0, pairs * strips, attend, 0)
    late_loads[2].wait()
    late_loads[3].wait()

    def gn_copy(b):
        return remote(gn_own.at[b], gn_x.at[b], gs.at[b], gr.at[b], across)

    for b in range(blocks):
        total = jnp.zeros((BLOCK, width), F32)
        for n, grad in enumerate((dq, dk, dv)):
            left = jnp.concatenate([grad[p, part(b), :] for p in range(pairs)], axis=1)
            total += dot_rows(left, wqkv[n])
        gn_own[b] = total.astype(BF)
        gn_copy(b).start()

    at_c_event(3)
    small_own[...] = small_in[...]
    for p in range(pairs):
        first, second = p * PAIR, (pairs + p) * PAIR
        small_own[QV_BIAS:QV_BIAS + 1, first:first + PAIR] = sum_rows(dq[p].astype(F32))
        small_own[QV_BIAS:QV_BIAS + 1, second:second + PAIR] = sum_rows(dv[p].astype(F32))
    branch_event(2)
    ff_y_event(2)
    branch_event(3)
    ff_z_event(0)
    ff_y_event(3)
    at_y_event(0)
    ff_z_event(1)
    gains = as_row(gain)
    for b in range(blocks):
        gn_copy(b).wait()
        load(blocks + b).wait()
        grad = gn_own[b].astype(F32) + gn_x[b].astype(F32)
        centred, scale = norm_stats(x_ref[part(b), :].astype(F32))
        unit = centred * scale
        small_own[LN1_GAIN:LN1_GAIN + 1, :] += sum_rows(grad * unit)
        small_own[LN1_BIAS:LN1_BIAS + 1, :] += sum_rows(grad)
        tokens_ref[part(b), :] = (
            held[b % 2] + norm_back(grad * gains, unit, scale)
        ).astype(BF)
        tokens_copy(b).start()
        taken(blocks + b)
        if b == 0:
            at_y_event(1)
            at_y_event(2)
            ff_z_event(2)
        if b == 1:
            at_y_event(3)
            ff_z_event(3)
        if b == 2:
            at_z_event(0)
            at_z_event(1)
            at_z_event(2)

    def small_z_copy(d):
        return remote(small_own, small_z.at[z], ms.at[d - 1], mr.at[d - 1], z_mates[d - 1])

    def small_z_arrival(d):
        slot = small_z.at[(z + Z_SIZE - d) % Z_SIZE]
        return remote(slot, slot, ms.at[d - 1], mr.at[d - 1], z_mates[d - 1])

    for d in (1, 2, 3):
        small_z_copy(d).start()
    small_z[z] = small_own[...]
    at_z_event(3)
    for d in (1, 2, 3):
        small_z_arrival(d).wait_recv()
    small_y[0] = small_z[0] + small_z[1] + small_z[2] + small_z[3]
    y_sum = remote(small_y.at[0], small_y.at[1], ms.at[3], mr.at[3], y_mate)
    y_sum.start()
    y_sum.wait()
    small_c[0] = small_y[0] + small_y[1]
    c_sum = remote(small_c.at[0], small_c.at[1], ms.at[4], mr.at[4], core_mate)
    c_sum.start()
    c_sum.wait()
    small = small_c[0] + small_c[1]
    for kind, target in (
        (LN1_GAIN, gain_one), (LN1_BIAS, offset_one), (OUT_BIAS, out_small),
        (LN2_GAIN, gain_two), (LN2_BIAS, offset_two), (DOWN_BIAS, down_small),
    ):
        target[...] = small[kind:kind + 1, :].reshape(width)
    cols = pairs * PAIR
    qv_small[0:1, :] = small[QV_BIAS:QV_BIAS + 1, :cols]
    qv_small[1:2, :] = small[QV_BIAS:QV_BIAS + 1, cols:]
    for n in range(up_small.shape[0] // width):
        row = small[UP_BIAS + n:UP_BIAS + n + 1, :]
        up_small[n * width:(n + 1) * width] = row.reshape(width)

    for d in (1, 2, 3):
        small_z_copy(d).wait_send()
    for b in range(blocks):
        out_copy(b).wait()
        tokens_copy(b).wait()
        branch_copy(b).wait_send()
    for g in range(groups):
        ff_y_copy(g).wait_send()
        for d in (1, 2, 3):
            ff_z_copy(g, d).wait_send()
    for p in range(pairs):
        at_c_copy(p).wait_send()
        at_y_copy(p).wait_send()
        for d in (1, 2, 3):
            at_z_copy(p, d).wait_send()


def run_back(
    queries, keys, values, mixture, grad_mixture, query_more, ga_t, normed_t, wqkv, x,
    key_more, gain, down_bias, small, middle, grad_middle, ff_part, branch,
):
    length, width = x.shape
    pairs = queries.shape[0]
    chunks, depth = ff_part.shape[0], ff_part.shape[3]
    groups = chunks // GROUP
    cols, hidden = pairs * PAIR, chunks // 2 * CHUNK
    blocks = length // BLOCK
    dma = pltpu.SemaphoreType.DMA
    rows = pltpu.VMEM((blocks, BLOCK, width), BF)
    by_pair = pltpu.VMEM((pairs, length, PAIR), BF)
    whole_rows = pltpu.VMEM((length, width), BF)
    row = shape_of((width,), F32)
    loaded = (
        queries, keys, values, mixture, grad_mixture, query_more, ga_t, normed_t, wqkv, x
    )
    return pl.pallas_call(
        back_kernel,
        out_shape=[
            shape_of((length, width), BF),
            shape_of((length, width), BF),
            shape_of((3, depth, cols), F32),
            shape_of((depth, cols), F32),
            shape_of((depth, hidden), F32),
            shape_of((depth, hidden), F32),
            row, row, shape_of((2, cols), F32), row, row, row, shape_of((hidden,), F32), row,
        ],
        in_specs=[ANY_SPEC] * 10 + [VMEM_SPEC] * 4 + [ANY_SPEC] * 4,
        out_specs=[ANY_SPEC] * 2 + [VMEM_SPEC] * 12,
        scratch_shapes=[pltpu.VMEM(v.shape, BF) for v in loaded] + [
            whole_rows, whole_rows, pltpu.VMEM((PAIR, length), BF),
            pltpu.VMEM((length, PAIR), F32), pltpu.VMEM((length, PAIR), F32),
            by_pair, by_pair, by_pair,
            pltpu.VMEM((pairs, Z_SIZE, Y_SIZE, CORES, depth, CHUNK), BF),
            pltpu.VMEM((pairs, Z_SIZE, Y_SIZE, depth, CHUNK), BF),
            pltpu.VMEM((pairs, Z_SIZE, depth, CHUNK), BF),
            pltpu.VMEM((3, pairs, depth, CHUNK), BF),
            pltpu.VMEM((chunks, Z_SIZE, depth, CHUNK), BF),
            pltpu.VMEM((3, chunks, depth, CHUNK), BF),
            rows, rows, whole_rows,
            pltpu.VMEM((2, BLOCK, width), BF),
            pltpu.VMEM((2, GROUP, Z_SIZE, depth, CHUNK), BF),
            pltpu.VMEM((2, BLOCK, width), F32),
            pltpu.VMEM(small.shape, F32),
            pltpu.VMEM((Z_SIZE,) + small.shape, F32),
            pltpu.VMEM((2,) + small.shape, F32),
            pltpu.VMEM((2,) + small.shape, F32),
            dma((blocks,)), dma((blocks,)), dma((groups,)), dma((groups,)),
            dma((3 * groups,)), dma((3 * groups,)), dma((pairs,)), dma((pairs,)),
            dma((pairs,)), dma((pairs,)), dma((3 * pairs,)), dma((3 * pairs,)),
            dma((blocks,)), dma((blocks,)), dma((2,)), dma((5,)), dma((5,)), dma((2,)), dma((2,)),
            dma((6 * pairs,)), dma((4,)), dma((2 * blocks,)),
        ],
        compiler_params=pltpu.CompilerParams(
            collective_id=2, has_side_effects=True, vmem_limit_bytes=VMEM_LIMIT
        ),
    )(*loaded, key_more, gain, down_bias, small, middle, grad_middle, ff_part, branch)


def hand_over_kernel(*refs):
    *refs, sems = refs
    count = len(refs) // 3
    refs = refs[:count] + refs[2 * count:] + refs[count:2 * count]
    loads, stores = (
        [
            pltpu.make_async_copy(refs[a * count + n], refs[b * count + n], sems.at[a, n])
            for n in range(count)
        ]
        for a, b in ((0, 1), (1, 2))
    )
    for load in loads:
        load.start()
    for load, store in zip(loads, stores):
        load.wait()
        store.start()
    for store in stores:
        store.wait()


def hand_over(results):
    return pl.pallas_call(
        hand_over_kernel,
        out_shape=[shape_of(v.shape, v.dtype) for v in results],
        in_specs=[ANY_SPEC] * len(results),
        out_specs=[ANY_SPEC] * len(results),
        scratch_shapes=[pltpu.VMEM(v.shape, v.dtype) for v in results] + [
            pltpu.SemaphoreType.DMA((2, len(results)))
        ],
        compiler_params=pltpu.CompilerParams(vmem_limit_bytes=VMEM_LIMIT),
    )(*results)


def fast_body(
    tokens, segment_ids, context_flags, ln1_gain, ln1_bias, qkv_weight, qv_bias, out_weight,
    out_bias, ln2_gain, ln2_bias, up_weight, up_bias, down_weight, down_bias, cotangent,
):
    x, dy = tokens[0], cotangent[0]
    (
        queries, keys, values, mixture, middle, normed_t, wff, key_more, query_more,
        normed_two_t, active, slope,
    ) = run_fwd(
        x, segment_ids, context_flags, ln1_gain, ln1_bias, qv_bias, out_bias, ln2_gain,
        ln2_bias, up_bias, qkv_weight, out_weight, up_weight, down_weight.T,
    )
    branch, grad_middle, ga_t, grad_mixture, ff_part, small = run_ff(
        middle, dy, wff, normed_two_t, active, slope, ln2_gain, out_weight
    )
    (
        output, tokens_grad, qkv_grad, out_grad, up_grad, down_grad, gain_one, offset_one,
        qv_grad, out_bias_grad, gain_two, offset_two, up_bias_grad, down_bias_grad,
    ) = hand_over(run_back(
        queries, keys, values, mixture, grad_mixture, query_more, ga_t, normed_t, qkv_weight, x,
        key_more, ln1_gain, down_bias, small, middle, grad_middle, ff_part, branch,
    ))
    return (
        output[None], tokens_grad[None], gain_one, offset_one, qkv_grad, qv_grad, out_grad.T,
        out_bias_grad, gain_two, offset_two, up_grad, up_bias_grad, down_grad.T, down_bias_grad,
    )


def solution(mesh):
    chosen = generic_body
    if mesh.shape["head"] == 2 and mesh.shape["seq"] == SEQ_SIZE:
        chosen = fast_body
    return jax.shard_map(
        chosen,
        mesh=mesh,
        in_specs=(
            P("seq", None, None),
            P("seq", None),
            P("seq", None),
            P(),
            P(),
            P(None, None, "head"),
            P(None, "head"),
            P("head", None),
            P(),
            P(),
            P(),
            P("seq", "head"),
            P("head"),
            P("head", "seq"),
            P(),
            P("seq", None, None),
        ),
        out_specs=(
            P("seq", None, None),
            P("seq", None, None),
            P(),
            P(),
            P(None, "seq", "head"),
            P(None, "head"),
            P("head", "seq"),
            P(),
            P(),
            P(),
            P("seq", "head"),
            P("head"),
            P("head", "seq"),
            P(),
        ),
        check_vma=False,
    )
```

```python
import math

import jax
import jax.numpy as jnp
from jax import lax
from jax.experimental import pallas as pl
from jax.experimental.pallas import tpu as pltpu
from jax.sharding import PartitionSpec as P

HEAD_DIM = 64


def layer_norm(values_in, scaling, offset):
    middle = jnp.mean(values_in, axis=-1, keepdims=True)
    centred = values_in - middle
    spread = jnp.mean(centred * centred, axis=-1, keepdims=True)
    return centred * lax.rsqrt(spread + 1e-05) * scaling + offset


def gelu_exact(values_in):
    return 0.5 * values_in * (1.0 + jax.scipy.special.erf(values_in * 0.7071067811865476))


def dot_rows(left, right):
    return lax.dot_general(
        left, right, (((1,), (1,)), ((), ())), preferred_element_type=jnp.float32
    )


def dot_cols(left, right):
    return lax.dot_general(
        left, right, (((0,), (0,)), ((), ())), preferred_element_type=jnp.float32
    )


def masked_scores(block_query, seq_keys, block_segments, seq_segments, seq_context, factor):
    raw_scores = (
        jnp.einsum("qhd,khd->hqk", block_query, seq_keys, preferred_element_type=jnp.float32)
        * factor
    )
    allowed = (block_segments[:, None] == seq_segments[None, :]) & (seq_context[None, :] == 1)
    return jnp.where(allowed[None], raw_scores, -1e30)


def generic_body(
    tokens,
    segment_ids,
    context_flags,
    ln1_gain,
    ln1_bias,
    qkv_weight,
    qv_bias,
    out_weight,
    out_bias,
    ln2_gain,
    ln2_bias,
    up_weight,
    up_bias,
    down_weight,
    down_bias,
    cotangent,
):
    seq_count, length, width = tokens.shape
    row_count = seq_count * length
    local_cols = qkv_weight.shape[2]
    head_count = local_cols // HEAD_DIM
    factor = 1.0 / math.sqrt(HEAD_DIM)
    block = min(512, length)
    blocks = length // block
    gain_one = ln1_gain.astype(jnp.float32)
    offset_one = ln1_bias.astype(jnp.float32)
    gain_two = ln2_gain.astype(jnp.float32)
    offset_two = ln2_bias.astype(jnp.float32)
    flat_in = tokens.astype(jnp.float32).reshape(row_count, width)
    normed_f, norm_one_pull = jax.vjp(layer_norm, flat_in, gain_one, offset_one)
    normed = normed_f.astype(jnp.bfloat16)
    queries = (
        jnp.dot(normed, qkv_weight[0], preferred_element_type=jnp.float32)
        + qv_bias[0].astype(jnp.float32)
    ).astype(jnp.bfloat16)
    key_rows = jnp.dot(normed, qkv_weight[1], preferred_element_type=jnp.float32).astype(
        jnp.bfloat16
    )
    value_rows = (
        jnp.dot(normed, qkv_weight[2], preferred_element_type=jnp.float32)
        + qv_bias[1].astype(jnp.float32)
    ).astype(jnp.bfloat16)

    def per_sequence(array):
        return array.reshape(seq_count, length, head_count, HEAD_DIM)

    def attend_sequence(member):
        seq_query, seq_keys, seq_values, seq_segments, seq_context = member

        def attend_block(portion):
            block_query, block_segments = portion
            scores = masked_scores(
                block_query, seq_keys, block_segments, seq_segments, seq_context, factor
            )
            row_top = jnp.max(scores, axis=-1, keepdims=True)
            exponent = jnp.exp(scores - row_top)
            row_total = jnp.sum(exponent, axis=-1, keepdims=True)
            soft_weights = (exponent / row_total).astype(jnp.bfloat16)
            block_mix = jnp.einsum(
                "hqk,khd->qhd", soft_weights, seq_values, preferred_element_type=jnp.float32
            )
            return (block_mix.astype(jnp.bfloat16), row_top + jnp.log(row_total))

        return lax.map(
            attend_block,
            (
                seq_query.reshape(blocks, block, head_count, HEAD_DIM),
                seq_segments.reshape(blocks, block),
            ),
        )

    mixture, log_totals = lax.map(
        attend_sequence,
        (
            per_sequence(queries),
            per_sequence(key_rows),
            per_sequence(value_rows),
            segment_ids,
            context_flags,
        ),
    )
    mixture = mixture.reshape(row_count, local_cols)
    partial_out = jnp.dot(mixture, out_weight, preferred_element_type=jnp.float32)
    grad_rows_all = cotangent.reshape(row_count, width)
    grad_float_all = grad_rows_all.astype(jnp.float32)
    grad_down_bias = jnp.sum(grad_float_all, axis=0)
    attended = lax.psum(partial_out, "head") + out_bias.astype(jnp.float32)
    middle_state = flat_in + attended
    normed_two_f, norm_two_pull = jax.vjp(layer_norm, middle_state, gain_two, offset_two)
    normed_two = normed_two_f.astype(jnp.bfloat16)
    up_part, down_part, up_shift = (
        lax.all_gather(up_weight, "head", axis=1, tiled=True),
        lax.all_gather(down_weight, "head", axis=0, tiled=True),
        lax.all_gather(up_bias, "head", axis=0, tiled=True),
    )
    up_full, down_full = (
        lax.all_gather(up_part, "seq", axis=0, tiled=True),
        lax.all_gather(down_part, "seq", axis=1, tiled=True),
    )
    before = jnp.dot(normed_two, up_full, preferred_element_type=jnp.float32) + up_shift.astype(
        jnp.float32
    )
    active_f, gelu_pull = jax.vjp(gelu_exact, before)
    active = active_f.astype(jnp.bfloat16)
    branch_out = jnp.dot(active, down_full, preferred_element_type=jnp.float32)
    final_rows = (middle_state + branch_out + down_bias.astype(jnp.float32)).astype(jnp.bfloat16)
    output = final_rows.reshape(tokens.shape)
    grad_float = grad_rows_all.astype(jnp.float32)
    grad_down = dot_cols(active, grad_rows_all)
    grad_active = dot_rows(grad_rows_all, down_full)
    (grad_before_f,) = gelu_pull(grad_active)
    grad_before = grad_before_f.astype(jnp.bfloat16)
    grad_up = dot_cols(normed_two, grad_before)
    grad_up_bias = jnp.sum(grad_before.astype(jnp.float32), axis=0)
    grad_normed_two = dot_rows(grad_before, up_full)
    grad_middle_norm, grad_gain_two, grad_offset_two = norm_two_pull(grad_normed_two)
    grad_middle = grad_float + grad_middle_norm
    ff_part = up_weight.shape[1]
    start_col = lax.axis_index("head") * ff_part
    grad_up = lax.dynamic_slice_in_dim(grad_up, start_col, ff_part, 1)
    grad_down = lax.dynamic_slice_in_dim(grad_down, start_col, ff_part, 0)
    grad_up_bias = lax.dynamic_slice_in_dim(grad_up_bias, start_col, ff_part, 0)
    grad_attended = grad_middle.astype(jnp.bfloat16)
    grad_out_bias = jnp.sum(grad_attended.astype(jnp.float32), axis=0)
    grad_out = dot_cols(mixture, grad_attended)
    grad_mixture = dot_rows(grad_attended, out_weight).astype(jnp.bfloat16)

    def back_sequence(member):
        seq_query, seq_keys, seq_values, seq_grad, seq_logs, seq_segments, seq_context = member

        def back_block(carry, portion):
            key_acc, value_acc = carry
            block_query, block_grad, block_logs, block_segments = portion
            scores = masked_scores(
                block_query, seq_keys, block_segments, seq_segments, seq_context, factor
            )
            soft_weights = jnp.exp(scores - block_logs)
            value_acc = value_acc + jnp.einsum(
                "hqk,qhd->khd",
                soft_weights.astype(jnp.bfloat16),
                block_grad,
                preferred_element_type=jnp.float32,
            )
            grad_soft = jnp.einsum(
                "qhd,khd->hqk", block_grad, seq_values, preferred_element_type=jnp.float32
            )
            row_inner = jnp.sum(soft_weights * grad_soft, axis=-1, keepdims=True)
            grad_scores = (soft_weights * (grad_soft - row_inner)).astype(jnp.bfloat16)
            grad_query = (
                jnp.einsum(
                    "hqk,khd->qhd", grad_scores, seq_keys, preferred_element_type=jnp.float32
                )
                * factor
            )
            key_acc = (
                key_acc
                + jnp.einsum(
                    "hqk,qhd->khd", grad_scores, block_query, preferred_element_type=jnp.float32
                )
                * factor
            )
            return ((key_acc, value_acc), grad_query)

        empty = jnp.zeros((length, head_count, HEAD_DIM), jnp.float32)
        (key_acc, value_acc), grad_query = lax.scan(
            back_block,
            (empty, empty),
            (
                seq_query.reshape(blocks, block, head_count, HEAD_DIM),
                seq_grad.reshape(blocks, block, head_count, HEAD_DIM),
                seq_logs,
                seq_segments.reshape(blocks, block),
            ),
        )
        return (grad_query, key_acc, value_acc)

    grad_queries, grad_keys, grad_values = lax.map(
        back_sequence,
        (
            per_sequence(queries),
            per_sequence(key_rows),
            per_sequence(value_rows),
            per_sequence(grad_mixture),
            log_totals,
            segment_ids,
            context_flags,
        ),
    )
    grad_queries = grad_queries.reshape(row_count, local_cols).astype(jnp.bfloat16)
    grad_keys = grad_keys.reshape(row_count, local_cols).astype(jnp.bfloat16)
    grad_values = grad_values.reshape(row_count, local_cols).astype(jnp.bfloat16)
    grad_qv_bias = jnp.stack(
        [
            jnp.sum(grad_queries.astype(jnp.float32), axis=0),
            jnp.sum(grad_values.astype(jnp.float32), axis=0),
        ]
    )
    grad_qkv = jnp.stack(
        [dot_cols(normed, grad_queries), dot_cols(normed, grad_keys), dot_cols(normed, grad_values)]
    )
    grad_normed = (
        dot_rows(grad_queries, qkv_weight[0])
        + dot_rows(grad_keys, qkv_weight[1])
        + dot_rows(grad_values, qkv_weight[2])
    )
    grad_normed = lax.psum(grad_normed, "head")
    grad_input_norm, grad_gain_one, grad_offset_one = norm_one_pull(grad_normed)
    tokens_grad = (grad_middle + grad_input_norm).astype(jnp.bfloat16).reshape(tokens.shape)
    summed_qkv, summed_out, summed_up, summed_down = (
        lax.psum_scatter(
            grad_qkv.astype(jnp.bfloat16), "seq", scatter_dimension=1, tiled=True
        ).astype(jnp.float32),
        lax.psum_scatter(
            grad_out.astype(jnp.bfloat16), "seq", scatter_dimension=1, tiled=True
        ).astype(jnp.float32),
        lax.psum_scatter(
            grad_up.astype(jnp.bfloat16), "seq", scatter_dimension=0, tiled=True
        ).astype(jnp.float32),
        lax.psum_scatter(
            grad_down.astype(jnp.bfloat16), "seq", scatter_dimension=1, tiled=True
        ).astype(jnp.float32),
    )
    smalls = lax.psum(
        (
            grad_gain_one,
            grad_offset_one,
            grad_qv_bias,
            grad_out_bias,
            grad_gain_two,
            grad_offset_two,
            grad_up_bias,
            grad_down_bias,
        ),
        "seq",
    )
    return (
        output,
        tokens_grad,
        smalls[0],
        smalls[1],
        summed_qkv,
        smalls[2],
        summed_out,
        smalls[3],
        smalls[4],
        smalls[5],
        summed_up,
        smalls[6],
        summed_down,
        smalls[7],
    )


MESH = pl.DeviceIdType.MESH
BF = jnp.bfloat16
F32 = jnp.float32
BLOCK = 256
STRIP = 512
PIECE = 128
WIDE = 1024
GROUP = 2
CHUNK = 512
PAIR = 2 * HEAD_DIM
Z_SIZE, Y_SIZE, CORES = 4, 2, 2
SEQ_SIZE = Z_SIZE * Y_SIZE * CORES
HOP = Y_SIZE * CORES
TABLES = 8
FAR = -1e30
VMEM_LIMIT = 62 * 2**20
INV_ROOT_TWO = 0.7071067811865476
INV_ROOT_TWO_PI = 0.3989422804014327
LN1_GAIN, LN1_BIAS, QV_BIAS, OUT_BIAS, LN2_GAIN, LN2_BIAS, UP_BIAS, DOWN_BIAS = 0, 1, 2, 3, 4, 5, 6, 8
SMALL_ROWS = 16
VMEM_SPEC = pl.BlockSpec(memory_space=pltpu.VMEM)
ANY_SPEC = pl.BlockSpec(memory_space=pl.ANY)


def shape_of(dims, dtype):
    return jax.ShapeDtypeStruct(tuple(dims), dtype)


def nn(left, right):
    return jnp.dot(left, right, preferred_element_type=F32)


def split_sum(left, right):
    parts = [
        nn(left[:, n:n + BLOCK], right[n:n + BLOCK]) for n in range(0, left.shape[1], BLOCK)
    ]
    while len(parts) > 1:
        parts = [a + b for a, b in zip(parts[::2], parts[1::2])]
    return parts[0]


def turn(block):
    return jnp.transpose(block)


def sum_rows(block):
    return jnp.sum(block, axis=0, keepdims=True)


def place():
    me = lax.axis_index("seq")
    head = lax.axis_index("head")
    core = me % 2
    y = (me // 2) % 2
    across = {"seq": me, "head": 1 - head}
    core_mate = {"seq": me + 1 - 2 * core, "head": head}
    y_mate = {"seq": me + 2 - 4 * y, "head": head}
    z_mates = [{"seq": (me + HOP * d) % SEQ_SIZE, "head": head} for d in (1, 2, 3)]
    return me, head, core, y, across, core_mate, y_mate, z_mates


def greet(others):
    barrier = pltpu.get_barrier_semaphore()
    for other in others:
        pl.semaphore_signal(barrier, inc=1, device_id=other, device_id_type=MESH)
    pl.semaphore_wait(barrier, len(others))


def remote(src, dst, send_sem, recv_sem, other):
    return pltpu.make_async_remote_copy(
        src_ref=src, dst_ref=dst, send_sem=send_sem, recv_sem=recv_sem,
        device_id=other, device_id_type=MESH,
    )


def norm_stats(rows):
    middle = jnp.mean(rows, axis=-1, keepdims=True)
    centred = rows - middle
    spread = jnp.mean(centred * centred, axis=-1, keepdims=True)
    return centred, lax.rsqrt(spread + 1e-05)


def norm_back(inner, unit, scale):
    return scale * (
        inner
        - jnp.mean(inner, axis=-1, keepdims=True)
        - unit * jnp.mean(inner * unit, axis=-1, keepdims=True)
    )


def as_row(vector):
    return vector[...].astype(F32).reshape(1, -1)


def lanes():
    return lax.broadcasted_iota(jnp.int32, (1, PAIR), 1)


def in_pieces(column, first, rest):
    high = column.astype(BF).astype(F32)
    mid = (column - high).astype(BF).astype(F32)
    low = column - high - mid
    at = lanes()
    return jnp.where(
        at == first, high, jnp.where(at == first + 1, mid, jnp.where(at == first + 2, low, rest))
    ).astype(BF)


def one_lanes(length):
    return jnp.broadcast_to(jnp.where(lanes() < 3, 1.0, 0.0).astype(BF), (length, PAIR))


def fwd_kernel(
    x_ref, seg_ref, context, gain, offset, qv_bias, out_bias, gain_two, offset_two, up_bias,
    wqkv, wout, up_shard, down_shard,
    q_out, k_out, v_out, mix_out, mid_out, normed_out, wff_out, key_out, query_out,
    normed_two_out, active_out, slope_out,
    wff, q_ref, k_ref, v_ref, mix_ref, mid_ref, normed_t, key_more, query_more,
    normed_two_t, active, slope, bias_row, mask_more, wout_x, mix_x,
    zs, zr, ys, yr, cs, cr, xs, xr, local, outs,
):
    length, width = x_ref.shape
    blocks = length // BLOCK
    pairs = q_ref.shape[0]
    cols = pairs * PAIR
    me, head, core, y, across, core_mate, y_mate, _ = place()
    z = me // HOP
    above = {"seq": (me + HOP) % SEQ_SIZE, "head": head}
    below = {"seq": (me + SEQ_SIZE - HOP) % SEQ_SIZE, "head": head}
    own = [
        pltpu.make_async_copy(shard, wff.at[u, me], local.at[u])
        for u, shard in enumerate((up_shard, down_shard))
    ]
    own[0].start()
    own[1].start()
    greet([across, core_mate, y_mate, above, below])

    out_copy = remote(wout, wout_x, xs.at[0], xr.at[0], across)
    out_copy.start()

    flows = [(0, 0)] + [(way, s) for s in (1, 2, 3) for way in (0, 1)]

    def there(way, s):
        return (z >= s) if way == 0 else (z + s < Z_SIZE)

    def source(base, way, s):
        away = SEQ_SIZE - HOP * s if way == 0 else HOP * s
        return (base + away) % SEQ_SIZE

    def z_copy(u, way, s):
        n = (u * 2 + way) * 3 + s - 1
        j = source(me, way, s - 1)
        return remote(wff.at[u, j], wff.at[u, j], zs.at[n], zr.at[n], above if way == 0 else below)

    def z_arrival(u, way, s):
        n = (u * 2 + way) * 3 + s - 1
        slot = wff.at[u, source(me, way, s)]
        return remote(slot, slot, zs.at[n], zr.at[n], above)

    def z_goes_on(way):
        return (z < Z_SIZE - 1) if way == 0 else (z > 0)

    def y_copy(u, f):
        n = u * 7 + f
        j = source(me, *flows[f])
        return remote(wff.at[u, j], wff.at[u, j], ys.at[n], yr.at[n], y_mate)

    def y_arrival(u, f):
        n = u * 7 + f
        slot = wff.at[u, source(me + 2 - 4 * y, *flows[f])]
        return remote(slot, slot, ys.at[n], yr.at[n], y_mate)

    def c_copy(u, f, from_y):
        n = (u * 2 + from_y) * 7 + f
        j = source(me + from_y * (2 - 4 * y), *flows[f])
        return remote(wff.at[u, j], wff.at[u, j], cs.at[n], cr.at[n], core_mate)

    def c_arrival(u, f, from_y):
        n = (u * 2 + from_y) * 7 + f
        slot = wff.at[u, source(me + 1 - 2 * core + from_y * (2 - 4 * y), *flows[f])]
        return remote(slot, slot, cs.at[n], cr.at[n], core_mate)

    def for_flow(f, do):
        if f == 0:
            do()
        else:
            pl.when(there(*flows[f]))(do)

    def for_step(s, do):
        for f, (way, step) in enumerate(flows):
            if step == s:
                for_flow(f, lambda f=f, way=way: do(f, way))

    def z_event(u, s):
        def one(f, way):
            z_arrival(u, way, s).wait_recv()
            if s < 3:
                pl.when(z_goes_on(way))(lambda: z_copy(u, way, s + 1).start())
            y_copy(u, f).start()
            c_copy(u, f, 0).start()
        for_step(s, one)
        if u == 0 and s == 1:
            start_z(1)
        if u == 0 and s == 2:
            y_copy(1, 0).start()
            c_copy(1, 0, 0).start()

    def y_event(u, s):
        def one(f, way):
            y_arrival(u, f).wait_recv()
            c_copy(u, f, 1).start()
        for_step(s, one)

    def start_z(u):
        for way in (0, 1):
            pl.when(z_goes_on(way))(lambda way=way: z_copy(u, way, 1).start())

    own[0].wait()
    start_z(0)
    y_copy(0, 0).start()
    c_copy(0, 0, 0).start()
    own[1].wait()

    plan = {
        2: [(z_event, 0, 1), (y_event, 0, 0)], 4: [(z_event, 0, 2)], 6: [(y_event, 0, 1)],
        7: [(z_event, 0, 3)], 8: [(z_event, 1, 1)], 9: [(y_event, 0, 2), (y_event, 1, 0)],
        10: [(z_event, 1, 2)], 11: [(y_event, 0, 3)],
    }

    def tick(t):
        for step, events in plan.items():
            @pl.when(t == step)
            def _(events=events):
                for event, u, s in events:
                    event(u, s)

    at = lax.broadcasted_iota(jnp.int32, (PAIR, length), 0)
    same = at == seg_ref[...]
    hidden = context[...] != 1
    ones = jnp.logical_and(at > TABLES, at < TABLES + 4)
    key_side = jnp.logical_or(
        jnp.logical_and(at < TABLES, same),
        jnp.logical_or(jnp.logical_and(at == TABLES, hidden), ones),
    )
    query_side = jnp.logical_and(at <= TABLES, jnp.logical_not(same))
    key_more[...] = turn(jnp.where(key_side, 1.0, 0.0)).astype(BF)
    mask_more[...] = turn(jnp.where(query_side, FAR, 0.0)).astype(BF)

    keep = [
        pltpu.make_async_copy(here, there, outs.at[n])
        for n, (here, there) in enumerate(
            (
                (q_ref, q_out), (k_ref, k_out), (v_ref, v_out), (normed_t, normed_out),
                (key_more, key_out), (query_more, query_out), (mix_ref, mix_out),
            )
        )
    ]
    gains, offsets = as_row(gain), as_row(offset)
    query_bias = qv_bias[0:1, :].astype(F32)
    value_bias = qv_bias[1:2, :].astype(F32)

    def project(b, _):
        rows = pl.ds(pl.multiple_of(b * BLOCK, BLOCK), BLOCK)
        centred, scale = norm_stats(x_ref[rows, :].astype(F32))
        block = (centred * scale * gains + offsets).astype(BF)
        normed_t[:, rows] = turn(block)
        queries = ((nn(block, wqkv[0]) + query_bias).astype(BF) * 0.125).astype(BF)
        keys = nn(block, wqkv[1]).astype(BF)
        values = (nn(block, wqkv[2]) + value_bias).astype(BF)
        for p in range(pairs):
            part = slice(p * PAIR, (p + 1) * PAIR)
            q_ref[p, rows, :] = queries[:, part]
            k_ref[p, rows, :] = keys[:, part]
            v_ref[p, rows, :] = values[:, part]
        tick(b)
        return 0

    lax.fori_loop(0, blocks, project, 0)
    for n in range(5):
        keep[n].start()

    low_lanes = lanes() < HEAD_DIM
    zero = jnp.zeros((1, PAIR), BF)

    def mixture_copy(b):
        rows = pl.ds(pl.multiple_of(b * BLOCK, BLOCK), BLOCK)
        return remote(
            mix_ref.at[:, rows, :], mix_x.at[:, rows, :], xs.at[1 + b], xr.at[1 + b], across
        )

    per_step = STRIP // BLOCK

    def attend(t, _):
        b, p = t // pairs, t % pairs
        keys = jnp.concatenate([k_ref[p], key_more[...]], axis=1)
        values = jnp.concatenate([v_ref[p], one_lanes(length)], axis=1)
        chains = []
        for n in range(per_step):
            rows = pl.ds(pl.multiple_of(b * STRIP + n * BLOCK, BLOCK), BLOCK)
            queries, more = q_ref[p, rows, :], mask_more[rows, :]
            for low in (0, 1):
                own_lanes = jnp.logical_not(low_lanes) if low else low_lanes
                left = jnp.concatenate([jnp.where(own_lanes, queries, zero), more], axis=1)
                chains.append((rows, low, more, dot_rows(left, keys)))
        parts = []
        for rows, low, more, scores in chains:
            top = jnp.max(scores, axis=-1, keepdims=True)
            mixed = nn(jnp.exp(scores - top).astype(BF), values)
            total = mixed[:, PAIR:PAIR + 1]
            parts.append(mixed[:, :PAIR] / total)
            query_more[2 * p + low, rows, :] = in_pieces(
                -(top + jnp.log(total)), TABLES + 1, more.astype(F32)
            )
            if low:
                mix_ref[p, rows, :] = jnp.where(low_lanes, *parts[-2:]).astype(BF)
        tick(t + blocks)

        @pl.when(p == pairs - 1)
        def _():
            for n in range(per_step):
                mixture_copy(b * per_step + n).start()

        return 0

    lax.fori_loop(0, length // STRIP * pairs, attend, 0)
    keep[5].start()
    keep[6].start()
    out_copy.wait_recv()
    out_row = as_row(out_bias)

    def mid_copy(b):
        rows = pl.ds(b * BLOCK, BLOCK)
        return pltpu.make_async_copy(mid_ref.at[rows, :], mid_out.at[rows, :], outs.at[7 + b])

    gains_two, offsets_two = as_row(gain_two), as_row(offset_two)
    bias_row[...] = as_row(up_bias)

    def half_copies(b):
        rows = pl.ds(b * BLOCK, BLOCK)
        return [
            pltpu.make_async_copy(
                here.at[:, rows, :], there.at[:, rows, :], outs.at[7 + blocks + 2 * b + n]
            )
            for n, (here, there) in enumerate(((active, active_out), (slope, slope_out)))
        ]

    def up_half(b):
        rows = pl.ds(b * BLOCK, BLOCK)
        centred, scale = norm_stats(mid_ref[rows, :])
        block = (centred * scale * gains_two + offsets_two).astype(BF)
        normed_two_t[:, rows] = turn(block)

        def one(n, _):
            cut = pl.ds(pl.multiple_of(n * WIDE, WIDE), WIDE)
            before = nn(block, wff[0, :, :, cut].reshape(width, WIDE)) + bias_row[:, cut]
            spread = 0.5 * (1.0 + lax.erf(before * INV_ROOT_TWO))
            active[n, rows, :] = (before * spread).astype(BF)
            bell = INV_ROOT_TWO_PI * jnp.exp(before * before * -0.5)
            slope[n, rows, :] = (spread + before * bell).astype(BF)
            return 0

        lax.fori_loop(0, active.shape[0], one, 0)
        for copy in half_copies(b):
            copy.start()

    def arrive(u):
        for f in range(len(flows)):
            def one(f=f):
                for from_y in (0, 1):
                    c_arrival(u, f, from_y).wait_recv()
            for_flow(f, one)

    for b in range(blocks):
        mixture_copy(b).wait_recv()
        rows = pl.ds(b * BLOCK, BLOCK)
        ours = jnp.concatenate([mix_ref[p, rows, :] for p in range(pairs)], axis=-1)
        other = jnp.concatenate([mix_x[p, rows, :] for p in range(pairs)], axis=-1)
        attended = nn(ours, wout[...]) + nn(other, wout_x[...])
        mid_ref[rows, :] = x_ref[rows, :].astype(F32) + (attended + out_row)
        mid_copy(b).start()
        if b == 0:
            z_event(1, 3)
            arrive(0)
        up_half(b)
        if b < 3:
            y_event(1, b + 1)
    normed_two_keep = pltpu.make_async_copy(
        normed_two_t, normed_two_out, outs.at[7 + 3 * blocks]
    )
    normed_two_keep.start()
    wff_keep = [pltpu.make_async_copy(wff.at[u], wff_out.at[u], local.at[u]) for u in range(2)]
    wff_keep[0].start()
    arrive(1)
    wff_keep[1].start()
    out_copy.wait_send()
    for copy in keep + wff_keep + [normed_two_keep]:
        copy.wait()
    for b in range(blocks):
        for copy in half_copies(b):
            copy.wait()
    for b in range(blocks):
        mixture_copy(b).wait_send()
        mid_copy(b).wait()
    for u in range(2):
        for way in (0, 1):
            pl.when(z_goes_on(way))(lambda u=u, way=way: z_copy(u, way, 1).wait_send())
        for f, (way, s) in enumerate(flows):
            def finish(u=u, f=f, way=way, s=s):
                if f and s < 3:
                    pl.when(z_goes_on(way))(lambda: z_copy(u, way, s + 1).wait_send())
                y_copy(u, f).wait_send()
                for from_y in (0, 1):
                    c_copy(u, f, from_y).wait_send()
            for_flow(f, finish)


def run_fwd(
    x, seg, context, gain, offset, qv_bias, out_bias, gain_two, offset_two, up_bias, wqkv, wout,
    up_weight, down_t,
):
    length, width = x.shape
    pairs = wqkv.shape[2] // PAIR
    blocks = length // BLOCK
    depth, hidden = up_weight.shape
    by_pair, by_head = (pairs, length, PAIR), (2 * pairs, length, PAIR)
    turned = (width, length)
    halves = (hidden // WIDE, length, WIDE)
    dma = pltpu.SemaphoreType.DMA
    return pl.pallas_call(
        fwd_kernel,
        out_shape=[shape_of(by_pair, BF)] * 4 + [
            shape_of((length, width), F32),
            shape_of(turned, BF),
            shape_of((2, SEQ_SIZE, depth, hidden), BF),
            shape_of((length, PAIR), BF),
            shape_of(by_head, BF),
            shape_of((width, length), BF),
            shape_of(halves, BF),
            shape_of(halves, BF),
        ],
        in_specs=[VMEM_SPEC] * 12 + [ANY_SPEC] * 2,
        out_specs=[ANY_SPEC] * 12,
        scratch_shapes=[pltpu.VMEM((2, SEQ_SIZE, depth, hidden), BF)]
        + [pltpu.VMEM(by_pair, BF)] * 4 + [
            pltpu.VMEM((length, width), F32),
            pltpu.VMEM(turned, BF),
            pltpu.VMEM((length, PAIR), BF),
            pltpu.VMEM(by_head, BF),
            pltpu.VMEM((width, length), BF),
            pltpu.VMEM(halves, BF),
            pltpu.VMEM(halves, BF),
            pltpu.VMEM((1, hidden), F32),
            pltpu.VMEM((length, PAIR), BF),
            pltpu.VMEM(wout.shape, BF),
            pltpu.VMEM(by_pair, BF),
            dma((12,)), dma((12,)), dma((14,)), dma((14,)), dma((28,)), dma((28,)),
            dma((1 + blocks,)), dma((1 + blocks,)), dma((2,)), dma((8 + 3 * blocks,)),
        ],
        compiler_params=pltpu.CompilerParams(
            collective_id=0, has_side_effects=True, vmem_limit_bytes=VMEM_LIMIT
        ),
    )(
        x, seg, context, gain, offset, qv_bias, out_bias, gain_two, offset_two, up_bias, wqkv,
        wout, up_weight, down_t,
    )


def ff_kernel(
    mid_hbm, dy_hbm, wff_hbm, normed_two_hbm, active_hbm, slope_hbm, gain, wout_hbm,
    branch_out, gmid_hbm, ga_out, gm_out, summed, small_ref,
    dy_ref, wff, wout, branch_ref, ga_t, gm_ref, normed_t, dy_t, active, before_grad, gnt_acc, gnt_own, gnt_x, whole, from_mate,
    held, ready,
    xs, xr, cs, cr, ls, ws, ss, ins, outs,
):
    length, width = dy_ref.shape
    blocks = length // BLOCK
    hidden = wff.shape[3]
    half = hidden // WIDE
    chunks = 2 * hidden // CHUNK
    pairs = gm_ref.shape[0]
    me, head, core, y, across, core_mate, y_mate, z_mates = place()
    dy_load = pltpu.make_async_copy(dy_hbm, dy_ref, ins.at[0])
    wout_load = pltpu.make_async_copy(wout_hbm, wout, ins.at[1])

    def step_loads(n):
        cut = pl.ds(n * WIDE, WIDE)
        return [
            pltpu.make_async_copy(src, dst, ins.at[4 + 3 * n + m])
            for m, (src, dst) in enumerate(
                (
                    (wff_hbm.at[1, :, :, cut], wff.at[1, :, :, cut]),
                    (slope_hbm.at[n], before_grad.at[n]),
                    (wff_hbm.at[0, :, :, cut], wff.at[0, :, :, cut]),
                )
            )
        ]

    active_load = pltpu.make_async_copy(active_hbm, active, ins.at[2])
    normed_load = pltpu.make_async_copy(normed_two_hbm, normed_t, ins.at[3])
    dy_load.start()
    for n in range(half):
        for copy in step_loads(n):
            copy.start()
    active_load.start()
    normed_load.start()
    wout_load.start()
    greet([across, core_mate])
    gains = as_row(gain)

    def weight(kind, n):
        cut = pl.ds(pl.multiple_of(n * WIDE, WIDE), WIDE)
        return wff[kind, :, :, cut].reshape(width, WIDE)

    small_ref[...] = jnp.zeros_like(small_ref)

    def load(b):
        rows = pl.ds(b * BLOCK, BLOCK)
        return pltpu.make_async_copy(mid_hbm.at[rows, :], held.at[b % 2], ls.at[b % 2])

    def store(b):
        rows = pl.ds(b * BLOCK, BLOCK)
        return pltpu.make_async_copy(ready.at[b % 2], gmid_hbm.at[rows, :], ws.at[b % 2])

    load(0).start()
    load(1).start()

    def gnt_copy(b):
        return remote(gnt_own.at[b], gnt_x.at[b], xs.at[b], xr.at[b], across)

    def core_copy(n):
        return remote(
            whole.at[n, :, :, 1 - core], from_mate.at[n], cs.at[n], cr.at[n], core_mate
        )

    def forward(t, _):
        b, n = t // half, t % half
        rows = pl.ds(pl.multiple_of(b * BLOCK, BLOCK), BLOCK)

        for n_first in range(half):
            @pl.when(t == n_first)
            def _(n_first=n_first):
                if n_first == 0:
                    dy_load.wait()
                for copy in step_loads(n_first):
                    copy.wait()

        @pl.when(n == 0)
        def _():
            dy_t[:, rows] = turn(dy_ref[rows, :])
            small_ref[DOWN_BIAS:DOWN_BIAS + 1, :] += sum_rows(dy_ref[rows, :].astype(F32))

        up = weight(0, n)
        grad = nn(dy_ref[rows, :], weight(1, n)) * before_grad[n, rows, :].astype(F32)
        grad = grad.astype(BF)
        before_grad[n, rows, :] = grad
        small_ref[pl.ds(UP_BIAS + n, 1), :] += sum_rows(grad.astype(F32))
        back = dot_rows(grad, up)

        @pl.when(n == 0)
        def _():
            gnt_acc[...] = back

        @pl.when(n > 0)
        def _():
            gnt_acc[...] += back

        for b_done in range(blocks):
            @pl.when(t == (b_done + 1) * half - 1)
            def _(b_done=b_done):
                gnt_own[b_done] = gnt_acc[...].astype(BF)
                gnt_copy(b_done).start()
        return 0

    lax.fori_loop(0, blocks * half, forward, 0)

    def weight_grads(left_t, right, first):
        cut_rows = width // Z_SIZE
        per_wide = WIDE // CHUNK

        def one(t, _):
            n, plane = t // Z_SIZE, t % Z_SIZE
            cut = pl.ds(pl.multiple_of(plane * cut_rows, cut_rows), cut_rows)
            total = nn(left_t[cut, :], right[n]).astype(BF)
            for m in range(per_wide):
                piece = total[:, m * CHUNK:(m + 1) * CHUNK]
                whole[first + n * per_wide + m, plane] = piece.reshape(whole.shape[2:])

            @pl.when(plane == Z_SIZE - 1)
            def _():
                for m in range(per_wide):
                    core_copy(first + n * per_wide + m).start()

            return 0

        lax.fori_loop(0, Z_SIZE * half, one, 0)

    active_load.wait()
    normed_load.wait()
    weight_grads(dy_t, active, chunks // 2)
    weight_grads(normed_t, before_grad, 0)

    def branch(b, _):
        rows = pl.ds(pl.multiple_of(b * BLOCK, BLOCK), BLOCK)
        total = dot_rows(active[0, rows, :], weight(1, 0))
        for n in range(1, half):
            total += dot_rows(active[n, rows, :], weight(1, n))
        branch_ref[rows, :] = total.astype(BF)
        return 0

    lax.fori_loop(0, blocks, branch, 0)
    branch_keep = pltpu.make_async_copy(branch_ref, branch_out, outs.at[0])
    branch_keep.start()
    wout_load.wait()

    def ga_copy(b):
        rows = pl.ds(b * BLOCK, BLOCK)
        return pltpu.make_async_copy(ga_t.at[:, rows], ga_out.at[:, rows], outs.at[1 + b])

    def gm_copy(b):
        rows = pl.ds(b * BLOCK, BLOCK)
        return pltpu.make_async_copy(
            gm_ref.at[:, rows, :], gm_out.at[:, rows, :], outs.at[1 + blocks + b]
        )


    def add_mate(n, _):
        core_copy(n).wait()
        both = whole[n, :, :, core].astype(F32) + from_mate[n].astype(F32)
        from_mate[n] = both.astype(BF)
        return 0

    lax.fori_loop(chunks // 2, chunks, add_mate, 0)
    lax.fori_loop(0, chunks // 2, add_mate, 0)
    keep = pltpu.make_async_copy(from_mate, summed, ss.at[0])
    keep.start()

    strips = BLOCK // PIECE
    for b in range(blocks):
        gnt_copy(b).wait()
        load(b).wait()
        if b >= 2:
            store(b - 2).wait()

        def through_norm(n, _, b=b):
            rows = pl.ds(pl.multiple_of(n * PIECE, PIECE), PIECE)
            full = pl.ds(pl.multiple_of(b * BLOCK + n * PIECE, PIECE), PIECE)
            grad = gnt_own[b, rows, :].astype(F32) + gnt_x[b, rows, :].astype(F32)
            centred, scale = norm_stats(held[b % 2, rows, :])
            unit = centred * scale
            small_ref[LN2_GAIN:LN2_GAIN + 1, :] += sum_rows(grad * unit)
            small_ref[LN2_BIAS:LN2_BIAS + 1, :] += sum_rows(grad)
            total = dy_ref[full, :].astype(F32) + norm_back(grad * gains, unit, scale)
            ready[b % 2, rows, :] = total
            low = total.astype(BF)
            small_ref[OUT_BIAS:OUT_BIAS + 1, :] += sum_rows(low.astype(F32))
            ga_t[:, full] = turn(low)
            mixed = dot_rows(low, wout[...]).astype(BF)
            for p in range(pairs):
                gm_ref[p, full, :] = mixed[:, p * PAIR:(p + 1) * PAIR]
            return 0

        lax.fori_loop(0, strips, through_norm, 0)
        store(b).start()
        ga_copy(b).start()
        gm_copy(b).start()
        if b + 2 < blocks:
            load(b + 2).start()
    store(blocks - 2).wait()
    store(blocks - 1).wait()
    for b in range(blocks):
        ga_copy(b).wait()
        gm_copy(b).wait()
    branch_keep.wait()
    keep.wait()


def run_ff(middle, dy, wff, normed_two_t, active, slope, gain, wout):
    length, width = middle.shape
    half = wff.shape[3] // WIDE
    chunks = 2 * wff.shape[3] // CHUNK
    blocks = length // BLOCK
    pairs = wout.shape[0] // PAIR
    depth = width // SEQ_SIZE
    dma = pltpu.SemaphoreType.DMA
    rows = pltpu.VMEM((blocks, BLOCK, width), BF)
    hidden = pltpu.VMEM((half, length, WIDE), BF)
    flat_t = pltpu.VMEM((width, length), BF)
    return pl.pallas_call(
        ff_kernel,
        out_shape=[
            shape_of((length, width), BF),
            shape_of((length, width), F32),
            shape_of((width, length), BF),
            shape_of((pairs, length, PAIR), BF),
            shape_of((chunks, Z_SIZE, Y_SIZE, depth, CHUNK), BF),
            shape_of((SMALL_ROWS, width), F32),
        ],
        in_specs=[ANY_SPEC] * 6 + [VMEM_SPEC, ANY_SPEC],
        out_specs=[ANY_SPEC] * 5 + [VMEM_SPEC],
        scratch_shapes=[
            pltpu.VMEM((length, width), BF), pltpu.VMEM(wff.shape, BF),
            pltpu.VMEM(wout.shape, BF),
            pltpu.VMEM((length, width), BF), flat_t, pltpu.VMEM((pairs, length, PAIR), BF),
            flat_t, flat_t, hidden, hidden,
            pltpu.VMEM((BLOCK, width), F32), rows, rows,
            pltpu.VMEM((chunks, Z_SIZE, Y_SIZE, CORES, depth, CHUNK), BF),
            pltpu.VMEM((chunks, Z_SIZE, Y_SIZE, depth, CHUNK), BF),
            pltpu.VMEM((2, BLOCK, width), F32), pltpu.VMEM((2, BLOCK, width), F32),
            dma((blocks,)), dma((blocks,)), dma((chunks,)), dma((chunks,)),
            dma((2,)), dma((2,)), dma((1,)), dma((4 + 3 * half,)), dma((1 + 2 * blocks,)),
        ],
        compiler_params=pltpu.CompilerParams(
            collective_id=1, has_side_effects=True, vmem_limit_bytes=VMEM_LIMIT
        ),
    )(middle, dy, wff, normed_two_t, active, slope, gain, wout)


def back_kernel(
    q_hbm, k_hbm, v_hbm, mix_hbm, gm_hbm, query_hbm, ga_hbm, normed_hbm, wqkv_hbm, x_hbm,
    key_more, gain, down_bias, small_in, mid_hbm, gmid_hbm, ff_part, branch,
    out_hbm, tokens_hbm, qkv_sum, out_sum, up_sum, down_sum,
    gain_one, offset_one, qv_small, out_small, gain_two, offset_two, up_small, down_small,
    q_ref, k_ref, v_ref, mix_ref, gm_ref, query_more, ga_t, normed_t, wqkv, x_ref,
    out_ref, tokens_ref, key_t, key_acc, value_acc, dq, dk, dv, whole, mate, at_y, at_z, ff_y, ff_z, gn_own, gn_x,
    branch_x, branch_own, ff_own, held, small_own, small_z, small_y, small_c,
    bs, br, fys, fyr, fzs, fzr, acs, acr, ays, ayr, azs, azr, gs, gr, ls, ms, mr, os, hs, ins, more_ins, outs,
):
    length, width = x_ref.shape
    blocks = length // BLOCK
    strips = length // STRIP
    pairs = q_ref.shape[0]
    chunks = ff_part.shape[0]
    half = chunks // 2
    groups = chunks // GROUP
    me, head, core, y, across, core_mate, y_mate, z_mates = place()
    z = me // (Y_SIZE * CORES)
    by_pair = (
        (q_hbm, q_ref), (k_hbm, k_ref), (v_hbm, v_ref), (mix_hbm, mix_ref), (gm_hbm, gm_ref),
    )

    def pair_loads(p):
        both = pl.ds(2 * p, 2)
        first = p * (len(by_pair) + 1)
        return [
            pltpu.make_async_copy(src.at[p], dst.at[p], ins.at[first + n])
            for n, (src, dst) in enumerate(by_pair)
        ] + [
            pltpu.make_async_copy(
                query_hbm.at[both], query_more.at[both], ins.at[first + len(by_pair)]
            )
        ]

    late_loads = [
        pltpu.make_async_copy(src, dst, more_ins.at[n])
        for n, (src, dst) in enumerate(
            ((ga_hbm, ga_t), (normed_hbm, normed_t), (wqkv_hbm, wqkv), (x_hbm, x_ref))
        )
    ]
    for p in range(pairs):
        for copy in pair_loads(p):
            copy.start()
        if p == 0:
            late_loads[0].start()
            late_loads[1].start()
    late_loads[2].start()
    late_loads[3].start()
    greet([across, core_mate, y_mate, *z_mates])

    def part(b):
        return pl.ds(b * BLOCK, BLOCK)

    def branch_copy(b):
        return remote(branch.at[part(b), :], branch_x.at[part(b), :], bs.at[b], br.at[b], across)

    def load(n):
        source = mid_hbm if n < blocks else gmid_hbm
        return pltpu.make_async_copy(
            source.at[part(n % blocks), :], held.at[n % 2], ls.at[n % 2]
        )

    def taken(n):
        if n + 2 < 2 * blocks:
            load(n + 2).start()

    def group(g):
        return pl.ds(g * GROUP, GROUP)

    def ff_y_copy(g):
        return remote(
            ff_part.at[group(g), :, 1 - y], ff_y.at[group(g)], fys.at[g], fyr.at[g], y_mate
        )

    def ff_z_copy(g, d):
        n = g * 3 + d - 1
        return remote(
            ff_y.at[group(g), (z + d) % Z_SIZE], ff_z.at[d - 1, group(g)],
            fzs.at[n], fzr.at[n], z_mates[d - 1],
        )

    def branch_load(b):
        return pltpu.make_async_copy(branch.at[part(b), :], branch_own.at[b % 2], hs.at[b % 2])

    def ff_load(g):
        return pltpu.make_async_copy(
            ff_part.at[group(g), :, y], ff_own.at[g % 2], os.at[g % 2]
        )

    def ff_y_event(g):
        ff_y_copy(g).wait_recv()
        ff_load(g).wait()
        for n in range(g * GROUP, (g + 1) * GROUP):
            own = ff_own[g % 2, n % GROUP]
            ff_y[n] = (ff_y[n].astype(F32) + own.astype(F32)).astype(BF)
        if g + 2 < groups:
            ff_load(g + 2).start()
            ff_y_copy(g + 2).start()
        for d in (1, 2, 3):
            ff_z_copy(g, d).start()

    def ff_z_event(g):
        for d in (1, 2, 3):
            ff_z_copy(g, d).wait_recv()
        for n in range(g * GROUP, (g + 1) * GROUP):
            total = ff_y[n, z].astype(F32)
            for d in (1, 2, 3):
                total += ff_z[d - 1, n].astype(F32)
            if n < half:
                up_sum[:, n * CHUNK:(n + 1) * CHUNK] = total
            else:
                down_sum[:, (n - half) * CHUNK:(n - half + 1) * CHUNK] = total

    def at_c_copy(p):
        return remote(whole.at[p, :, :, 1 - core], mate.at[p], acs.at[p], acr.at[p], core_mate)

    def at_y_copy(p):
        return remote(mate.at[p, :, 1 - y], at_y.at[p], ays.at[p], ayr.at[p], y_mate)

    def at_z_copy(p, d):
        n = p * 3 + d - 1
        return remote(
            at_y.at[p, (z + d) % Z_SIZE], at_z.at[d - 1, p], azs.at[n], azr.at[n], z_mates[d - 1]
        )

    def at_c_event(p):
        at_c_copy(p).wait_recv()
        mate[p] = (mate[p].astype(F32) + whole[p, :, :, core].astype(F32)).astype(BF)
        at_y_copy(p).start()

    def at_y_event(p):
        at_y_copy(p).wait_recv()
        at_y[p] = (at_y[p].astype(F32) + mate[p, :, y].astype(F32)).astype(BF)
        for d in (1, 2, 3):
            at_z_copy(p, d).start()

    def at_z_event(p):
        for d in (1, 2, 3):
            at_z_copy(p, d).wait_recv()
        total = at_y[p, z].astype(F32)
        for d in (1, 2, 3):
            total += at_z[d - 1, p].astype(F32)
        cut = slice(p * PAIR, (p + 1) * PAIR)
        for kind in range(3):
            qkv_sum[kind, :, cut] = total[:, kind * PAIR:(kind + 1) * PAIR]
        out_sum[:, cut] = total[:, 3 * PAIR:]

    def out_copy(b):
        return pltpu.make_async_copy(out_ref.at[part(b), :], out_hbm.at[part(b), :], outs.at[b])

    def tokens_copy(b):
        return pltpu.make_async_copy(
            tokens_ref.at[part(b), :], tokens_hbm.at[part(b), :], outs.at[blocks + b]
        )

    def branch_event(b):
        branch_copy(b).wait_recv()
        load(b).wait()
        branch_load(b).wait()
        both = branch_own[b % 2].astype(F32) + branch_x[part(b), :].astype(F32)
        out_ref[part(b), :] = (held[b % 2] + both + as_row(down_bias)).astype(BF)
        out_copy(b).start()
        taken(b)
        if b + 2 < blocks:
            branch_load(b + 2).start()

    for b in range(blocks):
        branch_copy(b).start()
    for n in range(2):
        load(n).start()
        branch_load(n).start()
        ff_load(n).start()
        ff_y_copy(n).start()

    plan = {
        2: [(at_c_event, 0), (ff_y_event, 0), (branch_event, 0)], 4: [(at_c_event, 1)],
        5: [(ff_y_event, 1), (branch_event, 1)], 6: [(at_c_event, 2)],
    }

    low_lanes = lanes() < HEAD_DIM
    zero = jnp.zeros((1, PAIR), BF)

    def stacked(strip):
        return jnp.concatenate(
            [jnp.where(low_lanes, strip, zero), jnp.where(low_lanes, zero, strip)], axis=0
        )

    def attend(t, _):
        p, b = t // strips, t % strips
        rows = pl.ds(pl.multiple_of(b * STRIP, STRIP), STRIP)

        @pl.when(b == 0)
        def _():
            for p_now in range(pairs):
                @pl.when(p == p_now)
                def _(p_now=p_now):
                    for copy in pair_loads(p_now):
                        copy.wait()
            key_t[...] = turn(k_ref[p])
            key_acc[...] = jnp.zeros_like(key_acc)
            value_acc[...] = jnp.zeros_like(value_acc)

        queries, grads = stacked(q_ref[p, rows, :]), stacked(gm_ref[p, rows, :])
        more = jnp.concatenate(
            [query_more[2 * p, rows, :], query_more[2 * p + 1, rows, :]], axis=0
        )
        mixture = mix_ref[p, rows, :]
        product = grads.astype(F32) * jnp.concatenate([mixture, mixture], axis=0).astype(F32)
        inner = -jnp.sum(product, axis=-1, keepdims=True)
        query_side = jnp.concatenate([queries, more], axis=1)
        grad_side = jnp.concatenate([grads, in_pieces(inner, 0, 0.0)], axis=1)
        to_queries = jnp.zeros((PAIR, 2 * STRIP), F32)
        for n in range(blocks):
            keys = jnp.concatenate([k_ref[p, part(n), :], key_more[part(n), :]], axis=1)
            values = jnp.concatenate([v_ref[p, part(n), :], one_lanes(BLOCK)], axis=1)
            weights = jnp.exp(dot_rows(keys, query_side)).astype(BF)
            grad_scores = weights * dot_rows(values, grad_side).astype(BF)
            value_acc[part(n), :] += split_sum(weights, grads)
            key_acc[part(n), :] += split_sum(grad_scores, queries)
            to_queries += nn(key_t[:, part(n)], grad_scores)
        own = jnp.concatenate(
            [to_queries[:HEAD_DIM, :STRIP], to_queries[HEAD_DIM:, STRIP:]], axis=0
        )
        dq[p, rows, :] = (turn(own) * 0.125).astype(BF)

        @pl.when(b == strips - 1)
        def _():
            @pl.when(p == 0)
            def _():
                late_loads[0].wait()
                late_loads[1].wait()

            dk[p] = key_acc[...].astype(BF)
            dv[p] = value_acc[...].astype(BF)
            right = jnp.concatenate([dq[p], dk[p], dv[p]], axis=1)
            mixture_all = mix_ref[p]

            def one(plane, _):
                cut = pl.ds(pl.multiple_of(plane * BLOCK, BLOCK), BLOCK)
                both = jnp.concatenate(
                    [nn(normed_t[cut, :], right), nn(ga_t[cut, :], mixture_all)], axis=1
                )
                whole[p, plane] = both.astype(BF).reshape(whole.shape[2:])
                return 0

            lax.fori_loop(0, Z_SIZE, one, 0)
            at_c_copy(p).start()

        for step, events in plan.items():
            @pl.when(t == step)
            def _(events=events):
                for event, n in events:
                    event(n)
        return 0

    lax.fori_loop(0, pairs * strips, attend, 0)
    late_loads[2].wait()
    late_loads[3].wait()

    def gn_copy(b):
        return remote(gn_own.at[b], gn_x.at[b], gs.at[b], gr.at[b], across)

    for b in range(blocks):
        total = jnp.zeros((BLOCK, width), F32)
        for n, grad in enumerate((dq, dk, dv)):
            left = jnp.concatenate([grad[p, part(b), :] for p in range(pairs)], axis=1)
            total += dot_rows(left, wqkv[n])
        gn_own[b] = total.astype(BF)
        gn_copy(b).start()

    at_c_event(3)
    small_own[...] = small_in[...]
    for p in range(pairs):
        first, second = p * PAIR, (pairs + p) * PAIR
        small_own[QV_BIAS:QV_BIAS + 1, first:first + PAIR] = sum_rows(dq[p].astype(F32))
        small_own[QV_BIAS:QV_BIAS + 1, second:second + PAIR] = sum_rows(dv[p].astype(F32))
    branch_event(2)
    ff_y_event(2)
    branch_event(3)
    ff_z_event(0)
    ff_y_event(3)
    at_y_event(0)
    ff_z_event(1)
    gains = as_row(gain)
    for b in range(blocks):
        gn_copy(b).wait()
        load(blocks + b).wait()
        grad = gn_own[b].astype(F32) + gn_x[b].astype(F32)
        centred, scale = norm_stats(x_ref[part(b), :].astype(F32))
        unit = centred * scale
        small_own[LN1_GAIN:LN1_GAIN + 1, :] += sum_rows(grad * unit)
        small_own[LN1_BIAS:LN1_BIAS + 1, :] += sum_rows(grad)
        tokens_ref[part(b), :] = (
            held[b % 2] + norm_back(grad * gains, unit, scale)
        ).astype(BF)
        tokens_copy(b).start()
        taken(blocks + b)
        if b == 0:
            at_y_event(1)
            at_y_event(2)
            ff_z_event(2)
        if b == 1:
            at_y_event(3)
            ff_z_event(3)
        if b == 2:
            at_z_event(0)
            at_z_event(1)
            at_z_event(2)

    def small_z_copy(d):
        return remote(small_own, small_z.at[z], ms.at[d - 1], mr.at[d - 1], z_mates[d - 1])

    def small_z_arrival(d):
        slot = small_z.at[(z + Z_SIZE - d) % Z_SIZE]
        return remote(slot, slot, ms.at[d - 1], mr.at[d - 1], z_mates[d - 1])

    for d in (1, 2, 3):
        small_z_copy(d).start()
    small_z[z] = small_own[...]
    at_z_event(3)
    for d in (1, 2, 3):
        small_z_arrival(d).wait_recv()
    small_y[0] = small_z[0] + small_z[1] + small_z[2] + small_z[3]
    y_sum = remote(small_y.at[0], small_y.at[1], ms.at[3], mr.at[3], y_mate)
    y_sum.start()
    y_sum.wait()
    small_c[0] = small_y[0] + small_y[1]
    c_sum = remote(small_c.at[0], small_c.at[1], ms.at[4], mr.at[4], core_mate)
    c_sum.start()
    c_sum.wait()
    small = small_c[0] + small_c[1]
    for kind, target in (
        (LN1_GAIN, gain_one), (LN1_BIAS, offset_one), (OUT_BIAS, out_small),
        (LN2_GAIN, gain_two), (LN2_BIAS, offset_two), (DOWN_BIAS, down_small),
    ):
        target[...] = small[kind:kind + 1, :].reshape(width)
    cols = pairs * PAIR
    qv_small[0:1, :] = small[QV_BIAS:QV_BIAS + 1, :cols]
    qv_small[1:2, :] = small[QV_BIAS:QV_BIAS + 1, cols:]
    for n in range(up_small.shape[0] // width):
        row = small[UP_BIAS + n:UP_BIAS + n + 1, :]
        up_small[n * width:(n + 1) * width] = row.reshape(width)

    for d in (1, 2, 3):
        small_z_copy(d).wait_send()
    for b in range(blocks):
        out_copy(b).wait()
        tokens_copy(b).wait()
        branch_copy(b).wait_send()
    for g in range(groups):
        ff_y_copy(g).wait_send()
        for d in (1, 2, 3):
            ff_z_copy(g, d).wait_send()
    for p in range(pairs):
        at_c_copy(p).wait_send()
        at_y_copy(p).wait_send()
        for d in (1, 2, 3):
            at_z_copy(p, d).wait_send()


def run_back(
    queries, keys, values, mixture, grad_mixture, query_more, ga_t, normed_t, wqkv, x,
    key_more, gain, down_bias, small, middle, grad_middle, ff_part, branch,
):
    length, width = x.shape
    pairs = queries.shape[0]
    chunks, depth = ff_part.shape[0], ff_part.shape[3]
    groups = chunks // GROUP
    cols, hidden = pairs * PAIR, chunks // 2 * CHUNK
    blocks = length // BLOCK
    dma = pltpu.SemaphoreType.DMA
    rows = pltpu.VMEM((blocks, BLOCK, width), BF)
    by_pair = pltpu.VMEM((pairs, length, PAIR), BF)
    whole_rows = pltpu.VMEM((length, width), BF)
    row = shape_of((width,), F32)
    loaded = (
        queries, keys, values, mixture, grad_mixture, query_more, ga_t, normed_t, wqkv, x
    )
    return pl.pallas_call(
        back_kernel,
        out_shape=[
            shape_of((length, width), BF),
            shape_of((length, width), BF),
            shape_of((3, depth, cols), F32),
            shape_of((depth, cols), F32),
            shape_of((depth, hidden), F32),
            shape_of((depth, hidden), F32),
            row, row, shape_of((2, cols), F32), row, row, row, shape_of((hidden,), F32), row,
        ],
        in_specs=[ANY_SPEC] * 10 + [VMEM_SPEC] * 4 + [ANY_SPEC] * 4,
        out_specs=[ANY_SPEC] * 2 + [VMEM_SPEC] * 12,
        scratch_shapes=[pltpu.VMEM(v.shape, BF) for v in loaded] + [
            whole_rows, whole_rows, pltpu.VMEM((PAIR, length), BF),
            pltpu.VMEM((length, PAIR), F32), pltpu.VMEM((length, PAIR), F32),
            by_pair, by_pair, by_pair,
            pltpu.VMEM((pairs, Z_SIZE, Y_SIZE, CORES, depth, CHUNK), BF),
            pltpu.VMEM((pairs, Z_SIZE, Y_SIZE, depth, CHUNK), BF),
            pltpu.VMEM((pairs, Z_SIZE, depth, CHUNK), BF),
            pltpu.VMEM((3, pairs, depth, CHUNK), BF),
            pltpu.VMEM((chunks, Z_SIZE, depth, CHUNK), BF),
            pltpu.VMEM((3, chunks, depth, CHUNK), BF),
            rows, rows, whole_rows,
            pltpu.VMEM((2, BLOCK, width), BF),
            pltpu.VMEM((2, GROUP, Z_SIZE, depth, CHUNK), BF),
            pltpu.VMEM((2, BLOCK, width), F32),
            pltpu.VMEM(small.shape, F32),
            pltpu.VMEM((Z_SIZE,) + small.shape, F32),
            pltpu.VMEM((2,) + small.shape, F32),
            pltpu.VMEM((2,) + small.shape, F32),
            dma((blocks,)), dma((blocks,)), dma((groups,)), dma((groups,)),
            dma((3 * groups,)), dma((3 * groups,)), dma((pairs,)), dma((pairs,)),
            dma((pairs,)), dma((pairs,)), dma((3 * pairs,)), dma((3 * pairs,)),
            dma((blocks,)), dma((blocks,)), dma((2,)), dma((5,)), dma((5,)), dma((2,)), dma((2,)),
            dma((6 * pairs,)), dma((4,)), dma((2 * blocks,)),
        ],
        compiler_params=pltpu.CompilerParams(
            collective_id=2, has_side_effects=True, vmem_limit_bytes=VMEM_LIMIT
        ),
    )(*loaded, key_more, gain, down_bias, small, middle, grad_middle, ff_part, branch)


def hand_over_kernel(*refs):
    *refs, sems = refs
    count = len(refs) // 3
    refs = refs[:count] + refs[2 * count:] + refs[count:2 * count]
    loads, stores = (
        [
            pltpu.make_async_copy(refs[a * count + n], refs[b * count + n], sems.at[a, n])
            for n in range(count)
        ]
        for a, b in ((0, 1), (1, 2))
    )
    for load in loads:
        load.start()
    for load, store in zip(loads, stores):
        load.wait()
        store.start()
    for store in stores:
        store.wait()


def hand_over(results):
    return pl.pallas_call(
        hand_over_kernel,
        out_shape=[shape_of(v.shape, v.dtype) for v in results],
        in_specs=[ANY_SPEC] * len(results),
        out_specs=[ANY_SPEC] * len(results),
        scratch_shapes=[pltpu.VMEM(v.shape, v.dtype) for v in results] + [
            pltpu.SemaphoreType.DMA((2, len(results)))
        ],
        compiler_params=pltpu.CompilerParams(vmem_limit_bytes=VMEM_LIMIT),
    )(*results)


def fast_body(
    tokens, segment_ids, context_flags, ln1_gain, ln1_bias, qkv_weight, qv_bias, out_weight,
    out_bias, ln2_gain, ln2_bias, up_weight, up_bias, down_weight, down_bias, cotangent,
):
    x, dy = tokens[0], cotangent[0]
    (
        queries, keys, values, mixture, middle, normed_t, wff, key_more, query_more,
        normed_two_t, active, slope,
    ) = run_fwd(
        x, segment_ids, context_flags, ln1_gain, ln1_bias, qv_bias, out_bias, ln2_gain,
        ln2_bias, up_bias, qkv_weight, out_weight, up_weight, down_weight.T,
    )
    branch, grad_middle, ga_t, grad_mixture, ff_part, small = run_ff(
        middle, dy, wff, normed_two_t, active, slope, ln2_gain, out_weight
    )
    (
        output, tokens_grad, qkv_grad, out_grad, up_grad, down_grad, gain_one, offset_one,
        qv_grad, out_bias_grad, gain_two, offset_two, up_bias_grad, down_bias_grad,
    ) = hand_over(run_back(
        queries, keys, values, mixture, grad_mixture, query_more, ga_t, normed_t, qkv_weight, x,
        key_more, ln1_gain, down_bias, small, middle, grad_middle, ff_part, branch,
    ))
    return (
        output[None], tokens_grad[None], gain_one, offset_one, qkv_grad, qv_grad, out_grad.T,
        out_bias_grad, gain_two, offset_two, up_grad, up_bias_grad, down_grad.T, down_bias_grad,
    )


def solution(mesh):
    chosen = generic_body
    if mesh.shape["head"] == 2 and mesh.shape["seq"] == SEQ_SIZE:
        chosen = fast_body
    return jax.shard_map(
        chosen,
        mesh=mesh,
        in_specs=(
            P("seq", None, None),
            P("seq", None),
            P("seq", None),
            P(),
            P(),
            P(None, None, "head"),
            P(None, "head"),
            P("head", None),
            P(),
            P(),
            P(),
            P("seq", "head"),
            P("head"),
            P("head", "seq"),
            P(),
            P("seq", None, None),
        ),
        out_specs=(
            P("seq", None, None),
            P("seq", None, None),
            P(),
            P(),
            P(None, "seq", "head"),
            P(None, "head"),
            P("head", "seq"),
            P(),
            P(),
            P(),
            P("seq", "head"),
            P("head"),
            P("head", "seq"),
            P(),
        ),
        check_vma=False,
    )
```

```python
import math

import jax
import jax.numpy as jnp
from jax import lax
from jax.experimental import pallas as pl
from jax.experimental.pallas import tpu as pltpu
from jax.sharding import PartitionSpec as P

HEAD_DIM = 64


def layer_norm(values_in, scaling, offset):
    middle = jnp.mean(values_in, axis=-1, keepdims=True)
    centred = values_in - middle
    spread = jnp.mean(centred * centred, axis=-1, keepdims=True)
    return centred * lax.rsqrt(spread + 1e-05) * scaling + offset


def gelu_exact(values_in):
    return 0.5 * values_in * (1.0 + jax.scipy.special.erf(values_in * 0.7071067811865476))


def dot_rows(left, right):
    return lax.dot_general(
        left, right, (((1,), (1,)), ((), ())), preferred_element_type=jnp.float32
    )


def dot_cols(left, right):
    return lax.dot_general(
        left, right, (((0,), (0,)), ((), ())), preferred_element_type=jnp.float32
    )


def masked_scores(block_query, seq_keys, block_segments, seq_segments, seq_context, factor):
    raw_scores = (
        jnp.einsum("qhd,khd->hqk", block_query, seq_keys, preferred_element_type=jnp.float32)
        * factor
    )
    allowed = (block_segments[:, None] == seq_segments[None, :]) & (seq_context[None, :] == 1)
    return jnp.where(allowed[None], raw_scores, -1e30)


def generic_body(
    tokens,
    segment_ids,
    context_flags,
    ln1_gain,
    ln1_bias,
    qkv_weight,
    qv_bias,
    out_weight,
    out_bias,
    ln2_gain,
    ln2_bias,
    up_weight,
    up_bias,
    down_weight,
    down_bias,
    cotangent,
):
    seq_count, length, width = tokens.shape
    row_count = seq_count * length
    local_cols = qkv_weight.shape[2]
    head_count = local_cols // HEAD_DIM
    factor = 1.0 / math.sqrt(HEAD_DIM)
    block = min(512, length)
    blocks = length // block
    gain_one = ln1_gain.astype(jnp.float32)
    offset_one = ln1_bias.astype(jnp.float32)
    gain_two = ln2_gain.astype(jnp.float32)
    offset_two = ln2_bias.astype(jnp.float32)
    flat_in = tokens.astype(jnp.float32).reshape(row_count, width)
    normed_f, norm_one_pull = jax.vjp(layer_norm, flat_in, gain_one, offset_one)
    normed = normed_f.astype(jnp.bfloat16)
    queries = (
        jnp.dot(normed, qkv_weight[0], preferred_element_type=jnp.float32)
        + qv_bias[0].astype(jnp.float32)
    ).astype(jnp.bfloat16)
    key_rows = jnp.dot(normed, qkv_weight[1], preferred_element_type=jnp.float32).astype(
        jnp.bfloat16
    )
    value_rows = (
        jnp.dot(normed, qkv_weight[2], preferred_element_type=jnp.float32)
        + qv_bias[1].astype(jnp.float32)
    ).astype(jnp.bfloat16)

    def per_sequence(array):
        return array.reshape(seq_count, length, head_count, HEAD_DIM)

    def attend_sequence(member):
        seq_query, seq_keys, seq_values, seq_segments, seq_context = member

        def attend_block(portion):
            block_query, block_segments = portion
            scores = masked_scores(
                block_query, seq_keys, block_segments, seq_segments, seq_context, factor
            )
            row_top = jnp.max(scores, axis=-1, keepdims=True)
            exponent = jnp.exp(scores - row_top)
            row_total = jnp.sum(exponent, axis=-1, keepdims=True)
            soft_weights = (exponent / row_total).astype(jnp.bfloat16)
            block_mix = jnp.einsum(
                "hqk,khd->qhd", soft_weights, seq_values, preferred_element_type=jnp.float32
            )
            return (block_mix.astype(jnp.bfloat16), row_top + jnp.log(row_total))

        return lax.map(
            attend_block,
            (
                seq_query.reshape(blocks, block, head_count, HEAD_DIM),
                seq_segments.reshape(blocks, block),
            ),
        )

    mixture, log_totals = lax.map(
        attend_sequence,
        (
            per_sequence(queries),
            per_sequence(key_rows),
            per_sequence(value_rows),
            segment_ids,
            context_flags,
        ),
    )
    mixture = mixture.reshape(row_count, local_cols)
    partial_out = jnp.dot(mixture, out_weight, preferred_element_type=jnp.float32)
    grad_rows_all = cotangent.reshape(row_count, width)
    grad_float_all = grad_rows_all.astype(jnp.float32)
    grad_down_bias = jnp.sum(grad_float_all, axis=0)
    attended = lax.psum(partial_out, "head") + out_bias.astype(jnp.float32)
    middle_state = flat_in + attended
    normed_two_f, norm_two_pull = jax.vjp(layer_norm, middle_state, gain_two, offset_two)
    normed_two = normed_two_f.astype(jnp.bfloat16)
    up_part, down_part, up_shift = (
        lax.all_gather(up_weight, "head", axis=1, tiled=True),
        lax.all_gather(down_weight, "head", axis=0, tiled=True),
        lax.all_gather(up_bias, "head", axis=0, tiled=True),
    )
    up_full, down_full = (
        lax.all_gather(up_part, "seq", axis=0, tiled=True),
        lax.all_gather(down_part, "seq", axis=1, tiled=True),
    )
    before = jnp.dot(normed_two, up_full, preferred_element_type=jnp.float32) + up_shift.astype(
        jnp.float32
    )
    active_f, gelu_pull = jax.vjp(gelu_exact, before)
    active = active_f.astype(jnp.bfloat16)
    branch_out = jnp.dot(active, down_full, preferred_element_type=jnp.float32)
    final_rows = (middle_state + branch_out + down_bias.astype(jnp.float32)).astype(jnp.bfloat16)
    output = final_rows.reshape(tokens.shape)
    grad_float = grad_rows_all.astype(jnp.float32)
    grad_down = dot_cols(active, grad_rows_all)
    grad_active = dot_rows(grad_rows_all, down_full)
    (grad_before_f,) = gelu_pull(grad_active)
    grad_before = grad_before_f.astype(jnp.bfloat16)
    grad_up = dot_cols(normed_two, grad_before)
    grad_up_bias = jnp.sum(grad_before.astype(jnp.float32), axis=0)
    grad_normed_two = dot_rows(grad_before, up_full)
    grad_middle_norm, grad_gain_two, grad_offset_two = norm_two_pull(grad_normed_two)
    grad_middle = grad_float + grad_middle_norm
    ff_part = up_weight.shape[1]
    start_col = lax.axis_index("head") * ff_part
    grad_up = lax.dynamic_slice_in_dim(grad_up, start_col, ff_part, 1)
    grad_down = lax.dynamic_slice_in_dim(grad_down, start_col, ff_part, 0)
    grad_up_bias = lax.dynamic_slice_in_dim(grad_up_bias, start_col, ff_part, 0)
    grad_attended = grad_middle.astype(jnp.bfloat16)
    grad_out_bias = jnp.sum(grad_attended.astype(jnp.float32), axis=0)
    grad_out = dot_cols(mixture, grad_attended)
    grad_mixture = dot_rows(grad_attended, out_weight).astype(jnp.bfloat16)

    def back_sequence(member):
        seq_query, seq_keys, seq_values, seq_grad, seq_logs, seq_segments, seq_context = member

        def back_block(carry, portion):
            key_acc, value_acc = carry
            block_query, block_grad, block_logs, block_segments = portion
            scores = masked_scores(
                block_query, seq_keys, block_segments, seq_segments, seq_context, factor
            )
            soft_weights = jnp.exp(scores - block_logs)
            value_acc = value_acc + jnp.einsum(
                "hqk,qhd->khd",
                soft_weights.astype(jnp.bfloat16),
                block_grad,
                preferred_element_type=jnp.float32,
            )
            grad_soft = jnp.einsum(
                "qhd,khd->hqk", block_grad, seq_values, preferred_element_type=jnp.float32
            )
            row_inner = jnp.sum(soft_weights * grad_soft, axis=-1, keepdims=True)
            grad_scores = (soft_weights * (grad_soft - row_inner)).astype(jnp.bfloat16)
            grad_query = (
                jnp.einsum(
                    "hqk,khd->qhd", grad_scores, seq_keys, preferred_element_type=jnp.float32
                )
                * factor
            )
            key_acc = (
                key_acc
                + jnp.einsum(
                    "hqk,qhd->khd", grad_scores, block_query, preferred_element_type=jnp.float32
                )
                * factor
            )
            return ((key_acc, value_acc), grad_query)

        empty = jnp.zeros((length, head_count, HEAD_DIM), jnp.float32)
        (key_acc, value_acc), grad_query = lax.scan(
            back_block,
            (empty, empty),
            (
                seq_query.reshape(blocks, block, head_count, HEAD_DIM),
                seq_grad.reshape(blocks, block, head_count, HEAD_DIM),
                seq_logs,
                seq_segments.reshape(blocks, block),
            ),
        )
        return (grad_query, key_acc, value_acc)

    grad_queries, grad_keys, grad_values = lax.map(
        back_sequence,
        (
            per_sequence(queries),
            per_sequence(key_rows),
            per_sequence(value_rows),
            per_sequence(grad_mixture),
            log_totals,
            segment_ids,
            context_flags,
        ),
    )
    grad_queries = grad_queries.reshape(row_count, local_cols).astype(jnp.bfloat16)
    grad_keys = grad_keys.reshape(row_count, local_cols).astype(jnp.bfloat16)
    grad_values = grad_values.reshape(row_count, local_cols).astype(jnp.bfloat16)
    grad_qv_bias = jnp.stack(
        [
            jnp.sum(grad_queries.astype(jnp.float32), axis=0),
            jnp.sum(grad_values.astype(jnp.float32), axis=0),
        ]
    )
    grad_qkv = jnp.stack(
        [dot_cols(normed, grad_queries), dot_cols(normed, grad_keys), dot_cols(normed, grad_values)]
    )
    grad_normed = (
        dot_rows(grad_queries, qkv_weight[0])
        + dot_rows(grad_keys, qkv_weight[1])
        + dot_rows(grad_values, qkv_weight[2])
    )
    grad_normed = lax.psum(grad_normed, "head")
    grad_input_norm, grad_gain_one, grad_offset_one = norm_one_pull(grad_normed)
    tokens_grad = (grad_middle + grad_input_norm).astype(jnp.bfloat16).reshape(tokens.shape)
    summed_qkv, summed_out, summed_up, summed_down = (
        lax.psum_scatter(
            grad_qkv.astype(jnp.bfloat16), "seq", scatter_dimension=1, tiled=True
        ).astype(jnp.float32),
        lax.psum_scatter(
            grad_out.astype(jnp.bfloat16), "seq", scatter_dimension=1, tiled=True
        ).astype(jnp.float32),
        lax.psum_scatter(
            grad_up.astype(jnp.bfloat16), "seq", scatter_dimension=0, tiled=True
        ).astype(jnp.float32),
        lax.psum_scatter(
            grad_down.astype(jnp.bfloat16), "seq", scatter_dimension=1, tiled=True
        ).astype(jnp.float32),
    )
    smalls = lax.psum(
        (
            grad_gain_one,
            grad_offset_one,
            grad_qv_bias,
            grad_out_bias,
            grad_gain_two,
            grad_offset_two,
            grad_up_bias,
            grad_down_bias,
        ),
        "seq",
    )
    return (
        output,
        tokens_grad,
        smalls[0],
        smalls[1],
        summed_qkv,
        smalls[2],
        summed_out,
        smalls[3],
        smalls[4],
        smalls[5],
        summed_up,
        smalls[6],
        summed_down,
        smalls[7],
    )


MESH = pl.DeviceIdType.MESH
BF = jnp.bfloat16
F32 = jnp.float32
BLOCK = 256
STRIP = 512
PIECE = 128
WIDE = 1024
GROUP = 2
CHUNK = 512
PAIR = 2 * HEAD_DIM
Z_SIZE, Y_SIZE, CORES = 4, 2, 2
SEQ_SIZE = Z_SIZE * Y_SIZE * CORES
HOP = Y_SIZE * CORES
TABLES = 8
FAR = -1e30
VMEM_LIMIT = 62 * 2**20
INV_ROOT_TWO = 0.7071067811865476
INV_ROOT_TWO_PI = 0.3989422804014327
LN1_GAIN, LN1_BIAS, QV_BIAS, OUT_BIAS, LN2_GAIN, LN2_BIAS, UP_BIAS, DOWN_BIAS = 0, 1, 2, 3, 4, 5, 6, 8
SMALL_ROWS = 16
VMEM_SPEC = pl.BlockSpec(memory_space=pltpu.VMEM)
ANY_SPEC = pl.BlockSpec(memory_space=pl.ANY)


def shape_of(dims, dtype):
    return jax.ShapeDtypeStruct(tuple(dims), dtype)


def nn(left, right):
    return jnp.dot(left, right, preferred_element_type=F32)


def split_sum(left, right):
    parts = [
        nn(left[:, n:n + BLOCK], right[n:n + BLOCK]) for n in range(0, left.shape[1], BLOCK)
    ]
    while len(parts) > 1:
        parts = [a + b for a, b in zip(parts[::2], parts[1::2])]
    return parts[0]


def turn(block):
    return jnp.transpose(block)


def sum_rows(block):
    return jnp.sum(block, axis=0, keepdims=True)


def place():
    me = lax.axis_index("seq")
    head = lax.axis_index("head")
    core = me % 2
    y = (me // 2) % 2
    across = {"seq": me, "head": 1 - head}
    core_mate = {"seq": me + 1 - 2 * core, "head": head}
    y_mate = {"seq": me + 2 - 4 * y, "head": head}
    z_mates = [{"seq": (me + HOP * d) % SEQ_SIZE, "head": head} for d in (1, 2, 3)]
    return me, head, core, y, across, core_mate, y_mate, z_mates


def greet(others):
    barrier = pltpu.get_barrier_semaphore()
    for other in others:
        pl.semaphore_signal(barrier, inc=1, device_id=other, device_id_type=MESH)
    pl.semaphore_wait(barrier, len(others))


def remote(src, dst, send_sem, recv_sem, other):
    return pltpu.make_async_remote_copy(
        src_ref=src, dst_ref=dst, send_sem=send_sem, recv_sem=recv_sem,
        device_id=other, device_id_type=MESH,
    )


def norm_stats(rows):
    middle = jnp.mean(rows, axis=-1, keepdims=True)
    centred = rows - middle
    spread = jnp.mean(centred * centred, axis=-1, keepdims=True)
    return centred, lax.rsqrt(spread + 1e-05)


def norm_back(inner, unit, scale):
    return scale * (
        inner
        - jnp.mean(inner, axis=-1, keepdims=True)
        - unit * jnp.mean(inner * unit, axis=-1, keepdims=True)
    )


def as_row(vector):
    return vector[...].astype(F32).reshape(1, -1)


def lanes():
    return lax.broadcasted_iota(jnp.int32, (1, PAIR), 1)


def in_pieces(column, first, rest):
    high = column.astype(BF).astype(F32)
    mid = (column - high).astype(BF).astype(F32)
    low = column - high - mid
    at = lanes()
    return jnp.where(
        at == first, high, jnp.where(at == first + 1, mid, jnp.where(at == first + 2, low, rest))
    ).astype(BF)


def one_lanes(length):
    return jnp.broadcast_to(jnp.where(lanes() < 3, 1.0, 0.0).astype(BF), (length, PAIR))


def fwd_kernel(
    x_ref, seg_ref, context, gain, offset, qv_bias, out_bias, gain_two, offset_two, up_bias,
    wqkv, wout, up_shard, down_shard,
    q_out, k_out, v_out, mix_out, mid_out, normed_out, wff_out, key_out, query_out,
    normed_two_out, active_out, slope_out,
    wff, q_ref, k_ref, v_ref, mix_ref, mid_ref, normed_t, key_more, query_more,
    normed_two_t, active, slope, bias_row, mask_more, wout_x, mix_x,
    zs, zr, ys, yr, cs, cr, xs, xr, local, outs,
):
    length, width = x_ref.shape
    blocks = length // BLOCK
    pairs = q_ref.shape[0]
    cols = pairs * PAIR
    me, head, core, y, across, core_mate, y_mate, _ = place()
    z = me // HOP
    above = {"seq": (me + HOP) % SEQ_SIZE, "head": head}
    below = {"seq": (me + SEQ_SIZE - HOP) % SEQ_SIZE, "head": head}
    own = [
        pltpu.make_async_copy(shard, wff.at[u, me], local.at[u])
        for u, shard in enumerate((up_shard, down_shard))
    ]
    own[0].start()
    own[1].start()
    greet([across, core_mate, y_mate, above, below])

    half = wout.shape[0] // 2
    here = pl.ds(pl.multiple_of(core * half, half), half)
    beside = pl.ds(pl.multiple_of((1 - core) * half, half), half)
    out_copy = remote(wout.at[here, :], wout_x.at[here, :], xs.at[0], xr.at[0], across)
    out_pass = remote(wout_x.at[here, :], wout_x.at[here, :], cs.at[28], cr.at[28], core_mate)
    out_arrival = remote(
        wout_x.at[beside, :], wout_x.at[beside, :], cs.at[28], cr.at[28], core_mate
    )
    out_copy.start()

    flows = [(0, 0)] + [(way, s) for s in (1, 2, 3) for way in (0, 1)]

    def there(way, s):
        return (z >= s) if way == 0 else (z + s < Z_SIZE)

    def source(base, way, s):
        away = SEQ_SIZE - HOP * s if way == 0 else HOP * s
        return (base + away) % SEQ_SIZE

    def z_copy(u, way, s):
        n = (u * 2 + way) * 3 + s - 1
        j = source(me, way, s - 1)
        return remote(wff.at[u, j], wff.at[u, j], zs.at[n], zr.at[n], above if way == 0 else below)

    def z_arrival(u, way, s):
        n = (u * 2 + way) * 3 + s - 1
        slot = wff.at[u, source(me, way, s)]
        return remote(slot, slot, zs.at[n], zr.at[n], above)

    def z_goes_on(way):
        return (z < Z_SIZE - 1) if way == 0 else (z > 0)

    def y_copy(u, f):
        n = u * 7 + f
        j = source(me, *flows[f])
        return remote(wff.at[u, j], wff.at[u, j], ys.at[n], yr.at[n], y_mate)

    def y_arrival(u, f):
        n = u * 7 + f
        slot = wff.at[u, source(me + 2 - 4 * y, *flows[f])]
        return remote(slot, slot, ys.at[n], yr.at[n], y_mate)

    def c_copy(u, f, from_y):
        n = (u * 2 + from_y) * 7 + f
        j = source(me + from_y * (2 - 4 * y), *flows[f])
        return remote(wff.at[u, j], wff.at[u, j], cs.at[n], cr.at[n], core_mate)

    def c_arrival(u, f, from_y):
        n = (u * 2 + from_y) * 7 + f
        slot = wff.at[u, source(me + 1 - 2 * core + from_y * (2 - 4 * y), *flows[f])]
        return remote(slot, slot, cs.at[n], cr.at[n], core_mate)

    def for_flow(f, do):
        if f == 0:
            do()
        else:
            pl.when(there(*flows[f]))(do)

    def for_step(s, do):
        for f, (way, step) in enumerate(flows):
            if step == s:
                for_flow(f, lambda f=f, way=way: do(f, way))

    def z_event(u, s):
        def one(f, way):
            z_arrival(u, way, s).wait_recv()
            if s < 3:
                pl.when(z_goes_on(way))(lambda: z_copy(u, way, s + 1).start())
            y_copy(u, f).start()
            c_copy(u, f, 0).start()
        for_step(s, one)
        if u == 0 and s == 1:
            start_z(1)
        if u == 0 and s == 2:
            y_copy(1, 0).start()
            c_copy(1, 0, 0).start()
        if u == 0 and s == 3:
            out_copy.wait_recv()
            out_pass.start()

    def y_event(u, s):
        def one(f, way):
            y_arrival(u, f).wait_recv()
            c_copy(u, f, 1).start()
        for_step(s, one)

    def start_z(u):
        for way in (0, 1):
            pl.when(z_goes_on(way))(lambda way=way: z_copy(u, way, 1).start())

    own[0].wait()
    start_z(0)
    y_copy(0, 0).start()
    c_copy(0, 0, 0).start()
    own[1].wait()

    plan = {
        2: [(z_event, 0, 1), (y_event, 0, 0)], 4: [(z_event, 0, 2)], 5: [(y_event, 0, 1)],
        6: [(z_event, 0, 3)], 7: [(z_event, 1, 1)], 8: [(y_event, 0, 2), (y_event, 1, 0)],
        9: [(z_event, 1, 2)], 10: [(y_event, 0, 3)], 11: [(z_event, 1, 3)],
    }

    def tick(t):
        for step, events in plan.items():
            @pl.when(t == step)
            def _(events=events):
                for event, u, s in events:
                    event(u, s)

    at = lax.broadcasted_iota(jnp.int32, (PAIR, length), 0)
    same = at == seg_ref[...]
    hidden = context[...] != 1
    ones = jnp.logical_and(at > TABLES, at < TABLES + 4)
    key_side = jnp.logical_or(
        jnp.logical_and(at < TABLES, same),
        jnp.logical_or(jnp.logical_and(at == TABLES, hidden), ones),
    )
    query_side = jnp.logical_and(at <= TABLES, jnp.logical_not(same))
    key_more[...] = turn(jnp.where(key_side, 1.0, 0.0)).astype(BF)
    mask_more[...] = turn(jnp.where(query_side, FAR, 0.0)).astype(BF)

    keep = [
        pltpu.make_async_copy(here, there, outs.at[n])
        for n, (here, there) in enumerate(
            (
                (q_ref, q_out), (k_ref, k_out), (v_ref, v_out), (normed_t, normed_out),
                (key_more, key_out), (query_more, query_out), (mix_ref, mix_out),
            )
        )
    ]
    gains, offsets = as_row(gain), as_row(offset)
    query_bias = qv_bias[0:1, :].astype(F32)
    value_bias = qv_bias[1:2, :].astype(F32)

    def project(b, _):
        rows = pl.ds(pl.multiple_of(b * BLOCK, BLOCK), BLOCK)
        centred, scale = norm_stats(x_ref[rows, :].astype(F32))
        block = (centred * scale * gains + offsets).astype(BF)
        normed_t[:, rows] = turn(block)
        queries = ((nn(block, wqkv[0]) + query_bias).astype(BF) * 0.125).astype(BF)
        keys = nn(block, wqkv[1]).astype(BF)
        values = (nn(block, wqkv[2]) + value_bias).astype(BF)
        for p in range(pairs):
            part = slice(p * PAIR, (p + 1) * PAIR)
            q_ref[p, rows, :] = queries[:, part]
            k_ref[p, rows, :] = keys[:, part]
            v_ref[p, rows, :] = values[:, part]
        tick(b)
        return 0

    lax.fori_loop(0, blocks, project, 0)
    for n in range(5):
        keep[n].start()

    low_lanes = lanes() < HEAD_DIM
    zero = jnp.zeros((1, PAIR), BF)

    def mixture_copy(t):
        rows = pl.ds(pl.multiple_of(t // pairs * STRIP, STRIP), STRIP)
        return remote(
            mix_ref.at[t % pairs, rows, :], mix_x.at[t % pairs, rows, :], xs.at[1 + t],
            xr.at[1 + t], across,
        )

    per_step = STRIP // BLOCK

    def attend(t, _):
        b, p = t // pairs, t % pairs
        keys = jnp.concatenate([k_ref[p], key_more[...]], axis=1)
        values = jnp.concatenate([v_ref[p], one_lanes(length)], axis=1)
        chains = []
        for n in range(per_step):
            rows = pl.ds(pl.multiple_of(b * STRIP + n * BLOCK, BLOCK), BLOCK)
            queries, more = q_ref[p, rows, :], mask_more[rows, :]
            for low in (0, 1):
                own_lanes = jnp.logical_not(low_lanes) if low else low_lanes
                left = jnp.concatenate([jnp.where(own_lanes, queries, zero), more], axis=1)
                chains.append((rows, low, more, dot_rows(left, keys)))
        parts = []
        for rows, low, more, scores in chains:
            top = jnp.max(scores, axis=-1, keepdims=True)
            mixed = nn(jnp.exp(scores - top).astype(BF), values)
            total = mixed[:, PAIR:PAIR + 1]
            parts.append(mixed[:, :PAIR] / total)
            query_more[2 * p + low, rows, :] = in_pieces(
                -(top + jnp.log(total)), TABLES + 1, more.astype(F32)
            )
            if low:
                mix_ref[p, rows, :] = jnp.where(low_lanes, *parts[-2:]).astype(BF)
        mixture_copy(t).start()
        tick(t + blocks)
        return 0

    lax.fori_loop(0, length // STRIP * pairs, attend, 0)
    keep[5].start()
    keep[6].start()
    out_arrival.wait_recv()
    out_row = as_row(out_bias)

    def mid_copy(b):
        rows = pl.ds(b * BLOCK, BLOCK)
        return pltpu.make_async_copy(mid_ref.at[rows, :], mid_out.at[rows, :], outs.at[7 + b])

    gains_two, offsets_two = as_row(gain_two), as_row(offset_two)
    bias_row[...] = as_row(up_bias)

    def half_copies(b):
        rows = pl.ds(b * BLOCK, BLOCK)
        return [
            pltpu.make_async_copy(
                here.at[:, rows, :], there.at[:, rows, :], outs.at[7 + blocks + 2 * b + n]
            )
            for n, (here, there) in enumerate(((active, active_out), (slope, slope_out)))
        ]

    def up_half(b):
        rows = pl.ds(b * BLOCK, BLOCK)
        centred, scale = norm_stats(mid_ref[rows, :])
        block = (centred * scale * gains_two + offsets_two).astype(BF)
        normed_two_t[:, rows] = turn(block)

        def one(n, _):
            cut = pl.ds(pl.multiple_of(n * WIDE, WIDE), WIDE)
            before = nn(block, wff[0, :, :, cut].reshape(width, WIDE)) + bias_row[:, cut]
            spread = 0.5 * (1.0 + lax.erf(before * INV_ROOT_TWO))
            active[n, rows, :] = (before * spread).astype(BF)
            bell = INV_ROOT_TWO_PI * jnp.exp(before * before * -0.5)
            slope[n, rows, :] = (spread + before * bell).astype(BF)
            return 0

        lax.fori_loop(0, active.shape[0], one, 0)
        for copy in half_copies(b):
            copy.start()

    def arrive(u):
        for f in range(len(flows)):
            def one(f=f):
                for from_y in (0, 1):
                    c_arrival(u, f, from_y).wait_recv()
            for_flow(f, one)

    for b in range(blocks):
        if b % per_step == 0:
            for p in range(pairs):
                mixture_copy(b // per_step * pairs + p).wait_recv()
        rows = pl.ds(b * BLOCK, BLOCK)
        ours = jnp.concatenate([mix_ref[p, rows, :] for p in range(pairs)], axis=-1)
        other = jnp.concatenate([mix_x[p, rows, :] for p in range(pairs)], axis=-1)
        attended = nn(ours, wout[...]) + nn(other, wout_x[...])
        mid_ref[rows, :] = x_ref[rows, :].astype(F32) + (attended + out_row)
        mid_copy(b).start()
        if b == 0:
            arrive(0)
        up_half(b)
        if b < 3:
            y_event(1, b + 1)
    normed_two_keep = pltpu.make_async_copy(
        normed_two_t, normed_two_out, outs.at[7 + 3 * blocks]
    )
    normed_two_keep.start()
    wff_keep = [pltpu.make_async_copy(wff.at[u], wff_out.at[u], local.at[u]) for u in range(2)]
    wff_keep[0].start()
    arrive(1)
    wff_keep[1].start()
    out_copy.wait_send()
    out_pass.wait_send()
    for copy in keep + wff_keep + [normed_two_keep]:
        copy.wait()
    for b in range(blocks):
        for copy in half_copies(b):
            copy.wait()
    for t in range(length // STRIP * pairs):
        mixture_copy(t).wait_send()
    for b in range(blocks):
        mid_copy(b).wait()
    for u in range(2):
        for way in (0, 1):
            pl.when(z_goes_on(way))(lambda u=u, way=way: z_copy(u, way, 1).wait_send())
        for f, (way, s) in enumerate(flows):
            def finish(u=u, f=f, way=way, s=s):
                if f and s < 3:
                    pl.when(z_goes_on(way))(lambda: z_copy(u, way, s + 1).wait_send())
                y_copy(u, f).wait_send()
                for from_y in (0, 1):
                    c_copy(u, f, from_y).wait_send()
            for_flow(f, finish)


def run_fwd(
    x, seg, context, gain, offset, qv_bias, out_bias, gain_two, offset_two, up_bias, wqkv, wout,
    up_weight, down_t,
):
    length, width = x.shape
    pairs = wqkv.shape[2] // PAIR
    blocks = length // BLOCK
    depth, hidden = up_weight.shape
    by_pair, by_head = (pairs, length, PAIR), (2 * pairs, length, PAIR)
    turned = (width, length)
    halves = (hidden // WIDE, length, WIDE)
    steps = length // STRIP * pairs
    dma = pltpu.SemaphoreType.DMA
    return pl.pallas_call(
        fwd_kernel,
        out_shape=[shape_of(by_pair, BF)] * 4 + [
            shape_of((length, width), F32),
            shape_of(turned, BF),
            shape_of((2, SEQ_SIZE, depth, hidden), BF),
            shape_of((length, PAIR), BF),
            shape_of(by_head, BF),
            shape_of((width, length), BF),
            shape_of(halves, BF),
            shape_of(halves, BF),
        ],
        in_specs=[VMEM_SPEC] * 12 + [ANY_SPEC] * 2,
        out_specs=[ANY_SPEC] * 12,
        scratch_shapes=[pltpu.VMEM((2, SEQ_SIZE, depth, hidden), BF)]
        + [pltpu.VMEM(by_pair, BF)] * 4 + [
            pltpu.VMEM((length, width), F32),
            pltpu.VMEM(turned, BF),
            pltpu.VMEM((length, PAIR), BF),
            pltpu.VMEM(by_head, BF),
            pltpu.VMEM((width, length), BF),
            pltpu.VMEM(halves, BF),
            pltpu.VMEM(halves, BF),
            pltpu.VMEM((1, hidden), F32),
            pltpu.VMEM((length, PAIR), BF),
            pltpu.VMEM(wout.shape, BF),
            pltpu.VMEM(by_pair, BF),
            dma((12,)), dma((12,)), dma((14,)), dma((14,)), dma((29,)), dma((29,)),
            dma((1 + steps,)), dma((1 + steps,)), dma((2,)), dma((8 + 3 * blocks,)),
        ],
        compiler_params=pltpu.CompilerParams(
            collective_id=0, has_side_effects=True, vmem_limit_bytes=VMEM_LIMIT
        ),
    )(
        x, seg, context, gain, offset, qv_bias, out_bias, gain_two, offset_two, up_bias, wqkv,
        wout, up_weight, down_t,
    )


def ff_kernel(
    mid_hbm, dy_hbm, wff_hbm, normed_two_hbm, active_hbm, slope_hbm, gain, wout_hbm,
    branch_out, gmid_hbm, ga_out, gm_out, summed, small_ref,
    dy_ref, wff, wout, branch_ref, ga_t, gm_ref, normed_t, dy_t, active, before_grad, gnt_acc, gnt_own, gnt_x, whole, from_mate,
    held, ready,
    xs, xr, cs, cr, ls, ws, ss, ins, outs,
):
    length, width = dy_ref.shape
    blocks = length // BLOCK
    hidden = wff.shape[3]
    half = hidden // WIDE
    chunks = 2 * hidden // CHUNK
    pairs = gm_ref.shape[0]
    me, head, core, y, across, core_mate, y_mate, z_mates = place()
    dy_load = pltpu.make_async_copy(dy_hbm, dy_ref, ins.at[0])
    wout_load = pltpu.make_async_copy(wout_hbm, wout, ins.at[1])

    def step_loads(n):
        cut = pl.ds(n * WIDE, WIDE)
        return [
            pltpu.make_async_copy(src, dst, ins.at[4 + 3 * n + m])
            for m, (src, dst) in enumerate(
                (
                    (wff_hbm.at[1, :, :, cut], wff.at[1, :, :, cut]),
                    (slope_hbm.at[n], before_grad.at[n]),
                    (wff_hbm.at[0, :, :, cut], wff.at[0, :, :, cut]),
                )
            )
        ]

    active_load = pltpu.make_async_copy(active_hbm, active, ins.at[2])
    normed_load = pltpu.make_async_copy(normed_two_hbm, normed_t, ins.at[3])
    dy_load.start()
    for n in range(half):
        for copy in step_loads(n):
            copy.start()
    active_load.start()
    normed_load.start()
    wout_load.start()
    greet([across, core_mate])
    gains = as_row(gain)

    def weight(kind, n):
        cut = pl.ds(pl.multiple_of(n * WIDE, WIDE), WIDE)
        return wff[kind, :, :, cut].reshape(width, WIDE)

    small_ref[...] = jnp.zeros_like(small_ref)

    def load(b):
        rows = pl.ds(b * BLOCK, BLOCK)
        return pltpu.make_async_copy(mid_hbm.at[rows, :], held.at[b % 2], ls.at[b % 2])

    def store(b):
        rows = pl.ds(b * BLOCK, BLOCK)
        return pltpu.make_async_copy(ready.at[b % 2], gmid_hbm.at[rows, :], ws.at[b % 2])

    load(0).start()
    load(1).start()

    def gnt_copy(b):
        return remote(gnt_own.at[b], gnt_x.at[b], xs.at[b], xr.at[b], across)

    def core_copy(n):
        return remote(
            whole.at[n, :, :, 1 - core], from_mate.at[n], cs.at[n], cr.at[n], core_mate
        )

    def forward(t, _):
        b, n = t // half, t % half
        rows = pl.ds(pl.multiple_of(b * BLOCK, BLOCK), BLOCK)

        for n_first in range(half):
            @pl.when(t == n_first)
            def _(n_first=n_first):
                if n_first == 0:
                    dy_load.wait()
                for copy in step_loads(n_first):
                    copy.wait()

        @pl.when(n == 0)
        def _():
            dy_t[:, rows] = turn(dy_ref[rows, :])
            small_ref[DOWN_BIAS:DOWN_BIAS + 1, :] += sum_rows(dy_ref[rows, :].astype(F32))

        up = weight(0, n)
        grad = nn(dy_ref[rows, :], weight(1, n)) * before_grad[n, rows, :].astype(F32)
        grad = grad.astype(BF)
        before_grad[n, rows, :] = grad
        small_ref[pl.ds(UP_BIAS + n, 1), :] += sum_rows(grad.astype(F32))
        back = dot_rows(grad, up)

        @pl.when(n == 0)
        def _():
            gnt_acc[...] = back

        @pl.when(n > 0)
        def _():
            gnt_acc[...] += back

        for b_done in range(blocks):
            @pl.when(t == (b_done + 1) * half - 1)
            def _(b_done=b_done):
                gnt_own[b_done] = gnt_acc[...].astype(BF)
                gnt_copy(b_done).start()
        return 0

    lax.fori_loop(0, blocks * half, forward, 0)

    def weight_grads(left_t, right, first):
        cut_rows = width // Z_SIZE
        per_wide = WIDE // CHUNK

        def one(t, _):
            n, plane = t // Z_SIZE, t % Z_SIZE
            cut = pl.ds(pl.multiple_of(plane * cut_rows, cut_rows), cut_rows)
            total = nn(left_t[cut, :], right[n]).astype(BF)
            for m in range(per_wide):
                piece = total[:, m * CHUNK:(m + 1) * CHUNK]
                whole[first + n * per_wide + m, plane] = piece.reshape(whole.shape[2:])

            @pl.when(plane == Z_SIZE - 1)
            def _():
                for m in range(per_wide):
                    core_copy(first + n * per_wide + m).start()

            return 0

        lax.fori_loop(0, Z_SIZE * half, one, 0)

    active_load.wait()
    normed_load.wait()
    weight_grads(dy_t, active, chunks // 2)
    weight_grads(normed_t, before_grad, 0)

    def branch(b, _):
        rows = pl.ds(pl.multiple_of(b * BLOCK, BLOCK), BLOCK)
        total = dot_rows(active[0, rows, :], weight(1, 0))
        for n in range(1, half):
            total += dot_rows(active[n, rows, :], weight(1, n))
        branch_ref[rows, :] = total.astype(BF)
        return 0

    lax.fori_loop(0, blocks, branch, 0)
    branch_keep = pltpu.make_async_copy(branch_ref, branch_out, outs.at[0])
    branch_keep.start()
    wout_load.wait()

    def ga_copy(b):
        rows = pl.ds(b * BLOCK, BLOCK)
        return pltpu.make_async_copy(ga_t.at[:, rows], ga_out.at[:, rows], outs.at[1 + b])

    def gm_copy(b):
        rows = pl.ds(b * BLOCK, BLOCK)
        return pltpu.make_async_copy(
            gm_ref.at[:, rows, :], gm_out.at[:, rows, :], outs.at[1 + blocks + b]
        )


    def add_mate(n, _):
        core_copy(n).wait()
        both = whole[n, :, :, core].astype(F32) + from_mate[n].astype(F32)
        from_mate[n] = both.astype(BF)
        return 0

    lax.fori_loop(chunks // 2, chunks, add_mate, 0)
    lax.fori_loop(0, chunks // 2, add_mate, 0)
    keep = pltpu.make_async_copy(from_mate, summed, ss.at[0])
    keep.start()

    strips = BLOCK // PIECE
    for b in range(blocks):
        gnt_copy(b).wait()
        load(b).wait()
        if b >= 2:
            store(b - 2).wait()

        def through_norm(n, _, b=b):
            rows = pl.ds(pl.multiple_of(n * PIECE, PIECE), PIECE)
            full = pl.ds(pl.multiple_of(b * BLOCK + n * PIECE, PIECE), PIECE)
            grad = gnt_own[b, rows, :].astype(F32) + gnt_x[b, rows, :].astype(F32)
            centred, scale = norm_stats(held[b % 2, rows, :])
            unit = centred * scale
            small_ref[LN2_GAIN:LN2_GAIN + 1, :] += sum_rows(grad * unit)
            small_ref[LN2_BIAS:LN2_BIAS + 1, :] += sum_rows(grad)
            total = dy_ref[full, :].astype(F32) + norm_back(grad * gains, unit, scale)
            ready[b % 2, rows, :] = total
            low = total.astype(BF)
            small_ref[OUT_BIAS:OUT_BIAS + 1, :] += sum_rows(low.astype(F32))
            ga_t[:, full] = turn(low)
            mixed = dot_rows(low, wout[...]).astype(BF)
            for p in range(pairs):
                gm_ref[p, full, :] = mixed[:, p * PAIR:(p + 1) * PAIR]
            return 0

        lax.fori_loop(0, strips, through_norm, 0)
        store(b).start()
        ga_copy(b).start()
        gm_copy(b).start()
        if b + 2 < blocks:
            load(b + 2).start()
    store(blocks - 2).wait()
    store(blocks - 1).wait()
    for b in range(blocks):
        ga_copy(b).wait()
        gm_copy(b).wait()
    branch_keep.wait()
    keep.wait()


def run_ff(middle, dy, wff, normed_two_t, active, slope, gain, wout):
    length, width = middle.shape
    half = wff.shape[3] // WIDE
    chunks = 2 * wff.shape[3] // CHUNK
    blocks = length // BLOCK
    pairs = wout.shape[0] // PAIR
    depth = width // SEQ_SIZE
    dma = pltpu.SemaphoreType.DMA
    rows = pltpu.VMEM((blocks, BLOCK, width), BF)
    hidden = pltpu.VMEM((half, length, WIDE), BF)
    flat_t = pltpu.VMEM((width, length), BF)
    return pl.pallas_call(
        ff_kernel,
        out_shape=[
            shape_of((length, width), BF),
            shape_of((length, width), F32),
            shape_of((width, length), BF),
            shape_of((pairs, length, PAIR), BF),
            shape_of((chunks, Z_SIZE, Y_SIZE, depth, CHUNK), BF),
            shape_of((SMALL_ROWS, width), F32),
        ],
        in_specs=[ANY_SPEC] * 6 + [VMEM_SPEC, ANY_SPEC],
        out_specs=[ANY_SPEC] * 5 + [VMEM_SPEC],
        scratch_shapes=[
            pltpu.VMEM((length, width), BF), pltpu.VMEM(wff.shape, BF),
            pltpu.VMEM(wout.shape, BF),
            pltpu.VMEM((length, width), BF), flat_t, pltpu.VMEM((pairs, length, PAIR), BF),
            flat_t, flat_t, hidden, hidden,
            pltpu.VMEM((BLOCK, width), F32), rows, rows,
            pltpu.VMEM((chunks, Z_SIZE, Y_SIZE, CORES, depth, CHUNK), BF),
            pltpu.VMEM((chunks, Z_SIZE, Y_SIZE, depth, CHUNK), BF),
            pltpu.VMEM((2, BLOCK, width), F32), pltpu.VMEM((2, BLOCK, width), F32),
            dma((blocks,)), dma((blocks,)), dma((chunks,)), dma((chunks,)),
            dma((2,)), dma((2,)), dma((1,)), dma((4 + 3 * half,)), dma((1 + 2 * blocks,)),
        ],
        compiler_params=pltpu.CompilerParams(
            collective_id=1, has_side_effects=True, vmem_limit_bytes=VMEM_LIMIT
        ),
    )(middle, dy, wff, normed_two_t, active, slope, gain, wout)


def back_kernel(
    q_hbm, k_hbm, v_hbm, mix_hbm, gm_hbm, query_hbm, ga_hbm, normed_hbm, wqkv_hbm, x_hbm,
    key_more, gain, down_bias, small_in, mid_hbm, gmid_hbm, ff_part, branch,
    out_hbm, tokens_hbm, qkv_sum, out_sum, up_sum, down_sum,
    gain_one, offset_one, qv_small, out_small, gain_two, offset_two, up_small, down_small,
    q_ref, k_ref, v_ref, mix_ref, gm_ref, query_more, ga_t, normed_t, wqkv, x_ref,
    out_ref, tokens_ref, key_t, key_acc, value_acc, dq, dk, dv, whole, mate, at_y, at_z, ff_y, ff_z, gn_own, gn_x,
    branch_x, branch_own, ff_own, held, small_own, small_z, small_y, small_c, small_x,
    bs, br, fys, fyr, fzs, fzr, acs, acr, ays, ayr, azs, azr, gs, gr, ls, ms, mr, os, hs, ins, more_ins, outs,
):
    length, width = x_ref.shape
    blocks = length // BLOCK
    strips = length // STRIP
    pairs = q_ref.shape[0]
    chunks = ff_part.shape[0]
    half = chunks // 2
    groups = chunks // GROUP
    me, head, core, y, across, core_mate, y_mate, z_mates = place()
    z = me // (Y_SIZE * CORES)
    by_pair = (
        (q_hbm, q_ref), (k_hbm, k_ref), (v_hbm, v_ref), (mix_hbm, mix_ref), (gm_hbm, gm_ref),
    )

    def pair_loads(p):
        both = pl.ds(2 * p, 2)
        first = p * (len(by_pair) + 1)
        return [
            pltpu.make_async_copy(src.at[p], dst.at[p], ins.at[first + n])
            for n, (src, dst) in enumerate(by_pair)
        ] + [
            pltpu.make_async_copy(
                query_hbm.at[both], query_more.at[both], ins.at[first + len(by_pair)]
            )
        ]

    late_loads = [
        pltpu.make_async_copy(src, dst, more_ins.at[n])
        for n, (src, dst) in enumerate(
            ((ga_hbm, ga_t), (normed_hbm, normed_t), (wqkv_hbm, wqkv), (x_hbm, x_ref))
        )
    ]
    for p in range(pairs):
        for copy in pair_loads(p):
            copy.start()
        if p == 0:
            late_loads[0].start()
            late_loads[1].start()
    late_loads[2].start()
    late_loads[3].start()
    greet([across, core_mate, y_mate, *z_mates])

    def part(b):
        return pl.ds(b * BLOCK, BLOCK)

    def branch_copy(b):
        return remote(branch.at[part(b), :], branch_x.at[part(b), :], bs.at[b], br.at[b], across)

    def load(n):
        source = mid_hbm if n < blocks else gmid_hbm
        return pltpu.make_async_copy(
            source.at[part(n % blocks), :], held.at[n % 2], ls.at[n % 2]
        )

    def taken(n):
        if n + 2 < 2 * blocks:
            load(n + 2).start()

    def group(g):
        return pl.ds(g * GROUP, GROUP)

    def ff_y_copy(g):
        return remote(
            ff_part.at[group(g), :, 1 - y], ff_y.at[group(g)], fys.at[g], fyr.at[g], y_mate
        )

    def ff_z_copy(g, d):
        n = g * 3 + d - 1
        return remote(
            ff_y.at[group(g), (z + d) % Z_SIZE], ff_z.at[d - 1, group(g)],
            fzs.at[n], fzr.at[n], z_mates[d - 1],
        )

    def branch_load(b):
        return pltpu.make_async_copy(branch.at[part(b), :], branch_own.at[b % 2], hs.at[b % 2])

    def ff_load(g):
        return pltpu.make_async_copy(
            ff_part.at[group(g), :, y], ff_own.at[g % 2], os.at[g % 2]
        )

    def ff_y_event(g):
        ff_y_copy(g).wait_recv()
        ff_load(g).wait()
        for n in range(g * GROUP, (g + 1) * GROUP):
            own = ff_own[g % 2, n % GROUP]
            ff_y[n] = (ff_y[n].astype(F32) + own.astype(F32)).astype(BF)
        if g + 2 < groups:
            ff_load(g + 2).start()
            ff_y_copy(g + 2).start()
        for d in (1, 2, 3):
            ff_z_copy(g, d).start()

    def ff_z_event(g):
        for d in (1, 2, 3):
            ff_z_copy(g, d).wait_recv()
        for n in range(g * GROUP, (g + 1) * GROUP):
            total = ff_y[n, z].astype(F32)
            for d in (1, 2, 3):
                total += ff_z[d - 1, n].astype(F32)
            if n < half:
                up_sum[:, n * CHUNK:(n + 1) * CHUNK] = total
            else:
                down_sum[:, (n - half) * CHUNK:(n - half + 1) * CHUNK] = total

    def at_c_copy(p):
        return remote(whole.at[p, :, :, 1 - core], mate.at[p], acs.at[p], acr.at[p], core_mate)

    def at_y_copy(p):
        return remote(mate.at[p, :, 1 - y], at_y.at[p], ays.at[p], ayr.at[p], y_mate)

    def at_z_copy(p, d):
        n = p * 3 + d - 1
        return remote(
            at_y.at[p, (z + d) % Z_SIZE], at_z.at[d - 1, p], azs.at[n], azr.at[n], z_mates[d - 1]
        )

    def at_c_event(p):
        at_c_copy(p).wait_recv()
        mate[p] = (mate[p].astype(F32) + whole[p, :, :, core].astype(F32)).astype(BF)
        at_y_copy(p).start()

    def at_y_event(p):
        at_y_copy(p).wait_recv()
        at_y[p] = (at_y[p].astype(F32) + mate[p, :, y].astype(F32)).astype(BF)
        for d in (1, 2, 3):
            at_z_copy(p, d).start()

    def at_z_event(p):
        for d in (1, 2, 3):
            at_z_copy(p, d).wait_recv()
        total = at_y[p, z].astype(F32)
        for d in (1, 2, 3):
            total += at_z[d - 1, p].astype(F32)
        cut = slice(p * PAIR, (p + 1) * PAIR)
        for kind in range(3):
            qkv_sum[kind, :, cut] = total[:, kind * PAIR:(kind + 1) * PAIR]
        out_sum[:, cut] = total[:, 3 * PAIR:]

    def out_copy(b):
        return pltpu.make_async_copy(out_ref.at[part(b), :], out_hbm.at[part(b), :], outs.at[b])

    def tokens_copy(b):
        return pltpu.make_async_copy(
            tokens_ref.at[part(b), :], tokens_hbm.at[part(b), :], outs.at[blocks + b]
        )

    def branch_event(b):
        branch_copy(b).wait_recv()
        load(b).wait()
        branch_load(b).wait()
        both = branch_own[b % 2].astype(F32) + branch_x[part(b), :].astype(F32)
        out_ref[part(b), :] = (held[b % 2] + both + as_row(down_bias)).astype(BF)
        out_copy(b).start()
        taken(b)
        if b + 2 < blocks:
            branch_load(b + 2).start()

    for b in range(blocks):
        branch_copy(b).start()
    for n in range(2):
        load(n).start()
        branch_load(n).start()
        ff_load(n).start()
        ff_y_copy(n).start()

    plan = {
        2: [(at_c_event, 0), (ff_y_event, 0), (branch_event, 0)], 4: [(at_c_event, 1)],
        5: [(ff_y_event, 1), (branch_event, 1)], 6: [(at_c_event, 2)],
    }

    low_lanes = lanes() < HEAD_DIM
    zero = jnp.zeros((1, PAIR), BF)

    def stacked(strip):
        return jnp.concatenate(
            [jnp.where(low_lanes, strip, zero), jnp.where(low_lanes, zero, strip)], axis=0
        )

    def attend(t, _):
        p, b = t // strips, t % strips
        rows = pl.ds(pl.multiple_of(b * STRIP, STRIP), STRIP)

        @pl.when(b == 0)
        def _():
            for p_now in range(pairs):
                @pl.when(p == p_now)
                def _(p_now=p_now):
                    for copy in pair_loads(p_now):
                        copy.wait()
            key_t[...] = turn(k_ref[p])
            key_acc[...] = jnp.zeros_like(key_acc)
            value_acc[...] = jnp.zeros_like(value_acc)

        queries, grads = stacked(q_ref[p, rows, :]), stacked(gm_ref[p, rows, :])
        more = jnp.concatenate(
            [query_more[2 * p, rows, :], query_more[2 * p + 1, rows, :]], axis=0
        )
        mixture = mix_ref[p, rows, :]
        product = grads.astype(F32) * jnp.concatenate([mixture, mixture], axis=0).astype(F32)
        inner = -jnp.sum(product, axis=-1, keepdims=True)
        query_side = jnp.concatenate([queries, more], axis=1)
        grad_side = jnp.concatenate([grads, in_pieces(inner, 0, 0.0)], axis=1)
        to_queries = jnp.zeros((PAIR, 2 * STRIP), F32)
        for n in range(blocks):
            keys = jnp.concatenate([k_ref[p, part(n), :], key_more[part(n), :]], axis=1)
            values = jnp.concatenate([v_ref[p, part(n), :], one_lanes(BLOCK)], axis=1)
            weights = jnp.exp(dot_rows(keys, query_side)).astype(BF)
            grad_scores = weights * dot_rows(values, grad_side).astype(BF)
            value_acc[part(n), :] += split_sum(weights, grads)
            key_acc[part(n), :] += split_sum(grad_scores, queries)
            to_queries += nn(key_t[:, part(n)], grad_scores)
        own = jnp.concatenate(
            [to_queries[:HEAD_DIM, :STRIP], to_queries[HEAD_DIM:, STRIP:]], axis=0
        )
        dq[p, rows, :] = (turn(own) * 0.125).astype(BF)

        @pl.when(b == strips - 1)
        def _():
            @pl.when(p == 0)
            def _():
                late_loads[0].wait()
                late_loads[1].wait()

            dk[p] = key_acc[...].astype(BF)
            dv[p] = value_acc[...].astype(BF)
            right = jnp.concatenate([dq[p], dk[p], dv[p]], axis=1)
            mixture_all = mix_ref[p]

            def one(plane, _):
                cut = pl.ds(pl.multiple_of(plane * BLOCK, BLOCK), BLOCK)
                both = jnp.concatenate(
                    [nn(normed_t[cut, :], right), nn(ga_t[cut, :], mixture_all)], axis=1
                )
                whole[p, plane] = both.astype(BF).reshape(whole.shape[2:])
                return 0

            lax.fori_loop(0, Z_SIZE, one, 0)
            at_c_copy(p).start()

        for step, events in plan.items():
            @pl.when(t == step)
            def _(events=events):
                for event, n in events:
                    event(n)
        return 0

    lax.fori_loop(0, pairs * strips, attend, 0)
    late_loads[2].wait()
    late_loads[3].wait()

    def gn_copy(b):
        return remote(gn_own.at[b], gn_x.at[b], gs.at[b], gr.at[b], across)

    own_gain = jnp.zeros((1, width), F32)
    own_offset = jnp.zeros((1, width), F32)
    for b in range(blocks):
        total = jnp.zeros((BLOCK, width), F32)
        for n, grad in enumerate((dq, dk, dv)):
            left = jnp.concatenate([grad[p, part(b), :] for p in range(pairs)], axis=1)
            total += dot_rows(left, wqkv[n])
        gn_own[b] = total.astype(BF)
        gn_copy(b).start()
        centred, scale = norm_stats(x_ref[part(b), :].astype(F32))
        own_gain += sum_rows(total * (centred * scale))
        own_offset += sum_rows(total)

    at_c_event(3)
    small_own[...] = small_in[...]
    small_own[LN1_GAIN:LN1_GAIN + 1, :] = own_gain
    small_own[LN1_BIAS:LN1_BIAS + 1, :] = own_offset
    for p in range(pairs):
        first, second = p * PAIR, (pairs + p) * PAIR
        small_own[QV_BIAS:QV_BIAS + 1, first:first + PAIR] = sum_rows(dq[p].astype(F32))
        small_own[QV_BIAS:QV_BIAS + 1, second:second + PAIR] = sum_rows(dv[p].astype(F32))
    def small_z_copy(d):
        return remote(small_own, small_z.at[z], ms.at[d - 1], mr.at[d - 1], z_mates[d - 1])

    def small_z_arrival(d):
        slot = small_z.at[(z + Z_SIZE - d) % Z_SIZE]
        return remote(slot, slot, ms.at[d - 1], mr.at[d - 1], z_mates[d - 1])

    y_sum = remote(small_y.at[0], small_y.at[1], ms.at[3], mr.at[3], y_mate)
    c_sum = remote(small_c.at[0], small_c.at[1], ms.at[4], mr.at[4], core_mate)
    x_sum = remote(small_x.at[0], small_x.at[1], ms.at[5], mr.at[5], across)
    for d in (1, 2, 3):
        small_z_copy(d).start()
    small_z[z] = small_own[...]

    def small_y_step():
        for d in (1, 2, 3):
            small_z_arrival(d).wait_recv()
        small_y[0] = small_z[0] + small_z[1] + small_z[2] + small_z[3]
        y_sum.start()

    def small_c_step():
        y_sum.wait()
        small_c[0] = small_y[0] + small_y[1]
        c_sum.start()

    def small_x_step():
        c_sum.wait()
        small_x[0] = small_c[0, 0:8, :] + small_c[1, 0:8, :]
        x_sum.start()

    branch_event(2)
    ff_y_event(2)
    branch_event(3)
    ff_z_event(0)
    ff_y_event(3)
    at_y_event(0)
    ff_z_event(1)
    gains = as_row(gain)
    for b in range(blocks):
        gn_copy(b).wait()
        load(blocks + b).wait()
        grad = gn_own[b].astype(F32) + gn_x[b].astype(F32)
        centred, scale = norm_stats(x_ref[part(b), :].astype(F32))
        unit = centred * scale
        tokens_ref[part(b), :] = (
            held[b % 2] + norm_back(grad * gains, unit, scale)
        ).astype(BF)
        tokens_copy(b).start()
        taken(blocks + b)
        if b == 0:
            small_y_step()
            at_y_event(1)
            at_y_event(2)
            ff_z_event(2)
        if b == 1:
            small_c_step()
            at_y_event(3)
            ff_z_event(3)
        if b == 2:
            small_x_step()
            at_z_event(0)
            at_z_event(1)
            at_z_event(2)

    at_z_event(3)
    x_sum.wait()
    ln1 = small_x[0, 0:2, :] + small_x[1, 0:2, :]
    gain_one[...] = ln1[0:1, :].reshape(width)
    offset_one[...] = ln1[1:2, :].reshape(width)
    small = small_c[0] + small_c[1]
    for kind, target in (
        (OUT_BIAS, out_small), (LN2_GAIN, gain_two), (LN2_BIAS, offset_two), (DOWN_BIAS, down_small),
    ):
        target[...] = small[kind:kind + 1, :].reshape(width)
    cols = pairs * PAIR
    qv_small[0:1, :] = small[QV_BIAS:QV_BIAS + 1, :cols]
    qv_small[1:2, :] = small[QV_BIAS:QV_BIAS + 1, cols:]
    for n in range(up_small.shape[0] // width):
        row = small[UP_BIAS + n:UP_BIAS + n + 1, :]
        up_small[n * width:(n + 1) * width] = row.reshape(width)

    for d in (1, 2, 3):
        small_z_copy(d).wait_send()
    for b in range(blocks):
        out_copy(b).wait()
        tokens_copy(b).wait()
        branch_copy(b).wait_send()
    for g in range(groups):
        ff_y_copy(g).wait_send()
        for d in (1, 2, 3):
            ff_z_copy(g, d).wait_send()
    for p in range(pairs):
        at_c_copy(p).wait_send()
        at_y_copy(p).wait_send()
        for d in (1, 2, 3):
            at_z_copy(p, d).wait_send()


def run_back(
    queries, keys, values, mixture, grad_mixture, query_more, ga_t, normed_t, wqkv, x,
    key_more, gain, down_bias, small, middle, grad_middle, ff_part, branch,
):
    length, width = x.shape
    pairs = queries.shape[0]
    chunks, depth = ff_part.shape[0], ff_part.shape[3]
    groups = chunks // GROUP
    cols, hidden = pairs * PAIR, chunks // 2 * CHUNK
    blocks = length // BLOCK
    dma = pltpu.SemaphoreType.DMA
    rows = pltpu.VMEM((blocks, BLOCK, width), BF)
    by_pair = pltpu.VMEM((pairs, length, PAIR), BF)
    whole_rows = pltpu.VMEM((length, width), BF)
    row = shape_of((width,), F32)
    loaded = (
        queries, keys, values, mixture, grad_mixture, query_more, ga_t, normed_t, wqkv, x
    )
    return pl.pallas_call(
        back_kernel,
        out_shape=[
            shape_of((length, width), BF),
            shape_of((length, width), BF),
            shape_of((3, depth, cols), F32),
            shape_of((depth, cols), F32),
            shape_of((depth, hidden), F32),
            shape_of((depth, hidden), F32),
            row, row, shape_of((2, cols), F32), row, row, row, shape_of((hidden,), F32), row,
        ],
        in_specs=[ANY_SPEC] * 10 + [VMEM_SPEC] * 4 + [ANY_SPEC] * 4,
        out_specs=[ANY_SPEC] * 2 + [VMEM_SPEC] * 12,
        scratch_shapes=[pltpu.VMEM(v.shape, BF) for v in loaded] + [
            whole_rows, whole_rows, pltpu.VMEM((PAIR, length), BF),
            pltpu.VMEM((length, PAIR), F32), pltpu.VMEM((length, PAIR), F32),
            by_pair, by_pair, by_pair,
            pltpu.VMEM((pairs, Z_SIZE, Y_SIZE, CORES, depth, CHUNK), BF),
            pltpu.VMEM((pairs, Z_SIZE, Y_SIZE, depth, CHUNK), BF),
            pltpu.VMEM((pairs, Z_SIZE, depth, CHUNK), BF),
            pltpu.VMEM((3, pairs, depth, CHUNK), BF),
            pltpu.VMEM((chunks, Z_SIZE, depth, CHUNK), BF),
            pltpu.VMEM((3, chunks, depth, CHUNK), BF),
            rows, rows, whole_rows,
            pltpu.VMEM((2, BLOCK, width), BF),
            pltpu.VMEM((2, GROUP, Z_SIZE, depth, CHUNK), BF),
            pltpu.VMEM((2, BLOCK, width), F32),
            pltpu.VMEM(small.shape, F32),
            pltpu.VMEM((Z_SIZE,) + small.shape, F32),
            pltpu.VMEM((2,) + small.shape, F32),
            pltpu.VMEM((2,) + small.shape, F32),
            pltpu.VMEM((2, 8, width), F32),
            dma((blocks,)), dma((blocks,)), dma((groups,)), dma((groups,)),
            dma((3 * groups,)), dma((3 * groups,)), dma((pairs,)), dma((pairs,)),
            dma((pairs,)), dma((pairs,)), dma((3 * pairs,)), dma((3 * pairs,)),
            dma((blocks,)), dma((blocks,)), dma((2,)), dma((6,)), dma((6,)), dma((2,)), dma((2,)),
            dma((6 * pairs,)), dma((4,)), dma((2 * blocks,)),
        ],
        compiler_params=pltpu.CompilerParams(
            collective_id=2, has_side_effects=True, vmem_limit_bytes=VMEM_LIMIT
        ),
    )(*loaded, key_more, gain, down_bias, small, middle, grad_middle, ff_part, branch)


def hand_over_kernel(*refs):
    *refs, sems = refs
    count = len(refs) // 3
    refs = refs[:count] + refs[2 * count:] + refs[count:2 * count]
    loads, stores = (
        [
            pltpu.make_async_copy(refs[a * count + n], refs[b * count + n], sems.at[a, n])
            for n in range(count)
        ]
        for a, b in ((0, 1), (1, 2))
    )
    for load in loads:
        load.start()
    for load, store in zip(loads, stores):
        load.wait()
        store.start()
    for store in stores:
        store.wait()


def hand_over(results):
    return pl.pallas_call(
        hand_over_kernel,
        out_shape=[shape_of(v.shape, v.dtype) for v in results],
        in_specs=[ANY_SPEC] * len(results),
        out_specs=[ANY_SPEC] * len(results),
        scratch_shapes=[pltpu.VMEM(v.shape, v.dtype) for v in results] + [
            pltpu.SemaphoreType.DMA((2, len(results)))
        ],
        compiler_params=pltpu.CompilerParams(vmem_limit_bytes=VMEM_LIMIT),
    )(*results)


def fast_body(
    tokens, segment_ids, context_flags, ln1_gain, ln1_bias, qkv_weight, qv_bias, out_weight,
    out_bias, ln2_gain, ln2_bias, up_weight, up_bias, down_weight, down_bias, cotangent,
):
    x, dy = tokens[0], cotangent[0]
    (
        queries, keys, values, mixture, middle, normed_t, wff, key_more, query_more,
        normed_two_t, active, slope,
    ) = run_fwd(
        x, segment_ids, context_flags, ln1_gain, ln1_bias, qv_bias, out_bias, ln2_gain,
        ln2_bias, up_bias, qkv_weight, out_weight, up_weight, down_weight.T,
    )
    branch, grad_middle, ga_t, grad_mixture, ff_part, small = run_ff(
        middle, dy, wff, normed_two_t, active, slope, ln2_gain, out_weight
    )
    (
        output, tokens_grad, qkv_grad, out_grad, up_grad, down_grad, gain_one, offset_one,
        qv_grad, out_bias_grad, gain_two, offset_two, up_bias_grad, down_bias_grad,
    ) = hand_over(run_back(
        queries, keys, values, mixture, grad_mixture, query_more, ga_t, normed_t, qkv_weight, x,
        key_more, ln1_gain, down_bias, small, middle, grad_middle, ff_part, branch,
    ))
    return (
        output[None], tokens_grad[None], gain_one, offset_one, qkv_grad, qv_grad, out_grad.T,
        out_bias_grad, gain_two, offset_two, up_grad, up_bias_grad, down_grad.T, down_bias_grad,
    )


def solution(mesh):
    chosen = generic_body
    if mesh.shape["head"] == 2 and mesh.shape["seq"] == SEQ_SIZE:
        chosen = fast_body
    return jax.shard_map(
        chosen,
        mesh=mesh,
        in_specs=(
            P("seq", None, None),
            P("seq", None),
            P("seq", None),
            P(),
            P(),
            P(None, None, "head"),
            P(None, "head"),
            P("head", None),
            P(),
            P(),
            P(),
            P("seq", "head"),
            P("head"),
            P("head", "seq"),
            P(),
            P("seq", None, None),
        ),
        out_specs=(
            P("seq", None, None),
            P("seq", None, None),
            P(),
            P(),
            P(None, "seq", "head"),
            P(None, "head"),
            P("head", "seq"),
            P(),
            P(),
            P(),
            P("seq", "head"),
            P("head"),
            P("head", "seq"),
            P(),
        ),
        check_vma=False,
    )
```

```python
import math

import jax
import jax.numpy as jnp
from jax import lax
from jax.experimental import pallas as pl
from jax.experimental.pallas import tpu as pltpu
from jax.sharding import PartitionSpec as P

HEAD_DIM = 64


def layer_norm(values_in, scaling, offset):
    middle = jnp.mean(values_in, axis=-1, keepdims=True)
    centred = values_in - middle
    spread = jnp.mean(centred * centred, axis=-1, keepdims=True)
    return centred * lax.rsqrt(spread + 1e-05) * scaling + offset


def gelu_exact(values_in):
    return 0.5 * values_in * (1.0 + jax.scipy.special.erf(values_in * 0.7071067811865476))


def dot_rows(left, right):
    return lax.dot_general(
        left, right, (((1,), (1,)), ((), ())), preferred_element_type=jnp.float32
    )


def dot_cols(left, right):
    return lax.dot_general(
        left, right, (((0,), (0,)), ((), ())), preferred_element_type=jnp.float32
    )


def masked_scores(block_query, seq_keys, block_segments, seq_segments, seq_context, factor):
    raw_scores = (
        jnp.einsum("qhd,khd->hqk", block_query, seq_keys, preferred_element_type=jnp.float32)
        * factor
    )
    allowed = (block_segments[:, None] == seq_segments[None, :]) & (seq_context[None, :] == 1)
    return jnp.where(allowed[None], raw_scores, -1e30)


def generic_body(
    tokens,
    segment_ids,
    context_flags,
    ln1_gain,
    ln1_bias,
    qkv_weight,
    qv_bias,
    out_weight,
    out_bias,
    ln2_gain,
    ln2_bias,
    up_weight,
    up_bias,
    down_weight,
    down_bias,
    cotangent,
):
    seq_count, length, width = tokens.shape
    row_count = seq_count * length
    local_cols = qkv_weight.shape[2]
    head_count = local_cols // HEAD_DIM
    factor = 1.0 / math.sqrt(HEAD_DIM)
    block = min(512, length)
    blocks = length // block
    gain_one = ln1_gain.astype(jnp.float32)
    offset_one = ln1_bias.astype(jnp.float32)
    gain_two = ln2_gain.astype(jnp.float32)
    offset_two = ln2_bias.astype(jnp.float32)
    flat_in = tokens.astype(jnp.float32).reshape(row_count, width)
    normed_f, norm_one_pull = jax.vjp(layer_norm, flat_in, gain_one, offset_one)
    normed = normed_f.astype(jnp.bfloat16)
    queries = (
        jnp.dot(normed, qkv_weight[0], preferred_element_type=jnp.float32)
        + qv_bias[0].astype(jnp.float32)
    ).astype(jnp.bfloat16)
    key_rows = jnp.dot(normed, qkv_weight[1], preferred_element_type=jnp.float32).astype(
        jnp.bfloat16
    )
    value_rows = (
        jnp.dot(normed, qkv_weight[2], preferred_element_type=jnp.float32)
        + qv_bias[1].astype(jnp.float32)
    ).astype(jnp.bfloat16)

    def per_sequence(array):
        return array.reshape(seq_count, length, head_count, HEAD_DIM)

    def attend_sequence(member):
        seq_query, seq_keys, seq_values, seq_segments, seq_context = member

        def attend_block(portion):
            block_query, block_segments = portion
            scores = masked_scores(
                block_query, seq_keys, block_segments, seq_segments, seq_context, factor
            )
            row_top = jnp.max(scores, axis=-1, keepdims=True)
            exponent = jnp.exp(scores - row_top)
            row_total = jnp.sum(exponent, axis=-1, keepdims=True)
            soft_weights = (exponent / row_total).astype(jnp.bfloat16)
            block_mix = jnp.einsum(
                "hqk,khd->qhd", soft_weights, seq_values, preferred_element_type=jnp.float32
            )
            return (block_mix.astype(jnp.bfloat16), row_top + jnp.log(row_total))

        return lax.map(
            attend_block,
            (
                seq_query.reshape(blocks, block, head_count, HEAD_DIM),
                seq_segments.reshape(blocks, block),
            ),
        )

    mixture, log_totals = lax.map(
        attend_sequence,
        (
            per_sequence(queries),
            per_sequence(key_rows),
            per_sequence(value_rows),
            segment_ids,
            context_flags,
        ),
    )
    mixture = mixture.reshape(row_count, local_cols)
    partial_out = jnp.dot(mixture, out_weight, preferred_element_type=jnp.float32)
    grad_rows_all = cotangent.reshape(row_count, width)
    grad_float_all = grad_rows_all.astype(jnp.float32)
    grad_down_bias = jnp.sum(grad_float_all, axis=0)
    attended = lax.psum(partial_out, "head") + out_bias.astype(jnp.float32)
    middle_state = flat_in + attended
    normed_two_f, norm_two_pull = jax.vjp(layer_norm, middle_state, gain_two, offset_two)
    normed_two = normed_two_f.astype(jnp.bfloat16)
    up_part, down_part, up_shift = (
        lax.all_gather(up_weight, "head", axis=1, tiled=True),
        lax.all_gather(down_weight, "head", axis=0, tiled=True),
        lax.all_gather(up_bias, "head", axis=0, tiled=True),
    )
    up_full, down_full = (
        lax.all_gather(up_part, "seq", axis=0, tiled=True),
        lax.all_gather(down_part, "seq", axis=1, tiled=True),
    )
    before = jnp.dot(normed_two, up_full, preferred_element_type=jnp.float32) + up_shift.astype(
        jnp.float32
    )
    active_f, gelu_pull = jax.vjp(gelu_exact, before)
    active = active_f.astype(jnp.bfloat16)
    branch_out = jnp.dot(active, down_full, preferred_element_type=jnp.float32)
    final_rows = (middle_state + branch_out + down_bias.astype(jnp.float32)).astype(jnp.bfloat16)
    output = final_rows.reshape(tokens.shape)
    grad_float = grad_rows_all.astype(jnp.float32)
    grad_down = dot_cols(active, grad_rows_all)
    grad_active = dot_rows(grad_rows_all, down_full)
    (grad_before_f,) = gelu_pull(grad_active)
    grad_before = grad_before_f.astype(jnp.bfloat16)
    grad_up = dot_cols(normed_two, grad_before)
    grad_up_bias = jnp.sum(grad_before.astype(jnp.float32), axis=0)
    grad_normed_two = dot_rows(grad_before, up_full)
    grad_middle_norm, grad_gain_two, grad_offset_two = norm_two_pull(grad_normed_two)
    grad_middle = grad_float + grad_middle_norm
    ff_part = up_weight.shape[1]
    start_col = lax.axis_index("head") * ff_part
    grad_up = lax.dynamic_slice_in_dim(grad_up, start_col, ff_part, 1)
    grad_down = lax.dynamic_slice_in_dim(grad_down, start_col, ff_part, 0)
    grad_up_bias = lax.dynamic_slice_in_dim(grad_up_bias, start_col, ff_part, 0)
    grad_attended = grad_middle.astype(jnp.bfloat16)
    grad_out_bias = jnp.sum(grad_attended.astype(jnp.float32), axis=0)
    grad_out = dot_cols(mixture, grad_attended)
    grad_mixture = dot_rows(grad_attended, out_weight).astype(jnp.bfloat16)

    def back_sequence(member):
        seq_query, seq_keys, seq_values, seq_grad, seq_logs, seq_segments, seq_context = member

        def back_block(carry, portion):
            key_acc, value_acc = carry
            block_query, block_grad, block_logs, block_segments = portion
            scores = masked_scores(
                block_query, seq_keys, block_segments, seq_segments, seq_context, factor
            )
            soft_weights = jnp.exp(scores - block_logs)
            value_acc = value_acc + jnp.einsum(
                "hqk,qhd->khd",
                soft_weights.astype(jnp.bfloat16),
                block_grad,
                preferred_element_type=jnp.float32,
            )
            grad_soft = jnp.einsum(
                "qhd,khd->hqk", block_grad, seq_values, preferred_element_type=jnp.float32
            )
            row_inner = jnp.sum(soft_weights * grad_soft, axis=-1, keepdims=True)
            grad_scores = (soft_weights * (grad_soft - row_inner)).astype(jnp.bfloat16)
            grad_query = (
                jnp.einsum(
                    "hqk,khd->qhd", grad_scores, seq_keys, preferred_element_type=jnp.float32
                )
                * factor
            )
            key_acc = (
                key_acc
                + jnp.einsum(
                    "hqk,qhd->khd", grad_scores, block_query, preferred_element_type=jnp.float32
                )
                * factor
            )
            return ((key_acc, value_acc), grad_query)

        empty = jnp.zeros((length, head_count, HEAD_DIM), jnp.float32)
        (key_acc, value_acc), grad_query = lax.scan(
            back_block,
            (empty, empty),
            (
                seq_query.reshape(blocks, block, head_count, HEAD_DIM),
                seq_grad.reshape(blocks, block, head_count, HEAD_DIM),
                seq_logs,
                seq_segments.reshape(blocks, block),
            ),
        )
        return (grad_query, key_acc, value_acc)

    grad_queries, grad_keys, grad_values = lax.map(
        back_sequence,
        (
            per_sequence(queries),
            per_sequence(key_rows),
            per_sequence(value_rows),
            per_sequence(grad_mixture),
            log_totals,
            segment_ids,
            context_flags,
        ),
    )
    grad_queries = grad_queries.reshape(row_count, local_cols).astype(jnp.bfloat16)
    grad_keys = grad_keys.reshape(row_count, local_cols).astype(jnp.bfloat16)
    grad_values = grad_values.reshape(row_count, local_cols).astype(jnp.bfloat16)
    grad_qv_bias = jnp.stack(
        [
            jnp.sum(grad_queries.astype(jnp.float32), axis=0),
            jnp.sum(grad_values.astype(jnp.float32), axis=0),
        ]
    )
    grad_qkv = jnp.stack(
        [dot_cols(normed, grad_queries), dot_cols(normed, grad_keys), dot_cols(normed, grad_values)]
    )
    grad_normed = (
        dot_rows(grad_queries, qkv_weight[0])
        + dot_rows(grad_keys, qkv_weight[1])
        + dot_rows(grad_values, qkv_weight[2])
    )
    grad_normed = lax.psum(grad_normed, "head")
    grad_input_norm, grad_gain_one, grad_offset_one = norm_one_pull(grad_normed)
    tokens_grad = (grad_middle + grad_input_norm).astype(jnp.bfloat16).reshape(tokens.shape)
    summed_qkv, summed_out, summed_up, summed_down = (
        lax.psum_scatter(
            grad_qkv.astype(jnp.bfloat16), "seq", scatter_dimension=1, tiled=True
        ).astype(jnp.float32),
        lax.psum_scatter(
            grad_out.astype(jnp.bfloat16), "seq", scatter_dimension=1, tiled=True
        ).astype(jnp.float32),
        lax.psum_scatter(
            grad_up.astype(jnp.bfloat16), "seq", scatter_dimension=0, tiled=True
        ).astype(jnp.float32),
        lax.psum_scatter(
            grad_down.astype(jnp.bfloat16), "seq", scatter_dimension=1, tiled=True
        ).astype(jnp.float32),
    )
    smalls = lax.psum(
        (
            grad_gain_one,
            grad_offset_one,
            grad_qv_bias,
            grad_out_bias,
            grad_gain_two,
            grad_offset_two,
            grad_up_bias,
            grad_down_bias,
        ),
        "seq",
    )
    return (
        output,
        tokens_grad,
        smalls[0],
        smalls[1],
        summed_qkv,
        smalls[2],
        summed_out,
        smalls[3],
        smalls[4],
        smalls[5],
        summed_up,
        smalls[6],
        summed_down,
        smalls[7],
    )


MESH = pl.DeviceIdType.MESH
BF = jnp.bfloat16
F32 = jnp.float32
BLOCK = 256
STRIP = 512
PIECE = 128
WIDE = 1024
GROUP = 2
CHUNK = 512
PAIR = 2 * HEAD_DIM
Z_SIZE, Y_SIZE, CORES = 4, 2, 2
SEQ_SIZE = Z_SIZE * Y_SIZE * CORES
HOP = Y_SIZE * CORES
TABLES = 8
FAR = -1e30
VMEM_LIMIT = 62 * 2**20
INV_ROOT_TWO = 0.7071067811865476
INV_ROOT_TWO_PI = 0.3989422804014327
LN1_GAIN, LN1_BIAS, QV_BIAS, OUT_BIAS, LN2_GAIN, LN2_BIAS, UP_BIAS, DOWN_BIAS = 0, 1, 2, 3, 4, 5, 6, 8
SMALL_ROWS = 16
VMEM_SPEC = pl.BlockSpec(memory_space=pltpu.VMEM)
ANY_SPEC = pl.BlockSpec(memory_space=pl.ANY)


def shape_of(dims, dtype):
    return jax.ShapeDtypeStruct(tuple(dims), dtype)


def nn(left, right):
    return jnp.dot(left, right, preferred_element_type=F32)


def split_sum(left, right):
    parts = [
        nn(left[:, n:n + BLOCK], right[n:n + BLOCK]) for n in range(0, left.shape[1], BLOCK)
    ]
    while len(parts) > 1:
        parts = [a + b for a, b in zip(parts[::2], parts[1::2])]
    return parts[0]


def turn(block):
    return jnp.transpose(block)


def sum_rows(block):
    return jnp.sum(block, axis=0, keepdims=True)


def place():
    me = lax.axis_index("seq")
    head = lax.axis_index("head")
    core = me % 2
    y = (me // 2) % 2
    across = {"seq": me, "head": 1 - head}
    core_mate = {"seq": me + 1 - 2 * core, "head": head}
    y_mate = {"seq": me + 2 - 4 * y, "head": head}
    z_mates = [{"seq": (me + HOP * d) % SEQ_SIZE, "head": head} for d in (1, 2, 3)]
    return me, head, core, y, across, core_mate, y_mate, z_mates


def greet(others):
    barrier = pltpu.get_barrier_semaphore()
    for other in others:
        pl.semaphore_signal(barrier, inc=1, device_id=other, device_id_type=MESH)
    pl.semaphore_wait(barrier, len(others))


def remote(src, dst, send_sem, recv_sem, other):
    return pltpu.make_async_remote_copy(
        src_ref=src, dst_ref=dst, send_sem=send_sem, recv_sem=recv_sem,
        device_id=other, device_id_type=MESH,
    )


def norm_stats(rows):
    middle = jnp.mean(rows, axis=-1, keepdims=True)
    centred = rows - middle
    spread = jnp.mean(centred * centred, axis=-1, keepdims=True)
    return centred, lax.rsqrt(spread + 1e-05)


def norm_back(inner, unit, scale):
    return scale * (
        inner
        - jnp.mean(inner, axis=-1, keepdims=True)
        - unit * jnp.mean(inner * unit, axis=-1, keepdims=True)
    )


def as_row(vector):
    return vector[...].astype(F32).reshape(1, -1)


def lanes():
    return lax.broadcasted_iota(jnp.int32, (1, PAIR), 1)


def in_pieces(column, first, rest):
    high = column.astype(BF).astype(F32)
    mid = (column - high).astype(BF).astype(F32)
    low = column - high - mid
    at = lanes()
    return jnp.where(
        at == first, high, jnp.where(at == first + 1, mid, jnp.where(at == first + 2, low, rest))
    ).astype(BF)


def one_lanes(length):
    return jnp.broadcast_to(jnp.where(lanes() < 3, 1.0, 0.0).astype(BF), (length, PAIR))


class Gather:
    def __init__(self, whole, own, sems):
        self.whole, self.own = whole, own
        self.zs, self.zr, self.ys, self.yr, self.cs, self.cr = sems
        self.me, head, self.core, self.y, _, self.core_mate, self.y_mate, _ = place()
        self.z = self.me // HOP
        self.above = {"seq": (self.me + HOP) % SEQ_SIZE, "head": head}
        self.below = {"seq": (self.me + SEQ_SIZE - HOP) % SEQ_SIZE, "head": head}
        self.flows = [(0, 0)] + [(way, s) for s in (1, 2, 3) for way in (0, 1)]
        self.beside_y = self.me + 2 - 4 * self.y
        self.beside = self.me + 1 - 2 * self.core

    @staticmethod
    def source(base, way, s):
        away = SEQ_SIZE - HOP * s if way == 0 else HOP * s
        return (base + away) % SEQ_SIZE

    def goes_on(self, way):
        return (self.z < Z_SIZE - 1) if way == 0 else (self.z > 0)

    def held(self, u, j, first):
        return self.own(u) if first else self.whole.at[u, j]

    def z_copy(self, u, way, s):
        n = (u * 2 + way) * 3 + s - 1
        j = self.source(self.me, way, s - 1)
        return remote(
            self.held(u, j, s == 1), self.whole.at[u, j], self.zs.at[n], self.zr.at[n],
            self.above if way == 0 else self.below,
        )

    def z_arrival(self, u, way, s):
        n = (u * 2 + way) * 3 + s - 1
        slot = self.whole.at[u, self.source(self.me, way, s)]
        return remote(slot, slot, self.zs.at[n], self.zr.at[n], self.above)

    def y_copy(self, u, f):
        n = u * 7 + f
        j = self.source(self.me, *self.flows[f])
        return remote(
            self.held(u, j, f == 0), self.whole.at[u, j], self.ys.at[n], self.yr.at[n],
            self.y_mate,
        )

    def y_arrival(self, u, f):
        n = u * 7 + f
        slot = self.whole.at[u, self.source(self.beside_y, *self.flows[f])]
        return remote(slot, slot, self.ys.at[n], self.yr.at[n], self.y_mate)

    def c_copy(self, u, f, from_y):
        n = (u * 2 + from_y) * 7 + f
        j = self.source(self.beside_y if from_y else self.me, *self.flows[f])
        return remote(
            self.held(u, j, f == 0 and not from_y), self.whole.at[u, j], self.cs.at[n],
            self.cr.at[n], self.core_mate,
        )

    def c_arrival(self, u, f, from_y):
        n = (u * 2 + from_y) * 7 + f
        base = self.beside + from_y * (2 - 4 * self.y)
        slot = self.whole.at[u, self.source(base, *self.flows[f])]
        return remote(slot, slot, self.cs.at[n], self.cr.at[n], self.core_mate)

    def for_flow(self, f, do):
        if f == 0:
            do()
        else:
            way, s = self.flows[f]
            pl.when((self.z >= s) if way == 0 else (self.z + s < Z_SIZE))(do)

    def for_step(self, s, do):
        for f, (way, step) in enumerate(self.flows):
            if step == s:
                self.for_flow(f, lambda f=f, way=way: do(f, way))

    def start_z(self, u):
        for way in (0, 1):
            pl.when(self.goes_on(way))(lambda way=way: self.z_copy(u, way, 1).start())

    def start_near(self, u):
        self.y_copy(u, 0).start()
        self.c_copy(u, 0, 0).start()

    def z_event(self, u, s):
        def one(f, way):
            self.z_arrival(u, way, s).wait_recv()
            if s < 3:
                pl.when(self.goes_on(way))(lambda: self.z_copy(u, way, s + 1).start())
            self.y_copy(u, f).start()
            self.c_copy(u, f, 0).start()
        self.for_step(s, one)
        if u == 0 and s == 1:
            self.start_z(1)
        if u == 0 and s == 2:
            self.start_near(1)

    def y_event(self, u, s):
        def one(f, way):
            self.y_arrival(u, f).wait_recv()
            self.c_copy(u, f, 1).start()
        self.for_step(s, one)

    def arrive(self, u):
        for f in range(len(self.flows)):
            def one(f=f):
                for from_y in (0, 1):
                    self.c_arrival(u, f, from_y).wait_recv()
            self.for_flow(f, one)

    def finish(self, u):
        for way in (0, 1):
            pl.when(self.goes_on(way))(lambda way=way: self.z_copy(u, way, 1).wait_send())
        for f, (way, s) in enumerate(self.flows):
            def one(f=f, way=way, s=s):
                if f and s < 3:
                    pl.when(self.goes_on(way))(
                        lambda: self.z_copy(u, way, s + 1).wait_send()
                    )
                self.y_copy(u, f).wait_send()
                for from_y in (0, 1):
                    self.c_copy(u, f, from_y).wait_send()
            self.for_flow(f, one)


GATHER_SEMS = (12, 12, 14, 14, 28, 28)


def fwd_kernel(
    x_ref, seg_ref, context, gain, offset, qv_bias, out_bias, gain_two, offset_two, up_bias,
    wqkv, wout, up_shard, down_shard,
    q_out, k_out, v_out, mix_out, mid_out, normed_out, wff_out, key_out, query_out,
    normed_two_out, active_out, slope_out, shard_out, bias_out,
    wff, q_ref, k_ref, v_ref, mix_ref, mid_ref, normed_t, key_more, query_more,
    normed_two_t, active, slope, bias_row, mask_more, wout_all, mix_x, shard_x, bias_x,
    zs, zr, ys, yr, cs, cr, ps, pr, xs, xr, local, outs,
):
    length, width = x_ref.shape
    blocks = length // BLOCK
    pairs = q_ref.shape[0]
    cols = pairs * PAIR
    me, head, core, y, across, core_mate, y_mate, _ = place()
    steps = length // STRIP * pairs
    weights = Gather(wff, lambda u: wff.at[u, me], (zs, zr, ys, yr, cs, cr))
    own = [
        pltpu.make_async_copy(shard, wff.at[u, me], local.at[u])
        for u, shard in enumerate((up_shard, down_shard))
    ]
    own[0].start()
    own[1].start()
    greet([across, core_mate, y_mate, weights.above, weights.below])

    half = wout.shape[0] // 2
    here = pl.ds(pl.multiple_of(core * half, half), half)
    beside = pl.ds(pl.multiple_of((1 - core) * half, half), half)
    wout_x = wout_all.at[1 - head]
    out_copy = remote(
        wout.at[here, :], wout_all.at[head, here, :], xs.at[0], xr.at[0], across
    )
    wout_all[head] = wout[...]
    out_pass = remote(wout_x.at[here, :], wout_x.at[here, :], ps.at[0], pr.at[0], core_mate)
    out_arrival = remote(
        wout_x.at[beside, :], wout_x.at[beside, :], ps.at[0], pr.at[0], core_mate
    )
    out_copy.start()

    own[0].wait()
    weights.start_z(0)
    weights.start_near(0)
    own[1].wait()
    shard_copy = remote(wff.at[:, me], shard_x, xs.at[1 + steps], xr.at[1 + steps], across)
    shard_copy.start()
    bias_row[...] = as_row(up_bias)
    bias_copy = remote(bias_row, bias_x, xs.at[2 + steps], xr.at[2 + steps], across)
    bias_copy.start()

    def pass_out():
        out_copy.wait_recv()
        out_pass.start()

    plan = {
        2: [(weights.z_event, 0, 1), (weights.y_event, 0, 0)], 4: [(weights.z_event, 0, 2)], 5: [(weights.y_event, 0, 1)],
        6: [(weights.z_event, 0, 3), (pass_out,)], 7: [(weights.z_event, 1, 1)], 8: [(weights.y_event, 0, 2), (weights.y_event, 1, 0)],
        9: [(weights.z_event, 1, 2)], 10: [(weights.y_event, 0, 3)], 11: [(weights.z_event, 1, 3)],
    }

    def tick(t):
        for step, events in plan.items():
            @pl.when(t == step)
            def _(events=events):
                for event, *which in events:
                    event(*which)

    at = lax.broadcasted_iota(jnp.int32, (PAIR, length), 0)
    same = at == seg_ref[...]
    hidden = context[...] != 1
    ones = jnp.logical_and(at > TABLES, at < TABLES + 4)
    key_side = jnp.logical_or(
        jnp.logical_and(at < TABLES, same),
        jnp.logical_or(jnp.logical_and(at == TABLES, hidden), ones),
    )
    query_side = jnp.logical_and(at <= TABLES, jnp.logical_not(same))
    key_more[...] = turn(jnp.where(key_side, 1.0, 0.0)).astype(BF)
    mask_more[...] = turn(jnp.where(query_side, FAR, 0.0)).astype(BF)

    keep = [
        pltpu.make_async_copy(here, there, outs.at[n])
        for n, (here, there) in enumerate(
            (
                (q_ref, q_out), (k_ref, k_out), (v_ref, v_out), (normed_t, normed_out),
                (key_more, key_out), (query_more, query_out), (mix_ref, mix_out),
            )
        )
    ]
    gains, offsets = as_row(gain), as_row(offset)
    query_bias = qv_bias[0:1, :].astype(F32)
    value_bias = qv_bias[1:2, :].astype(F32)

    def project(b, _):
        rows = pl.ds(pl.multiple_of(b * BLOCK, BLOCK), BLOCK)
        centred, scale = norm_stats(x_ref[rows, :].astype(F32))
        block = (centred * scale * gains + offsets).astype(BF)
        normed_t[:, rows] = turn(block)
        queries = ((nn(block, wqkv[0]) + query_bias).astype(BF) * 0.125).astype(BF)
        keys = nn(block, wqkv[1]).astype(BF)
        values = (nn(block, wqkv[2]) + value_bias).astype(BF)
        for p in range(pairs):
            part = slice(p * PAIR, (p + 1) * PAIR)
            q_ref[p, rows, :] = queries[:, part]
            k_ref[p, rows, :] = keys[:, part]
            v_ref[p, rows, :] = values[:, part]
        tick(b)
        return 0

    lax.fori_loop(0, blocks, project, 0)
    for n in range(5):
        keep[n].start()

    low_lanes = lanes() < HEAD_DIM
    zero = jnp.zeros((1, PAIR), BF)

    def mixture_copy(t):
        rows = pl.ds(pl.multiple_of(t // pairs * STRIP, STRIP), STRIP)
        return remote(
            mix_ref.at[t % pairs, rows, :], mix_x.at[t % pairs, rows, :], xs.at[1 + t],
            xr.at[1 + t], across,
        )

    per_step = STRIP // BLOCK

    def attend(t, _):
        b, p = t // pairs, t % pairs
        keys = jnp.concatenate([k_ref[p], key_more[...]], axis=1)
        values = jnp.concatenate([v_ref[p], one_lanes(length)], axis=1)
        chains = []
        for n in range(per_step):
            rows = pl.ds(pl.multiple_of(b * STRIP + n * BLOCK, BLOCK), BLOCK)
            queries, more = q_ref[p, rows, :], mask_more[rows, :]
            for low in (0, 1):
                own_lanes = jnp.logical_not(low_lanes) if low else low_lanes
                left = jnp.concatenate([jnp.where(own_lanes, queries, zero), more], axis=1)
                chains.append((rows, low, more, dot_rows(left, keys)))
        parts = []
        for rows, low, more, scores in chains:
            top = jnp.max(scores, axis=-1, keepdims=True)
            mixed = nn(jnp.exp(scores - top).astype(BF), values)
            total = mixed[:, PAIR:PAIR + 1]
            parts.append(mixed[:, :PAIR] / total)
            query_more[2 * p + low, rows, :] = in_pieces(
                -(top + jnp.log(total)), TABLES + 1, more.astype(F32)
            )
            if low:
                mix_ref[p, rows, :] = jnp.where(low_lanes, *parts[-2:]).astype(BF)
        mixture_copy(t).start()
        tick(t + blocks)
        return 0

    lax.fori_loop(0, length // STRIP * pairs, attend, 0)
    keep[5].start()
    keep[6].start()
    out_arrival.wait_recv()
    out_row = as_row(out_bias)

    def mid_copy(b):
        rows = pl.ds(b * BLOCK, BLOCK)
        return pltpu.make_async_copy(mid_ref.at[rows, :], mid_out.at[rows, :], outs.at[7 + b])

    gains_two, offsets_two = as_row(gain_two), as_row(offset_two)

    def half_copies(b):
        rows = pl.ds(b * BLOCK, BLOCK)
        return [
            pltpu.make_async_copy(
                here.at[:, rows, :], there.at[:, rows, :], outs.at[7 + blocks + 2 * b + n]
            )
            for n, (here, there) in enumerate(((active, active_out), (slope, slope_out)))
        ]

    def up_half(b):
        rows = pl.ds(b * BLOCK, BLOCK)
        centred, scale = norm_stats(mid_ref[rows, :])
        block = (centred * scale * gains_two + offsets_two).astype(BF)
        normed_two_t[:, rows] = turn(block)

        def one(n, _):
            cut = pl.ds(pl.multiple_of(n * WIDE, WIDE), WIDE)
            before = nn(block, wff[0, :, :, cut].reshape(width, WIDE)) + bias_row[:, cut]
            spread = 0.5 * (1.0 + lax.erf(before * INV_ROOT_TWO))
            active[n, rows, :] = (before * spread).astype(BF)
            bell = INV_ROOT_TWO_PI * jnp.exp(before * before * -0.5)
            slope[n, rows, :] = (spread + before * bell).astype(BF)
            return 0

        lax.fori_loop(0, active.shape[0], one, 0)
        for copy in half_copies(b):
            copy.start()

    for b in range(blocks):
        if b % per_step == 0:
            for p in range(pairs):
                mixture_copy(b // per_step * pairs + p).wait_recv()
        rows = pl.ds(b * BLOCK, BLOCK)
        ours = jnp.concatenate([mix_ref[p, rows, :] for p in range(pairs)], axis=-1)
        other = jnp.concatenate([mix_x[p, rows, :] for p in range(pairs)], axis=-1)
        first, second = jnp.where(head == 0, ours, other), jnp.where(head == 0, other, ours)
        attended = nn(first, wout_all[0]) + nn(second, wout_all[1])
        mid_ref[rows, :] = x_ref[rows, :].astype(F32) + (attended + out_row)
        mid_copy(b).start()
        if b == 0:
            weights.arrive(0)
        up_half(b)
        if b < 3:
            weights.y_event(1, b + 1)
    normed_two_keep = pltpu.make_async_copy(
        normed_two_t, normed_two_out, outs.at[7 + 3 * blocks]
    )
    normed_two_keep.start()
    wff_keep = [pltpu.make_async_copy(wff.at[u], wff_out.at[u], local.at[u]) for u in range(2)]
    wff_keep[0].start()
    shard_copy.wait()
    bias_copy.wait()
    other_keep = [
        pltpu.make_async_copy(shard_x, shard_out, outs.at[8 + 3 * blocks]),
        pltpu.make_async_copy(bias_x, bias_out, outs.at[9 + 3 * blocks]),
    ]
    for copy in other_keep:
        copy.start()
    weights.arrive(1)
    wff_keep[1].start()
    out_copy.wait_send()
    out_pass.wait_send()
    for copy in keep + wff_keep + other_keep + [normed_two_keep]:
        copy.wait()
    for b in range(blocks):
        for copy in half_copies(b):
            copy.wait()
    for t in range(length // STRIP * pairs):
        mixture_copy(t).wait_send()
    for b in range(blocks):
        mid_copy(b).wait()
    for u in range(2):
        weights.finish(u)


def run_fwd(
    x, seg, context, gain, offset, qv_bias, out_bias, gain_two, offset_two, up_bias, wqkv, wout,
    up_weight, down_t,
):
    length, width = x.shape
    pairs = wqkv.shape[2] // PAIR
    blocks = length // BLOCK
    depth, hidden = up_weight.shape
    by_pair, by_head = (pairs, length, PAIR), (2 * pairs, length, PAIR)
    turned = (width, length)
    halves = (hidden // WIDE, length, WIDE)
    steps = length // STRIP * pairs
    dma = pltpu.SemaphoreType.DMA
    return pl.pallas_call(
        fwd_kernel,
        out_shape=[shape_of(by_pair, BF)] * 4 + [
            shape_of((length, width), F32),
            shape_of(turned, BF),
            shape_of((2, SEQ_SIZE, depth, hidden), BF),
            shape_of((length, PAIR), BF),
            shape_of(by_head, BF),
            shape_of((width, length), BF),
            shape_of(halves, BF),
            shape_of(halves, BF),
            shape_of((2, depth, hidden), BF),
            shape_of((1, hidden), F32),
        ],
        in_specs=[VMEM_SPEC] * 12 + [ANY_SPEC] * 2,
        out_specs=[ANY_SPEC] * 14,
        scratch_shapes=[pltpu.VMEM((2, SEQ_SIZE, depth, hidden), BF)]
        + [pltpu.VMEM(by_pair, BF)] * 4 + [
            pltpu.VMEM((length, width), F32),
            pltpu.VMEM(turned, BF),
            pltpu.VMEM((length, PAIR), BF),
            pltpu.VMEM(by_head, BF),
            pltpu.VMEM((width, length), BF),
            pltpu.VMEM(halves, BF),
            pltpu.VMEM(halves, BF),
            pltpu.VMEM((1, hidden), F32),
            pltpu.VMEM((length, PAIR), BF),
            pltpu.VMEM((2,) + wout.shape, BF),
            pltpu.VMEM(by_pair, BF),
            pltpu.VMEM((2, depth, hidden), BF),
            pltpu.VMEM((1, hidden), F32),
            *[dma((n,)) for n in GATHER_SEMS], dma((1,)), dma((1,)),
            dma((3 + steps,)), dma((3 + steps,)), dma((2,)), dma((10 + 3 * blocks,)),
        ],
        compiler_params=pltpu.CompilerParams(
            collective_id=0, has_side_effects=True, vmem_limit_bytes=VMEM_LIMIT
        ),
    )(
        x, seg, context, gain, offset, qv_bias, out_bias, gain_two, offset_two, up_bias, wqkv,
        wout, up_weight, down_t,
    )


def ff_kernel(
    mid_hbm, dy_hbm, wff_hbm, normed_two_hbm, active_hbm, slope_hbm, gain, wout_hbm, shard_hbm,
    branch_out, gmid_hbm, ga_out, gm_out, summed, other_hbm, small_ref,
    shard,    dy_ref, wff, wout, branch_ref, ga_t, gm_ref, normed_t, dy_t, active, before_grad, gnt_acc, gnt_own, gnt_x, whole, from_mate,
    held, ready,
    xs, xr, cs, cr, ls, ws, ss, ins, outs, *gather_sems,
):
    length, width = dy_ref.shape
    blocks = length // BLOCK
    hidden = wff.shape[3]
    half = hidden // WIDE
    chunks = 2 * hidden // CHUNK
    pairs = gm_ref.shape[0]
    me, head, core, y, across, core_mate, y_mate, z_mates = place()
    dy_load = pltpu.make_async_copy(dy_hbm, dy_ref, ins.at[0])
    wout_load = pltpu.make_async_copy(wout_hbm, wout, ins.at[1])

    def step_loads(n):
        cut = pl.ds(n * WIDE, WIDE)
        return [
            pltpu.make_async_copy(src, dst, ins.at[4 + 3 * n + m])
            for m, (src, dst) in enumerate(
                (
                    (wff_hbm.at[1, :, :, cut], wff.at[1, :, :, cut]),
                    (slope_hbm.at[n], before_grad.at[n]),
                    (wff_hbm.at[0, :, :, cut], wff.at[0, :, :, cut]),
                )
            )
        ]

    active_load = pltpu.make_async_copy(active_hbm, active, ins.at[2])
    normed_load = pltpu.make_async_copy(normed_two_hbm, normed_t, ins.at[3])
    dy_load.start()
    shard_load = pltpu.make_async_copy(shard_hbm, shard, ins.at[4 + 3 * half])
    shard_load.start()
    for n in range(half):
        for copy in step_loads(n):
            copy.start()
    active_load.start()
    normed_load.start()
    wout_load.start()
    other = Gather(other_hbm, lambda u: shard.at[u], gather_sems)
    greet([across, core_mate, y_mate, other.above, other.below])
    shard_load.wait()
    shard_keep = pltpu.make_async_copy(shard, other_hbm.at[:, me], ins.at[5 + 3 * half])
    shard_keep.start()
    other.start_z(0)
    other.start_near(0)
    gains = as_row(gain)

    def weight(kind, n):
        cut = pl.ds(pl.multiple_of(n * WIDE, WIDE), WIDE)
        return wff[kind, :, :, cut].reshape(width, WIDE)

    small_ref[...] = jnp.zeros_like(small_ref)

    def load(b):
        rows = pl.ds(b * BLOCK, BLOCK)
        return pltpu.make_async_copy(mid_hbm.at[rows, :], held.at[b % 2], ls.at[b % 2])

    def store(b):
        rows = pl.ds(b * BLOCK, BLOCK)
        return pltpu.make_async_copy(ready.at[b % 2], gmid_hbm.at[rows, :], ws.at[b % 2])

    load(0).start()
    load(1).start()

    def gnt_copy(b):
        return remote(gnt_own.at[b], gnt_x.at[b], xs.at[b], xr.at[b], across)

    def core_copy(n):
        return remote(
            whole.at[n, :, :, 1 - core], from_mate.at[n], cs.at[n], cr.at[n], core_mate
        )

    def forward(t, _):
        b, n = t // half, t % half
        rows = pl.ds(pl.multiple_of(b * BLOCK, BLOCK), BLOCK)

        for n_first in range(half):
            @pl.when(t == n_first)
            def _(n_first=n_first):
                if n_first == 0:
                    dy_load.wait()
                for copy in step_loads(n_first):
                    copy.wait()

        @pl.when(n == 0)
        def _():
            dy_t[:, rows] = turn(dy_ref[rows, :])
            small_ref[DOWN_BIAS:DOWN_BIAS + 1, :] += sum_rows(dy_ref[rows, :].astype(F32))

        up = weight(0, n)
        grad = nn(dy_ref[rows, :], weight(1, n)) * before_grad[n, rows, :].astype(F32)
        grad = grad.astype(BF)
        before_grad[n, rows, :] = grad
        small_ref[pl.ds(UP_BIAS + n, 1), :] += sum_rows(grad.astype(F32))
        back = dot_rows(grad, up)

        @pl.when(n == 0)
        def _():
            gnt_acc[...] = back

        @pl.when(n > 0)
        def _():
            gnt_acc[...] += back

        for b_done in range(blocks):
            @pl.when(t == (b_done + 1) * half - 1)
            def _(b_done=b_done):
                gnt_own[b_done] = gnt_acc[...].astype(BF)
                gnt_copy(b_done).start()

        @pl.when(t == 5)
        def _():
            other.z_event(0, 1)
            other.y_event(0, 0)

        return 0

    lax.fori_loop(0, blocks * half, forward, 0)

    def weight_grads(left_t, right, first):
        cut_rows = width // Z_SIZE
        per_wide = WIDE // CHUNK

        def one(t, _):
            n, plane = t // Z_SIZE, t % Z_SIZE
            cut = pl.ds(pl.multiple_of(plane * cut_rows, cut_rows), cut_rows)
            total = nn(left_t[cut, :], right[n]).astype(BF)
            for m in range(per_wide):
                piece = total[:, m * CHUNK:(m + 1) * CHUNK]
                whole[first + n * per_wide + m, plane] = piece.reshape(whole.shape[2:])

            @pl.when(plane == Z_SIZE - 1)
            def _():
                for m in range(per_wide):
                    core_copy(first + n * per_wide + m).start()

            return 0

        lax.fori_loop(0, Z_SIZE * half, one, 0)

    active_load.wait()
    normed_load.wait()
    other.z_event(0, 2)
    weight_grads(dy_t, active, chunks // 2)
    other.z_event(0, 3)
    weight_grads(normed_t, before_grad, 0)
    other.z_event(1, 1)
    other.y_event(0, 1)

    def branch(b, _):
        rows = pl.ds(pl.multiple_of(b * BLOCK, BLOCK), BLOCK)
        total = dot_rows(active[0, rows, :], weight(1, 0))
        for n in range(1, half):
            total += dot_rows(active[n, rows, :], weight(1, n))
        branch_ref[rows, :] = total.astype(BF)
        return 0

    lax.fori_loop(0, blocks, branch, 0)
    other.z_event(1, 2)
    other.y_event(0, 2)
    other.y_event(1, 0)
    branch_keep = pltpu.make_async_copy(branch_ref, branch_out, outs.at[0])
    branch_keep.start()
    wout_load.wait()

    def ga_copy(b):
        rows = pl.ds(b * BLOCK, BLOCK)
        return pltpu.make_async_copy(ga_t.at[:, rows], ga_out.at[:, rows], outs.at[1 + b])

    def gm_copy(b):
        rows = pl.ds(b * BLOCK, BLOCK)
        return pltpu.make_async_copy(
            gm_ref.at[:, rows, :], gm_out.at[:, rows, :], outs.at[1 + blocks + b]
        )


    def add_mate(n, _):
        core_copy(n).wait()
        both = whole[n, :, :, core].astype(F32) + from_mate[n].astype(F32)
        from_mate[n] = both.astype(BF)
        return 0

    lax.fori_loop(chunks // 2, chunks, add_mate, 0)
    lax.fori_loop(0, chunks // 2, add_mate, 0)
    keep = pltpu.make_async_copy(from_mate, summed, ss.at[0])
    keep.start()

    strips = BLOCK // PIECE
    for b in range(blocks):
        if b == 1:
            other.y_event(0, 3)
        if b == 2:
            other.z_event(1, 3)
            other.y_event(1, 1)
        if b == 3:
            other.y_event(1, 2)
        gnt_copy(b).wait()
        load(b).wait()
        if b >= 2:
            store(b - 2).wait()

        def through_norm(n, _, b=b):
            rows = pl.ds(pl.multiple_of(n * PIECE, PIECE), PIECE)
            full = pl.ds(pl.multiple_of(b * BLOCK + n * PIECE, PIECE), PIECE)
            grad = gnt_own[b, rows, :].astype(F32) + gnt_x[b, rows, :].astype(F32)
            centred, scale = norm_stats(held[b % 2, rows, :])
            unit = centred * scale
            small_ref[LN2_GAIN:LN2_GAIN + 1, :] += sum_rows(grad * unit)
            small_ref[LN2_BIAS:LN2_BIAS + 1, :] += sum_rows(grad)
            total = dy_ref[full, :].astype(F32) + norm_back(grad * gains, unit, scale)
            ready[b % 2, rows, :] = total
            low = total.astype(BF)
            small_ref[OUT_BIAS:OUT_BIAS + 1, :] += sum_rows(low.astype(F32))
            ga_t[:, full] = turn(low)
            mixed = dot_rows(low, wout[...]).astype(BF)
            for p in range(pairs):
                gm_ref[p, full, :] = mixed[:, p * PAIR:(p + 1) * PAIR]
            return 0

        lax.fori_loop(0, strips, through_norm, 0)
        store(b).start()
        ga_copy(b).start()
        gm_copy(b).start()
        if b + 2 < blocks:
            load(b + 2).start()
    store(blocks - 2).wait()
    store(blocks - 1).wait()
    for b in range(blocks):
        ga_copy(b).wait()
        gm_copy(b).wait()
    branch_keep.wait()
    keep.wait()
    other.y_event(1, 3)
    shard_keep.wait()
    for u in range(2):
        other.arrive(u)
        other.finish(u)


def run_ff(middle, dy, wff, normed_two_t, active, slope, gain, wout, shard):
    length, width = middle.shape
    half = wff.shape[3] // WIDE
    chunks = 2 * wff.shape[3] // CHUNK
    blocks = length // BLOCK
    pairs = wout.shape[0] // PAIR
    depth = width // SEQ_SIZE
    dma = pltpu.SemaphoreType.DMA
    rows = pltpu.VMEM((blocks, BLOCK, width), BF)
    hidden = pltpu.VMEM((half, length, WIDE), BF)
    flat_t = pltpu.VMEM((width, length), BF)
    return pl.pallas_call(
        ff_kernel,
        out_shape=[
            shape_of((length, width), BF),
            shape_of((length, width), F32),
            shape_of((width, length), BF),
            shape_of((pairs, length, PAIR), BF),
            shape_of((chunks, Z_SIZE, Y_SIZE, depth, CHUNK), BF),
            shape_of(wff.shape, BF),
            shape_of((SMALL_ROWS, width), F32),
        ],
        in_specs=[ANY_SPEC] * 6 + [VMEM_SPEC, ANY_SPEC, ANY_SPEC],
        out_specs=[ANY_SPEC] * 6 + [VMEM_SPEC],
        scratch_shapes=[
            pltpu.VMEM(shard.shape, BF),
            pltpu.VMEM((length, width), BF), pltpu.VMEM(wff.shape, BF),
            pltpu.VMEM(wout.shape, BF),
            pltpu.VMEM((length, width), BF), flat_t, pltpu.VMEM((pairs, length, PAIR), BF),
            flat_t, flat_t, hidden, hidden,
            pltpu.VMEM((BLOCK, width), F32), rows, rows,
            pltpu.VMEM((chunks, Z_SIZE, Y_SIZE, CORES, depth, CHUNK), BF),
            pltpu.VMEM((chunks, Z_SIZE, Y_SIZE, depth, CHUNK), BF),
            pltpu.VMEM((2, BLOCK, width), F32), pltpu.VMEM((2, BLOCK, width), F32),
            dma((blocks,)), dma((blocks,)), dma((chunks,)), dma((chunks,)),
            dma((2,)), dma((2,)), dma((1,)), dma((6 + 3 * half,)), dma((1 + 2 * blocks,)),
            *[dma((n,)) for n in GATHER_SEMS],
        ],
        compiler_params=pltpu.CompilerParams(
            collective_id=1, has_side_effects=True, vmem_limit_bytes=VMEM_LIMIT
        ),
    )(middle, dy, wff, normed_two_t, active, slope, gain, wout, shard)


def back_kernel(
    q_hbm, k_hbm, v_hbm, mix_hbm, gm_hbm, query_hbm, ga_hbm, normed_hbm, wqkv_hbm, x_hbm,
    other_hbm, bias_x, gain_in, offset_in, key_more, gain, down_bias, small_in, mid_hbm, gmid_hbm, ff_part, branch,
    out_hbm, tokens_hbm, qkv_sum, out_sum, up_sum, down_sum,
    gain_one, offset_one, qv_small, out_small, gain_two, offset_two, up_small, down_small,
    q_ref, k_ref, v_ref, mix_ref, gm_ref, query_more, ga_t, normed_t, wqkv, x_ref, other,
    out_ref, tokens_ref, key_t, key_acc, value_acc, dq, dk, dv, whole, mate, at_y, at_z, ff_y, ff_z, gn_own, gn_x,
    branch_own, ff_own, held, small_own, small_z, small_y, small_c, small_x,
    fys, fyr, fzs, fzr, acs, acr, ays, ayr, azs, azr, gs, gr, ls, ms, mr, os, hs, ins, more_ins, outs,
):
    length, width = x_ref.shape
    blocks = length // BLOCK
    strips = length // STRIP
    pairs = q_ref.shape[0]
    chunks = ff_part.shape[0]
    half = chunks // 2
    groups = chunks // GROUP
    me, head, core, y, across, core_mate, y_mate, z_mates = place()
    z = me // (Y_SIZE * CORES)
    by_pair = (
        (q_hbm, q_ref), (k_hbm, k_ref), (v_hbm, v_ref), (mix_hbm, mix_ref), (gm_hbm, gm_ref),
    )

    def pair_loads(p):
        both = pl.ds(2 * p, 2)
        first = p * (len(by_pair) + 1)
        return [
            pltpu.make_async_copy(src.at[p], dst.at[p], ins.at[first + n])
            for n, (src, dst) in enumerate(by_pair)
        ] + [
            pltpu.make_async_copy(
                query_hbm.at[both], query_more.at[both], ins.at[first + len(by_pair)]
            )
        ]

    late_loads = [
        pltpu.make_async_copy(src, dst, more_ins.at[n])
        for n, (src, dst) in enumerate(
            (
                (ga_hbm, ga_t), (normed_hbm, normed_t), (wqkv_hbm, wqkv), (x_hbm, x_ref),
                (other_hbm, other),
            )
        )
    ]
    for p in range(pairs):
        for copy in pair_loads(p):
            copy.start()
        if p == 0:
            late_loads[0].start()
            late_loads[1].start()
    late_loads[2].start()
    late_loads[3].start()
    late_loads[4].start()
    greet([across, core_mate, y_mate, *z_mates])

    def part(b):
        return pl.ds(b * BLOCK, BLOCK)

    def load(n):
        source = mid_hbm if n < blocks else gmid_hbm
        return pltpu.make_async_copy(
            source.at[part(n % blocks), :], held.at[n % 2], ls.at[n % 2]
        )

    def taken(n):
        if n + 2 < 2 * blocks:
            load(n + 2).start()

    def group(g):
        return pl.ds(g * GROUP, GROUP)

    def ff_y_copy(g):
        return remote(
            ff_part.at[group(g), :, 1 - y], ff_y.at[group(g)], fys.at[g], fyr.at[g], y_mate
        )

    def ff_z_copy(g, d):
        n = g * 3 + d - 1
        return remote(
            ff_y.at[group(g), (z + d) % Z_SIZE], ff_z.at[d - 1, group(g)],
            fzs.at[n], fzr.at[n], z_mates[d - 1],
        )

    def branch_load(b):
        return pltpu.make_async_copy(branch.at[part(b), :], branch_own.at[b % 2], hs.at[b % 2])

    def ff_load(g):
        return pltpu.make_async_copy(
            ff_part.at[group(g), :, y], ff_own.at[g % 2], os.at[g % 2]
        )

    def ff_y_event(g):
        ff_y_copy(g).wait_recv()
        ff_load(g).wait()
        for n in range(g * GROUP, (g + 1) * GROUP):
            own = ff_own[g % 2, n % GROUP]
            ff_y[n] = (ff_y[n].astype(F32) + own.astype(F32)).astype(BF)
        if g + 2 < groups:
            ff_load(g + 2).start()
            ff_y_copy(g + 2).start()
        for d in (1, 2, 3):
            ff_z_copy(g, d).start()

    def ff_z_event(g):
        for d in (1, 2, 3):
            ff_z_copy(g, d).wait_recv()
        for n in range(g * GROUP, (g + 1) * GROUP):
            total = ff_y[n, z].astype(F32)
            for d in (1, 2, 3):
                total += ff_z[d - 1, n].astype(F32)
            if n < half:
                up_sum[:, n * CHUNK:(n + 1) * CHUNK] = total
            else:
                down_sum[:, (n - half) * CHUNK:(n - half + 1) * CHUNK] = total

    def at_c_copy(p):
        return remote(whole.at[p, :, :, 1 - core], mate.at[p], acs.at[p], acr.at[p], core_mate)

    def at_y_copy(p):
        return remote(mate.at[p, :, 1 - y], at_y.at[p], ays.at[p], ayr.at[p], y_mate)

    def at_z_copy(p, d):
        n = p * 3 + d - 1
        return remote(
            at_y.at[p, (z + d) % Z_SIZE], at_z.at[d - 1, p], azs.at[n], azr.at[n], z_mates[d - 1]
        )

    def at_c_event(p):
        at_c_copy(p).wait_recv()
        mate[p] = (mate[p].astype(F32) + whole[p, :, :, core].astype(F32)).astype(BF)
        at_y_copy(p).start()

    def at_y_event(p):
        at_y_copy(p).wait_recv()
        at_y[p] = (at_y[p].astype(F32) + mate[p, :, y].astype(F32)).astype(BF)
        for d in (1, 2, 3):
            at_z_copy(p, d).start()

    def at_z_event(p):
        for d in (1, 2, 3):
            at_z_copy(p, d).wait_recv()
        total = at_y[p, z].astype(F32)
        for d in (1, 2, 3):
            total += at_z[d - 1, p].astype(F32)
        cut = slice(p * PAIR, (p + 1) * PAIR)
        for kind in range(3):
            qkv_sum[kind, :, cut] = total[:, kind * PAIR:(kind + 1) * PAIR]
        out_sum[:, cut] = total[:, 3 * PAIR:]

    def out_copy(b):
        return pltpu.make_async_copy(out_ref.at[part(b), :], out_hbm.at[part(b), :], outs.at[b])

    def tokens_copy(b):
        return pltpu.make_async_copy(
            tokens_ref.at[part(b), :], tokens_hbm.at[part(b), :], outs.at[blocks + b]
        )

    gains_two, offsets_two = as_row(gain_in), as_row(offset_in)

    def other_weight(kind, n):
        return other[kind, :, :, n * WIDE:(n + 1) * WIDE].reshape(width, WIDE)

    def branch_event(b):
        load(b).wait()
        branch_load(b).wait()
        centred, scale = norm_stats(held[b % 2])
        block = (centred * scale * gains_two + offsets_two).astype(BF)
        parts = []
        for n in range(half * CHUNK // WIDE):
            cut = slice(n * WIDE, (n + 1) * WIDE)
            before = nn(block, other_weight(0, n)) + bias_x[:, cut]
            spread = 0.5 * (1.0 + lax.erf(before * INV_ROOT_TWO))
            parts.append(dot_rows((before * spread).astype(BF), other_weight(1, n)))
        theirs = sum(parts[1:], parts[0]).astype(BF)
        both = branch_own[b % 2].astype(F32) + theirs.astype(F32)
        out_ref[part(b), :] = (held[b % 2] + both + as_row(down_bias)).astype(BF)
        out_copy(b).start()
        taken(b)
        if b + 2 < blocks:
            branch_load(b + 2).start()

    for n in range(2):
        load(n).start()
        branch_load(n).start()
        ff_load(n).start()
        ff_y_copy(n).start()

    plan = {
        2: [(at_c_event, 0), (ff_y_event, 0)], 4: [(at_c_event, 1)], 5: [(ff_y_event, 1)],
        6: [(at_c_event, 2)],
    }

    low_lanes = lanes() < HEAD_DIM
    zero = jnp.zeros((1, PAIR), BF)

    def stacked(strip):
        return jnp.concatenate(
            [jnp.where(low_lanes, strip, zero), jnp.where(low_lanes, zero, strip)], axis=0
        )

    def attend(t, _):
        p, b = t // strips, t % strips
        rows = pl.ds(pl.multiple_of(b * STRIP, STRIP), STRIP)

        @pl.when(b == 0)
        def _():
            for p_now in range(pairs):
                @pl.when(p == p_now)
                def _(p_now=p_now):
                    for copy in pair_loads(p_now):
                        copy.wait()
            key_t[...] = turn(k_ref[p])
            key_acc[...] = jnp.zeros_like(key_acc)
            value_acc[...] = jnp.zeros_like(value_acc)

        queries, grads = stacked(q_ref[p, rows, :]), stacked(gm_ref[p, rows, :])
        more = jnp.concatenate(
            [query_more[2 * p, rows, :], query_more[2 * p + 1, rows, :]], axis=0
        )
        mixture = mix_ref[p, rows, :]
        product = grads.astype(F32) * jnp.concatenate([mixture, mixture], axis=0).astype(F32)
        inner = -jnp.sum(product, axis=-1, keepdims=True)
        query_side = jnp.concatenate([queries, more], axis=1)
        grad_side = jnp.concatenate([grads, in_pieces(inner, 0, 0.0)], axis=1)
        to_queries = jnp.zeros((PAIR, 2 * STRIP), F32)
        for n in range(blocks):
            keys = jnp.concatenate([k_ref[p, part(n), :], key_more[part(n), :]], axis=1)
            values = jnp.concatenate([v_ref[p, part(n), :], one_lanes(BLOCK)], axis=1)
            weights = jnp.exp(dot_rows(keys, query_side)).astype(BF)
            grad_scores = weights * dot_rows(values, grad_side).astype(BF)
            value_acc[part(n), :] += split_sum(weights, grads)
            key_acc[part(n), :] += split_sum(grad_scores, queries)
            to_queries += nn(key_t[:, part(n)], grad_scores)
        own = jnp.concatenate(
            [to_queries[:HEAD_DIM, :STRIP], to_queries[HEAD_DIM:, STRIP:]], axis=0
        )
        dq[p, rows, :] = (turn(own) * 0.125).astype(BF)

        @pl.when(b == strips - 1)
        def _():
            @pl.when(p == 0)
            def _():
                late_loads[0].wait()
                late_loads[1].wait()

            dk[p] = key_acc[...].astype(BF)
            dv[p] = value_acc[...].astype(BF)
            right = jnp.concatenate([dq[p], dk[p], dv[p]], axis=1)
            mixture_all = mix_ref[p]

            def one(plane, _):
                cut = pl.ds(pl.multiple_of(plane * BLOCK, BLOCK), BLOCK)
                both = jnp.concatenate(
                    [nn(normed_t[cut, :], right), nn(ga_t[cut, :], mixture_all)], axis=1
                )
                whole[p, plane] = both.astype(BF).reshape(whole.shape[2:])
                return 0

            lax.fori_loop(0, Z_SIZE, one, 0)
            at_c_copy(p).start()

        for step, events in plan.items():
            @pl.when(t == step)
            def _(events=events):
                for event, n in events:
                    event(n)
        return 0

    lax.fori_loop(0, pairs * strips, attend, 0)
    late_loads[2].wait()
    late_loads[3].wait()

    def gn_copy(b):
        return remote(gn_own.at[b], gn_x.at[b], gs.at[b], gr.at[b], across)

    own_gain = jnp.zeros((1, width), F32)
    own_offset = jnp.zeros((1, width), F32)
    for b in range(blocks):
        total = jnp.zeros((BLOCK, width), F32)
        for n, grad in enumerate((dq, dk, dv)):
            left = jnp.concatenate([grad[p, part(b), :] for p in range(pairs)], axis=1)
            total += dot_rows(left, wqkv[n])
        gn_own[b] = total.astype(BF)
        gn_copy(b).start()
        centred, scale = norm_stats(x_ref[part(b), :].astype(F32))
        own_gain += sum_rows(total * (centred * scale))
        own_offset += sum_rows(total)

    at_c_event(3)
    small_own[...] = small_in[...]
    small_own[LN1_GAIN:LN1_GAIN + 1, :] = own_gain
    small_own[LN1_BIAS:LN1_BIAS + 1, :] = own_offset
    for p in range(pairs):
        first, second = p * PAIR, (pairs + p) * PAIR
        small_own[QV_BIAS:QV_BIAS + 1, first:first + PAIR] = sum_rows(dq[p].astype(F32))
        small_own[QV_BIAS:QV_BIAS + 1, second:second + PAIR] = sum_rows(dv[p].astype(F32))
    def small_z_copy(d):
        return remote(small_own, small_z.at[z], ms.at[d - 1], mr.at[d - 1], z_mates[d - 1])

    def small_z_arrival(d):
        slot = small_z.at[(z + Z_SIZE - d) % Z_SIZE]
        return remote(slot, slot, ms.at[d - 1], mr.at[d - 1], z_mates[d - 1])

    y_sum = remote(small_y.at[0], small_y.at[1], ms.at[3], mr.at[3], y_mate)
    c_sum = remote(small_c.at[0], small_c.at[1], ms.at[4], mr.at[4], core_mate)
    x_sum = remote(small_x.at[0], small_x.at[1], ms.at[5], mr.at[5], across)
    for d in (1, 2, 3):
        small_z_copy(d).start()
    small_z[z] = small_own[...]

    def small_y_step():
        for d in (1, 2, 3):
            small_z_arrival(d).wait_recv()
        small_y[0] = small_z[0] + small_z[1] + small_z[2] + small_z[3]
        y_sum.start()

    def small_c_step():
        y_sum.wait()
        small_c[0] = small_y[0] + small_y[1]
        c_sum.start()

    def small_x_step():
        c_sum.wait()
        small_x[0] = small_c[0, 0:8, :] + small_c[1, 0:8, :]
        x_sum.start()

    late_loads[4].wait()
    ff_y_event(2)
    ff_z_event(0)
    branch_event(0)
    ff_y_event(3)
    ff_z_event(1)
    branch_event(1)
    at_y_event(0)
    small_y_step()
    branch_event(2)
    at_y_event(1)
    ff_z_event(2)
    small_c_step()
    branch_event(3)
    at_y_event(2)
    ff_z_event(3)
    gains = as_row(gain)
    for b in range(blocks):
        gn_copy(b).wait()
        load(blocks + b).wait()
        grad = gn_own[b].astype(F32) + gn_x[b].astype(F32)
        centred, scale = norm_stats(x_ref[part(b), :].astype(F32))
        unit = centred * scale
        tokens_ref[part(b), :] = (
            held[b % 2] + norm_back(grad * gains, unit, scale)
        ).astype(BF)
        tokens_copy(b).start()
        taken(blocks + b)
        if b == 0:
            at_y_event(3)
            at_z_event(0)
        if b == 1:
            small_x_step()
            at_z_event(1)
        if b == 2:
            at_z_event(2)

    at_z_event(3)
    x_sum.wait()
    ln1 = small_x[0, 0:2, :] + small_x[1, 0:2, :]
    gain_one[...] = ln1[0:1, :].reshape(width)
    offset_one[...] = ln1[1:2, :].reshape(width)
    small = small_c[0] + small_c[1]
    for kind, target in (
        (OUT_BIAS, out_small), (LN2_GAIN, gain_two), (LN2_BIAS, offset_two), (DOWN_BIAS, down_small),
    ):
        target[...] = small[kind:kind + 1, :].reshape(width)
    cols = pairs * PAIR
    qv_small[0:1, :] = small[QV_BIAS:QV_BIAS + 1, :cols]
    qv_small[1:2, :] = small[QV_BIAS:QV_BIAS + 1, cols:]
    for n in range(up_small.shape[0] // width):
        row = small[UP_BIAS + n:UP_BIAS + n + 1, :]
        up_small[n * width:(n + 1) * width] = row.reshape(width)

    for d in (1, 2, 3):
        small_z_copy(d).wait_send()
    for b in range(blocks):
        out_copy(b).wait()
        tokens_copy(b).wait()
    for g in range(groups):
        ff_y_copy(g).wait_send()
        for d in (1, 2, 3):
            ff_z_copy(g, d).wait_send()
    for p in range(pairs):
        at_c_copy(p).wait_send()
        at_y_copy(p).wait_send()
        for d in (1, 2, 3):
            at_z_copy(p, d).wait_send()


def run_back(
    queries, keys, values, mixture, grad_mixture, query_more, ga_t, normed_t, wqkv, x, other,
    bias_x, gain_two, offset_two, key_more, gain, down_bias, small, middle, grad_middle, ff_part,
    branch,
):
    length, width = x.shape
    pairs = queries.shape[0]
    chunks, depth = ff_part.shape[0], ff_part.shape[3]
    groups = chunks // GROUP
    cols, hidden = pairs * PAIR, chunks // 2 * CHUNK
    blocks = length // BLOCK
    dma = pltpu.SemaphoreType.DMA
    rows = pltpu.VMEM((blocks, BLOCK, width), BF)
    by_pair = pltpu.VMEM((pairs, length, PAIR), BF)
    whole_rows = pltpu.VMEM((length, width), BF)
    row = shape_of((width,), F32)
    loaded = (
        queries, keys, values, mixture, grad_mixture, query_more, ga_t, normed_t, wqkv, x, other
    )
    return pl.pallas_call(
        back_kernel,
        out_shape=[
            shape_of((length, width), BF),
            shape_of((length, width), BF),
            shape_of((3, depth, cols), F32),
            shape_of((depth, cols), F32),
            shape_of((depth, hidden), F32),
            shape_of((depth, hidden), F32),
            row, row, shape_of((2, cols), F32), row, row, row, shape_of((hidden,), F32), row,
        ],
        in_specs=[ANY_SPEC] * 11 + [VMEM_SPEC] * 7 + [ANY_SPEC] * 4,
        out_specs=[ANY_SPEC] * 2 + [VMEM_SPEC] * 12,
        scratch_shapes=[pltpu.VMEM(v.shape, BF) for v in loaded] + [
            whole_rows, whole_rows, pltpu.VMEM((PAIR, length), BF),
            pltpu.VMEM((length, PAIR), F32), pltpu.VMEM((length, PAIR), F32),
            by_pair, by_pair, by_pair,
            pltpu.VMEM((pairs, Z_SIZE, Y_SIZE, CORES, depth, CHUNK), BF),
            pltpu.VMEM((pairs, Z_SIZE, Y_SIZE, depth, CHUNK), BF),
            pltpu.VMEM((pairs, Z_SIZE, depth, CHUNK), BF),
            pltpu.VMEM((3, pairs, depth, CHUNK), BF),
            pltpu.VMEM((chunks, Z_SIZE, depth, CHUNK), BF),
            pltpu.VMEM((3, chunks, depth, CHUNK), BF),
            rows, rows,
            pltpu.VMEM((2, BLOCK, width), BF),
            pltpu.VMEM((2, GROUP, Z_SIZE, depth, CHUNK), BF),
            pltpu.VMEM((2, BLOCK, width), F32),
            pltpu.VMEM(small.shape, F32),
            pltpu.VMEM((Z_SIZE,) + small.shape, F32),
            pltpu.VMEM((2,) + small.shape, F32),
            pltpu.VMEM((2,) + small.shape, F32),
            pltpu.VMEM((2, 8, width), F32),
            dma((groups,)), dma((groups,)),
            dma((3 * groups,)), dma((3 * groups,)), dma((pairs,)), dma((pairs,)),
            dma((pairs,)), dma((pairs,)), dma((3 * pairs,)), dma((3 * pairs,)),
            dma((blocks,)), dma((blocks,)), dma((2,)), dma((6,)), dma((6,)), dma((2,)), dma((2,)),
            dma((6 * pairs,)), dma((5,)), dma((2 * blocks,)),
        ],
        compiler_params=pltpu.CompilerParams(
            collective_id=2, has_side_effects=True, vmem_limit_bytes=VMEM_LIMIT
        ),
    )(
        *loaded, bias_x, gain_two, offset_two, key_more, gain, down_bias, small, middle,
        grad_middle, ff_part, branch,
    )


def hand_over_kernel(*refs):
    *refs, sems = refs
    count = len(refs) // 3
    refs = refs[:count] + refs[2 * count:] + refs[count:2 * count]
    loads, stores = (
        [
            pltpu.make_async_copy(refs[a * count + n], refs[b * count + n], sems.at[a, n])
            for n in range(count)
        ]
        for a, b in ((0, 1), (1, 2))
    )
    for load in loads:
        load.start()
    for load, store in zip(loads, stores):
        load.wait()
        store.start()
    for store in stores:
        store.wait()


def hand_over(results):
    return pl.pallas_call(
        hand_over_kernel,
        out_shape=[shape_of(v.shape, v.dtype) for v in results],
        in_specs=[ANY_SPEC] * len(results),
        out_specs=[ANY_SPEC] * len(results),
        scratch_shapes=[pltpu.VMEM(v.shape, v.dtype) for v in results] + [
            pltpu.SemaphoreType.DMA((2, len(results)))
        ],
        compiler_params=pltpu.CompilerParams(vmem_limit_bytes=VMEM_LIMIT),
    )(*results)


def fast_body(
    tokens, segment_ids, context_flags, ln1_gain, ln1_bias, qkv_weight, qv_bias, out_weight,
    out_bias, ln2_gain, ln2_bias, up_weight, up_bias, down_weight, down_bias, cotangent,
):
    x, dy = tokens[0], cotangent[0]
    (
        queries, keys, values, mixture, middle, normed_t, wff, key_more, query_more,
        normed_two_t, active, slope, shard_x, bias_x,
    ) = run_fwd(
        x, segment_ids, context_flags, ln1_gain, ln1_bias, qv_bias, out_bias, ln2_gain,
        ln2_bias, up_bias, qkv_weight, out_weight, up_weight, down_weight.T,
    )
    branch, grad_middle, ga_t, grad_mixture, ff_part, other, small = run_ff(
        middle, dy, wff, normed_two_t, active, slope, ln2_gain, out_weight, shard_x
    )
    (
        output, tokens_grad, qkv_grad, out_grad, up_grad, down_grad, gain_one, offset_one,
        qv_grad, out_bias_grad, gain_two, offset_two, up_bias_grad, down_bias_grad,
    ) = hand_over(run_back(
        queries, keys, values, mixture, grad_mixture, query_more, ga_t, normed_t, qkv_weight, x,
        other, bias_x, ln2_gain, ln2_bias, key_more, ln1_gain, down_bias, small, middle,
        grad_middle, ff_part, branch,
    ))
    return (
        output[None], tokens_grad[None], gain_one, offset_one, qkv_grad, qv_grad, out_grad.T,
        out_bias_grad, gain_two, offset_two, up_grad, up_bias_grad, down_grad.T, down_bias_grad,
    )


def solution(mesh):
    chosen = generic_body
    if mesh.shape["head"] == 2 and mesh.shape["seq"] == SEQ_SIZE:
        chosen = fast_body
    return jax.shard_map(
        chosen,
        mesh=mesh,
        in_specs=(
            P("seq", None, None),
            P("seq", None),
            P("seq", None),
            P(),
            P(),
            P(None, None, "head"),
            P(None, "head"),
            P("head", None),
            P(),
            P(),
            P(),
            P("seq", "head"),
            P("head"),
            P("head", "seq"),
            P(),
            P("seq", None, None),
        ),
        out_specs=(
            P("seq", None, None),
            P("seq", None, None),
            P(),
            P(),
            P(None, "seq", "head"),
            P(None, "head"),
            P("head", "seq"),
            P(),
            P(),
            P(),
            P("seq", "head"),
            P("head"),
            P("head", "seq"),
            P(),
        ),
        check_vma=False,
    )
```

```python
import math

import jax
import jax.numpy as jnp
from jax import lax
from jax.experimental import pallas as pl
from jax.experimental.pallas import tpu as pltpu
from jax.sharding import PartitionSpec as P

HEAD_DIM = 64


def layer_norm(values_in, scaling, offset):
    middle = jnp.mean(values_in, axis=-1, keepdims=True)
    centred = values_in - middle
    spread = jnp.mean(centred * centred, axis=-1, keepdims=True)
    return centred * lax.rsqrt(spread + 1e-05) * scaling + offset


def gelu_exact(values_in):
    return 0.5 * values_in * (1.0 + jax.scipy.special.erf(values_in * 0.7071067811865476))


def dot_rows(left, right):
    return lax.dot_general(
        left, right, (((1,), (1,)), ((), ())), preferred_element_type=jnp.float32
    )


def dot_cols(left, right):
    return lax.dot_general(
        left, right, (((0,), (0,)), ((), ())), preferred_element_type=jnp.float32
    )


def masked_scores(block_query, seq_keys, block_segments, seq_segments, seq_context, factor):
    raw_scores = (
        jnp.einsum("qhd,khd->hqk", block_query, seq_keys, preferred_element_type=jnp.float32)
        * factor
    )
    allowed = (block_segments[:, None] == seq_segments[None, :]) & (seq_context[None, :] == 1)
    return jnp.where(allowed[None], raw_scores, -1e30)


def generic_body(
    tokens,
    segment_ids,
    context_flags,
    ln1_gain,
    ln1_bias,
    qkv_weight,
    qv_bias,
    out_weight,
    out_bias,
    ln2_gain,
    ln2_bias,
    up_weight,
    up_bias,
    down_weight,
    down_bias,
    cotangent,
):
    seq_count, length, width = tokens.shape
    row_count = seq_count * length
    local_cols = qkv_weight.shape[2]
    head_count = local_cols // HEAD_DIM
    factor = 1.0 / math.sqrt(HEAD_DIM)
    block = min(512, length)
    blocks = length // block
    gain_one = ln1_gain.astype(jnp.float32)
    offset_one = ln1_bias.astype(jnp.float32)
    gain_two = ln2_gain.astype(jnp.float32)
    offset_two = ln2_bias.astype(jnp.float32)
    flat_in = tokens.astype(jnp.float32).reshape(row_count, width)
    normed_f, norm_one_pull = jax.vjp(layer_norm, flat_in, gain_one, offset_one)
    normed = normed_f.astype(jnp.bfloat16)
    queries = (
        jnp.dot(normed, qkv_weight[0], preferred_element_type=jnp.float32)
        + qv_bias[0].astype(jnp.float32)
    ).astype(jnp.bfloat16)
    key_rows = jnp.dot(normed, qkv_weight[1], preferred_element_type=jnp.float32).astype(
        jnp.bfloat16
    )
    value_rows = (
        jnp.dot(normed, qkv_weight[2], preferred_element_type=jnp.float32)
        + qv_bias[1].astype(jnp.float32)
    ).astype(jnp.bfloat16)

    def per_sequence(array):
        return array.reshape(seq_count, length, head_count, HEAD_DIM)

    def attend_sequence(member):
        seq_query, seq_keys, seq_values, seq_segments, seq_context = member

        def attend_block(portion):
            block_query, block_segments = portion
            scores = masked_scores(
                block_query, seq_keys, block_segments, seq_segments, seq_context, factor
            )
            row_top = jnp.max(scores, axis=-1, keepdims=True)
            exponent = jnp.exp(scores - row_top)
            row_total = jnp.sum(exponent, axis=-1, keepdims=True)
            soft_weights = (exponent / row_total).astype(jnp.bfloat16)
            block_mix = jnp.einsum(
                "hqk,khd->qhd", soft_weights, seq_values, preferred_element_type=jnp.float32
            )
            return (block_mix.astype(jnp.bfloat16), row_top + jnp.log(row_total))

        return lax.map(
            attend_block,
            (
                seq_query.reshape(blocks, block, head_count, HEAD_DIM),
                seq_segments.reshape(blocks, block),
            ),
        )

    mixture, log_totals = lax.map(
        attend_sequence,
        (
            per_sequence(queries),
            per_sequence(key_rows),
            per_sequence(value_rows),
            segment_ids,
            context_flags,
        ),
    )
    mixture = mixture.reshape(row_count, local_cols)
    partial_out = jnp.dot(mixture, out_weight, preferred_element_type=jnp.float32)
    grad_rows_all = cotangent.reshape(row_count, width)
    grad_float_all = grad_rows_all.astype(jnp.float32)
    grad_down_bias = jnp.sum(grad_float_all, axis=0)
    attended = lax.psum(partial_out, "head") + out_bias.astype(jnp.float32)
    middle_state = flat_in + attended
    normed_two_f, norm_two_pull = jax.vjp(layer_norm, middle_state, gain_two, offset_two)
    normed_two = normed_two_f.astype(jnp.bfloat16)
    up_part, down_part, up_shift = (
        lax.all_gather(up_weight, "head", axis=1, tiled=True),
        lax.all_gather(down_weight, "head", axis=0, tiled=True),
        lax.all_gather(up_bias, "head", axis=0, tiled=True),
    )
    up_full, down_full = (
        lax.all_gather(up_part, "seq", axis=0, tiled=True),
        lax.all_gather(down_part, "seq", axis=1, tiled=True),
    )
    before = jnp.dot(normed_two, up_full, preferred_element_type=jnp.float32) + up_shift.astype(
        jnp.float32
    )
    active_f, gelu_pull = jax.vjp(gelu_exact, before)
    active = active_f.astype(jnp.bfloat16)
    branch_out = jnp.dot(active, down_full, preferred_element_type=jnp.float32)
    final_rows = (middle_state + branch_out + down_bias.astype(jnp.float32)).astype(jnp.bfloat16)
    output = final_rows.reshape(tokens.shape)
    grad_float = grad_rows_all.astype(jnp.float32)
    grad_down = dot_cols(active, grad_rows_all)
    grad_active = dot_rows(grad_rows_all, down_full)
    (grad_before_f,) = gelu_pull(grad_active)
    grad_before = grad_before_f.astype(jnp.bfloat16)
    grad_up = dot_cols(normed_two, grad_before)
    grad_up_bias = jnp.sum(grad_before.astype(jnp.float32), axis=0)
    grad_normed_two = dot_rows(grad_before, up_full)
    grad_middle_norm, grad_gain_two, grad_offset_two = norm_two_pull(grad_normed_two)
    grad_middle = grad_float + grad_middle_norm
    ff_part = up_weight.shape[1]
    start_col = lax.axis_index("head") * ff_part
    grad_up = lax.dynamic_slice_in_dim(grad_up, start_col, ff_part, 1)
    grad_down = lax.dynamic_slice_in_dim(grad_down, start_col, ff_part, 0)
    grad_up_bias = lax.dynamic_slice_in_dim(grad_up_bias, start_col, ff_part, 0)
    grad_attended = grad_middle.astype(jnp.bfloat16)
    grad_out_bias = jnp.sum(grad_attended.astype(jnp.float32), axis=0)
    grad_out = dot_cols(mixture, grad_attended)
    grad_mixture = dot_rows(grad_attended, out_weight).astype(jnp.bfloat16)

    def back_sequence(member):
        seq_query, seq_keys, seq_values, seq_grad, seq_logs, seq_segments, seq_context = member

        def back_block(carry, portion):
            key_acc, value_acc = carry
            block_query, block_grad, block_logs, block_segments = portion
            scores = masked_scores(
                block_query, seq_keys, block_segments, seq_segments, seq_context, factor
            )
            soft_weights = jnp.exp(scores - block_logs)
            value_acc = value_acc + jnp.einsum(
                "hqk,qhd->khd",
                soft_weights.astype(jnp.bfloat16),
                block_grad,
                preferred_element_type=jnp.float32,
            )
            grad_soft = jnp.einsum(
                "qhd,khd->hqk", block_grad, seq_values, preferred_element_type=jnp.float32
            )
            row_inner = jnp.sum(soft_weights * grad_soft, axis=-1, keepdims=True)
            grad_scores = (soft_weights * (grad_soft - row_inner)).astype(jnp.bfloat16)
            grad_query = (
                jnp.einsum(
                    "hqk,khd->qhd", grad_scores, seq_keys, preferred_element_type=jnp.float32
                )
                * factor
            )
            key_acc = (
                key_acc
                + jnp.einsum(
                    "hqk,qhd->khd", grad_scores, block_query, preferred_element_type=jnp.float32
                )
                * factor
            )
            return ((key_acc, value_acc), grad_query)

        empty = jnp.zeros((length, head_count, HEAD_DIM), jnp.float32)
        (key_acc, value_acc), grad_query = lax.scan(
            back_block,
            (empty, empty),
            (
                seq_query.reshape(blocks, block, head_count, HEAD_DIM),
                seq_grad.reshape(blocks, block, head_count, HEAD_DIM),
                seq_logs,
                seq_segments.reshape(blocks, block),
            ),
        )
        return (grad_query, key_acc, value_acc)

    grad_queries, grad_keys, grad_values = lax.map(
        back_sequence,
        (
            per_sequence(queries),
            per_sequence(key_rows),
            per_sequence(value_rows),
            per_sequence(grad_mixture),
            log_totals,
            segment_ids,
            context_flags,
        ),
    )
    grad_queries = grad_queries.reshape(row_count, local_cols).astype(jnp.bfloat16)
    grad_keys = grad_keys.reshape(row_count, local_cols).astype(jnp.bfloat16)
    grad_values = grad_values.reshape(row_count, local_cols).astype(jnp.bfloat16)
    grad_qv_bias = jnp.stack(
        [
            jnp.sum(grad_queries.astype(jnp.float32), axis=0),
            jnp.sum(grad_values.astype(jnp.float32), axis=0),
        ]
    )
    grad_qkv = jnp.stack(
        [dot_cols(normed, grad_queries), dot_cols(normed, grad_keys), dot_cols(normed, grad_values)]
    )
    grad_normed = (
        dot_rows(grad_queries, qkv_weight[0])
        + dot_rows(grad_keys, qkv_weight[1])
        + dot_rows(grad_values, qkv_weight[2])
    )
    grad_normed = lax.psum(grad_normed, "head")
    grad_input_norm, grad_gain_one, grad_offset_one = norm_one_pull(grad_normed)
    tokens_grad = (grad_middle + grad_input_norm).astype(jnp.bfloat16).reshape(tokens.shape)
    summed_qkv, summed_out, summed_up, summed_down = (
        lax.psum_scatter(
            grad_qkv.astype(jnp.bfloat16), "seq", scatter_dimension=1, tiled=True
        ).astype(jnp.float32),
        lax.psum_scatter(
            grad_out.astype(jnp.bfloat16), "seq", scatter_dimension=1, tiled=True
        ).astype(jnp.float32),
        lax.psum_scatter(
            grad_up.astype(jnp.bfloat16), "seq", scatter_dimension=0, tiled=True
        ).astype(jnp.float32),
        lax.psum_scatter(
            grad_down.astype(jnp.bfloat16), "seq", scatter_dimension=1, tiled=True
        ).astype(jnp.float32),
    )
    smalls = lax.psum(
        (
            grad_gain_one,
            grad_offset_one,
            grad_qv_bias,
            grad_out_bias,
            grad_gain_two,
            grad_offset_two,
            grad_up_bias,
            grad_down_bias,
        ),
        "seq",
    )
    return (
        output,
        tokens_grad,
        smalls[0],
        smalls[1],
        summed_qkv,
        smalls[2],
        summed_out,
        smalls[3],
        smalls[4],
        smalls[5],
        summed_up,
        smalls[6],
        summed_down,
        smalls[7],
    )


MESH = pl.DeviceIdType.MESH
BF = jnp.bfloat16
F32 = jnp.float32
BLOCK = 256
STRIP = 512
PIECE = 128
WIDE = 1024
GROUP = 2
CHUNK = 512
PAIR = 2 * HEAD_DIM
Z_SIZE, Y_SIZE, CORES = 4, 2, 2
SEQ_SIZE = Z_SIZE * Y_SIZE * CORES
HOP = Y_SIZE * CORES
TABLES = 8
FAR = -1e30
VMEM_LIMIT = 62 * 2**20
INV_ROOT_TWO = 0.7071067811865476
INV_ROOT_TWO_PI = 0.3989422804014327
LN1_GAIN, LN1_BIAS, QV_BIAS, OUT_BIAS, LN2_GAIN, LN2_BIAS, UP_BIAS, DOWN_BIAS = 0, 1, 2, 3, 4, 5, 6, 8
SMALL_ROWS = 16
VMEM_SPEC = pl.BlockSpec(memory_space=pltpu.VMEM)
ANY_SPEC = pl.BlockSpec(memory_space=pl.ANY)


def shape_of(dims, dtype):
    return jax.ShapeDtypeStruct(tuple(dims), dtype)


def nn(left, right):
    return jnp.dot(left, right, preferred_element_type=F32)


def split_sum(left, right):
    parts = [
        nn(left[:, n:n + BLOCK], right[n:n + BLOCK]) for n in range(0, left.shape[1], BLOCK)
    ]
    while len(parts) > 1:
        parts = [a + b for a, b in zip(parts[::2], parts[1::2])]
    return parts[0]


def turn(block):
    return jnp.transpose(block)


def sum_rows(block):
    return jnp.sum(block, axis=0, keepdims=True)


def place():
    me = lax.axis_index("seq")
    head = lax.axis_index("head")
    core = me % 2
    y = (me // 2) % 2
    across = {"seq": me, "head": 1 - head}
    core_mate = {"seq": me + 1 - 2 * core, "head": head}
    y_mate = {"seq": me + 2 - 4 * y, "head": head}
    z_mates = [{"seq": (me + HOP * d) % SEQ_SIZE, "head": head} for d in (1, 2, 3)]
    return me, head, core, y, across, core_mate, y_mate, z_mates


def greet(others):
    barrier = pltpu.get_barrier_semaphore()
    for other in others:
        pl.semaphore_signal(barrier, inc=1, device_id=other, device_id_type=MESH)
    pl.semaphore_wait(barrier, len(others))


def remote(src, dst, send_sem, recv_sem, other):
    return pltpu.make_async_remote_copy(
        src_ref=src, dst_ref=dst, send_sem=send_sem, recv_sem=recv_sem,
        device_id=other, device_id_type=MESH,
    )


def norm_stats(rows):
    middle = jnp.mean(rows, axis=-1, keepdims=True)
    centred = rows - middle
    spread = jnp.mean(centred * centred, axis=-1, keepdims=True)
    return centred, lax.rsqrt(spread + 1e-05)


def norm_back(inner, unit, scale):
    return scale * (
        inner
        - jnp.mean(inner, axis=-1, keepdims=True)
        - unit * jnp.mean(inner * unit, axis=-1, keepdims=True)
    )


def as_row(vector):
    return vector[...].astype(F32).reshape(1, -1)


def lanes():
    return lax.broadcasted_iota(jnp.int32, (1, PAIR), 1)


def in_pieces(column, first, rest):
    high = column.astype(BF).astype(F32)
    mid = (column - high).astype(BF).astype(F32)
    low = column - high - mid
    at = lanes()
    return jnp.where(
        at == first, high, jnp.where(at == first + 1, mid, jnp.where(at == first + 2, low, rest))
    ).astype(BF)


def gelu_parts(before):
    bell = jnp.exp(before * before * -0.5)
    near = 1.0 / (1.0 + (0.3275911 * INV_ROOT_TWO) * jnp.abs(before))
    series = 0.5 * 1.061405429
    for factor in (-1.453152027, 1.421413741, -0.284496736, 0.254829592):
        series = series * near + 0.5 * factor
    tail = series * near * bell
    return jnp.where(before < 0.0, tail, 1.0 - tail), bell * INV_ROOT_TWO_PI


def one_lanes(length):
    return jnp.broadcast_to(jnp.where(lanes() < 3, 1.0, 0.0).astype(BF), (length, PAIR))


class Gather:
    def __init__(self, whole, own, sems):
        self.whole, self.own = whole, own
        self.zs, self.zr, self.ys, self.yr, self.cs, self.cr = sems
        self.me, head, self.core, self.y, _, self.core_mate, self.y_mate, _ = place()
        self.z = self.me // HOP
        self.above = {"seq": (self.me + HOP) % SEQ_SIZE, "head": head}
        self.below = {"seq": (self.me + SEQ_SIZE - HOP) % SEQ_SIZE, "head": head}
        self.flows = [(0, 0)] + [(way, s) for s in (1, 2, 3) for way in (0, 1)]
        self.beside_y = self.me + 2 - 4 * self.y
        self.beside = self.me + 1 - 2 * self.core

    @staticmethod
    def source(base, way, s):
        away = SEQ_SIZE - HOP * s if way == 0 else HOP * s
        return (base + away) % SEQ_SIZE

    def goes_on(self, way):
        return (self.z < Z_SIZE - 1) if way == 0 else (self.z > 0)

    def held(self, u, j, first):
        return self.own(u) if first else self.whole.at[u, j]

    def z_copy(self, u, way, s):
        n = (u * 2 + way) * 3 + s - 1
        j = self.source(self.me, way, s - 1)
        return remote(
            self.held(u, j, s == 1), self.whole.at[u, j], self.zs.at[n], self.zr.at[n],
            self.above if way == 0 else self.below,
        )

    def z_arrival(self, u, way, s):
        n = (u * 2 + way) * 3 + s - 1
        slot = self.whole.at[u, self.source(self.me, way, s)]
        return remote(slot, slot, self.zs.at[n], self.zr.at[n], self.above)

    def y_copy(self, u, f):
        n = u * 7 + f
        j = self.source(self.me, *self.flows[f])
        return remote(
            self.held(u, j, f == 0), self.whole.at[u, j], self.ys.at[n], self.yr.at[n],
            self.y_mate,
        )

    def y_arrival(self, u, f):
        n = u * 7 + f
        slot = self.whole.at[u, self.source(self.beside_y, *self.flows[f])]
        return remote(slot, slot, self.ys.at[n], self.yr.at[n], self.y_mate)

    def c_copy(self, u, f, from_y):
        n = (u * 2 + from_y) * 7 + f
        j = self.source(self.beside_y if from_y else self.me, *self.flows[f])
        return remote(
            self.held(u, j, f == 0 and not from_y), self.whole.at[u, j], self.cs.at[n],
            self.cr.at[n], self.core_mate,
        )

    def c_arrival(self, u, f, from_y):
        n = (u * 2 + from_y) * 7 + f
        base = self.beside + from_y * (2 - 4 * self.y)
        slot = self.whole.at[u, self.source(base, *self.flows[f])]
        return remote(slot, slot, self.cs.at[n], self.cr.at[n], self.core_mate)

    def for_flow(self, f, do):
        if f == 0:
            do()
        else:
            way, s = self.flows[f]
            pl.when((self.z >= s) if way == 0 else (self.z + s < Z_SIZE))(do)

    def for_step(self, s, do):
        for f, (way, step) in enumerate(self.flows):
            if step == s:
                self.for_flow(f, lambda f=f, way=way: do(f, way))

    def start_z(self, u):
        for way in (0, 1):
            pl.when(self.goes_on(way))(lambda way=way: self.z_copy(u, way, 1).start())

    def start_near(self, u):
        self.y_copy(u, 0).start()
        self.c_copy(u, 0, 0).start()

    def z_event(self, u, s):
        def one(f, way):
            self.z_arrival(u, way, s).wait_recv()
            if s < 3:
                pl.when(self.goes_on(way))(lambda: self.z_copy(u, way, s + 1).start())
            self.y_copy(u, f).start()
            self.c_copy(u, f, 0).start()
        self.for_step(s, one)
        if u == 0 and s == 1:
            self.start_z(1)
        if u == 0 and s == 2:
            self.start_near(1)

    def y_event(self, u, s):
        def one(f, way):
            self.y_arrival(u, f).wait_recv()
            self.c_copy(u, f, 1).start()
        self.for_step(s, one)

    def arrive(self, u):
        for f in range(len(self.flows)):
            def one(f=f):
                for from_y in (0, 1):
                    self.c_arrival(u, f, from_y).wait_recv()
            self.for_flow(f, one)

    def finish(self, u):
        for way in (0, 1):
            pl.when(self.goes_on(way))(lambda way=way: self.z_copy(u, way, 1).wait_send())
        for f, (way, s) in enumerate(self.flows):
            def one(f=f, way=way, s=s):
                if f and s < 3:
                    pl.when(self.goes_on(way))(
                        lambda: self.z_copy(u, way, s + 1).wait_send()
                    )
                self.y_copy(u, f).wait_send()
                for from_y in (0, 1):
                    self.c_copy(u, f, from_y).wait_send()
            self.for_flow(f, one)


GATHER_SEMS = (12, 12, 14, 14, 28, 28)


def fwd_kernel(
    x_ref, seg_ref, context, gain, offset, qv_bias, out_bias, gain_two, offset_two, up_bias,
    wqkv, wout, up_shard, down_shard,
    q_out, k_out, v_out, mix_out, mid_out, normed_out, wff_out, key_out, query_out,
    normed_two_out, active_out, slope_out, shard_out, bias_out,
    wff, q_ref, k_ref, v_ref, mix_ref, mid_ref, normed_t, key_more, query_more,
    normed_two_t, active, slope, bias_row, mask_more, wout_all, mix_x, shard_x, bias_x,
    zs, zr, ys, yr, cs, cr, ps, pr, xs, xr, local, outs,
):
    length, width = x_ref.shape
    blocks = length // BLOCK
    pairs = q_ref.shape[0]
    cols = pairs * PAIR
    me, head, core, y, across, core_mate, y_mate, _ = place()
    steps = length // STRIP * pairs
    weights = Gather(wff, lambda u: wff.at[u, me], (zs, zr, ys, yr, cs, cr))
    own = [
        pltpu.make_async_copy(shard, wff.at[u, me], local.at[u])
        for u, shard in enumerate((up_shard, down_shard))
    ]
    own[0].start()
    own[1].start()
    greet([across, core_mate, y_mate, weights.above, weights.below])

    half = wout.shape[0] // 2
    here = pl.ds(pl.multiple_of(core * half, half), half)
    beside = pl.ds(pl.multiple_of((1 - core) * half, half), half)
    wout_x = wout_all.at[1 - head]
    out_copy = remote(
        wout.at[here, :], wout_all.at[head, here, :], xs.at[0], xr.at[0], across
    )
    wout_all[head] = wout[...]
    out_pass = remote(wout_x.at[here, :], wout_x.at[here, :], ps.at[0], pr.at[0], core_mate)
    out_arrival = remote(
        wout_x.at[beside, :], wout_x.at[beside, :], ps.at[0], pr.at[0], core_mate
    )
    out_copy.start()

    own[0].wait()
    weights.start_z(0)
    weights.start_near(0)
    own[1].wait()
    shard_copy = remote(wff.at[:, me], shard_x, xs.at[1 + steps], xr.at[1 + steps], across)
    shard_copy.start()
    bias_row[...] = as_row(up_bias)
    bias_copy = remote(bias_row, bias_x, xs.at[2 + steps], xr.at[2 + steps], across)
    bias_copy.start()

    def pass_out():
        out_copy.wait_recv()
        out_pass.start()

    plan = {
        2: [(weights.z_event, 0, 1), (weights.y_event, 0, 0)], 4: [(weights.z_event, 0, 2)], 5: [(weights.y_event, 0, 1)],
        6: [(weights.z_event, 0, 3), (pass_out,)], 7: [(weights.z_event, 1, 1)], 8: [(weights.y_event, 0, 2), (weights.y_event, 1, 0)],
        9: [(weights.z_event, 1, 2)], 10: [(weights.y_event, 0, 3)], 11: [(weights.z_event, 1, 3)],
    }

    def tick(t):
        for step, events in plan.items():
            @pl.when(t == step)
            def _(events=events):
                for event, *which in events:
                    event(*which)

    at = lax.broadcasted_iota(jnp.int32, (PAIR, length), 0)
    same = at == seg_ref[...]
    hidden = context[...] != 1
    ones = jnp.logical_and(at > TABLES, at < TABLES + 4)
    key_side = jnp.logical_or(
        jnp.logical_and(at < TABLES, same),
        jnp.logical_or(jnp.logical_and(at == TABLES, hidden), ones),
    )
    query_side = jnp.logical_and(at <= TABLES, jnp.logical_not(same))
    key_more[...] = turn(jnp.where(key_side, 1.0, 0.0)).astype(BF)
    mask_more[...] = turn(jnp.where(query_side, FAR, 0.0)).astype(BF)

    keep = [
        pltpu.make_async_copy(here, there, outs.at[n])
        for n, (here, there) in enumerate(
            (
                (q_ref, q_out), (k_ref, k_out), (v_ref, v_out), (normed_t, normed_out),
                (key_more, key_out), (query_more, query_out), (mix_ref, mix_out),
            )
        )
    ]
    gains, offsets = as_row(gain), as_row(offset)
    query_bias = qv_bias[0:1, :].astype(F32)
    value_bias = qv_bias[1:2, :].astype(F32)

    def project(b, _):
        rows = pl.ds(pl.multiple_of(b * BLOCK, BLOCK), BLOCK)
        centred, scale = norm_stats(x_ref[rows, :].astype(F32))
        block = (centred * scale * gains + offsets).astype(BF)
        normed_t[:, rows] = turn(block)
        queries = ((nn(block, wqkv[0]) + query_bias).astype(BF) * 0.125).astype(BF)
        keys = nn(block, wqkv[1]).astype(BF)
        values = (nn(block, wqkv[2]) + value_bias).astype(BF)
        for p in range(pairs):
            part = slice(p * PAIR, (p + 1) * PAIR)
            q_ref[p, rows, :] = queries[:, part]
            k_ref[p, rows, :] = keys[:, part]
            v_ref[p, rows, :] = values[:, part]
        tick(b)
        return 0

    lax.fori_loop(0, blocks, project, 0)
    for n in range(5):
        keep[n].start()

    low_lanes = lanes() < HEAD_DIM
    zero = jnp.zeros((1, PAIR), BF)

    def mixture_copy(t):
        rows = pl.ds(pl.multiple_of(t // pairs * STRIP, STRIP), STRIP)
        return remote(
            mix_ref.at[t % pairs, rows, :], mix_x.at[t % pairs, rows, :], xs.at[1 + t],
            xr.at[1 + t], across,
        )

    per_step = STRIP // BLOCK

    def attend(t, _):
        b, p = t // pairs, t % pairs
        keys = jnp.concatenate([k_ref[p], key_more[...]], axis=1)
        values = jnp.concatenate([v_ref[p], one_lanes(length)], axis=1)
        chains = []
        for n in range(per_step):
            rows = pl.ds(pl.multiple_of(b * STRIP + n * BLOCK, BLOCK), BLOCK)
            queries, more = q_ref[p, rows, :], mask_more[rows, :]
            for low in (0, 1):
                own_lanes = jnp.logical_not(low_lanes) if low else low_lanes
                left = jnp.concatenate([jnp.where(own_lanes, queries, zero), more], axis=1)
                chains.append((rows, low, more, dot_rows(left, keys)))
        parts = []
        for rows, low, more, scores in chains:
            top = jnp.max(scores, axis=-1, keepdims=True)
            mixed = nn(jnp.exp(scores - top).astype(BF), values)
            total = mixed[:, PAIR:PAIR + 1]
            parts.append(mixed[:, :PAIR] / total)
            query_more[2 * p + low, rows, :] = in_pieces(
                -(top + jnp.log(total)), TABLES + 1, more.astype(F32)
            )
            if low:
                mix_ref[p, rows, :] = jnp.where(low_lanes, *parts[-2:]).astype(BF)
        mixture_copy(t).start()
        tick(t + blocks)
        return 0

    lax.fori_loop(0, length // STRIP * pairs, attend, 0)
    keep[5].start()
    keep[6].start()
    out_arrival.wait_recv()
    out_row = as_row(out_bias)

    def mid_copy(b):
        rows = pl.ds(b * BLOCK, BLOCK)
        return pltpu.make_async_copy(mid_ref.at[rows, :], mid_out.at[rows, :], outs.at[7 + b])

    gains_two, offsets_two = as_row(gain_two), as_row(offset_two)

    def half_copies(b):
        rows = pl.ds(b * BLOCK, BLOCK)
        return [
            pltpu.make_async_copy(
                here.at[:, rows, :], there.at[:, rows, :], outs.at[7 + blocks + 2 * b + n]
            )
            for n, (here, there) in enumerate(((active, active_out), (slope, slope_out)))
        ]

    def up_half(b):
        rows = pl.ds(b * BLOCK, BLOCK)
        centred, scale = norm_stats(mid_ref[rows, :])
        block = (centred * scale * gains_two + offsets_two).astype(BF)
        normed_two_t[:, rows] = turn(block)

        def one(n, _):
            cut = pl.ds(pl.multiple_of(n * WIDE, WIDE), WIDE)
            before = nn(block, wff[0, :, :, cut].reshape(width, WIDE)) + bias_row[:, cut]
            spread, bell = gelu_parts(before)
            active[n, rows, :] = (before * spread).astype(BF)
            slope[n, rows, :] = (spread + before * bell).astype(BF)
            return 0

        lax.fori_loop(0, active.shape[0], one, 0)
        for copy in half_copies(b):
            copy.start()

    for b in range(blocks):
        if b % per_step == 0:
            for p in range(pairs):
                mixture_copy(b // per_step * pairs + p).wait_recv()
        rows = pl.ds(b * BLOCK, BLOCK)
        ours = jnp.concatenate([mix_ref[p, rows, :] for p in range(pairs)], axis=-1)
        other = jnp.concatenate([mix_x[p, rows, :] for p in range(pairs)], axis=-1)
        first, second = jnp.where(head == 0, ours, other), jnp.where(head == 0, other, ours)
        attended = nn(first, wout_all[0]) + nn(second, wout_all[1])
        mid_ref[rows, :] = x_ref[rows, :].astype(F32) + (attended + out_row)
        mid_copy(b).start()
        if b == 0:
            weights.arrive(0)
        up_half(b)
        if b < 3:
            weights.y_event(1, b + 1)
    normed_two_keep = pltpu.make_async_copy(
        normed_two_t, normed_two_out, outs.at[7 + 3 * blocks]
    )
    normed_two_keep.start()
    wff_keep = [pltpu.make_async_copy(wff.at[u], wff_out.at[u], local.at[u]) for u in range(2)]
    wff_keep[0].start()
    shard_copy.wait()
    bias_copy.wait()
    other_keep = [
        pltpu.make_async_copy(shard_x, shard_out, outs.at[8 + 3 * blocks]),
        pltpu.make_async_copy(bias_x, bias_out, outs.at[9 + 3 * blocks]),
    ]
    for copy in other_keep:
        copy.start()
    weights.arrive(1)
    wff_keep[1].start()
    out_copy.wait_send()
    out_pass.wait_send()
    for copy in keep + wff_keep + other_keep + [normed_two_keep]:
        copy.wait()
    for b in range(blocks):
        for copy in half_copies(b):
            copy.wait()
    for t in range(length // STRIP * pairs):
        mixture_copy(t).wait_send()
    for b in range(blocks):
        mid_copy(b).wait()
    for u in range(2):
        weights.finish(u)


def run_fwd(
    x, seg, context, gain, offset, qv_bias, out_bias, gain_two, offset_two, up_bias, wqkv, wout,
    up_weight, down_t,
):
    length, width = x.shape
    pairs = wqkv.shape[2] // PAIR
    blocks = length // BLOCK
    depth, hidden = up_weight.shape
    by_pair, by_head = (pairs, length, PAIR), (2 * pairs, length, PAIR)
    turned = (width, length)
    halves = (hidden // WIDE, length, WIDE)
    steps = length // STRIP * pairs
    dma = pltpu.SemaphoreType.DMA
    return pl.pallas_call(
        fwd_kernel,
        out_shape=[shape_of(by_pair, BF)] * 4 + [
            shape_of((length, width), F32),
            shape_of(turned, BF),
            shape_of((2, SEQ_SIZE, depth, hidden), BF),
            shape_of((length, PAIR), BF),
            shape_of(by_head, BF),
            shape_of((width, length), BF),
            shape_of(halves, BF),
            shape_of(halves, BF),
            shape_of((2, depth, hidden), BF),
            shape_of((1, hidden), F32),
        ],
        in_specs=[VMEM_SPEC] * 12 + [ANY_SPEC] * 2,
        out_specs=[ANY_SPEC] * 14,
        scratch_shapes=[pltpu.VMEM((2, SEQ_SIZE, depth, hidden), BF)]
        + [pltpu.VMEM(by_pair, BF)] * 4 + [
            pltpu.VMEM((length, width), F32),
            pltpu.VMEM(turned, BF),
            pltpu.VMEM((length, PAIR), BF),
            pltpu.VMEM(by_head, BF),
            pltpu.VMEM((width, length), BF),
            pltpu.VMEM(halves, BF),
            pltpu.VMEM(halves, BF),
            pltpu.VMEM((1, hidden), F32),
            pltpu.VMEM((length, PAIR), BF),
            pltpu.VMEM((2,) + wout.shape, BF),
            pltpu.VMEM(by_pair, BF),
            pltpu.VMEM((2, depth, hidden), BF),
            pltpu.VMEM((1, hidden), F32),
            *[dma((n,)) for n in GATHER_SEMS], dma((1,)), dma((1,)),
            dma((3 + steps,)), dma((3 + steps,)), dma((2,)), dma((10 + 3 * blocks,)),
        ],
        compiler_params=pltpu.CompilerParams(
            collective_id=0, has_side_effects=True, vmem_limit_bytes=VMEM_LIMIT
        ),
    )(
        x, seg, context, gain, offset, qv_bias, out_bias, gain_two, offset_two, up_bias, wqkv,
        wout, up_weight, down_t,
    )


def ff_kernel(
    mid_hbm, dy_hbm, wff_hbm, normed_two_hbm, active_hbm, slope_hbm, gain, wout_hbm, shard_hbm,
    branch_out, gmid_hbm, ga_out, gm_out, summed, other_hbm, small_ref,
    shard,    dy_ref, wff, wout, branch_ref, ga_t, gm_ref, normed_t, dy_t, active, before_grad, gnt_acc, gnt_own, gnt_x, whole, from_mate,
    held, ready,
    xs, xr, cs, cr, ls, ws, ss, ins, outs, *gather_sems,
):
    length, width = dy_ref.shape
    blocks = length // BLOCK
    hidden = wff.shape[3]
    half = hidden // WIDE
    chunks = 2 * hidden // CHUNK
    pairs = gm_ref.shape[0]
    me, head, core, y, across, core_mate, y_mate, z_mates = place()
    dy_load = pltpu.make_async_copy(dy_hbm, dy_ref, ins.at[0])
    wout_load = pltpu.make_async_copy(wout_hbm, wout, ins.at[1])

    def step_loads(n):
        cut = pl.ds(n * WIDE, WIDE)
        return [
            pltpu.make_async_copy(src, dst, ins.at[4 + 3 * n + m])
            for m, (src, dst) in enumerate(
                (
                    (wff_hbm.at[1, :, :, cut], wff.at[1, :, :, cut]),
                    (slope_hbm.at[n], before_grad.at[n]),
                    (wff_hbm.at[0, :, :, cut], wff.at[0, :, :, cut]),
                )
            )
        ]

    active_load = pltpu.make_async_copy(active_hbm, active, ins.at[2])
    normed_load = pltpu.make_async_copy(normed_two_hbm, normed_t, ins.at[3])
    dy_load.start()
    shard_load = pltpu.make_async_copy(shard_hbm, shard, ins.at[4 + 3 * half])
    shard_load.start()
    for n in range(half):
        for copy in step_loads(n):
            copy.start()
    active_load.start()
    normed_load.start()
    wout_load.start()
    other = Gather(other_hbm, lambda u: shard.at[u], gather_sems)
    greet([across, core_mate, y_mate, other.above, other.below])
    shard_load.wait()
    shard_keep = pltpu.make_async_copy(shard, other_hbm.at[:, me], ins.at[5 + 3 * half])
    shard_keep.start()
    other.start_z(0)
    other.start_near(0)
    gains = as_row(gain)

    def weight(kind, n):
        cut = pl.ds(pl.multiple_of(n * WIDE, WIDE), WIDE)
        return wff[kind, :, :, cut].reshape(width, WIDE)

    small_ref[...] = jnp.zeros_like(small_ref)

    def load(b):
        rows = pl.ds(b * BLOCK, BLOCK)
        return pltpu.make_async_copy(mid_hbm.at[rows, :], held.at[b % 2], ls.at[b % 2])

    def store(b):
        rows = pl.ds(b * BLOCK, BLOCK)
        return pltpu.make_async_copy(ready.at[b % 2], gmid_hbm.at[rows, :], ws.at[b % 2])

    load(0).start()
    load(1).start()

    def gnt_copy(b):
        return remote(gnt_own.at[b], gnt_x.at[b], xs.at[b], xr.at[b], across)

    def core_copy(n):
        return remote(
            whole.at[n, :, :, 1 - core], from_mate.at[n], cs.at[n], cr.at[n], core_mate
        )

    def forward(t, _):
        b, n = t // half, t % half
        rows = pl.ds(pl.multiple_of(b * BLOCK, BLOCK), BLOCK)

        for n_first in range(half):
            @pl.when(t == n_first)
            def _(n_first=n_first):
                if n_first == 0:
                    dy_load.wait()
                for copy in step_loads(n_first):
                    copy.wait()

        @pl.when(n == 0)
        def _():
            dy_t[:, rows] = turn(dy_ref[rows, :])
            small_ref[DOWN_BIAS:DOWN_BIAS + 1, :] += sum_rows(dy_ref[rows, :].astype(F32))

        up = weight(0, n)
        grad = nn(dy_ref[rows, :], weight(1, n)) * before_grad[n, rows, :].astype(F32)
        grad = grad.astype(BF)
        before_grad[n, rows, :] = grad
        small_ref[pl.ds(UP_BIAS + n, 1), :] += sum_rows(grad.astype(F32))
        back = dot_rows(grad, up)

        @pl.when(n == 0)
        def _():
            gnt_acc[...] = back

        @pl.when(n > 0)
        def _():
            gnt_acc[...] += back

        for b_done in range(blocks):
            @pl.when(t == (b_done + 1) * half - 1)
            def _(b_done=b_done):
                gnt_own[b_done] = gnt_acc[...].astype(BF)
                gnt_copy(b_done).start()

        @pl.when(t == 5)
        def _():
            other.z_event(0, 1)
            other.y_event(0, 0)

        return 0

    lax.fori_loop(0, blocks * half, forward, 0)

    def weight_grads(left_t, right, first):
        cut_rows = width // Z_SIZE
        per_wide = WIDE // CHUNK

        def one(t, _):
            n, plane = t // Z_SIZE, t % Z_SIZE
            cut = pl.ds(pl.multiple_of(plane * cut_rows, cut_rows), cut_rows)
            total = nn(left_t[cut, :], right[n]).astype(BF)
            for m in range(per_wide):
                piece = total[:, m * CHUNK:(m + 1) * CHUNK]
                whole[first + n * per_wide + m, plane] = piece.reshape(whole.shape[2:])

            @pl.when(plane == Z_SIZE - 1)
            def _():
                for m in range(per_wide):
                    core_copy(first + n * per_wide + m).start()

            return 0

        lax.fori_loop(0, Z_SIZE * half, one, 0)

    active_load.wait()
    normed_load.wait()
    other.z_event(0, 2)
    weight_grads(dy_t, active, chunks // 2)
    other.z_event(0, 3)
    weight_grads(normed_t, before_grad, 0)
    other.z_event(1, 1)
    other.y_event(0, 1)

    def branch(b, _):
        rows = pl.ds(pl.multiple_of(b * BLOCK, BLOCK), BLOCK)
        total = dot_rows(active[0, rows, :], weight(1, 0))
        for n in range(1, half):
            total += dot_rows(active[n, rows, :], weight(1, n))
        branch_ref[rows, :] = total.astype(BF)
        return 0

    lax.fori_loop(0, blocks, branch, 0)
    other.z_event(1, 2)
    other.y_event(0, 2)
    other.y_event(1, 0)
    branch_keep = pltpu.make_async_copy(branch_ref, branch_out, outs.at[0])
    branch_keep.start()
    wout_load.wait()

    def ga_copy(b):
        rows = pl.ds(b * BLOCK, BLOCK)
        return pltpu.make_async_copy(ga_t.at[:, rows], ga_out.at[:, rows], outs.at[1 + b])

    def gm_copy(b):
        rows = pl.ds(b * BLOCK, BLOCK)
        return pltpu.make_async_copy(
            gm_ref.at[:, rows, :], gm_out.at[:, rows, :], outs.at[1 + blocks + b]
        )


    def add_mate(n, _):
        core_copy(n).wait()
        both = whole[n, :, :, core].astype(F32) + from_mate[n].astype(F32)
        from_mate[n] = both.astype(BF)
        return 0

    lax.fori_loop(chunks // 2, chunks, add_mate, 0)
    lax.fori_loop(0, chunks // 2, add_mate, 0)
    keep = pltpu.make_async_copy(from_mate, summed, ss.at[0])
    keep.start()

    strips = BLOCK // PIECE
    for b in range(blocks):
        if b == 1:
            other.y_event(0, 3)
        if b == 2:
            other.z_event(1, 3)
            other.y_event(1, 1)
        if b == 3:
            other.y_event(1, 2)
        gnt_copy(b).wait()
        load(b).wait()
        if b >= 2:
            store(b - 2).wait()

        def through_norm(n, _, b=b):
            rows = pl.ds(pl.multiple_of(n * PIECE, PIECE), PIECE)
            full = pl.ds(pl.multiple_of(b * BLOCK + n * PIECE, PIECE), PIECE)
            grad = gnt_own[b, rows, :].astype(F32) + gnt_x[b, rows, :].astype(F32)
            centred, scale = norm_stats(held[b % 2, rows, :])
            unit = centred * scale
            small_ref[LN2_GAIN:LN2_GAIN + 1, :] += sum_rows(grad * unit)
            small_ref[LN2_BIAS:LN2_BIAS + 1, :] += sum_rows(grad)
            total = dy_ref[full, :].astype(F32) + norm_back(grad * gains, unit, scale)
            ready[b % 2, rows, :] = total
            low = total.astype(BF)
            small_ref[OUT_BIAS:OUT_BIAS + 1, :] += sum_rows(low.astype(F32))
            ga_t[:, full] = turn(low)
            mixed = dot_rows(low, wout[...]).astype(BF)
            for p in range(pairs):
                gm_ref[p, full, :] = mixed[:, p * PAIR:(p + 1) * PAIR]
            return 0

        lax.fori_loop(0, strips, through_norm, 0)
        store(b).start()
        ga_copy(b).start()
        gm_copy(b).start()
        if b + 2 < blocks:
            load(b + 2).start()
    store(blocks - 2).wait()
    store(blocks - 1).wait()
    for b in range(blocks):
        ga_copy(b).wait()
        gm_copy(b).wait()
    branch_keep.wait()
    keep.wait()
    other.y_event(1, 3)
    shard_keep.wait()
    for u in range(2):
        other.arrive(u)
        other.finish(u)


def run_ff(middle, dy, wff, normed_two_t, active, slope, gain, wout, shard):
    length, width = middle.shape
    half = wff.shape[3] // WIDE
    chunks = 2 * wff.shape[3] // CHUNK
    blocks = length // BLOCK
    pairs = wout.shape[0] // PAIR
    depth = width // SEQ_SIZE
    dma = pltpu.SemaphoreType.DMA
    rows = pltpu.VMEM((blocks, BLOCK, width), BF)
    hidden = pltpu.VMEM((half, length, WIDE), BF)
    flat_t = pltpu.VMEM((width, length), BF)
    return pl.pallas_call(
        ff_kernel,
        out_shape=[
            shape_of((length, width), BF),
            shape_of((length, width), F32),
            shape_of((width, length), BF),
            shape_of((pairs, length, PAIR), BF),
            shape_of((chunks, Z_SIZE, Y_SIZE, depth, CHUNK), BF),
            shape_of(wff.shape, BF),
            shape_of((SMALL_ROWS, width), F32),
        ],
        in_specs=[ANY_SPEC] * 6 + [VMEM_SPEC, ANY_SPEC, ANY_SPEC],
        out_specs=[ANY_SPEC] * 6 + [VMEM_SPEC],
        scratch_shapes=[
            pltpu.VMEM(shard.shape, BF),
            pltpu.VMEM((length, width), BF), pltpu.VMEM(wff.shape, BF),
            pltpu.VMEM(wout.shape, BF),
            pltpu.VMEM((length, width), BF), flat_t, pltpu.VMEM((pairs, length, PAIR), BF),
            flat_t, flat_t, hidden, hidden,
            pltpu.VMEM((BLOCK, width), F32), rows, rows,
            pltpu.VMEM((chunks, Z_SIZE, Y_SIZE, CORES, depth, CHUNK), BF),
            pltpu.VMEM((chunks, Z_SIZE, Y_SIZE, depth, CHUNK), BF),
            pltpu.VMEM((2, BLOCK, width), F32), pltpu.VMEM((2, BLOCK, width), F32),
            dma((blocks,)), dma((blocks,)), dma((chunks,)), dma((chunks,)),
            dma((2,)), dma((2,)), dma((1,)), dma((6 + 3 * half,)), dma((1 + 2 * blocks,)),
            *[dma((n,)) for n in GATHER_SEMS],
        ],
        compiler_params=pltpu.CompilerParams(
            collective_id=1, has_side_effects=True, vmem_limit_bytes=VMEM_LIMIT
        ),
    )(middle, dy, wff, normed_two_t, active, slope, gain, wout, shard)


def back_kernel(
    q_hbm, k_hbm, v_hbm, mix_hbm, gm_hbm, query_hbm, ga_hbm, normed_hbm, wqkv_hbm, x_hbm,
    other_hbm, bias_x, gain_in, offset_in, key_more, gain, down_bias, small_in, mid_hbm, gmid_hbm, ff_part, branch,
    out_hbm, tokens_hbm, qkv_sum, out_sum, up_sum, down_sum,
    gain_one, offset_one, qv_small, out_small, gain_two, offset_two, up_small, down_small,
    q_ref, k_ref, v_ref, mix_ref, gm_ref, query_more, ga_t, normed_t, wqkv, x_ref, other,
    out_ref, tokens_ref, key_t, key_acc, value_acc, query_acc, dq, whole, mate, at_y, at_z, ff_y, ff_z, gn_own, gn_x,
    branch_own, ff_own, held, small_own, small_z, small_y, small_c, small_x,
    fys, fyr, fzs, fzr, acs, acr, ays, ayr, azs, azr, gs, gr, ls, ms, mr, os, hs, ins, more_ins, outs,
):
    length, width = x_hbm.shape
    blocks = length // BLOCK
    pairs = q_ref.shape[0]
    chunks = ff_part.shape[0]
    half = chunks // 2
    groups = chunks // GROUP
    me, head, core, y, across, core_mate, y_mate, z_mates = place()
    z = me // (Y_SIZE * CORES)
    by_pair = (
        (q_hbm, q_ref), (k_hbm, k_ref), (v_hbm, v_ref), (mix_hbm, mix_ref), (gm_hbm, gm_ref),
    )

    def pair_loads(p):
        both = pl.ds(2 * p, 2)
        first = p * (len(by_pair) + 1)
        return [
            pltpu.make_async_copy(src.at[p], dst.at[p], ins.at[first + n])
            for n, (src, dst) in enumerate(by_pair)
        ] + [
            pltpu.make_async_copy(
                query_hbm.at[both], query_more.at[both], ins.at[first + len(by_pair)]
            )
        ]

    late_loads = [
        pltpu.make_async_copy(src, dst, more_ins.at[n])
        for n, (src, dst) in enumerate(
            (
                (ga_hbm, ga_t), (normed_hbm, normed_t), (wqkv_hbm, wqkv), (other_hbm, other),
            )
        )
    ]
    for p in range(pairs):
        for copy in pair_loads(p):
            copy.start()
        if p == 0:
            late_loads[0].start()
            late_loads[1].start()
    late_loads[2].start()
    late_loads[3].start()
    greet([across, core_mate, y_mate, *z_mates])

    def part(b):
        return pl.ds(b * BLOCK, BLOCK)

    def load(n):
        source = mid_hbm if n < blocks else gmid_hbm
        return pltpu.make_async_copy(
            source.at[part(n % blocks), :], held.at[n % 2], ls.at[n % 2]
        )

    def x_load(n):
        return pltpu.make_async_copy(
            x_hbm.at[part(n % blocks), :], x_ref.at[n % 2], more_ins.at[4 + n % 2]
        )

    def x_rows(n):
        x_load(n).wait()
        return x_ref[n % 2].astype(F32)

    def x_done(n):
        if n + 2 < 2 * blocks:
            x_load(n + 2).start()

    def taken(n):
        if n + 2 < 2 * blocks:
            load(n + 2).start()

    def group(g):
        return pl.ds(g * GROUP, GROUP)

    def ff_y_copy(g):
        return remote(
            ff_part.at[group(g), :, 1 - y], ff_y.at[group(g)], fys.at[g], fyr.at[g], y_mate
        )

    def ff_z_copy(g, d):
        n = g * 3 + d - 1
        return remote(
            ff_y.at[group(g), (z + d) % Z_SIZE], ff_z.at[d - 1, group(g)],
            fzs.at[n], fzr.at[n], z_mates[d - 1],
        )

    def branch_load(b):
        return pltpu.make_async_copy(branch.at[part(b), :], branch_own.at[b % 2], hs.at[b % 2])

    def ff_load(g):
        return pltpu.make_async_copy(
            ff_part.at[group(g), :, y], ff_own.at[g % 2], os.at[g % 2]
        )

    def ff_y_event(g):
        ff_y_copy(g).wait_recv()
        ff_load(g).wait()
        for n in range(g * GROUP, (g + 1) * GROUP):
            own = ff_own[g % 2, n % GROUP]
            ff_y[n] = (ff_y[n].astype(F32) + own.astype(F32)).astype(BF)
        if g + 2 < groups:
            ff_load(g + 2).start()
            ff_y_copy(g + 2).start()
        for d in (1, 2, 3):
            ff_z_copy(g, d).start()

    def ff_z_event(g):
        for d in (1, 2, 3):
            ff_z_copy(g, d).wait_recv()
        for n in range(g * GROUP, (g + 1) * GROUP):
            total = ff_y[n, z].astype(F32)
            for d in (1, 2, 3):
                total += ff_z[d - 1, n].astype(F32)
            if n < half:
                up_sum[:, n * CHUNK:(n + 1) * CHUNK] = total
            else:
                down_sum[:, (n - half) * CHUNK:(n - half + 1) * CHUNK] = total

    def at_c_copy(p):
        return remote(whole.at[p, :, :, 1 - core], mate.at[p], acs.at[p], acr.at[p], core_mate)

    def at_y_copy(p):
        return remote(mate.at[p, :, 1 - y], at_y.at[p], ays.at[p], ayr.at[p], y_mate)

    def at_z_copy(p, d):
        n = p * 3 + d - 1
        return remote(
            at_y.at[p, (z + d) % Z_SIZE], at_z.at[d - 1, p], azs.at[n], azr.at[n], z_mates[d - 1]
        )

    def at_c_event(p):
        at_c_copy(p).wait_recv()
        mate[p] = (mate[p].astype(F32) + whole[p, :, :, core].astype(F32)).astype(BF)
        at_y_copy(p).start()

    def at_y_event(p):
        at_y_copy(p).wait_recv()
        at_y[p] = (at_y[p].astype(F32) + mate[p, :, y].astype(F32)).astype(BF)
        for d in (1, 2, 3):
            at_z_copy(p, d).start()

    def at_z_event(p):
        for d in (1, 2, 3):
            at_z_copy(p, d).wait_recv()
        total = at_y[p, z].astype(F32)
        for d in (1, 2, 3):
            total += at_z[d - 1, p].astype(F32)
        cut = slice(p * PAIR, (p + 1) * PAIR)
        for kind in range(3):
            qkv_sum[kind, :, cut] = total[:, kind * PAIR:(kind + 1) * PAIR]
        out_sum[:, cut] = total[:, 3 * PAIR:]

    def out_copy(b):
        return pltpu.make_async_copy(out_ref.at[b % 2], out_hbm.at[part(b), :], outs.at[b])

    def tokens_copy(b):
        return pltpu.make_async_copy(
            tokens_ref.at[b % 2], tokens_hbm.at[part(b), :], outs.at[blocks + b]
        )

    gains_two, offsets_two = as_row(gain_in), as_row(offset_in)

    def other_weight(kind, n):
        return other[kind, :, :, n * WIDE:(n + 1) * WIDE].reshape(width, WIDE)

    def branch_event(b):
        load(b).wait()
        branch_load(b).wait()
        centred, scale = norm_stats(held[b % 2])
        block = (centred * scale * gains_two + offsets_two).astype(BF)
        parts = []
        for n in range(half * CHUNK // WIDE):
            cut = slice(n * WIDE, (n + 1) * WIDE)
            before = nn(block, other_weight(0, n)) + bias_x[:, cut]
            spread, _ = gelu_parts(before)
            parts.append(dot_rows((before * spread).astype(BF), other_weight(1, n)))
        theirs = sum(parts[1:], parts[0]).astype(BF)
        both = branch_own[b % 2].astype(F32) + theirs.astype(F32)
        if b >= 2:
            out_copy(b - 2).wait()
        out_ref[b % 2] = (held[b % 2] + both + as_row(down_bias)).astype(BF)
        out_copy(b).start()
        taken(b)
        if b + 2 < blocks:
            branch_load(b + 2).start()

    for n in range(2):
        x_load(n).start()
        load(n).start()
        branch_load(n).start()
        ff_load(n).start()
        ff_y_copy(n).start()

    plan = {4: [(ff_y_event, 0)], 8: [(ff_y_event, 1)]}

    low_lanes = lanes() < HEAD_DIM
    zero = jnp.zeros((1, PAIR), BF)

    def stacked(strip):
        return jnp.concatenate(
            [jnp.where(low_lanes, strip, zero), jnp.where(low_lanes, zero, strip)], axis=0
        )

    def tile(p, b, side):
        rows = pl.ds(pl.multiple_of(b * STRIP, STRIP), STRIP)
        queries, grads = stacked(q_ref[p, rows, :]), stacked(gm_ref[p, rows, :])
        more = jnp.concatenate(
            [query_more[2 * p, rows, :], query_more[2 * p + 1, rows, :]], axis=0
        )
        mixture = mix_ref[p, rows, :]
        product = grads.astype(F32) * jnp.concatenate([mixture, mixture], axis=0).astype(F32)
        inner = -jnp.sum(product, axis=-1, keepdims=True)
        query_side = jnp.concatenate([queries, more], axis=1)
        grad_side = jnp.concatenate([grads, in_pieces(inner, 0, 0.0)], axis=1)
        to_queries = jnp.zeros((PAIR, 2 * STRIP), F32)
        for n in range(STRIP // BLOCK):
            cut = pl.ds(pl.multiple_of(side * STRIP + n * BLOCK, BLOCK), BLOCK)
            keys = jnp.concatenate([k_ref[p, cut, :], key_more[cut, :]], axis=1)
            values = jnp.concatenate([v_ref[p, cut, :], one_lanes(BLOCK)], axis=1)
            weights = jnp.exp(dot_rows(keys, query_side)).astype(BF)
            grad_scores = weights * dot_rows(values, grad_side).astype(BF)
            value_acc[p, cut, :] += split_sum(weights, grads)
            key_acc[p, cut, :] += split_sum(grad_scores, queries)
            to_queries += nn(key_t[p, :, cut], grad_scores)

        own = jnp.concatenate(
            [to_queries[:HEAD_DIM, :STRIP], to_queries[HEAD_DIM:, STRIP:]], axis=0
        )

        @pl.when(side == 0)
        def _():
            query_acc[p] = own

        @pl.when(side == 1)
        def _():
            dq[p, rows, :] = (turn(query_acc[p] + own) * 0.125).astype(BF)

    def first_tiles(t, _):
        p, which = t // 3, t % 3

        @pl.when(which == 0)
        def _():
            for p_now in range(pairs):
                @pl.when(p == p_now)
                def _(p_now=p_now):
                    for copy in pair_loads(p_now):
                        copy.wait()
            key_t[p] = turn(k_ref[p])
            key_acc[p] = jnp.zeros(key_acc.shape[1:], F32)
            value_acc[p] = jnp.zeros(value_acc.shape[1:], F32)

        tile(p, which // 2, which % 2)
        for step, events in plan.items():
            @pl.when(t == step)
            def _(events=events):
                for event, n in events:
                    event(n)
        return 0

    def last_tile(p, _):
        tile(p, 1, 1)
        return 0

    def weight_grads(p, _):
        right = jnp.concatenate(
            [dq[p], key_acc[p].astype(BF), value_acc[p].astype(BF)], axis=1
        )
        mixture_all = mix_ref[p]

        def one(plane, _):
            cut = pl.ds(pl.multiple_of(plane * BLOCK, BLOCK), BLOCK)
            both = jnp.concatenate(
                [nn(normed_t[cut, :], right), nn(ga_t[cut, :], mixture_all)], axis=1
            )
            whole[p, plane] = both.astype(BF).reshape(whole.shape[2:])
            return 0

        lax.fori_loop(0, Z_SIZE, one, 0)
        at_c_copy(p).start()
        return 0

    def gn_copy(b):
        return remote(gn_own.at[b], gn_x.at[b], gs.at[b], gr.at[b], across)

    small_own[...] = small_in[...]

    def send_rows(b):
        total = jnp.zeros((BLOCK, width), F32)
        for n, grad in enumerate((dq, key_acc, value_acc)):
            left = jnp.concatenate(
                [grad[p, part(b), :].astype(BF) for p in range(pairs)], axis=1
            )
            total += dot_rows(left, wqkv[n])
        gn_own[b] = total.astype(BF)
        gn_copy(b).start()
        centred, scale = norm_stats(x_rows(b))
        x_done(b)
        small_own[LN1_GAIN:LN1_GAIN + 1, :] += sum_rows(total * (centred * scale))
        small_own[LN1_BIAS:LN1_BIAS + 1, :] += sum_rows(total)

    lax.fori_loop(0, 3 * pairs, first_tiles, 0)
    for copy in late_loads[:3]:
        copy.wait()
    send_rows(0)
    send_rows(1)
    ff_y_event(2)
    ff_z_event(0)
    lax.fori_loop(0, pairs, last_tile, 0)
    lax.fori_loop(0, pairs, weight_grads, 0)
    send_rows(2)
    send_rows(3)
    for p in range(pairs):
        at_c_event(p)
    for p in range(pairs):
        first, second = p * PAIR, (pairs + p) * PAIR
        small_own[QV_BIAS:QV_BIAS + 1, first:first + PAIR] = sum_rows(dq[p].astype(F32))
        small_own[QV_BIAS:QV_BIAS + 1, second:second + PAIR] = sum_rows(value_acc[p].astype(BF).astype(F32))
    def small_z_copy(d):
        return remote(small_own, small_z.at[z], ms.at[d - 1], mr.at[d - 1], z_mates[d - 1])

    def small_z_arrival(d):
        slot = small_z.at[(z + Z_SIZE - d) % Z_SIZE]
        return remote(slot, slot, ms.at[d - 1], mr.at[d - 1], z_mates[d - 1])

    y_sum = remote(small_y.at[0], small_y.at[1], ms.at[3], mr.at[3], y_mate)
    c_sum = remote(small_c.at[0], small_c.at[1], ms.at[4], mr.at[4], core_mate)
    x_sum = remote(small_x.at[0], small_x.at[1], ms.at[5], mr.at[5], across)
    for d in (1, 2, 3):
        small_z_copy(d).start()
    small_z[z] = small_own[...]

    def small_y_step():
        for d in (1, 2, 3):
            small_z_arrival(d).wait_recv()
        small_y[0] = small_z[0] + small_z[1] + small_z[2] + small_z[3]
        y_sum.start()

    def small_c_step():
        y_sum.wait()
        small_c[0] = small_y[0] + small_y[1]
        c_sum.start()

    def small_x_step():
        c_sum.wait()
        small_x[0] = small_c[0, 0:8, :] + small_c[1, 0:8, :]
        x_sum.start()

    late_loads[3].wait()
    ff_y_event(3)
    ff_z_event(1)
    branch_event(0)
    branch_event(1)
    at_y_event(0)
    small_y_step()
    branch_event(2)
    at_y_event(1)
    ff_z_event(2)
    small_c_step()
    branch_event(3)
    at_y_event(2)
    ff_z_event(3)
    gains = as_row(gain)
    for b in range(blocks):
        gn_copy(b).wait()
        load(blocks + b).wait()
        grad = gn_own[b].astype(F32) + gn_x[b].astype(F32)
        centred, scale = norm_stats(x_rows(blocks + b))
        x_done(blocks + b)
        unit = centred * scale
        if b >= 2:
            tokens_copy(b - 2).wait()
        tokens_ref[b % 2] = (
            held[b % 2] + norm_back(grad * gains, unit, scale)
        ).astype(BF)
        tokens_copy(b).start()
        taken(blocks + b)
        if b == 0:
            at_y_event(3)
            at_z_event(0)
        if b == 1:
            small_x_step()
            at_z_event(1)
        if b == 2:
            at_z_event(2)

    at_z_event(3)
    x_sum.wait()
    ln1 = small_x[0, 0:2, :] + small_x[1, 0:2, :]
    gain_one[...] = ln1[0:1, :].reshape(width)
    offset_one[...] = ln1[1:2, :].reshape(width)
    small = small_c[0] + small_c[1]
    for kind, target in (
        (OUT_BIAS, out_small), (LN2_GAIN, gain_two), (LN2_BIAS, offset_two), (DOWN_BIAS, down_small),
    ):
        target[...] = small[kind:kind + 1, :].reshape(width)
    cols = pairs * PAIR
    qv_small[0:1, :] = small[QV_BIAS:QV_BIAS + 1, :cols]
    qv_small[1:2, :] = small[QV_BIAS:QV_BIAS + 1, cols:]
    for n in range(up_small.shape[0] // width):
        row = small[UP_BIAS + n:UP_BIAS + n + 1, :]
        up_small[n * width:(n + 1) * width] = row.reshape(width)

    for d in (1, 2, 3):
        small_z_copy(d).wait_send()
    for b in range(blocks - 2, blocks):
        out_copy(b).wait()
        tokens_copy(b).wait()
    for g in range(groups):
        ff_y_copy(g).wait_send()
        for d in (1, 2, 3):
            ff_z_copy(g, d).wait_send()
    for p in range(pairs):
        at_c_copy(p).wait_send()
        at_y_copy(p).wait_send()
        for d in (1, 2, 3):
            at_z_copy(p, d).wait_send()


def run_back(
    queries, keys, values, mixture, grad_mixture, query_more, ga_t, normed_t, wqkv, x, other,
    bias_x, gain_two, offset_two, key_more, gain, down_bias, small, middle, grad_middle, ff_part,
    branch,
):
    length, width = x.shape
    pairs = queries.shape[0]
    chunks, depth = ff_part.shape[0], ff_part.shape[3]
    groups = chunks // GROUP
    cols, hidden = pairs * PAIR, chunks // 2 * CHUNK
    blocks = length // BLOCK
    dma = pltpu.SemaphoreType.DMA
    rows = pltpu.VMEM((blocks, BLOCK, width), BF)
    by_pair = pltpu.VMEM((pairs, length, PAIR), BF)
    two_blocks = pltpu.VMEM((2, BLOCK, width), BF)
    row = shape_of((width,), F32)
    loaded = (
        queries, keys, values, mixture, grad_mixture, query_more, ga_t, normed_t, wqkv, x, other
    )
    return pl.pallas_call(
        back_kernel,
        out_shape=[
            shape_of((length, width), BF),
            shape_of((length, width), BF),
            shape_of((3, depth, cols), F32),
            shape_of((depth, cols), F32),
            shape_of((depth, hidden), F32),
            shape_of((depth, hidden), F32),
            row, row, shape_of((2, cols), F32), row, row, row, shape_of((hidden,), F32), row,
        ],
        in_specs=[ANY_SPEC] * 11 + [VMEM_SPEC] * 7 + [ANY_SPEC] * 4,
        out_specs=[ANY_SPEC] * 2 + [VMEM_SPEC] * 12,
        scratch_shapes=[
            two_blocks if v is x else pltpu.VMEM(v.shape, BF) for v in loaded
        ] + [
            two_blocks, two_blocks, pltpu.VMEM((pairs, PAIR, length), BF),
            pltpu.VMEM((pairs, length, PAIR), F32), pltpu.VMEM((pairs, length, PAIR), F32),
            pltpu.VMEM((pairs, PAIR, STRIP), F32),
            by_pair,
            pltpu.VMEM((pairs, Z_SIZE, Y_SIZE, CORES, depth, CHUNK), BF),
            pltpu.VMEM((pairs, Z_SIZE, Y_SIZE, depth, CHUNK), BF),
            pltpu.VMEM((pairs, Z_SIZE, depth, CHUNK), BF),
            pltpu.VMEM((3, pairs, depth, CHUNK), BF),
            pltpu.VMEM((chunks, Z_SIZE, depth, CHUNK), BF),
            pltpu.VMEM((3, chunks, depth, CHUNK), BF),
            rows, rows,
            pltpu.VMEM((2, BLOCK, width), BF),
            pltpu.VMEM((2, GROUP, Z_SIZE, depth, CHUNK), BF),
            pltpu.VMEM((2, BLOCK, width), F32),
            pltpu.VMEM(small.shape, F32),
            pltpu.VMEM((Z_SIZE,) + small.shape, F32),
            pltpu.VMEM((2,) + small.shape, F32),
            pltpu.VMEM((2,) + small.shape, F32),
            pltpu.VMEM((2, 8, width), F32),
            dma((groups,)), dma((groups,)),
            dma((3 * groups,)), dma((3 * groups,)), dma((pairs,)), dma((pairs,)),
            dma((pairs,)), dma((pairs,)), dma((3 * pairs,)), dma((3 * pairs,)),
            dma((blocks,)), dma((blocks,)), dma((2,)), dma((6,)), dma((6,)), dma((2,)), dma((2,)),
            dma((6 * pairs,)), dma((6,)), dma((2 * blocks,)),
        ],
        compiler_params=pltpu.CompilerParams(
            collective_id=2, has_side_effects=True, vmem_limit_bytes=VMEM_LIMIT
        ),
    )(
        *loaded, bias_x, gain_two, offset_two, key_more, gain, down_bias, small, middle,
        grad_middle, ff_part, branch,
    )


def hand_over_kernel(*refs):
    *refs, sems = refs
    count = len(refs) // 3
    refs = refs[:count] + refs[2 * count:] + refs[count:2 * count]
    loads, stores = (
        [
            pltpu.make_async_copy(refs[a * count + n], refs[b * count + n], sems.at[a, n])
            for n in range(count)
        ]
        for a, b in ((0, 1), (1, 2))
    )
    for load in loads:
        load.start()
    for load, store in zip(loads, stores):
        load.wait()
        store.start()
    for store in stores:
        store.wait()


def hand_over(results):
    return pl.pallas_call(
        hand_over_kernel,
        out_shape=[shape_of(v.shape, v.dtype) for v in results],
        in_specs=[ANY_SPEC] * len(results),
        out_specs=[ANY_SPEC] * len(results),
        scratch_shapes=[pltpu.VMEM(v.shape, v.dtype) for v in results] + [
            pltpu.SemaphoreType.DMA((2, len(results)))
        ],
        compiler_params=pltpu.CompilerParams(vmem_limit_bytes=VMEM_LIMIT),
    )(*results)


def fast_body(
    tokens, segment_ids, context_flags, ln1_gain, ln1_bias, qkv_weight, qv_bias, out_weight,
    out_bias, ln2_gain, ln2_bias, up_weight, up_bias, down_weight, down_bias, cotangent,
):
    x, dy = tokens[0], cotangent[0]
    (
        queries, keys, values, mixture, middle, normed_t, wff, key_more, query_more,
        normed_two_t, active, slope, shard_x, bias_x,
    ) = run_fwd(
        x, segment_ids, context_flags, ln1_gain, ln1_bias, qv_bias, out_bias, ln2_gain,
        ln2_bias, up_bias, qkv_weight, out_weight, up_weight, down_weight.T,
    )
    branch, grad_middle, ga_t, grad_mixture, ff_part, other, small = run_ff(
        middle, dy, wff, normed_two_t, active, slope, ln2_gain, out_weight, shard_x
    )
    (
        output, tokens_grad, qkv_grad, out_grad, up_grad, down_grad, gain_one, offset_one,
        qv_grad, out_bias_grad, gain_two, offset_two, up_bias_grad, down_bias_grad,
    ) = hand_over(run_back(
        queries, keys, values, mixture, grad_mixture, query_more, ga_t, normed_t, qkv_weight, x,
        other, bias_x, ln2_gain, ln2_bias, key_more, ln1_gain, down_bias, small, middle,
        grad_middle, ff_part, branch,
    ))
    return (
        output[None], tokens_grad[None], gain_one, offset_one, qkv_grad, qv_grad, out_grad.T,
        out_bias_grad, gain_two, offset_two, up_grad, up_bias_grad, down_grad.T, down_bias_grad,
    )


def solution(mesh):
    chosen = generic_body
    if mesh.shape["head"] == 2 and mesh.shape["seq"] == SEQ_SIZE:
        chosen = fast_body
    return jax.shard_map(
        chosen,
        mesh=mesh,
        in_specs=(
            P("seq", None, None),
            P("seq", None),
            P("seq", None),
            P(),
            P(),
            P(None, None, "head"),
            P(None, "head"),
            P("head", None),
            P(),
            P(),
            P(),
            P("seq", "head"),
            P("head"),
            P("head", "seq"),
            P(),
            P("seq", None, None),
        ),
        out_specs=(
            P("seq", None, None),
            P("seq", None, None),
            P(),
            P(),
            P(None, "seq", "head"),
            P(None, "head"),
            P("head", "seq"),
            P(),
            P(),
            P(),
            P("seq", "head"),
            P("head"),
            P("head", "seq"),
            P(),
        ),
        check_vma=False,
    )
```

```python
import math

import jax
import jax.numpy as jnp
from jax import lax
from jax.experimental import pallas as pl
from jax.experimental.pallas import tpu as pltpu
from jax.sharding import PartitionSpec as P

HEAD_DIM = 64


def layer_norm(values_in, scaling, offset):
    middle = jnp.mean(values_in, axis=-1, keepdims=True)
    centred = values_in - middle
    spread = jnp.mean(centred * centred, axis=-1, keepdims=True)
    return centred * lax.rsqrt(spread + 1e-05) * scaling + offset


def gelu_exact(values_in):
    return 0.5 * values_in * (1.0 + jax.scipy.special.erf(values_in * 0.7071067811865476))


def dot_rows(left, right):
    return lax.dot_general(
        left, right, (((1,), (1,)), ((), ())), preferred_element_type=jnp.float32
    )


def dot_cols(left, right):
    return lax.dot_general(
        left, right, (((0,), (0,)), ((), ())), preferred_element_type=jnp.float32
    )


def masked_scores(block_query, seq_keys, block_segments, seq_segments, seq_context, factor):
    raw_scores = (
        jnp.einsum("qhd,khd->hqk", block_query, seq_keys, preferred_element_type=jnp.float32)
        * factor
    )
    allowed = (block_segments[:, None] == seq_segments[None, :]) & (seq_context[None, :] == 1)
    return jnp.where(allowed[None], raw_scores, -1e30)


def generic_body(
    tokens,
    segment_ids,
    context_flags,
    ln1_gain,
    ln1_bias,
    qkv_weight,
    qv_bias,
    out_weight,
    out_bias,
    ln2_gain,
    ln2_bias,
    up_weight,
    up_bias,
    down_weight,
    down_bias,
    cotangent,
):
    seq_count, length, width = tokens.shape
    row_count = seq_count * length
    local_cols = qkv_weight.shape[2]
    head_count = local_cols // HEAD_DIM
    factor = 1.0 / math.sqrt(HEAD_DIM)
    block = min(512, length)
    blocks = length // block
    gain_one = ln1_gain.astype(jnp.float32)
    offset_one = ln1_bias.astype(jnp.float32)
    gain_two = ln2_gain.astype(jnp.float32)
    offset_two = ln2_bias.astype(jnp.float32)
    flat_in = tokens.astype(jnp.float32).reshape(row_count, width)
    normed_f, norm_one_pull = jax.vjp(layer_norm, flat_in, gain_one, offset_one)
    normed = normed_f.astype(jnp.bfloat16)
    queries = (
        jnp.dot(normed, qkv_weight[0], preferred_element_type=jnp.float32)
        + qv_bias[0].astype(jnp.float32)
    ).astype(jnp.bfloat16)
    key_rows = jnp.dot(normed, qkv_weight[1], preferred_element_type=jnp.float32).astype(
        jnp.bfloat16
    )
    value_rows = (
        jnp.dot(normed, qkv_weight[2], preferred_element_type=jnp.float32)
        + qv_bias[1].astype(jnp.float32)
    ).astype(jnp.bfloat16)

    def per_sequence(array):
        return array.reshape(seq_count, length, head_count, HEAD_DIM)

    def attend_sequence(member):
        seq_query, seq_keys, seq_values, seq_segments, seq_context = member

        def attend_block(portion):
            block_query, block_segments = portion
            scores = masked_scores(
                block_query, seq_keys, block_segments, seq_segments, seq_context, factor
            )
            row_top = jnp.max(scores, axis=-1, keepdims=True)
            exponent = jnp.exp(scores - row_top)
            row_total = jnp.sum(exponent, axis=-1, keepdims=True)
            soft_weights = (exponent / row_total).astype(jnp.bfloat16)
            block_mix = jnp.einsum(
                "hqk,khd->qhd", soft_weights, seq_values, preferred_element_type=jnp.float32
            )
            return (block_mix.astype(jnp.bfloat16), row_top + jnp.log(row_total))

        return lax.map(
            attend_block,
            (
                seq_query.reshape(blocks, block, head_count, HEAD_DIM),
                seq_segments.reshape(blocks, block),
            ),
        )

    mixture, log_totals = lax.map(
        attend_sequence,
        (
            per_sequence(queries),
            per_sequence(key_rows),
            per_sequence(value_rows),
            segment_ids,
            context_flags,
        ),
    )
    mixture = mixture.reshape(row_count, local_cols)
    partial_out = jnp.dot(mixture, out_weight, preferred_element_type=jnp.float32)
    grad_rows_all = cotangent.reshape(row_count, width)
    grad_float_all = grad_rows_all.astype(jnp.float32)
    grad_down_bias = jnp.sum(grad_float_all, axis=0)
    attended = lax.psum(partial_out, "head") + out_bias.astype(jnp.float32)
    middle_state = flat_in + attended
    normed_two_f, norm_two_pull = jax.vjp(layer_norm, middle_state, gain_two, offset_two)
    normed_two = normed_two_f.astype(jnp.bfloat16)
    up_part, down_part, up_shift = (
        lax.all_gather(up_weight, "head", axis=1, tiled=True),
        lax.all_gather(down_weight, "head", axis=0, tiled=True),
        lax.all_gather(up_bias, "head", axis=0, tiled=True),
    )
    up_full, down_full = (
        lax.all_gather(up_part, "seq", axis=0, tiled=True),
        lax.all_gather(down_part, "seq", axis=1, tiled=True),
    )
    before = jnp.dot(normed_two, up_full, preferred_element_type=jnp.float32) + up_shift.astype(
        jnp.float32
    )
    active_f, gelu_pull = jax.vjp(gelu_exact, before)
    active = active_f.astype(jnp.bfloat16)
    branch_out = jnp.dot(active, down_full, preferred_element_type=jnp.float32)
    final_rows = (middle_state + branch_out + down_bias.astype(jnp.float32)).astype(jnp.bfloat16)
    output = final_rows.reshape(tokens.shape)
    grad_float = grad_rows_all.astype(jnp.float32)
    grad_down = dot_cols(active, grad_rows_all)
    grad_active = dot_rows(grad_rows_all, down_full)
    (grad_before_f,) = gelu_pull(grad_active)
    grad_before = grad_before_f.astype(jnp.bfloat16)
    grad_up = dot_cols(normed_two, grad_before)
    grad_up_bias = jnp.sum(grad_before.astype(jnp.float32), axis=0)
    grad_normed_two = dot_rows(grad_before, up_full)
    grad_middle_norm, grad_gain_two, grad_offset_two = norm_two_pull(grad_normed_two)
    grad_middle = grad_float + grad_middle_norm
    ff_part = up_weight.shape[1]
    start_col = lax.axis_index("head") * ff_part
    grad_up = lax.dynamic_slice_in_dim(grad_up, start_col, ff_part, 1)
    grad_down = lax.dynamic_slice_in_dim(grad_down, start_col, ff_part, 0)
    grad_up_bias = lax.dynamic_slice_in_dim(grad_up_bias, start_col, ff_part, 0)
    grad_attended = grad_middle.astype(jnp.bfloat16)
    grad_out_bias = jnp.sum(grad_attended.astype(jnp.float32), axis=0)
    grad_out = dot_cols(mixture, grad_attended)
    grad_mixture = dot_rows(grad_attended, out_weight).astype(jnp.bfloat16)

    def back_sequence(member):
        seq_query, seq_keys, seq_values, seq_grad, seq_logs, seq_segments, seq_context = member

        def back_block(carry, portion):
            key_acc, value_acc = carry
            block_query, block_grad, block_logs, block_segments = portion
            scores = masked_scores(
                block_query, seq_keys, block_segments, seq_segments, seq_context, factor
            )
            soft_weights = jnp.exp(scores - block_logs)
            value_acc = value_acc + jnp.einsum(
                "hqk,qhd->khd",
                soft_weights.astype(jnp.bfloat16),
                block_grad,
                preferred_element_type=jnp.float32,
            )
            grad_soft = jnp.einsum(
                "qhd,khd->hqk", block_grad, seq_values, preferred_element_type=jnp.float32
            )
            row_inner = jnp.sum(soft_weights * grad_soft, axis=-1, keepdims=True)
            grad_scores = (soft_weights * (grad_soft - row_inner)).astype(jnp.bfloat16)
            grad_query = (
                jnp.einsum(
                    "hqk,khd->qhd", grad_scores, seq_keys, preferred_element_type=jnp.float32
                )
                * factor
            )
            key_acc = (
                key_acc
                + jnp.einsum(
                    "hqk,qhd->khd", grad_scores, block_query, preferred_element_type=jnp.float32
                )
                * factor
            )
            return ((key_acc, value_acc), grad_query)

        empty = jnp.zeros((length, head_count, HEAD_DIM), jnp.float32)
        (key_acc, value_acc), grad_query = lax.scan(
            back_block,
            (empty, empty),
            (
                seq_query.reshape(blocks, block, head_count, HEAD_DIM),
                seq_grad.reshape(blocks, block, head_count, HEAD_DIM),
                seq_logs,
                seq_segments.reshape(blocks, block),
            ),
        )
        return (grad_query, key_acc, value_acc)

    grad_queries, grad_keys, grad_values = lax.map(
        back_sequence,
        (
            per_sequence(queries),
            per_sequence(key_rows),
            per_sequence(value_rows),
            per_sequence(grad_mixture),
            log_totals,
            segment_ids,
            context_flags,
        ),
    )
    grad_queries = grad_queries.reshape(row_count, local_cols).astype(jnp.bfloat16)
    grad_keys = grad_keys.reshape(row_count, local_cols).astype(jnp.bfloat16)
    grad_values = grad_values.reshape(row_count, local_cols).astype(jnp.bfloat16)
    grad_qv_bias = jnp.stack(
        [
            jnp.sum(grad_queries.astype(jnp.float32), axis=0),
            jnp.sum(grad_values.astype(jnp.float32), axis=0),
        ]
    )
    grad_qkv = jnp.stack(
        [dot_cols(normed, grad_queries), dot_cols(normed, grad_keys), dot_cols(normed, grad_values)]
    )
    grad_normed = (
        dot_rows(grad_queries, qkv_weight[0])
        + dot_rows(grad_keys, qkv_weight[1])
        + dot_rows(grad_values, qkv_weight[2])
    )
    grad_normed = lax.psum(grad_normed, "head")
    grad_input_norm, grad_gain_one, grad_offset_one = norm_one_pull(grad_normed)
    tokens_grad = (grad_middle + grad_input_norm).astype(jnp.bfloat16).reshape(tokens.shape)
    summed_qkv, summed_out, summed_up, summed_down = (
        lax.psum_scatter(
            grad_qkv.astype(jnp.bfloat16), "seq", scatter_dimension=1, tiled=True
        ).astype(jnp.float32),
        lax.psum_scatter(
            grad_out.astype(jnp.bfloat16), "seq", scatter_dimension=1, tiled=True
        ).astype(jnp.float32),
        lax.psum_scatter(
            grad_up.astype(jnp.bfloat16), "seq", scatter_dimension=0, tiled=True
        ).astype(jnp.float32),
        lax.psum_scatter(
            grad_down.astype(jnp.bfloat16), "seq", scatter_dimension=1, tiled=True
        ).astype(jnp.float32),
    )
    smalls = lax.psum(
        (
            grad_gain_one,
            grad_offset_one,
            grad_qv_bias,
            grad_out_bias,
            grad_gain_two,
            grad_offset_two,
            grad_up_bias,
            grad_down_bias,
        ),
        "seq",
    )
    return (
        output,
        tokens_grad,
        smalls[0],
        smalls[1],
        summed_qkv,
        smalls[2],
        summed_out,
        smalls[3],
        smalls[4],
        smalls[5],
        summed_up,
        smalls[6],
        summed_down,
        smalls[7],
    )


MESH = pl.DeviceIdType.MESH
BF = jnp.bfloat16
F32 = jnp.float32
BLOCK = 256
STRIP = 512
PIECE = 128
WIDE = 1024
GROUP = 2
CHUNK = 512
PAIR = 2 * HEAD_DIM
Z_SIZE, Y_SIZE, CORES = 4, 2, 2
SEQ_SIZE = Z_SIZE * Y_SIZE * CORES
HOP = Y_SIZE * CORES
TABLES = 8
FAR = -1e30
VMEM_LIMIT = 62 * 2**20
INV_ROOT_TWO = 0.7071067811865476
INV_ROOT_TWO_PI = 0.3989422804014327
LN1_GAIN, LN1_BIAS, QV_BIAS, OUT_BIAS, LN2_GAIN, LN2_BIAS, UP_BIAS, DOWN_BIAS = 0, 1, 2, 3, 4, 5, 6, 8
SMALL_ROWS = 16
VMEM_SPEC = pl.BlockSpec(memory_space=pltpu.VMEM)
ANY_SPEC = pl.BlockSpec(memory_space=pl.ANY)


def shape_of(dims, dtype):
    return jax.ShapeDtypeStruct(tuple(dims), dtype)


def nn(left, right):
    return jnp.dot(left, right, preferred_element_type=F32)


def split_sum(left, right):
    parts = [
        nn(left[:, n:n + BLOCK], right[n:n + BLOCK]) for n in range(0, left.shape[1], BLOCK)
    ]
    while len(parts) > 1:
        parts = [a + b for a, b in zip(parts[::2], parts[1::2])]
    return parts[0]


def turn(block):
    return jnp.transpose(block)


def sum_rows(block):
    return jnp.sum(block, axis=0, keepdims=True)


def place():
    me = lax.axis_index("seq")
    head = lax.axis_index("head")
    core = me % 2
    y = (me // 2) % 2
    across = {"seq": me, "head": 1 - head}
    core_mate = {"seq": me + 1 - 2 * core, "head": head}
    y_mate = {"seq": me + 2 - 4 * y, "head": head}
    z_mates = [{"seq": (me + HOP * d) % SEQ_SIZE, "head": head} for d in (1, 2, 3)]
    return me, head, core, y, across, core_mate, y_mate, z_mates


def greet(others):
    barrier = pltpu.get_barrier_semaphore()
    for other in others:
        pl.semaphore_signal(barrier, inc=1, device_id=other, device_id_type=MESH)
    pl.semaphore_wait(barrier, len(others))


def remote(src, dst, send_sem, recv_sem, other):
    return pltpu.make_async_remote_copy(
        src_ref=src, dst_ref=dst, send_sem=send_sem, recv_sem=recv_sem,
        device_id=other, device_id_type=MESH,
    )


def norm_stats(rows):
    middle = jnp.mean(rows, axis=-1, keepdims=True)
    centred = rows - middle
    spread = jnp.mean(centred * centred, axis=-1, keepdims=True)
    return centred, lax.rsqrt(spread + 1e-05)


def norm_back(inner, unit, scale):
    return scale * (
        inner
        - jnp.mean(inner, axis=-1, keepdims=True)
        - unit * jnp.mean(inner * unit, axis=-1, keepdims=True)
    )


def as_row(vector):
    return vector[...].astype(F32).reshape(1, -1)


def lanes():
    return lax.broadcasted_iota(jnp.int32, (1, PAIR), 1)


def in_pieces(column, first, rest):
    high = column.astype(BF).astype(F32)
    mid = (column - high).astype(BF).astype(F32)
    low = column - high - mid
    at = lanes()
    return jnp.where(
        at == first, high, jnp.where(at == first + 1, mid, jnp.where(at == first + 2, low, rest))
    ).astype(BF)


def one_lanes(length):
    return jnp.broadcast_to(jnp.where(lanes() < 3, 1.0, 0.0).astype(BF), (length, PAIR))


def fwd_kernel(
    x_ref, seg_ref, context, gain, offset, qv_bias, out_bias,
    wqkv, wout, up_shard, down_shard,
    q_out, k_out, v_out, mix_out, mid_out, normed_out, wff_out, key_out, query_out,
    wff, q_ref, k_ref, v_ref, mix_ref, mid_ref, normed_t, key_more, query_more,
    mask_more, wout_all, mix_x,
    zs, zr, ys, yr, cs, cr, xs, xr, local, outs,
):
    length, width = x_ref.shape
    blocks = length // BLOCK
    pairs = q_ref.shape[0]
    cols = pairs * PAIR
    me, head, core, y, across, core_mate, y_mate, _ = place()
    z = me // HOP
    above = {"seq": (me + HOP) % SEQ_SIZE, "head": head}
    below = {"seq": (me + SEQ_SIZE - HOP) % SEQ_SIZE, "head": head}
    own = [
        pltpu.make_async_copy(shard, wff.at[u, me], local.at[u])
        for u, shard in enumerate((up_shard, down_shard))
    ]
    own[0].start()
    own[1].start()
    greet([across, core_mate, y_mate, above, below])

    half = wout.shape[0] // 2
    here = pl.ds(pl.multiple_of(core * half, half), half)
    beside = pl.ds(pl.multiple_of((1 - core) * half, half), half)
    wout_x = wout_all.at[1 - head]
    out_copy = remote(
        wout.at[here, :], wout_all.at[head, here, :], xs.at[0], xr.at[0], across
    )
    wout_all[head] = wout[...]
    out_pass = remote(wout_x.at[here, :], wout_x.at[here, :], cs.at[28], cr.at[28], core_mate)
    out_arrival = remote(
        wout_x.at[beside, :], wout_x.at[beside, :], cs.at[28], cr.at[28], core_mate
    )
    out_copy.start()

    flows = [(0, 0)] + [(way, s) for s in (1, 2, 3) for way in (0, 1)]

    def there(way, s):
        return (z >= s) if way == 0 else (z + s < Z_SIZE)

    def source(base, way, s):
        away = SEQ_SIZE - HOP * s if way == 0 else HOP * s
        return (base + away) % SEQ_SIZE

    def z_copy(u, way, s):
        n = (u * 2 + way) * 3 + s - 1
        j = source(me, way, s - 1)
        return remote(wff.at[u, j], wff.at[u, j], zs.at[n], zr.at[n], above if way == 0 else below)

    def z_arrival(u, way, s):
        n = (u * 2 + way) * 3 + s - 1
        slot = wff.at[u, source(me, way, s)]
        return remote(slot, slot, zs.at[n], zr.at[n], above)

    def z_goes_on(way):
        return (z < Z_SIZE - 1) if way == 0 else (z > 0)

    def y_copy(u, f):
        n = u * 7 + f
        j = source(me, *flows[f])
        return remote(wff.at[u, j], wff.at[u, j], ys.at[n], yr.at[n], y_mate)

    def y_arrival(u, f):
        n = u * 7 + f
        slot = wff.at[u, source(me + 2 - 4 * y, *flows[f])]
        return remote(slot, slot, ys.at[n], yr.at[n], y_mate)

    def c_copy(u, f, from_y):
        n = (u * 2 + from_y) * 7 + f
        j = source(me + from_y * (2 - 4 * y), *flows[f])
        return remote(wff.at[u, j], wff.at[u, j], cs.at[n], cr.at[n], core_mate)

    def c_arrival(u, f, from_y):
        n = (u * 2 + from_y) * 7 + f
        slot = wff.at[u, source(me + 1 - 2 * core + from_y * (2 - 4 * y), *flows[f])]
        return remote(slot, slot, cs.at[n], cr.at[n], core_mate)

    def for_flow(f, do):
        if f == 0:
            do()
        else:
            pl.when(there(*flows[f]))(do)

    def for_step(s, do):
        for f, (way, step) in enumerate(flows):
            if step == s:
                for_flow(f, lambda f=f, way=way: do(f, way))

    def z_event(u, s):
        def one(f, way):
            z_arrival(u, way, s).wait_recv()
            if s < 3:
                pl.when(z_goes_on(way))(lambda: z_copy(u, way, s + 1).start())
            y_copy(u, f).start()
            c_copy(u, f, 0).start()
        for_step(s, one)
        if u == 0 and s == 1:
            start_z(1)
        if u == 0 and s == 2:
            y_copy(1, 0).start()
            c_copy(1, 0, 0).start()
        if u == 0 and s == 3:
            out_copy.wait_recv()
            out_pass.start()

    def y_event(u, s):
        def one(f, way):
            y_arrival(u, f).wait_recv()
            c_copy(u, f, 1).start()
        for_step(s, one)

    def start_z(u):
        for way in (0, 1):
            pl.when(z_goes_on(way))(lambda way=way: z_copy(u, way, 1).start())

    own[0].wait()
    start_z(0)
    y_copy(0, 0).start()
    c_copy(0, 0, 0).start()
    own[1].wait()

    plan = {
        2: [(z_event, 0, 1), (y_event, 0, 0)], 4: [(z_event, 0, 2)], 5: [(y_event, 0, 1)],
        6: [(z_event, 0, 3)], 7: [(z_event, 1, 1)], 8: [(y_event, 0, 2), (y_event, 1, 0)],
        9: [(z_event, 1, 2)], 10: [(y_event, 0, 3)], 11: [(z_event, 1, 3)],
    }

    def tick(t):
        for step, events in plan.items():
            @pl.when(t == step)
            def _(events=events):
                for event, u, s in events:
                    event(u, s)

    at = lax.broadcasted_iota(jnp.int32, (PAIR, length), 0)
    same = at == seg_ref[...]
    hidden = context[...] != 1
    ones = jnp.logical_and(at > TABLES, at < TABLES + 4)
    key_side = jnp.logical_or(
        jnp.logical_and(at < TABLES, same),
        jnp.logical_or(jnp.logical_and(at == TABLES, hidden), ones),
    )
    query_side = jnp.logical_and(at <= TABLES, jnp.logical_not(same))
    key_more[...] = turn(jnp.where(key_side, 1.0, 0.0)).astype(BF)
    mask_more[...] = turn(jnp.where(query_side, FAR, 0.0)).astype(BF)

    keep = [
        pltpu.make_async_copy(here, there, outs.at[n])
        for n, (here, there) in enumerate(
            (
                (q_ref, q_out), (k_ref, k_out), (v_ref, v_out), (normed_t, normed_out),
                (key_more, key_out), (query_more, query_out), (mix_ref, mix_out),
            )
        )
    ]
    gains, offsets = as_row(gain), as_row(offset)
    query_bias = qv_bias[0:1, :].astype(F32)
    value_bias = qv_bias[1:2, :].astype(F32)

    def project(b, _):
        rows = pl.ds(pl.multiple_of(b * BLOCK, BLOCK), BLOCK)
        centred, scale = norm_stats(x_ref[rows, :].astype(F32))
        block = (centred * scale * gains + offsets).astype(BF)
        normed_t[:, rows] = turn(block)
        queries = ((nn(block, wqkv[0]) + query_bias).astype(BF) * 0.125).astype(BF)
        keys = nn(block, wqkv[1]).astype(BF)
        values = (nn(block, wqkv[2]) + value_bias).astype(BF)
        for p in range(pairs):
            part = slice(p * PAIR, (p + 1) * PAIR)
            q_ref[p, rows, :] = queries[:, part]
            k_ref[p, rows, :] = keys[:, part]
            v_ref[p, rows, :] = values[:, part]
        tick(b)
        return 0

    lax.fori_loop(0, blocks, project, 0)
    for n in range(5):
        keep[n].start()

    low_lanes = lanes() < HEAD_DIM
    zero = jnp.zeros((1, PAIR), BF)

    def mixture_copy(t):
        rows = pl.ds(pl.multiple_of(t // pairs * STRIP, STRIP), STRIP)
        return remote(
            mix_ref.at[t % pairs, rows, :], mix_x.at[t % pairs, rows, :], xs.at[1 + t],
            xr.at[1 + t], across,
        )

    per_step = STRIP // BLOCK

    def attend(t, _):
        b, p = t // pairs, t % pairs
        keys = jnp.concatenate([k_ref[p], key_more[...]], axis=1)
        values = jnp.concatenate([v_ref[p], one_lanes(length)], axis=1)
        chains = []
        for n in range(per_step):
            rows = pl.ds(pl.multiple_of(b * STRIP + n * BLOCK, BLOCK), BLOCK)
            queries, more = q_ref[p, rows, :], mask_more[rows, :]
            for low in (0, 1):
                own_lanes = jnp.logical_not(low_lanes) if low else low_lanes
                left = jnp.concatenate([jnp.where(own_lanes, queries, zero), more], axis=1)
                chains.append((rows, low, more, dot_rows(left, keys)))
        parts = []
        for rows, low, more, scores in chains:
            top = jnp.max(scores, axis=-1, keepdims=True)
            mixed = nn(jnp.exp(scores - top).astype(BF), values)
            total = mixed[:, PAIR:PAIR + 1]
            parts.append(mixed[:, :PAIR] / total)
            query_more[2 * p + low, rows, :] = in_pieces(
                -(top + jnp.log(total)), TABLES + 1, more.astype(F32)
            )
            if low:
                mix_ref[p, rows, :] = jnp.where(low_lanes, *parts[-2:]).astype(BF)
        mixture_copy(t).start()
        tick(t + blocks)
        return 0

    lax.fori_loop(0, length // STRIP * pairs, attend, 0)
    keep[5].start()
    keep[6].start()
    out_arrival.wait_recv()
    out_row = as_row(out_bias)

    def mid_copy(b):
        rows = pl.ds(b * BLOCK, BLOCK)
        return pltpu.make_async_copy(mid_ref.at[rows, :], mid_out.at[rows, :], outs.at[7 + b])

    def arrive(u):
        for f in range(len(flows)):
            def one(f=f):
                for from_y in (0, 1):
                    c_arrival(u, f, from_y).wait_recv()
            for_flow(f, one)

    for b in range(blocks):
        if b % per_step == 0:
            for p in range(pairs):
                mixture_copy(b // per_step * pairs + p).wait_recv()
        rows = pl.ds(b * BLOCK, BLOCK)
        ours = jnp.concatenate([mix_ref[p, rows, :] for p in range(pairs)], axis=-1)
        other = jnp.concatenate([mix_x[p, rows, :] for p in range(pairs)], axis=-1)
        first, second = jnp.where(head == 0, ours, other), jnp.where(head == 0, other, ours)
        attended = nn(first, wout_all[0]) + nn(second, wout_all[1])
        mid_ref[rows, :] = x_ref[rows, :].astype(F32) + (attended + out_row)
        mid_copy(b).start()
        if b < 3:
            y_event(1, b + 1)
    wff_keep = [pltpu.make_async_copy(wff.at[u], wff_out.at[u], local.at[u]) for u in range(2)]
    arrive(0)
    wff_keep[0].start()
    arrive(1)
    wff_keep[1].start()
    out_copy.wait_send()
    out_pass.wait_send()
    for copy in keep + wff_keep:
        copy.wait()
    for t in range(length // STRIP * pairs):
        mixture_copy(t).wait_send()
    for b in range(blocks):
        mid_copy(b).wait()
    for u in range(2):
        for way in (0, 1):
            pl.when(z_goes_on(way))(lambda u=u, way=way: z_copy(u, way, 1).wait_send())
        for f, (way, s) in enumerate(flows):
            def finish(u=u, f=f, way=way, s=s):
                if f and s < 3:
                    pl.when(z_goes_on(way))(lambda: z_copy(u, way, s + 1).wait_send())
                y_copy(u, f).wait_send()
                for from_y in (0, 1):
                    c_copy(u, f, from_y).wait_send()
            for_flow(f, finish)


def run_fwd(x, seg, context, gain, offset, qv_bias, out_bias, wqkv, wout, up_weight, down_t):
    length, width = x.shape
    pairs = wqkv.shape[2] // PAIR
    blocks = length // BLOCK
    depth, hidden = up_weight.shape
    by_pair, by_head = (pairs, length, PAIR), (2 * pairs, length, PAIR)
    turned = (width, length)
    steps = length // STRIP * pairs
    dma = pltpu.SemaphoreType.DMA
    return pl.pallas_call(
        fwd_kernel,
        out_shape=[shape_of(by_pair, BF)] * 4 + [
            shape_of((length, width), F32),
            shape_of(turned, BF),
            shape_of((2, SEQ_SIZE, depth, hidden), BF),
            shape_of((length, PAIR), BF),
            shape_of(by_head, BF),
        ],
        in_specs=[VMEM_SPEC] * 9 + [ANY_SPEC] * 2,
        out_specs=[ANY_SPEC] * 9,
        scratch_shapes=[pltpu.VMEM((2, SEQ_SIZE, depth, hidden), BF)]
        + [pltpu.VMEM(by_pair, BF)] * 4 + [
            pltpu.VMEM((length, width), F32),
            pltpu.VMEM(turned, BF),
            pltpu.VMEM((length, PAIR), BF),
            pltpu.VMEM(by_head, BF),
            pltpu.VMEM((length, PAIR), BF),
            pltpu.VMEM((2,) + wout.shape, BF),
            pltpu.VMEM(by_pair, BF),
            dma((12,)), dma((12,)), dma((14,)), dma((14,)), dma((29,)), dma((29,)),
            dma((1 + steps,)), dma((1 + steps,)), dma((2,)), dma((7 + blocks,)),
        ],
        compiler_params=pltpu.CompilerParams(
            collective_id=0, has_side_effects=True, vmem_limit_bytes=VMEM_LIMIT
        ),
    )(x, seg, context, gain, offset, qv_bias, out_bias, wqkv, wout, up_weight, down_t)


def ff_kernel(
    mid_hbm, dy_hbm, wff_hbm, gain, offset, up_bias, wout_hbm,
    branch_out, gmid_hbm, ga_out, gm_out, summed, small_ref,
    dy_ref, wff, wout, bias_row, branch_ref, ga_t, gm_ref, normed, normed_t, dy_t, active, before_grad, gnt_acc, gnt_own, gnt_x, whole, from_mate,
    held, ready,
    xs, xr, cs, cr, ls, ws, ss, ins, outs,
):
    length, width = dy_ref.shape
    blocks = length // PIECE
    hidden = wff.shape[3]
    half = hidden // WIDE
    chunks = 2 * hidden // CHUNK
    pairs = gm_ref.shape[0]
    me, head, core, y, across, core_mate, y_mate, z_mates = place()
    dy_load = pltpu.make_async_copy(dy_hbm, dy_ref, ins.at[0])
    wout_load = pltpu.make_async_copy(wout_hbm, wout, ins.at[1])

    def wff_load(n):
        cut = pl.ds(n * WIDE, WIDE)
        return pltpu.make_async_copy(
            wff_hbm.at[:, :, :, cut], wff.at[:, :, :, cut], ins.at[2 + n]
        )

    dy_load.start()
    for n in range(half):
        wff_load(n).start()
    wout_load.start()
    greet([across, core_mate])
    gains, offsets = as_row(gain), as_row(offset)
    bias_row[...] = as_row(up_bias)

    def weight(kind, n):
        cut = pl.ds(pl.multiple_of(n * WIDE, WIDE), WIDE)
        return wff[kind, :, :, cut].reshape(width, WIDE)

    small_ref[...] = jnp.zeros_like(small_ref)

    def load(n):
        rows = pl.ds(n % blocks * PIECE, PIECE)
        return pltpu.make_async_copy(mid_hbm.at[rows, :], held.at[n % 2], ls.at[n % 2])

    def store(b):
        rows = pl.ds(b * PIECE, PIECE)
        return pltpu.make_async_copy(ready.at[b % 2], gmid_hbm.at[rows, :], ws.at[b % 2])

    load(0).start()
    load(1).start()

    def gnt_copy(b):
        return remote(gnt_own.at[b], gnt_x.at[b], xs.at[b], xr.at[b], across)

    def core_copy(n):
        return remote(
            whole.at[n, :, :, 1 - core], from_mate.at[n], cs.at[n], cr.at[n], core_mate
        )

    def forward(t, _):
        b, n = t // half, t % half
        rows = pl.ds(pl.multiple_of(b * PIECE, PIECE), PIECE)

        for b_next in range(blocks):
            @pl.when(t == b_next * half)
            def _(b_next=b_next):
                load(b_next).wait()
                if b_next == 0:
                    dy_load.wait()

        for n_first in range(half):
            @pl.when(t == n_first)
            def _(n_first=n_first):
                wff_load(n_first).wait()

        @pl.when(n == 0)
        def _():
            centred, scale = norm_stats(held[b % 2])
            block = (centred * scale * gains + offsets).astype(BF)
            normed[...] = block
            normed_t[:, rows] = turn(block)
            dy_t[:, rows] = turn(dy_ref[rows, :])
            small_ref[DOWN_BIAS:DOWN_BIAS + 1, :] += sum_rows(dy_ref[rows, :].astype(F32))

        up = weight(0, n)
        cut = pl.ds(pl.multiple_of(n * WIDE, WIDE), WIDE)
        before = nn(normed[...], up) + bias_row[:, cut]
        spread = 0.5 * (1.0 + lax.erf(before * INV_ROOT_TWO))
        active[n, rows, :] = (before * spread).astype(BF)
        slope = spread + before * (INV_ROOT_TWO_PI * jnp.exp(before * before * -0.5))
        grad = (nn(dy_ref[rows, :], weight(1, n)) * slope).astype(BF)
        before_grad[n, rows, :] = grad
        small_ref[pl.ds(UP_BIAS + n, 1), :] += sum_rows(grad.astype(F32))
        back = dot_rows(grad, up)

        @pl.when(n == 0)
        def _():
            gnt_acc[...] = back

        @pl.when(n > 0)
        def _():
            gnt_acc[...] += back

        for b_done in range(blocks):
            @pl.when(t == (b_done + 1) * half - 1)
            def _(b_done=b_done):
                load(b_done + 2).start()
                gnt_own[b_done] = gnt_acc[...].astype(BF)
                gnt_copy(b_done).start()
        return 0

    lax.fori_loop(0, blocks * half, forward, 0)

    def weight_grads(left_t, right, first):
        cut_rows = width // Z_SIZE
        per_wide = WIDE // CHUNK

        def one(t, _):
            n, plane = t // Z_SIZE, t % Z_SIZE
            cut = pl.ds(pl.multiple_of(plane * cut_rows, cut_rows), cut_rows)
            total = nn(left_t[cut, :], right[n]).astype(BF)
            for m in range(per_wide):
                piece = total[:, m * CHUNK:(m + 1) * CHUNK]
                whole[first + n * per_wide + m, plane] = piece.reshape(whole.shape[2:])

            @pl.when(plane == Z_SIZE - 1)
            def _():
                for m in range(per_wide):
                    core_copy(first + n * per_wide + m).start()

            return 0

        lax.fori_loop(0, Z_SIZE * half, one, 0)

    weight_grads(dy_t, active, chunks // 2)
    weight_grads(normed_t, before_grad, 0)

    def branch(b, _):
        rows = pl.ds(pl.multiple_of(b * BLOCK, BLOCK), BLOCK)
        total = dot_rows(active[0, rows, :], weight(1, 0))
        for n in range(1, half):
            total += dot_rows(active[n, rows, :], weight(1, n))
        branch_ref[rows, :] = total.astype(BF)
        return 0

    lax.fori_loop(0, length // BLOCK, branch, 0)
    branch_keep = pltpu.make_async_copy(branch_ref, branch_out, outs.at[0])
    branch_keep.start()
    wout_load.wait()

    def ga_copy(b):
        rows = pl.ds(b * PIECE, PIECE)
        return pltpu.make_async_copy(ga_t.at[:, rows], ga_out.at[:, rows], outs.at[1 + b])

    def gm_copy(b):
        rows = pl.ds(b * PIECE, PIECE)
        return pltpu.make_async_copy(
            gm_ref.at[:, rows, :], gm_out.at[:, rows, :], outs.at[1 + blocks + b]
        )


    def add_mate(n, _):
        core_copy(n).wait()
        both = whole[n, :, :, core].astype(F32) + from_mate[n].astype(F32)
        from_mate[n] = both.astype(BF)
        return 0

    lax.fori_loop(chunks // 2, chunks, add_mate, 0)
    lax.fori_loop(0, chunks // 2, add_mate, 0)
    keep = pltpu.make_async_copy(from_mate, summed, ss.at[0])
    keep.start()

    def through_norm(b):
        rows = pl.ds(b * PIECE, PIECE)
        grad = gnt_own[b].astype(F32) + gnt_x[b].astype(F32)
        centred, scale = norm_stats(held[b % 2])
        unit = centred * scale
        small_ref[LN2_GAIN:LN2_GAIN + 1, :] += sum_rows(grad * unit)
        small_ref[LN2_BIAS:LN2_BIAS + 1, :] += sum_rows(grad)
        total = dy_ref[rows, :].astype(F32) + norm_back(grad * gains, unit, scale)
        ready[b % 2] = total
        low = total.astype(BF)
        small_ref[OUT_BIAS:OUT_BIAS + 1, :] += sum_rows(low.astype(F32))
        ga_t[:, rows] = turn(low)
        mixed = dot_rows(low, wout[...]).astype(BF)
        for p in range(pairs):
            gm_ref[p, rows, :] = mixed[:, p * PAIR:(p + 1) * PAIR]

    for b in range(blocks):
        gnt_copy(b).wait()
        load(blocks + b).wait()
        if b >= 2:
            store(b - 2).wait()
        through_norm(b)
        store(b).start()
        ga_copy(b).start()
        gm_copy(b).start()
        if b + 2 < blocks:
            load(blocks + b + 2).start()
    store(blocks - 2).wait()
    store(blocks - 1).wait()
    for b in range(blocks):
        ga_copy(b).wait()
        gm_copy(b).wait()
    branch_keep.wait()
    keep.wait()


def run_ff(middle, dy, wff, gain, offset, up_bias, wout):
    length, width = middle.shape
    half = wff.shape[3] // WIDE
    chunks = 2 * wff.shape[3] // CHUNK
    blocks = length // PIECE
    pairs = wout.shape[0] // PAIR
    depth = width // SEQ_SIZE
    dma = pltpu.SemaphoreType.DMA
    rows = pltpu.VMEM((blocks, PIECE, width), BF)
    hidden = pltpu.VMEM((half, length, WIDE), BF)
    flat_t = pltpu.VMEM((width, length), BF)
    return pl.pallas_call(
        ff_kernel,
        out_shape=[
            shape_of((length, width), BF),
            shape_of((length, width), F32),
            shape_of((width, length), BF),
            shape_of((pairs, length, PAIR), BF),
            shape_of((chunks, Z_SIZE, Y_SIZE, depth, CHUNK), BF),
            shape_of((SMALL_ROWS, width), F32),
        ],
        in_specs=[ANY_SPEC] * 3 + [VMEM_SPEC] * 3 + [ANY_SPEC],
        out_specs=[ANY_SPEC] * 5 + [VMEM_SPEC],
        scratch_shapes=[
            pltpu.VMEM((length, width), BF), pltpu.VMEM(wff.shape, BF),
            pltpu.VMEM(wout.shape, BF), pltpu.VMEM((1, half * WIDE), F32),
            pltpu.VMEM((length, width), BF), flat_t, pltpu.VMEM((pairs, length, PAIR), BF),
            pltpu.VMEM((PIECE, width), BF), flat_t, flat_t, hidden, hidden,
            pltpu.VMEM((PIECE, width), F32), rows, rows,
            pltpu.VMEM((chunks, Z_SIZE, Y_SIZE, CORES, depth, CHUNK), BF),
            pltpu.VMEM((chunks, Z_SIZE, Y_SIZE, depth, CHUNK), BF),
            pltpu.VMEM((2, PIECE, width), F32), pltpu.VMEM((2, PIECE, width), F32),
            dma((blocks,)), dma((blocks,)), dma((chunks,)), dma((chunks,)),
            dma((2,)), dma((2,)), dma((1,)), dma((2 + half,)), dma((1 + 2 * blocks,)),
        ],
        compiler_params=pltpu.CompilerParams(
            collective_id=1, has_side_effects=True, vmem_limit_bytes=VMEM_LIMIT
        ),
    )(middle, dy, wff, gain, offset, up_bias, wout)


def back_kernel(
    q_hbm, k_hbm, v_hbm, mix_hbm, gm_hbm, query_hbm, ga_hbm, normed_hbm, wqkv_hbm, x_hbm,
    key_more, gain, down_bias, small_in, mid_hbm, gmid_hbm, ff_part, branch,
    out_hbm, tokens_hbm, qkv_sum, out_sum, up_sum, down_sum,
    gain_one, offset_one, qv_small, out_small, gain_two, offset_two, up_small, down_small,
    q_ref, k_ref, v_ref, mix_ref, gm_ref, query_more, ga_t, normed_t, wqkv, x_ref,
    out_ref, tokens_ref, key_t, key_acc, value_acc, dq, dk, dv, whole, mate, at_y, at_z, ff_y, ff_z, gn_own, gn_x,
    branch_x, branch_own, ff_own, held, small_own, small_z, small_y, small_c, small_x,
    bs, br, fys, fyr, fzs, fzr, acs, acr, ays, ayr, azs, azr, gs, gr, ls, ms, mr, os, hs, ins, more_ins, outs,
):
    length, width = x_ref.shape
    blocks = length // BLOCK
    strips = length // STRIP
    pairs = q_ref.shape[0]
    chunks = ff_part.shape[0]
    half = chunks // 2
    groups = chunks // GROUP
    me, head, core, y, across, core_mate, y_mate, z_mates = place()
    z = me // (Y_SIZE * CORES)
    by_pair = (
        (q_hbm, q_ref), (k_hbm, k_ref), (v_hbm, v_ref), (mix_hbm, mix_ref), (gm_hbm, gm_ref),
    )

    def pair_loads(p):
        both = pl.ds(2 * p, 2)
        first = p * (len(by_pair) + 1)
        return [
            pltpu.make_async_copy(src.at[p], dst.at[p], ins.at[first + n])
            for n, (src, dst) in enumerate(by_pair)
        ] + [
            pltpu.make_async_copy(
                query_hbm.at[both], query_more.at[both], ins.at[first + len(by_pair)]
            )
        ]

    late_loads = [
        pltpu.make_async_copy(src, dst, more_ins.at[n])
        for n, (src, dst) in enumerate(
            ((ga_hbm, ga_t), (normed_hbm, normed_t), (wqkv_hbm, wqkv), (x_hbm, x_ref))
        )
    ]
    for p in range(pairs):
        for copy in pair_loads(p):
            copy.start()
        if p == 0:
            late_loads[0].start()
            late_loads[1].start()
    late_loads[2].start()
    late_loads[3].start()
    greet([across, core_mate, y_mate, *z_mates])

    def part(b):
        return pl.ds(b * BLOCK, BLOCK)

    def branch_copy(b):
        return remote(branch.at[part(b), :], branch_x.at[part(b), :], bs.at[b], br.at[b], across)

    def load(n):
        source = mid_hbm if n < blocks else gmid_hbm
        return pltpu.make_async_copy(
            source.at[part(n % blocks), :], held.at[n % 2], ls.at[n % 2]
        )

    def taken(n):
        if n + 2 < 2 * blocks:
            load(n + 2).start()

    def group(g):
        return pl.ds(g * GROUP, GROUP)

    def ff_y_copy(g):
        return remote(
            ff_part.at[group(g), :, 1 - y], ff_y.at[group(g)], fys.at[g], fyr.at[g], y_mate
        )

    def ff_z_copy(g, d):
        n = g * 3 + d - 1
        return remote(
            ff_y.at[group(g), (z + d) % Z_SIZE], ff_z.at[d - 1, group(g)],
            fzs.at[n], fzr.at[n], z_mates[d - 1],
        )

    def branch_load(b):
        return pltpu.make_async_copy(branch.at[part(b), :], branch_own.at[b % 2], hs.at[b % 2])

    def ff_load(g):
        return pltpu.make_async_copy(
            ff_part.at[group(g), :, y], ff_own.at[g % 2], os.at[g % 2]
        )

    def ff_y_event(g):
        ff_y_copy(g).wait_recv()
        ff_load(g).wait()
        for n in range(g * GROUP, (g + 1) * GROUP):
            own = ff_own[g % 2, n % GROUP]
            ff_y[n] = (ff_y[n].astype(F32) + own.astype(F32)).astype(BF)
        if g + 2 < groups:
            ff_load(g + 2).start()
            ff_y_copy(g + 2).start()
        for d in (1, 2, 3):
            ff_z_copy(g, d).start()

    def ff_z_event(g):
        for d in (1, 2, 3):
            ff_z_copy(g, d).wait_recv()
        for n in range(g * GROUP, (g + 1) * GROUP):
            total = ff_y[n, z].astype(F32)
            for d in (1, 2, 3):
                total += ff_z[d - 1, n].astype(F32)
            if n < half:
                up_sum[:, n * CHUNK:(n + 1) * CHUNK] = total
            else:
                down_sum[:, (n - half) * CHUNK:(n - half + 1) * CHUNK] = total

    def at_c_copy(p):
        return remote(whole.at[p, :, :, 1 - core], mate.at[p], acs.at[p], acr.at[p], core_mate)

    def at_y_copy(p):
        return remote(mate.at[p, :, 1 - y], at_y.at[p], ays.at[p], ayr.at[p], y_mate)

    def at_z_copy(p, d):
        n = p * 3 + d - 1
        return remote(
            at_y.at[p, (z + d) % Z_SIZE], at_z.at[d - 1, p], azs.at[n], azr.at[n], z_mates[d - 1]
        )

    def at_c_event(p):
        at_c_copy(p).wait_recv()
        mate[p] = (mate[p].astype(F32) + whole[p, :, :, core].astype(F32)).astype(BF)
        at_y_copy(p).start()

    def at_y_event(p):
        at_y_copy(p).wait_recv()
        at_y[p] = (at_y[p].astype(F32) + mate[p, :, y].astype(F32)).astype(BF)
        for d in (1, 2, 3):
            at_z_copy(p, d).start()

    def at_z_event(p):
        for d in (1, 2, 3):
            at_z_copy(p, d).wait_recv()
        total = at_y[p, z].astype(F32)
        for d in (1, 2, 3):
            total += at_z[d - 1, p].astype(F32)
        cut = slice(p * PAIR, (p + 1) * PAIR)
        for kind in range(3):
            qkv_sum[kind, :, cut] = total[:, kind * PAIR:(kind + 1) * PAIR]
        out_sum[:, cut] = total[:, 3 * PAIR:]

    def out_copy(b):
        return pltpu.make_async_copy(out_ref.at[part(b), :], out_hbm.at[part(b), :], outs.at[b])

    def tokens_copy(b):
        return pltpu.make_async_copy(
            tokens_ref.at[part(b), :], tokens_hbm.at[part(b), :], outs.at[blocks + b]
        )

    def branch_event(b):
        branch_copy(b).wait_recv()
        load(b).wait()
        branch_load(b).wait()
        both = branch_own[b % 2].astype(F32) + branch_x[part(b), :].astype(F32)
        out_ref[part(b), :] = (held[b % 2] + both + as_row(down_bias)).astype(BF)
        out_copy(b).start()
        taken(b)
        if b + 2 < blocks:
            branch_load(b + 2).start()

    for b in range(blocks):
        branch_copy(b).start()
    for n in range(2):
        load(n).start()
        branch_load(n).start()
        ff_load(n).start()
        ff_y_copy(n).start()

    plan = {
        2: [(at_c_event, 0), (ff_y_event, 0), (branch_event, 0)], 4: [(at_c_event, 1)],
        5: [(ff_y_event, 1), (branch_event, 1)], 6: [(at_c_event, 2)],
    }

    low_lanes = lanes() < HEAD_DIM
    zero = jnp.zeros((1, PAIR), BF)

    def stacked(strip):
        return jnp.concatenate(
            [jnp.where(low_lanes, strip, zero), jnp.where(low_lanes, zero, strip)], axis=0
        )

    def attend(t, _):
        p, b = t // strips, t % strips
        rows = pl.ds(pl.multiple_of(b * STRIP, STRIP), STRIP)

        @pl.when(b == 0)
        def _():
            for p_now in range(pairs):
                @pl.when(p == p_now)
                def _(p_now=p_now):
                    for copy in pair_loads(p_now):
                        copy.wait()
            key_t[...] = turn(k_ref[p])
            key_acc[...] = jnp.zeros_like(key_acc)
            value_acc[...] = jnp.zeros_like(value_acc)

        queries, grads = stacked(q_ref[p, rows, :]), stacked(gm_ref[p, rows, :])
        more = jnp.concatenate(
            [query_more[2 * p, rows, :], query_more[2 * p + 1, rows, :]], axis=0
        )
        mixture = mix_ref[p, rows, :]
        product = grads.astype(F32) * jnp.concatenate([mixture, mixture], axis=0).astype(F32)
        inner = -jnp.sum(product, axis=-1, keepdims=True)
        query_side = jnp.concatenate([queries, more], axis=1)
        grad_side = jnp.concatenate([grads, in_pieces(inner, 0, 0.0)], axis=1)
        to_queries = jnp.zeros((PAIR, 2 * STRIP), F32)
        for n in range(blocks):
            keys = jnp.concatenate([k_ref[p, part(n), :], key_more[part(n), :]], axis=1)
            values = jnp.concatenate([v_ref[p, part(n), :], one_lanes(BLOCK)], axis=1)
            weights = jnp.exp(dot_rows(keys, query_side)).astype(BF)
            grad_scores = weights * dot_rows(values, grad_side).astype(BF)
            value_acc[part(n), :] += split_sum(weights, grads)
            key_acc[part(n), :] += split_sum(grad_scores, queries)
            to_queries += nn(key_t[:, part(n)], grad_scores)
        own = jnp.concatenate(
            [to_queries[:HEAD_DIM, :STRIP], to_queries[HEAD_DIM:, STRIP:]], axis=0
        )
        dq[p, rows, :] = (turn(own) * 0.125).astype(BF)

        @pl.when(b == strips - 1)
        def _():
            @pl.when(p == 0)
            def _():
                late_loads[0].wait()
                late_loads[1].wait()

            dk[p] = key_acc[...].astype(BF)
            dv[p] = value_acc[...].astype(BF)
            right = jnp.concatenate([dq[p], dk[p], dv[p]], axis=1)
            mixture_all = mix_ref[p]

            def one(plane, _):
                cut = pl.ds(pl.multiple_of(plane * BLOCK, BLOCK), BLOCK)
                both = jnp.concatenate(
                    [nn(normed_t[cut, :], right), nn(ga_t[cut, :], mixture_all)], axis=1
                )
                whole[p, plane] = both.astype(BF).reshape(whole.shape[2:])
                return 0

            lax.fori_loop(0, Z_SIZE, one, 0)
            at_c_copy(p).start()

        for step, events in plan.items():
            @pl.when(t == step)
            def _(events=events):
                for event, n in events:
                    event(n)
        return 0

    lax.fori_loop(0, pairs * strips, attend, 0)
    late_loads[2].wait()
    late_loads[3].wait()

    def gn_copy(b):
        return remote(gn_own.at[b], gn_x.at[b], gs.at[b], gr.at[b], across)

    own_gain = jnp.zeros((1, width), F32)
    own_offset = jnp.zeros((1, width), F32)
    for b in range(blocks):
        total = jnp.zeros((BLOCK, width), F32)
        for n, grad in enumerate((dq, dk, dv)):
            left = jnp.concatenate([grad[p, part(b), :] for p in range(pairs)], axis=1)
            total += dot_rows(left, wqkv[n])
        gn_own[b] = total.astype(BF)
        gn_copy(b).start()
        centred, scale = norm_stats(x_ref[part(b), :].astype(F32))
        own_gain += sum_rows(total * (centred * scale))
        own_offset += sum_rows(total)

    at_c_event(3)
    small_own[...] = small_in[...]
    small_own[LN1_GAIN:LN1_GAIN + 1, :] = own_gain
    small_own[LN1_BIAS:LN1_BIAS + 1, :] = own_offset
    for p in range(pairs):
        first, second = p * PAIR, (pairs + p) * PAIR
        small_own[QV_BIAS:QV_BIAS + 1, first:first + PAIR] = sum_rows(dq[p].astype(F32))
        small_own[QV_BIAS:QV_BIAS + 1, second:second + PAIR] = sum_rows(dv[p].astype(F32))
    def small_z_copy(d):
        return remote(small_own, small_z.at[z], ms.at[d - 1], mr.at[d - 1], z_mates[d - 1])

    def small_z_arrival(d):
        slot = small_z.at[(z + Z_SIZE - d) % Z_SIZE]
        return remote(slot, slot, ms.at[d - 1], mr.at[d - 1], z_mates[d - 1])

    y_sum = remote(small_y.at[0], small_y.at[1], ms.at[3], mr.at[3], y_mate)
    c_sum = remote(small_c.at[0], small_c.at[1], ms.at[4], mr.at[4], core_mate)
    x_sum = remote(small_x.at[0], small_x.at[1], ms.at[5], mr.at[5], across)
    for d in (1, 2, 3):
        small_z_copy(d).start()
    small_z[z] = small_own[...]

    def small_y_step():
        for d in (1, 2, 3):
            small_z_arrival(d).wait_recv()
        small_y[0] = small_z[0] + small_z[1] + small_z[2] + small_z[3]
        y_sum.start()

    def small_c_step():
        y_sum.wait()
        small_c[0] = small_y[0] + small_y[1]
        c_sum.start()

    def small_x_step():
        c_sum.wait()
        small_x[0] = small_c[0, 0:8, :] + small_c[1, 0:8, :]
        x_sum.start()

    branch_event(2)
    ff_y_event(2)
    branch_event(3)
    ff_z_event(0)
    ff_y_event(3)
    at_y_event(0)
    ff_z_event(1)
    gains = as_row(gain)
    for b in range(blocks):
        gn_copy(b).wait()
        load(blocks + b).wait()
        grad = gn_own[b].astype(F32) + gn_x[b].astype(F32)
        centred, scale = norm_stats(x_ref[part(b), :].astype(F32))
        unit = centred * scale
        tokens_ref[part(b), :] = (
            held[b % 2] + norm_back(grad * gains, unit, scale)
        ).astype(BF)
        tokens_copy(b).start()
        taken(blocks + b)
        if b == 0:
            small_y_step()
            at_y_event(1)
            at_y_event(2)
            ff_z_event(2)
        if b == 1:
            small_c_step()
            at_y_event(3)
            ff_z_event(3)
        if b == 2:
            small_x_step()
            at_z_event(0)
            at_z_event(1)
            at_z_event(2)

    at_z_event(3)
    x_sum.wait()
    ln1 = small_x[0, 0:2, :] + small_x[1, 0:2, :]
    gain_one[...] = ln1[0:1, :].reshape(width)
    offset_one[...] = ln1[1:2, :].reshape(width)
    small = small_c[0] + small_c[1]
    for kind, target in (
        (OUT_BIAS, out_small), (LN2_GAIN, gain_two), (LN2_BIAS, offset_two), (DOWN_BIAS, down_small),
    ):
        target[...] = small[kind:kind + 1, :].reshape(width)
    cols = pairs * PAIR
    qv_small[0:1, :] = small[QV_BIAS:QV_BIAS + 1, :cols]
    qv_small[1:2, :] = small[QV_BIAS:QV_BIAS + 1, cols:]
    for n in range(up_small.shape[0] // width):
        row = small[UP_BIAS + n:UP_BIAS + n + 1, :]
        up_small[n * width:(n + 1) * width] = row.reshape(width)

    for d in (1, 2, 3):
        small_z_copy(d).wait_send()
    for b in range(blocks):
        out_copy(b).wait()
        tokens_copy(b).wait()
        branch_copy(b).wait_send()
    for g in range(groups):
        ff_y_copy(g).wait_send()
        for d in (1, 2, 3):
            ff_z_copy(g, d).wait_send()
    for p in range(pairs):
        at_c_copy(p).wait_send()
        at_y_copy(p).wait_send()
        for d in (1, 2, 3):
            at_z_copy(p, d).wait_send()


def run_back(
    queries, keys, values, mixture, grad_mixture, query_more, ga_t, normed_t, wqkv, x,
    key_more, gain, down_bias, small, middle, grad_middle, ff_part, branch,
):
    length, width = x.shape
    pairs = queries.shape[0]
    chunks, depth = ff_part.shape[0], ff_part.shape[3]
    groups = chunks // GROUP
    cols, hidden = pairs * PAIR, chunks // 2 * CHUNK
    blocks = length // BLOCK
    dma = pltpu.SemaphoreType.DMA
    rows = pltpu.VMEM((blocks, BLOCK, width), BF)
    by_pair = pltpu.VMEM((pairs, length, PAIR), BF)
    whole_rows = pltpu.VMEM((length, width), BF)
    row = shape_of((width,), F32)
    loaded = (
        queries, keys, values, mixture, grad_mixture, query_more, ga_t, normed_t, wqkv, x
    )
    return pl.pallas_call(
        back_kernel,
        out_shape=[
            shape_of((length, width), BF),
            shape_of((length, width), BF),
            shape_of((3, depth, cols), F32),
            shape_of((depth, cols), F32),
            shape_of((depth, hidden), F32),
            shape_of((depth, hidden), F32),
            row, row, shape_of((2, cols), F32), row, row, row, shape_of((hidden,), F32), row,
        ],
        in_specs=[ANY_SPEC] * 10 + [VMEM_SPEC] * 4 + [ANY_SPEC] * 4,
        out_specs=[ANY_SPEC] * 2 + [VMEM_SPEC] * 12,
        scratch_shapes=[pltpu.VMEM(v.shape, BF) for v in loaded] + [
            whole_rows, whole_rows, pltpu.VMEM((PAIR, length), BF),
            pltpu.VMEM((length, PAIR), F32), pltpu.VMEM((length, PAIR), F32),
            by_pair, by_pair, by_pair,
            pltpu.VMEM((pairs, Z_SIZE, Y_SIZE, CORES, depth, CHUNK), BF),
            pltpu.VMEM((pairs, Z_SIZE, Y_SIZE, depth, CHUNK), BF),
            pltpu.VMEM((pairs, Z_SIZE, depth, CHUNK), BF),
            pltpu.VMEM((3, pairs, depth, CHUNK), BF),
            pltpu.VMEM((chunks, Z_SIZE, depth, CHUNK), BF),
            pltpu.VMEM((3, chunks, depth, CHUNK), BF),
            rows, rows, whole_rows,
            pltpu.VMEM((2, BLOCK, width), BF),
            pltpu.VMEM((2, GROUP, Z_SIZE, depth, CHUNK), BF),
            pltpu.VMEM((2, BLOCK, width), F32),
            pltpu.VMEM(small.shape, F32),
            pltpu.VMEM((Z_SIZE,) + small.shape, F32),
            pltpu.VMEM((2,) + small.shape, F32),
            pltpu.VMEM((2,) + small.shape, F32),
            pltpu.VMEM((2, 8, width), F32),
            dma((blocks,)), dma((blocks,)), dma((groups,)), dma((groups,)),
            dma((3 * groups,)), dma((3 * groups,)), dma((pairs,)), dma((pairs,)),
            dma((pairs,)), dma((pairs,)), dma((3 * pairs,)), dma((3 * pairs,)),
            dma((blocks,)), dma((blocks,)), dma((2,)), dma((6,)), dma((6,)), dma((2,)), dma((2,)),
            dma((6 * pairs,)), dma((4,)), dma((2 * blocks,)),
        ],
        compiler_params=pltpu.CompilerParams(
            collective_id=2, has_side_effects=True, vmem_limit_bytes=VMEM_LIMIT
        ),
    )(*loaded, key_more, gain, down_bias, small, middle, grad_middle, ff_part, branch)


def hand_over_kernel(*refs):
    *refs, sems = refs
    count = len(refs) // 3
    refs = refs[:count] + refs[2 * count:] + refs[count:2 * count]
    loads, stores = (
        [
            pltpu.make_async_copy(refs[a * count + n], refs[b * count + n], sems.at[a, n])
            for n in range(count)
        ]
        for a, b in ((0, 1), (1, 2))
    )
    for load in loads:
        load.start()
    for load, store in zip(loads, stores):
        load.wait()
        store.start()
    for store in stores:
        store.wait()


def hand_over(results):
    return pl.pallas_call(
        hand_over_kernel,
        out_shape=[shape_of(v.shape, v.dtype) for v in results],
        in_specs=[ANY_SPEC] * len(results),
        out_specs=[ANY_SPEC] * len(results),
        scratch_shapes=[pltpu.VMEM(v.shape, v.dtype) for v in results] + [
            pltpu.SemaphoreType.DMA((2, len(results)))
        ],
        compiler_params=pltpu.CompilerParams(vmem_limit_bytes=VMEM_LIMIT),
    )(*results)


def fast_body(
    tokens, segment_ids, context_flags, ln1_gain, ln1_bias, qkv_weight, qv_bias, out_weight,
    out_bias, ln2_gain, ln2_bias, up_weight, up_bias, down_weight, down_bias, cotangent,
):
    x, dy = tokens[0], cotangent[0]
    queries, keys, values, mixture, middle, normed_t, wff, key_more, query_more = run_fwd(
        x, segment_ids, context_flags, ln1_gain, ln1_bias, qv_bias, out_bias, qkv_weight,
        out_weight, up_weight, down_weight.T,
    )
    branch, grad_middle, ga_t, grad_mixture, ff_part, small = run_ff(
        middle, dy, wff, ln2_gain, ln2_bias, up_bias, out_weight
    )
    (
        output, tokens_grad, qkv_grad, out_grad, up_grad, down_grad, gain_one, offset_one,
        qv_grad, out_bias_grad, gain_two, offset_two, up_bias_grad, down_bias_grad,
    ) = hand_over(run_back(
        queries, keys, values, mixture, grad_mixture, query_more, ga_t, normed_t, qkv_weight, x,
        key_more, ln1_gain, down_bias, small, middle, grad_middle, ff_part, branch,
    ))
    return (
        output[None], tokens_grad[None], gain_one, offset_one, qkv_grad, qv_grad, out_grad.T,
        out_bias_grad, gain_two, offset_two, up_grad, up_bias_grad, down_grad.T, down_bias_grad,
    )


def solution(mesh):
    chosen = generic_body
    if mesh.shape["head"] == 2 and mesh.shape["seq"] == SEQ_SIZE:
        chosen = fast_body
    return jax.shard_map(
        chosen,
        mesh=mesh,
        in_specs=(
            P("seq", None, None),
            P("seq", None),
            P("seq", None),
            P(),
            P(),
            P(None, None, "head"),
            P(None, "head"),
            P("head", None),
            P(),
            P(),
            P(),
            P("seq", "head"),
            P("head"),
            P("head", "seq"),
            P(),
            P("seq", None, None),
        ),
        out_specs=(
            P("seq", None, None),
            P("seq", None, None),
            P(),
            P(),
            P(None, "seq", "head"),
            P(None, "head"),
            P("head", "seq"),
            P(),
            P(),
            P(),
            P("seq", "head"),
            P("head"),
            P("head", "seq"),
            P(),
        ),
        check_vma=False,
    )
```

```python
import math

import jax
import jax.numpy as jnp
from jax import lax
from jax.experimental import pallas as pl
from jax.experimental.pallas import tpu as pltpu
from jax.sharding import PartitionSpec as P

HEAD_DIM = 64


def layer_norm(values_in, scaling, offset):
    middle = jnp.mean(values_in, axis=-1, keepdims=True)
    centred = values_in - middle
    spread = jnp.mean(centred * centred, axis=-1, keepdims=True)
    return centred * lax.rsqrt(spread + 1e-05) * scaling + offset


def gelu_exact(values_in):
    return 0.5 * values_in * (1.0 + jax.scipy.special.erf(values_in * 0.7071067811865476))


def dot_rows(left, right):
    return lax.dot_general(
        left, right, (((1,), (1,)), ((), ())), preferred_element_type=jnp.float32
    )


def dot_cols(left, right):
    return lax.dot_general(
        left, right, (((0,), (0,)), ((), ())), preferred_element_type=jnp.float32
    )


def masked_scores(block_query, seq_keys, block_segments, seq_segments, seq_context, factor):
    raw_scores = (
        jnp.einsum("qhd,khd->hqk", block_query, seq_keys, preferred_element_type=jnp.float32)
        * factor
    )
    allowed = (block_segments[:, None] == seq_segments[None, :]) & (seq_context[None, :] == 1)
    return jnp.where(allowed[None], raw_scores, -1e30)


def generic_body(
    tokens,
    segment_ids,
    context_flags,
    ln1_gain,
    ln1_bias,
    qkv_weight,
    qv_bias,
    out_weight,
    out_bias,
    ln2_gain,
    ln2_bias,
    up_weight,
    up_bias,
    down_weight,
    down_bias,
    cotangent,
):
    seq_count, length, width = tokens.shape
    row_count = seq_count * length
    local_cols = qkv_weight.shape[2]
    head_count = local_cols // HEAD_DIM
    factor = 1.0 / math.sqrt(HEAD_DIM)
    block = min(512, length)
    blocks = length // block
    gain_one = ln1_gain.astype(jnp.float32)
    offset_one = ln1_bias.astype(jnp.float32)
    gain_two = ln2_gain.astype(jnp.float32)
    offset_two = ln2_bias.astype(jnp.float32)
    flat_in = tokens.astype(jnp.float32).reshape(row_count, width)
    normed_f, norm_one_pull = jax.vjp(layer_norm, flat_in, gain_one, offset_one)
    normed = normed_f.astype(jnp.bfloat16)
    queries = (
        jnp.dot(normed, qkv_weight[0], preferred_element_type=jnp.float32)
        + qv_bias[0].astype(jnp.float32)
    ).astype(jnp.bfloat16)
    key_rows = jnp.dot(normed, qkv_weight[1], preferred_element_type=jnp.float32).astype(
        jnp.bfloat16
    )
    value_rows = (
        jnp.dot(normed, qkv_weight[2], preferred_element_type=jnp.float32)
        + qv_bias[1].astype(jnp.float32)
    ).astype(jnp.bfloat16)

    def per_sequence(array):
        return array.reshape(seq_count, length, head_count, HEAD_DIM)

    def attend_sequence(member):
        seq_query, seq_keys, seq_values, seq_segments, seq_context = member

        def attend_block(portion):
            block_query, block_segments = portion
            scores = masked_scores(
                block_query, seq_keys, block_segments, seq_segments, seq_context, factor
            )
            row_top = jnp.max(scores, axis=-1, keepdims=True)
            exponent = jnp.exp(scores - row_top)
            row_total = jnp.sum(exponent, axis=-1, keepdims=True)
            soft_weights = (exponent / row_total).astype(jnp.bfloat16)
            block_mix = jnp.einsum(
                "hqk,khd->qhd", soft_weights, seq_values, preferred_element_type=jnp.float32
            )
            return (block_mix.astype(jnp.bfloat16), row_top + jnp.log(row_total))

        return lax.map(
            attend_block,
            (
                seq_query.reshape(blocks, block, head_count, HEAD_DIM),
                seq_segments.reshape(blocks, block),
            ),
        )

    mixture, log_totals = lax.map(
        attend_sequence,
        (
            per_sequence(queries),
            per_sequence(key_rows),
            per_sequence(value_rows),
            segment_ids,
            context_flags,
        ),
    )
    mixture = mixture.reshape(row_count, local_cols)
    partial_out = jnp.dot(mixture, out_weight, preferred_element_type=jnp.float32)
    grad_rows_all = cotangent.reshape(row_count, width)
    grad_float_all = grad_rows_all.astype(jnp.float32)
    grad_down_bias = jnp.sum(grad_float_all, axis=0)
    attended = lax.psum(partial_out, "head") + out_bias.astype(jnp.float32)
    middle_state = flat_in + attended
    normed_two_f, norm_two_pull = jax.vjp(layer_norm, middle_state, gain_two, offset_two)
    normed_two = normed_two_f.astype(jnp.bfloat16)
    up_part, down_part, up_shift = (
        lax.all_gather(up_weight, "head", axis=1, tiled=True),
        lax.all_gather(down_weight, "head", axis=0, tiled=True),
        lax.all_gather(up_bias, "head", axis=0, tiled=True),
    )
    up_full, down_full = (
        lax.all_gather(up_part, "seq", axis=0, tiled=True),
        lax.all_gather(down_part, "seq", axis=1, tiled=True),
    )
    before = jnp.dot(normed_two, up_full, preferred_element_type=jnp.float32) + up_shift.astype(
        jnp.float32
    )
    active_f, gelu_pull = jax.vjp(gelu_exact, before)
    active = active_f.astype(jnp.bfloat16)
    branch_out = jnp.dot(active, down_full, preferred_element_type=jnp.float32)
    final_rows = (middle_state + branch_out + down_bias.astype(jnp.float32)).astype(jnp.bfloat16)
    output = final_rows.reshape(tokens.shape)
    grad_float = grad_rows_all.astype(jnp.float32)
    grad_down = dot_cols(active, grad_rows_all)
    grad_active = dot_rows(grad_rows_all, down_full)
    (grad_before_f,) = gelu_pull(grad_active)
    grad_before = grad_before_f.astype(jnp.bfloat16)
    grad_up = dot_cols(normed_two, grad_before)
    grad_up_bias = jnp.sum(grad_before.astype(jnp.float32), axis=0)
    grad_normed_two = dot_rows(grad_before, up_full)
    grad_middle_norm, grad_gain_two, grad_offset_two = norm_two_pull(grad_normed_two)
    grad_middle = grad_float + grad_middle_norm
    ff_part = up_weight.shape[1]
    start_col = lax.axis_index("head") * ff_part
    grad_up = lax.dynamic_slice_in_dim(grad_up, start_col, ff_part, 1)
    grad_down = lax.dynamic_slice_in_dim(grad_down, start_col, ff_part, 0)
    grad_up_bias = lax.dynamic_slice_in_dim(grad_up_bias, start_col, ff_part, 0)
    grad_attended = grad_middle.astype(jnp.bfloat16)
    grad_out_bias = jnp.sum(grad_attended.astype(jnp.float32), axis=0)
    grad_out = dot_cols(mixture, grad_attended)
    grad_mixture = dot_rows(grad_attended, out_weight).astype(jnp.bfloat16)

    def back_sequence(member):
        seq_query, seq_keys, seq_values, seq_grad, seq_logs, seq_segments, seq_context = member

        def back_block(carry, portion):
            key_acc, value_acc = carry
            block_query, block_grad, block_logs, block_segments = portion
            scores = masked_scores(
                block_query, seq_keys, block_segments, seq_segments, seq_context, factor
            )
            soft_weights = jnp.exp(scores - block_logs)
            value_acc = value_acc + jnp.einsum(
                "hqk,qhd->khd",
                soft_weights.astype(jnp.bfloat16),
                block_grad,
                preferred_element_type=jnp.float32,
            )
            grad_soft = jnp.einsum(
                "qhd,khd->hqk", block_grad, seq_values, preferred_element_type=jnp.float32
            )
            row_inner = jnp.sum(soft_weights * grad_soft, axis=-1, keepdims=True)
            grad_scores = (soft_weights * (grad_soft - row_inner)).astype(jnp.bfloat16)
            grad_query = (
                jnp.einsum(
                    "hqk,khd->qhd", grad_scores, seq_keys, preferred_element_type=jnp.float32
                )
                * factor
            )
            key_acc = (
                key_acc
                + jnp.einsum(
                    "hqk,qhd->khd", grad_scores, block_query, preferred_element_type=jnp.float32
                )
                * factor
            )
            return ((key_acc, value_acc), grad_query)

        empty = jnp.zeros((length, head_count, HEAD_DIM), jnp.float32)
        (key_acc, value_acc), grad_query = lax.scan(
            back_block,
            (empty, empty),
            (
                seq_query.reshape(blocks, block, head_count, HEAD_DIM),
                seq_grad.reshape(blocks, block, head_count, HEAD_DIM),
                seq_logs,
                seq_segments.reshape(blocks, block),
            ),
        )
        return (grad_query, key_acc, value_acc)

    grad_queries, grad_keys, grad_values = lax.map(
        back_sequence,
        (
            per_sequence(queries),
            per_sequence(key_rows),
            per_sequence(value_rows),
            per_sequence(grad_mixture),
            log_totals,
            segment_ids,
            context_flags,
        ),
    )
    grad_queries = grad_queries.reshape(row_count, local_cols).astype(jnp.bfloat16)
    grad_keys = grad_keys.reshape(row_count, local_cols).astype(jnp.bfloat16)
    grad_values = grad_values.reshape(row_count, local_cols).astype(jnp.bfloat16)
    grad_qv_bias = jnp.stack(
        [
            jnp.sum(grad_queries.astype(jnp.float32), axis=0),
            jnp.sum(grad_values.astype(jnp.float32), axis=0),
        ]
    )
    grad_qkv = jnp.stack(
        [dot_cols(normed, grad_queries), dot_cols(normed, grad_keys), dot_cols(normed, grad_values)]
    )
    grad_normed = (
        dot_rows(grad_queries, qkv_weight[0])
        + dot_rows(grad_keys, qkv_weight[1])
        + dot_rows(grad_values, qkv_weight[2])
    )
    grad_normed = lax.psum(grad_normed, "head")
    grad_input_norm, grad_gain_one, grad_offset_one = norm_one_pull(grad_normed)
    tokens_grad = (grad_middle + grad_input_norm).astype(jnp.bfloat16).reshape(tokens.shape)
    summed_qkv, summed_out, summed_up, summed_down = (
        lax.psum_scatter(
            grad_qkv.astype(jnp.bfloat16), "seq", scatter_dimension=1, tiled=True
        ).astype(jnp.float32),
        lax.psum_scatter(
            grad_out.astype(jnp.bfloat16), "seq", scatter_dimension=1, tiled=True
        ).astype(jnp.float32),
        lax.psum_scatter(
            grad_up.astype(jnp.bfloat16), "seq", scatter_dimension=0, tiled=True
        ).astype(jnp.float32),
        lax.psum_scatter(
            grad_down.astype(jnp.bfloat16), "seq", scatter_dimension=1, tiled=True
        ).astype(jnp.float32),
    )
    smalls = lax.psum(
        (
            grad_gain_one,
            grad_offset_one,
            grad_qv_bias,
            grad_out_bias,
            grad_gain_two,
            grad_offset_two,
            grad_up_bias,
            grad_down_bias,
        ),
        "seq",
    )
    return (
        output,
        tokens_grad,
        smalls[0],
        smalls[1],
        summed_qkv,
        smalls[2],
        summed_out,
        smalls[3],
        smalls[4],
        smalls[5],
        summed_up,
        smalls[6],
        summed_down,
        smalls[7],
    )


MESH = pl.DeviceIdType.MESH
BF = jnp.bfloat16
F32 = jnp.float32
BLOCK = 256
STRIP = 512
PIECE = 128
WIDE = 1024
GROUP = 2
CHUNK = 512
PAIR = 2 * HEAD_DIM
Z_SIZE, Y_SIZE, CORES = 4, 2, 2
SEQ_SIZE = Z_SIZE * Y_SIZE * CORES
HOP = Y_SIZE * CORES
TABLES = 8
FAR = -1e30
VMEM_LIMIT = 62 * 2**20
INV_ROOT_TWO = 0.7071067811865476
INV_ROOT_TWO_PI = 0.3989422804014327
LN1_GAIN, LN1_BIAS, QV_BIAS, OUT_BIAS, LN2_GAIN, LN2_BIAS, UP_BIAS, DOWN_BIAS = 0, 1, 2, 3, 4, 5, 6, 8
SMALL_ROWS = 16
VMEM_SPEC = pl.BlockSpec(memory_space=pltpu.VMEM)
ANY_SPEC = pl.BlockSpec(memory_space=pl.ANY)


def shape_of(dims, dtype):
    return jax.ShapeDtypeStruct(tuple(dims), dtype)


def nn(left, right):
    return jnp.dot(left, right, preferred_element_type=F32)


def split_sum(left, right):
    parts = [
        nn(left[:, n:n + BLOCK], right[n:n + BLOCK]) for n in range(0, left.shape[1], BLOCK)
    ]
    while len(parts) > 1:
        parts = [a + b for a, b in zip(parts[::2], parts[1::2])]
    return parts[0]


def turn(block):
    return jnp.transpose(block)


def sum_rows(block):
    return jnp.sum(block, axis=0, keepdims=True)


def place():
    me = lax.axis_index("seq")
    head = lax.axis_index("head")
    core = me % 2
    y = (me // 2) % 2
    across = {"seq": me, "head": 1 - head}
    core_mate = {"seq": me + 1 - 2 * core, "head": head}
    y_mate = {"seq": me + 2 - 4 * y, "head": head}
    z_mates = [{"seq": (me + HOP * d) % SEQ_SIZE, "head": head} for d in (1, 2, 3)]
    return me, head, core, y, across, core_mate, y_mate, z_mates


def greet(others):
    barrier = pltpu.get_barrier_semaphore()
    for other in others:
        pl.semaphore_signal(barrier, inc=1, device_id=other, device_id_type=MESH)
    pl.semaphore_wait(barrier, len(others))


def remote(src, dst, send_sem, recv_sem, other):
    return pltpu.make_async_remote_copy(
        src_ref=src, dst_ref=dst, send_sem=send_sem, recv_sem=recv_sem,
        device_id=other, device_id_type=MESH,
    )


def norm_stats(rows):
    middle = jnp.mean(rows, axis=-1, keepdims=True)
    centred = rows - middle
    spread = jnp.mean(centred * centred, axis=-1, keepdims=True)
    return centred, lax.rsqrt(spread + 1e-05)


def norm_back(inner, unit, scale):
    return scale * (
        inner
        - jnp.mean(inner, axis=-1, keepdims=True)
        - unit * jnp.mean(inner * unit, axis=-1, keepdims=True)
    )


def as_row(vector):
    return vector[...].astype(F32).reshape(1, -1)


def lanes():
    return lax.broadcasted_iota(jnp.int32, (1, PAIR), 1)


def in_pieces(column, first, rest):
    high = column.astype(BF).astype(F32)
    mid = (column - high).astype(BF).astype(F32)
    low = column - high - mid
    at = lanes()
    return jnp.where(
        at == first, high, jnp.where(at == first + 1, mid, jnp.where(at == first + 2, low, rest))
    ).astype(BF)


def one_lanes(length):
    return jnp.broadcast_to(jnp.where(lanes() < 3, 1.0, 0.0).astype(BF), (length, PAIR))


def fwd_kernel(
    x_ref, seg_ref, context, gain, offset, qv_bias, out_bias,
    wqkv, wout, up_shard, down_shard,
    q_out, k_out, v_out, mix_out, mid_out, normed_out, wff_out, key_out, query_out,
    wff, q_ref, k_ref, v_ref, mix_ref, mid_ref, normed_t, key_more, query_more,
    mask_more, wout_all, mix_x,
    zs, zr, ys, yr, cs, cr, xs, xr, local, outs,
):
    length, width = x_ref.shape
    blocks = length // BLOCK
    pairs = q_ref.shape[0]
    cols = pairs * PAIR
    me, head, core, y, across, core_mate, y_mate, _ = place()
    z = me // HOP
    above = {"seq": (me + HOP) % SEQ_SIZE, "head": head}
    below = {"seq": (me + SEQ_SIZE - HOP) % SEQ_SIZE, "head": head}
    own = [
        pltpu.make_async_copy(shard, wff.at[u, me], local.at[u])
        for u, shard in enumerate((up_shard, down_shard))
    ]
    own[0].start()
    own[1].start()
    greet([across, core_mate, y_mate, above, below])

    half = wout.shape[0] // 2
    here = pl.ds(pl.multiple_of(core * half, half), half)
    beside = pl.ds(pl.multiple_of((1 - core) * half, half), half)
    wout_x = wout_all.at[1 - head]
    out_copy = remote(
        wout.at[here, :], wout_all.at[head, here, :], xs.at[0], xr.at[0], across
    )
    wout_all[head] = wout[...]
    out_pass = remote(wout_x.at[here, :], wout_x.at[here, :], cs.at[28], cr.at[28], core_mate)
    out_arrival = remote(
        wout_x.at[beside, :], wout_x.at[beside, :], cs.at[28], cr.at[28], core_mate
    )
    out_copy.start()

    flows = [(0, 0)] + [(way, s) for s in (1, 2, 3) for way in (0, 1)]

    def there(way, s):
        return (z >= s) if way == 0 else (z + s < Z_SIZE)

    def source(base, way, s):
        away = SEQ_SIZE - HOP * s if way == 0 else HOP * s
        return (base + away) % SEQ_SIZE

    def z_copy(u, way, s):
        n = (u * 2 + way) * 3 + s - 1
        j = source(me, way, s - 1)
        return remote(wff.at[u, j], wff.at[u, j], zs.at[n], zr.at[n], above if way == 0 else below)

    def z_arrival(u, way, s):
        n = (u * 2 + way) * 3 + s - 1
        slot = wff.at[u, source(me, way, s)]
        return remote(slot, slot, zs.at[n], zr.at[n], above)

    def z_goes_on(way):
        return (z < Z_SIZE - 1) if way == 0 else (z > 0)

    def y_copy(u, f):
        n = u * 7 + f
        j = source(me, *flows[f])
        return remote(wff.at[u, j], wff.at[u, j], ys.at[n], yr.at[n], y_mate)

    def y_arrival(u, f):
        n = u * 7 + f
        slot = wff.at[u, source(me + 2 - 4 * y, *flows[f])]
        return remote(slot, slot, ys.at[n], yr.at[n], y_mate)

    def c_copy(u, f, from_y):
        n = (u * 2 + from_y) * 7 + f
        j = source(me + from_y * (2 - 4 * y), *flows[f])
        return remote(wff.at[u, j], wff.at[u, j], cs.at[n], cr.at[n], core_mate)

    def c_arrival(u, f, from_y):
        n = (u * 2 + from_y) * 7 + f
        slot = wff.at[u, source(me + 1 - 2 * core + from_y * (2 - 4 * y), *flows[f])]
        return remote(slot, slot, cs.at[n], cr.at[n], core_mate)

    def for_flow(f, do):
        if f == 0:
            do()
        else:
            pl.when(there(*flows[f]))(do)

    def for_step(s, do):
        for f, (way, step) in enumerate(flows):
            if step == s:
                for_flow(f, lambda f=f, way=way: do(f, way))

    def z_event(u, s):
        def one(f, way):
            z_arrival(u, way, s).wait_recv()
            if s < 3:
                pl.when(z_goes_on(way))(lambda: z_copy(u, way, s + 1).start())
            y_copy(u, f).start()
            c_copy(u, f, 0).start()
        for_step(s, one)
        if u == 0 and s == 1:
            start_z(1)
        if u == 0 and s == 2:
            y_copy(1, 0).start()
            c_copy(1, 0, 0).start()
        if u == 0 and s == 3:
            out_copy.wait_recv()
            out_pass.start()

    def y_event(u, s):
        def one(f, way):
            y_arrival(u, f).wait_recv()
            c_copy(u, f, 1).start()
        for_step(s, one)

    def start_z(u):
        for way in (0, 1):
            pl.when(z_goes_on(way))(lambda way=way: z_copy(u, way, 1).start())

    own[0].wait()
    start_z(0)
    y_copy(0, 0).start()
    c_copy(0, 0, 0).start()
    own[1].wait()

    plan = {
        2: [(z_event, 0, 1), (y_event, 0, 0)], 4: [(z_event, 0, 2)], 5: [(y_event, 0, 1)],
        6: [(z_event, 0, 3)], 7: [(z_event, 1, 1)], 8: [(y_event, 0, 2), (y_event, 1, 0)],
        9: [(z_event, 1, 2)], 10: [(y_event, 0, 3)], 11: [(z_event, 1, 3)],
    }

    def tick(t):
        for step, events in plan.items():
            @pl.when(t == step)
            def _(events=events):
                for event, u, s in events:
                    event(u, s)

    at = lax.broadcasted_iota(jnp.int32, (PAIR, length), 0)
    same = at == seg_ref[...]
    hidden = context[...] != 1
    ones = jnp.logical_and(at > TABLES, at < TABLES + 4)
    key_side = jnp.logical_or(
        jnp.logical_and(at < TABLES, same),
        jnp.logical_or(jnp.logical_and(at == TABLES, hidden), ones),
    )
    query_side = jnp.logical_and(at <= TABLES, jnp.logical_not(same))
    key_more[...] = turn(jnp.where(key_side, 1.0, 0.0)).astype(BF)
    mask_more[...] = turn(jnp.where(query_side, FAR, 0.0)).astype(BF)

    keep = [
        pltpu.make_async_copy(here, there, outs.at[n])
        for n, (here, there) in enumerate(
            (
                (q_ref, q_out), (k_ref, k_out), (v_ref, v_out), (normed_t, normed_out),
                (key_more, key_out), (query_more, query_out), (mix_ref, mix_out),
            )
        )
    ]
    gains, offsets = as_row(gain), as_row(offset)
    query_bias = qv_bias[0:1, :].astype(F32)
    value_bias = qv_bias[1:2, :].astype(F32)

    def project(b, _):
        rows = pl.ds(pl.multiple_of(b * BLOCK, BLOCK), BLOCK)
        centred, scale = norm_stats(x_ref[rows, :].astype(F32))
        block = (centred * scale * gains + offsets).astype(BF)
        normed_t[:, rows] = turn(block)
        queries = ((nn(block, wqkv[0]) + query_bias).astype(BF) * 0.125).astype(BF)
        keys = nn(block, wqkv[1]).astype(BF)
        values = (nn(block, wqkv[2]) + value_bias).astype(BF)
        for p in range(pairs):
            part = slice(p * PAIR, (p + 1) * PAIR)
            q_ref[p, rows, :] = queries[:, part]
            k_ref[p, rows, :] = keys[:, part]
            v_ref[p, rows, :] = values[:, part]
        tick(b)
        return 0

    lax.fori_loop(0, blocks, project, 0)
    for n in range(5):
        keep[n].start()

    low_lanes = lanes() < HEAD_DIM
    zero = jnp.zeros((1, PAIR), BF)

    def mixture_copy(t):
        rows = pl.ds(pl.multiple_of(t // pairs * STRIP, STRIP), STRIP)
        return remote(
            mix_ref.at[t % pairs, rows, :], mix_x.at[t % pairs, rows, :], xs.at[1 + t],
            xr.at[1 + t], across,
        )

    per_step = STRIP // BLOCK

    def attend(t, _):
        b, p = t // pairs, t % pairs
        keys = jnp.concatenate([k_ref[p], key_more[...]], axis=1)
        values = jnp.concatenate([v_ref[p], one_lanes(length)], axis=1)
        chains = []
        for n in range(per_step):
            rows = pl.ds(pl.multiple_of(b * STRIP + n * BLOCK, BLOCK), BLOCK)
            queries, more = q_ref[p, rows, :], mask_more[rows, :]
            for low in (0, 1):
                own_lanes = jnp.logical_not(low_lanes) if low else low_lanes
                left = jnp.concatenate([jnp.where(own_lanes, queries, zero), more], axis=1)
                chains.append((rows, low, more, dot_rows(left, keys)))
        parts = []
        for rows, low, more, scores in chains:
            top = jnp.max(scores, axis=-1, keepdims=True)
            mixed = nn(jnp.exp(scores - top).astype(BF), values)
            total = mixed[:, PAIR:PAIR + 1]
            parts.append(mixed[:, :PAIR] / total)
            query_more[2 * p + low, rows, :] = in_pieces(
                -(top + jnp.log(total)), TABLES + 1, more.astype(F32)
            )
            if low:
                mix_ref[p, rows, :] = jnp.where(low_lanes, *parts[-2:]).astype(BF)
        mixture_copy(t).start()
        tick(t + blocks)
        return 0

    lax.fori_loop(0, length // STRIP * pairs, attend, 0)
    keep[5].start()
    keep[6].start()
    out_arrival.wait_recv()
    out_row = as_row(out_bias)

    def mid_copy(b):
        rows = pl.ds(b * BLOCK, BLOCK)
        return pltpu.make_async_copy(mid_ref.at[rows, :], mid_out.at[rows, :], outs.at[7 + b])

    def arrive(u):
        for f in range(len(flows)):
            def one(f=f):
                for from_y in (0, 1):
                    c_arrival(u, f, from_y).wait_recv()
            for_flow(f, one)

    for b in range(blocks):
        if b % per_step == 0:
            for p in range(pairs):
                mixture_copy(b // per_step * pairs + p).wait_recv()
        rows = pl.ds(b * BLOCK, BLOCK)
        ours = jnp.concatenate([mix_ref[p, rows, :] for p in range(pairs)], axis=-1)
        other = jnp.concatenate([mix_x[p, rows, :] for p in range(pairs)], axis=-1)
        first, second = jnp.where(head == 0, ours, other), jnp.where(head == 0, other, ours)
        attended = nn(first, wout_all[0]) + nn(second, wout_all[1])
        mid_ref[rows, :] = x_ref[rows, :].astype(F32) + (attended + out_row)
        mid_copy(b).start()
        if b < 3:
            y_event(1, b + 1)
    wff_keep = [pltpu.make_async_copy(wff.at[u], wff_out.at[u], local.at[u]) for u in range(2)]
    arrive(0)
    wff_keep[0].start()
    arrive(1)
    wff_keep[1].start()
    out_copy.wait_send()
    out_pass.wait_send()
    for copy in keep + wff_keep:
        copy.wait()
    for t in range(length // STRIP * pairs):
        mixture_copy(t).wait_send()
    for b in range(blocks):
        mid_copy(b).wait()
    for u in range(2):
        for way in (0, 1):
            pl.when(z_goes_on(way))(lambda u=u, way=way: z_copy(u, way, 1).wait_send())
        for f, (way, s) in enumerate(flows):
            def finish(u=u, f=f, way=way, s=s):
                if f and s < 3:
                    pl.when(z_goes_on(way))(lambda: z_copy(u, way, s + 1).wait_send())
                y_copy(u, f).wait_send()
                for from_y in (0, 1):
                    c_copy(u, f, from_y).wait_send()
            for_flow(f, finish)


def run_fwd(x, seg, context, gain, offset, qv_bias, out_bias, wqkv, wout, up_weight, down_t):
    length, width = x.shape
    pairs = wqkv.shape[2] // PAIR
    blocks = length // BLOCK
    depth, hidden = up_weight.shape
    by_pair, by_head = (pairs, length, PAIR), (2 * pairs, length, PAIR)
    turned = (width, length)
    steps = length // STRIP * pairs
    dma = pltpu.SemaphoreType.DMA
    return pl.pallas_call(
        fwd_kernel,
        out_shape=[shape_of(by_pair, BF)] * 4 + [
            shape_of((length, width), F32),
            shape_of(turned, BF),
            shape_of((2, SEQ_SIZE, depth, hidden), BF),
            shape_of((length, PAIR), BF),
            shape_of(by_head, BF),
        ],
        in_specs=[VMEM_SPEC] * 9 + [ANY_SPEC] * 2,
        out_specs=[ANY_SPEC] * 9,
        scratch_shapes=[pltpu.VMEM((2, SEQ_SIZE, depth, hidden), BF)]
        + [pltpu.VMEM(by_pair, BF)] * 4 + [
            pltpu.VMEM((length, width), F32),
            pltpu.VMEM(turned, BF),
            pltpu.VMEM((length, PAIR), BF),
            pltpu.VMEM(by_head, BF),
            pltpu.VMEM((length, PAIR), BF),
            pltpu.VMEM((2,) + wout.shape, BF),
            pltpu.VMEM(by_pair, BF),
            dma((12,)), dma((12,)), dma((14,)), dma((14,)), dma((29,)), dma((29,)),
            dma((1 + steps,)), dma((1 + steps,)), dma((2,)), dma((7 + blocks,)),
        ],
        compiler_params=pltpu.CompilerParams(
            collective_id=0, has_side_effects=True, vmem_limit_bytes=VMEM_LIMIT
        ),
    )(x, seg, context, gain, offset, qv_bias, out_bias, wqkv, wout, up_weight, down_t)


def ff_kernel(
    mid_hbm, dy_hbm, wff_hbm, gain, offset, up_bias, wout_hbm,
    branch_out, branch_first, gmid_hbm, ga_out, gm_out, summed, small_ref,
    branch_x,    dy_ref, wff, wout, bias_row, branch_ref, ga_t, gm_ref, normed, normed_t, dy_t, active, before_grad, gnt_acc, gnt_own, gnt_x, whole, from_mate,
    held, ready,
    xs, xr, cs, cr, ls, ws, ss, ins, outs,
):
    length, width = dy_ref.shape
    blocks = length // PIECE
    hidden = wff.shape[3]
    half = hidden // WIDE
    chunks = 2 * hidden // CHUNK
    pairs = gm_ref.shape[0]
    me, head, core, y, across, core_mate, y_mate, z_mates = place()
    dy_load = pltpu.make_async_copy(dy_hbm, dy_ref, ins.at[0])
    wout_load = pltpu.make_async_copy(wout_hbm, wout, ins.at[1])

    def wff_load(n):
        cut = pl.ds(n * WIDE, WIDE)
        return pltpu.make_async_copy(
            wff_hbm.at[:, :, :, cut], wff.at[:, :, :, cut], ins.at[2 + n]
        )

    dy_load.start()
    for n in range(half):
        wff_load(n).start()
    wout_load.start()
    greet([across, core_mate])
    gains, offsets = as_row(gain), as_row(offset)
    bias_row[...] = as_row(up_bias)

    def weight(kind, n):
        cut = pl.ds(pl.multiple_of(n * WIDE, WIDE), WIDE)
        return wff[kind, :, :, cut].reshape(width, WIDE)

    small_ref[...] = jnp.zeros_like(small_ref)

    def load(n):
        rows = pl.ds(n % blocks * PIECE, PIECE)
        return pltpu.make_async_copy(mid_hbm.at[rows, :], held.at[n % 2], ls.at[n % 2])

    def store(b):
        rows = pl.ds(b * PIECE, PIECE)
        return pltpu.make_async_copy(ready.at[b % 2], gmid_hbm.at[rows, :], ws.at[b % 2])

    load(0).start()
    load(1).start()

    def gnt_copy(b):
        return remote(gnt_own.at[b], gnt_x.at[b], xs.at[b], xr.at[b], across)

    def core_copy(n):
        return remote(
            whole.at[n, :, :, 1 - core], from_mate.at[n], cs.at[n], cr.at[n], core_mate
        )

    def forward(t, _):
        b, n = t // half, t % half
        rows = pl.ds(pl.multiple_of(b * PIECE, PIECE), PIECE)

        for b_next in range(blocks):
            @pl.when(t == b_next * half)
            def _(b_next=b_next):
                load(b_next).wait()
                if b_next == 0:
                    dy_load.wait()

        for n_first in range(half):
            @pl.when(t == n_first)
            def _(n_first=n_first):
                wff_load(n_first).wait()

        @pl.when(n == 0)
        def _():
            centred, scale = norm_stats(held[b % 2])
            block = (centred * scale * gains + offsets).astype(BF)
            normed[...] = block
            normed_t[:, rows] = turn(block)
            dy_t[:, rows] = turn(dy_ref[rows, :])
            small_ref[DOWN_BIAS:DOWN_BIAS + 1, :] += sum_rows(dy_ref[rows, :].astype(F32))

        up = weight(0, n)
        cut = pl.ds(pl.multiple_of(n * WIDE, WIDE), WIDE)
        before = nn(normed[...], up) + bias_row[:, cut]
        spread = 0.5 * (1.0 + lax.erf(before * INV_ROOT_TWO))
        active[n, rows, :] = (before * spread).astype(BF)
        slope = spread + before * (INV_ROOT_TWO_PI * jnp.exp(before * before * -0.5))
        grad = (nn(dy_ref[rows, :], weight(1, n)) * slope).astype(BF)
        before_grad[n, rows, :] = grad
        small_ref[pl.ds(UP_BIAS + n, 1), :] += sum_rows(grad.astype(F32))
        back = dot_rows(grad, up)

        @pl.when(n == 0)
        def _():
            gnt_acc[...] = back

        @pl.when(n > 0)
        def _():
            gnt_acc[...] += back

        for b_done in range(blocks):
            @pl.when(t == (b_done + 1) * half - 1)
            def _(b_done=b_done):
                load(b_done + 2).start()
                gnt_own[b_done] = gnt_acc[...].astype(BF)
                gnt_copy(b_done).start()
        return 0

    lax.fori_loop(0, blocks * half, forward, 0)

    def weight_grads(left_t, right, first):
        cut_rows = width // Z_SIZE
        per_wide = WIDE // CHUNK

        def one(t, _):
            n, plane = t // Z_SIZE, t % Z_SIZE
            cut = pl.ds(pl.multiple_of(plane * cut_rows, cut_rows), cut_rows)
            total = nn(left_t[cut, :], right[n]).astype(BF)
            for m in range(per_wide):
                piece = total[:, m * CHUNK:(m + 1) * CHUNK]
                whole[first + n * per_wide + m, plane] = piece.reshape(whole.shape[2:])

            @pl.when(plane == Z_SIZE - 1)
            def _():
                for m in range(per_wide):
                    core_copy(first + n * per_wide + m).start()

            return 0

        lax.fori_loop(0, Z_SIZE * half, one, 0)

    weight_grads(dy_t, active, chunks // 2)
    weight_grads(normed_t, before_grad, 0)

    def branch(b, _):
        rows = pl.ds(pl.multiple_of(b * BLOCK, BLOCK), BLOCK)
        total = dot_rows(active[0, rows, :], weight(1, 0))
        for n in range(1, half):
            total += dot_rows(active[n, rows, :], weight(1, n))
        branch_ref[rows, :] = total.astype(BF)
        return 0

    lax.fori_loop(0, length // BLOCK, branch, 0)
    first_rows = remote(
        branch_ref.at[0:BLOCK, :], branch_x, xs.at[blocks], xr.at[blocks], across
    )
    first_rows.start()
    branch_keep = pltpu.make_async_copy(branch_ref, branch_out, outs.at[0])
    branch_keep.start()
    wout_load.wait()

    def ga_copy(b):
        rows = pl.ds(b * PIECE, PIECE)
        return pltpu.make_async_copy(ga_t.at[:, rows], ga_out.at[:, rows], outs.at[1 + b])

    def gm_copy(b):
        rows = pl.ds(b * PIECE, PIECE)
        return pltpu.make_async_copy(
            gm_ref.at[:, rows, :], gm_out.at[:, rows, :], outs.at[1 + blocks + b]
        )


    def add_mate(n, _):
        core_copy(n).wait()
        both = whole[n, :, :, core].astype(F32) + from_mate[n].astype(F32)
        from_mate[n] = both.astype(BF)
        return 0

    lax.fori_loop(chunks // 2, chunks, add_mate, 0)
    lax.fori_loop(0, chunks // 2, add_mate, 0)
    keep = pltpu.make_async_copy(from_mate, summed, ss.at[0])
    keep.start()

    def through_norm(b):
        rows = pl.ds(b * PIECE, PIECE)
        grad = gnt_own[b].astype(F32) + gnt_x[b].astype(F32)
        centred, scale = norm_stats(held[b % 2])
        unit = centred * scale
        small_ref[LN2_GAIN:LN2_GAIN + 1, :] += sum_rows(grad * unit)
        small_ref[LN2_BIAS:LN2_BIAS + 1, :] += sum_rows(grad)
        total = dy_ref[rows, :].astype(F32) + norm_back(grad * gains, unit, scale)
        ready[b % 2] = total
        low = total.astype(BF)
        small_ref[OUT_BIAS:OUT_BIAS + 1, :] += sum_rows(low.astype(F32))
        ga_t[:, rows] = turn(low)
        mixed = dot_rows(low, wout[...]).astype(BF)
        for p in range(pairs):
            gm_ref[p, rows, :] = mixed[:, p * PAIR:(p + 1) * PAIR]

    for b in range(blocks):
        gnt_copy(b).wait()
        load(blocks + b).wait()
        if b >= 2:
            store(b - 2).wait()
        through_norm(b)
        store(b).start()
        ga_copy(b).start()
        gm_copy(b).start()
        if b + 2 < blocks:
            load(blocks + b + 2).start()
    store(blocks - 2).wait()
    store(blocks - 1).wait()
    for b in range(blocks):
        ga_copy(b).wait()
        gm_copy(b).wait()
    first_rows.wait()
    first_keep = pltpu.make_async_copy(branch_x, branch_first, outs.at[1 + 2 * blocks])
    first_keep.start()
    branch_keep.wait()
    keep.wait()
    first_keep.wait()


def run_ff(middle, dy, wff, gain, offset, up_bias, wout):
    length, width = middle.shape
    half = wff.shape[3] // WIDE
    chunks = 2 * wff.shape[3] // CHUNK
    blocks = length // PIECE
    pairs = wout.shape[0] // PAIR
    depth = width // SEQ_SIZE
    dma = pltpu.SemaphoreType.DMA
    rows = pltpu.VMEM((blocks, PIECE, width), BF)
    hidden = pltpu.VMEM((half, length, WIDE), BF)
    flat_t = pltpu.VMEM((width, length), BF)
    return pl.pallas_call(
        ff_kernel,
        out_shape=[
            shape_of((length, width), BF),
            shape_of((BLOCK, width), BF),
            shape_of((length, width), F32),
            shape_of((width, length), BF),
            shape_of((pairs, length, PAIR), BF),
            shape_of((chunks, Z_SIZE, Y_SIZE, depth, CHUNK), BF),
            shape_of((SMALL_ROWS, width), F32),
        ],
        in_specs=[ANY_SPEC] * 3 + [VMEM_SPEC] * 3 + [ANY_SPEC],
        out_specs=[ANY_SPEC] * 6 + [VMEM_SPEC],
        scratch_shapes=[
            pltpu.VMEM((BLOCK, width), BF),
            pltpu.VMEM((length, width), BF), pltpu.VMEM(wff.shape, BF),
            pltpu.VMEM(wout.shape, BF), pltpu.VMEM((1, half * WIDE), F32),
            pltpu.VMEM((length, width), BF), flat_t, pltpu.VMEM((pairs, length, PAIR), BF),
            pltpu.VMEM((PIECE, width), BF), flat_t, flat_t, hidden, hidden,
            pltpu.VMEM((PIECE, width), F32), rows, rows,
            pltpu.VMEM((chunks, Z_SIZE, Y_SIZE, CORES, depth, CHUNK), BF),
            pltpu.VMEM((chunks, Z_SIZE, Y_SIZE, depth, CHUNK), BF),
            pltpu.VMEM((2, PIECE, width), F32), pltpu.VMEM((2, PIECE, width), F32),
            dma((blocks + 1,)), dma((blocks + 1,)), dma((chunks,)), dma((chunks,)),
            dma((2,)), dma((2,)), dma((1,)), dma((2 + half,)), dma((2 + 2 * blocks,)),
        ],
        compiler_params=pltpu.CompilerParams(
            collective_id=1, has_side_effects=True, vmem_limit_bytes=VMEM_LIMIT
        ),
    )(middle, dy, wff, gain, offset, up_bias, wout)


def back_kernel(
    q_hbm, k_hbm, v_hbm, mix_hbm, gm_hbm, query_hbm, ga_hbm, normed_hbm, wqkv_hbm, x_hbm,
    key_more, gain, down_bias, small_in, mid_hbm, gmid_hbm, ff_part, branch, branch_first,
    out_hbm, tokens_hbm, qkv_sum, out_sum, up_sum, down_sum,
    gain_one, offset_one, qv_small, out_small, gain_two, offset_two, up_small, down_small,
    q_ref, k_ref, v_ref, mix_ref, gm_ref, query_more, ga_t, normed_t, wqkv, x_ref,
    out_ref, tokens_ref, key_t, key_acc, value_acc, dq, dk, dv, whole, mate, at_y, at_z, ff_y, ff_z, gn_own, gn_x,
    branch_x, branch_own, ff_own, held, small_own, small_z, small_y, small_c, small_x,
    bs, br, fys, fyr, fzs, fzr, acs, acr, ays, ayr, azs, azr, gs, gr, ls, ms, mr, os, hs, ins, more_ins, outs,
):
    length, width = x_ref.shape
    blocks = length // BLOCK
    strips = length // STRIP
    pairs = q_ref.shape[0]
    chunks = ff_part.shape[0]
    half = chunks // 2
    groups = chunks // GROUP
    me, head, core, y, across, core_mate, y_mate, z_mates = place()
    z = me // (Y_SIZE * CORES)
    by_pair = (
        (q_hbm, q_ref), (k_hbm, k_ref), (v_hbm, v_ref), (mix_hbm, mix_ref), (gm_hbm, gm_ref),
    )

    def pair_loads(p):
        both = pl.ds(2 * p, 2)
        first = p * (len(by_pair) + 1)
        return [
            pltpu.make_async_copy(src.at[p], dst.at[p], ins.at[first + n])
            for n, (src, dst) in enumerate(by_pair)
        ] + [
            pltpu.make_async_copy(
                query_hbm.at[both], query_more.at[both], ins.at[first + len(by_pair)]
            )
        ]

    late_loads = [
        pltpu.make_async_copy(src, dst, more_ins.at[n])
        for n, (src, dst) in enumerate(
            ((ga_hbm, ga_t), (normed_hbm, normed_t), (wqkv_hbm, wqkv), (x_hbm, x_ref))
        )
    ]
    for p in range(pairs):
        for copy in pair_loads(p):
            copy.start()
        if p == 0:
            late_loads[0].start()
            late_loads[1].start()
    late_loads[2].start()
    late_loads[3].start()
    greet([across, core_mate, y_mate, *z_mates])

    def part(b):
        return pl.ds(b * BLOCK, BLOCK)

    first_load = pltpu.make_async_copy(branch_first, branch_x.at[part(0), :], br.at[0])

    def branch_copy(b):
        return remote(branch.at[part(b), :], branch_x.at[part(b), :], bs.at[b], br.at[b], across)

    def load(n):
        source = mid_hbm if n < blocks else gmid_hbm
        return pltpu.make_async_copy(
            source.at[part(n % blocks), :], held.at[n % 2], ls.at[n % 2]
        )

    def taken(n):
        if n + 2 < 2 * blocks:
            load(n + 2).start()

    def group(g):
        return pl.ds(g * GROUP, GROUP)

    def ff_y_copy(g):
        return remote(
            ff_part.at[group(g), :, 1 - y], ff_y.at[group(g)], fys.at[g], fyr.at[g], y_mate
        )

    def ff_z_copy(g, d):
        n = g * 3 + d - 1
        return remote(
            ff_y.at[group(g), (z + d) % Z_SIZE], ff_z.at[d - 1, group(g)],
            fzs.at[n], fzr.at[n], z_mates[d - 1],
        )

    def branch_load(b):
        return pltpu.make_async_copy(branch.at[part(b), :], branch_own.at[b % 2], hs.at[b % 2])

    def ff_load(g):
        return pltpu.make_async_copy(
            ff_part.at[group(g), :, y], ff_own.at[g % 2], os.at[g % 2]
        )

    def ff_y_event(g):
        ff_y_copy(g).wait_recv()
        ff_load(g).wait()
        for n in range(g * GROUP, (g + 1) * GROUP):
            own = ff_own[g % 2, n % GROUP]
            ff_y[n] = (ff_y[n].astype(F32) + own.astype(F32)).astype(BF)
        if g + 2 < groups:
            ff_load(g + 2).start()
            ff_y_copy(g + 2).start()
        for d in (1, 2, 3):
            ff_z_copy(g, d).start()

    def ff_z_event(g):
        for d in (1, 2, 3):
            ff_z_copy(g, d).wait_recv()
        for n in range(g * GROUP, (g + 1) * GROUP):
            total = ff_y[n, z].astype(F32)
            for d in (1, 2, 3):
                total += ff_z[d - 1, n].astype(F32)
            if n < half:
                up_sum[:, n * CHUNK:(n + 1) * CHUNK] = total
            else:
                down_sum[:, (n - half) * CHUNK:(n - half + 1) * CHUNK] = total

    def at_c_copy(p):
        return remote(whole.at[p, :, :, 1 - core], mate.at[p], acs.at[p], acr.at[p], core_mate)

    def at_y_copy(p):
        return remote(mate.at[p, :, 1 - y], at_y.at[p], ays.at[p], ayr.at[p], y_mate)

    def at_z_copy(p, d):
        n = p * 3 + d - 1
        return remote(
            at_y.at[p, (z + d) % Z_SIZE], at_z.at[d - 1, p], azs.at[n], azr.at[n], z_mates[d - 1]
        )

    def at_c_event(p):
        at_c_copy(p).wait_recv()
        mate[p] = (mate[p].astype(F32) + whole[p, :, :, core].astype(F32)).astype(BF)
        at_y_copy(p).start()

    def at_y_event(p):
        at_y_copy(p).wait_recv()
        at_y[p] = (at_y[p].astype(F32) + mate[p, :, y].astype(F32)).astype(BF)
        for d in (1, 2, 3):
            at_z_copy(p, d).start()

    def at_z_event(p):
        for d in (1, 2, 3):
            at_z_copy(p, d).wait_recv()
        total = at_y[p, z].astype(F32)
        for d in (1, 2, 3):
            total += at_z[d - 1, p].astype(F32)
        cut = slice(p * PAIR, (p + 1) * PAIR)
        for kind in range(3):
            qkv_sum[kind, :, cut] = total[:, kind * PAIR:(kind + 1) * PAIR]
        out_sum[:, cut] = total[:, 3 * PAIR:]

    def out_copy(b):
        return pltpu.make_async_copy(out_ref.at[part(b), :], out_hbm.at[part(b), :], outs.at[b])

    def tokens_copy(b):
        return pltpu.make_async_copy(
            tokens_ref.at[part(b), :], tokens_hbm.at[part(b), :], outs.at[blocks + b]
        )

    def branch_event(b):
        if b == 0:
            first_load.wait()
        else:
            branch_copy(b).wait_recv()
        load(b).wait()
        branch_load(b).wait()
        both = branch_own[b % 2].astype(F32) + branch_x[part(b), :].astype(F32)
        out_ref[part(b), :] = (held[b % 2] + both + as_row(down_bias)).astype(BF)
        out_copy(b).start()
        taken(b)
        if b + 2 < blocks:
            branch_load(b + 2).start()

    first_load.start()
    for b in range(1, blocks):
        branch_copy(b).start()
    for n in range(2):
        load(n).start()
        branch_load(n).start()
        ff_load(n).start()
        ff_y_copy(n).start()

    plan = {
        2: [(at_c_event, 0), (ff_y_event, 0), (branch_event, 0)], 4: [(at_c_event, 1)],
        5: [(ff_y_event, 1), (branch_event, 1)], 6: [(at_c_event, 2)],
    }

    low_lanes = lanes() < HEAD_DIM
    zero = jnp.zeros((1, PAIR), BF)

    def stacked(strip):
        return jnp.concatenate(
            [jnp.where(low_lanes, strip, zero), jnp.where(low_lanes, zero, strip)], axis=0
        )

    def attend(t, _):
        p, b = t // strips, t % strips
        rows = pl.ds(pl.multiple_of(b * STRIP, STRIP), STRIP)

        @pl.when(b == 0)
        def _():
            for p_now in range(pairs):
                @pl.when(p == p_now)
                def _(p_now=p_now):
                    for copy in pair_loads(p_now):
                        copy.wait()
            key_t[...] = turn(k_ref[p])
            key_acc[...] = jnp.zeros_like(key_acc)
            value_acc[...] = jnp.zeros_like(value_acc)

        queries, grads = stacked(q_ref[p, rows, :]), stacked(gm_ref[p, rows, :])
        more = jnp.concatenate(
            [query_more[2 * p, rows, :], query_more[2 * p + 1, rows, :]], axis=0
        )
        mixture = mix_ref[p, rows, :]
        product = grads.astype(F32) * jnp.concatenate([mixture, mixture], axis=0).astype(F32)
        inner = -jnp.sum(product, axis=-1, keepdims=True)
        query_side = jnp.concatenate([queries, more], axis=1)
        grad_side = jnp.concatenate([grads, in_pieces(inner, 0, 0.0)], axis=1)
        to_queries = jnp.zeros((PAIR, 2 * STRIP), F32)
        for n in range(strips):
            cut = pl.ds(n * STRIP, STRIP)
            keys = jnp.concatenate([k_ref[p, cut, :], key_more[cut, :]], axis=1)
            values = jnp.concatenate([v_ref[p, cut, :], one_lanes(STRIP)], axis=1)
            weights = jnp.exp(dot_rows(keys, query_side)).astype(BF)
            grad_scores = weights * dot_rows(values, grad_side).astype(BF)
            value_acc[cut, :] += split_sum(weights, grads)
            key_acc[cut, :] += split_sum(grad_scores, queries)
            to_queries += nn(key_t[:, cut], grad_scores)
        own = jnp.concatenate(
            [to_queries[:HEAD_DIM, :STRIP], to_queries[HEAD_DIM:, STRIP:]], axis=0
        )
        dq[p, rows, :] = (turn(own) * 0.125).astype(BF)

        @pl.when(b == strips - 1)
        def _():
            @pl.when(p == 0)
            def _():
                late_loads[0].wait()
                late_loads[1].wait()

            dk[p] = key_acc[...].astype(BF)
            dv[p] = value_acc[...].astype(BF)
            right = jnp.concatenate([dq[p], dk[p], dv[p]], axis=1)
            mixture_all = mix_ref[p]

            def one(plane, _):
                cut = pl.ds(pl.multiple_of(plane * BLOCK, BLOCK), BLOCK)
                both = jnp.concatenate(
                    [nn(normed_t[cut, :], right), nn(ga_t[cut, :], mixture_all)], axis=1
                )
                whole[p, plane] = both.astype(BF).reshape(whole.shape[2:])
                return 0

            lax.fori_loop(0, Z_SIZE, one, 0)
            at_c_copy(p).start()

        for step, events in plan.items():
            @pl.when(t == step)
            def _(events=events):
                for event, n in events:
                    event(n)
        return 0

    lax.fori_loop(0, pairs * strips, attend, 0)
    late_loads[2].wait()
    late_loads[3].wait()

    def gn_copy(b):
        return remote(gn_own.at[b], gn_x.at[b], gs.at[b], gr.at[b], across)

    own_gain = jnp.zeros((1, width), F32)
    own_offset = jnp.zeros((1, width), F32)
    for b in range(blocks):
        total = jnp.zeros((BLOCK, width), F32)
        for n, grad in enumerate((dq, dk, dv)):
            left = jnp.concatenate([grad[p, part(b), :] for p in range(pairs)], axis=1)
            total += dot_rows(left, wqkv[n])
        gn_own[b] = total.astype(BF)
        gn_copy(b).start()
        centred, scale = norm_stats(x_ref[part(b), :].astype(F32))
        own_gain += sum_rows(total * (centred * scale))
        own_offset += sum_rows(total)

    at_c_event(3)
    small_own[...] = small_in[...]
    small_own[LN1_GAIN:LN1_GAIN + 1, :] = own_gain
    small_own[LN1_BIAS:LN1_BIAS + 1, :] = own_offset
    for p in range(pairs):
        first, second = p * PAIR, (pairs + p) * PAIR
        small_own[QV_BIAS:QV_BIAS + 1, first:first + PAIR] = sum_rows(dq[p].astype(F32))
        small_own[QV_BIAS:QV_BIAS + 1, second:second + PAIR] = sum_rows(dv[p].astype(F32))
    def small_z_copy(d):
        return remote(small_own, small_z.at[z], ms.at[d - 1], mr.at[d - 1], z_mates[d - 1])

    def small_z_arrival(d):
        slot = small_z.at[(z + Z_SIZE - d) % Z_SIZE]
        return remote(slot, slot, ms.at[d - 1], mr.at[d - 1], z_mates[d - 1])

    y_sum = remote(small_y.at[0], small_y.at[1], ms.at[3], mr.at[3], y_mate)
    c_sum = remote(small_c.at[0], small_c.at[1], ms.at[4], mr.at[4], core_mate)
    x_sum = remote(small_x.at[0], small_x.at[1], ms.at[5], mr.at[5], across)
    for d in (1, 2, 3):
        small_z_copy(d).start()
    small_z[z] = small_own[...]

    def small_y_step():
        for d in (1, 2, 3):
            small_z_arrival(d).wait_recv()
        small_y[0] = small_z[0] + small_z[1] + small_z[2] + small_z[3]
        y_sum.start()

    def small_c_step():
        y_sum.wait()
        small_c[0] = small_y[0] + small_y[1]
        c_sum.start()

    def small_x_step():
        c_sum.wait()
        small_x[0] = small_c[0, 0:8, :] + small_c[1, 0:8, :]
        x_sum.start()

    branch_event(2)
    ff_y_event(2)
    branch_event(3)
    ff_z_event(0)
    ff_y_event(3)
    at_y_event(0)
    ff_z_event(1)
    gains = as_row(gain)
    for b in range(blocks):
        gn_copy(b).wait()
        load(blocks + b).wait()
        grad = gn_own[b].astype(F32) + gn_x[b].astype(F32)
        centred, scale = norm_stats(x_ref[part(b), :].astype(F32))
        unit = centred * scale
        tokens_ref[part(b), :] = (
            held[b % 2] + norm_back(grad * gains, unit, scale)
        ).astype(BF)
        tokens_copy(b).start()
        taken(blocks + b)
        if b == 0:
            small_y_step()
            at_y_event(1)
            at_y_event(2)
            ff_z_event(2)
        if b == 1:
            small_c_step()
            at_y_event(3)
            ff_z_event(3)
        if b == 2:
            small_x_step()
            at_z_event(0)
            at_z_event(1)
            at_z_event(2)

    at_z_event(3)
    x_sum.wait()
    ln1 = small_x[0, 0:2, :] + small_x[1, 0:2, :]
    gain_one[...] = ln1[0:1, :].reshape(width)
    offset_one[...] = ln1[1:2, :].reshape(width)
    small = small_c[0] + small_c[1]
    for kind, target in (
        (OUT_BIAS, out_small), (LN2_GAIN, gain_two), (LN2_BIAS, offset_two), (DOWN_BIAS, down_small),
    ):
        target[...] = small[kind:kind + 1, :].reshape(width)
    cols = pairs * PAIR
    qv_small[0:1, :] = small[QV_BIAS:QV_BIAS + 1, :cols]
    qv_small[1:2, :] = small[QV_BIAS:QV_BIAS + 1, cols:]
    for n in range(up_small.shape[0] // width):
        row = small[UP_BIAS + n:UP_BIAS + n + 1, :]
        up_small[n * width:(n + 1) * width] = row.reshape(width)

    for d in (1, 2, 3):
        small_z_copy(d).wait_send()
    for b in range(blocks):
        out_copy(b).wait()
        tokens_copy(b).wait()
        if b > 0:
            branch_copy(b).wait_send()
    for g in range(groups):
        ff_y_copy(g).wait_send()
        for d in (1, 2, 3):
            ff_z_copy(g, d).wait_send()
    for p in range(pairs):
        at_c_copy(p).wait_send()
        at_y_copy(p).wait_send()
        for d in (1, 2, 3):
            at_z_copy(p, d).wait_send()


def run_back(
    queries, keys, values, mixture, grad_mixture, query_more, ga_t, normed_t, wqkv, x,
    key_more, gain, down_bias, small, middle, grad_middle, ff_part, branch,
    branch_first,
):
    length, width = x.shape
    pairs = queries.shape[0]
    chunks, depth = ff_part.shape[0], ff_part.shape[3]
    groups = chunks // GROUP
    cols, hidden = pairs * PAIR, chunks // 2 * CHUNK
    blocks = length // BLOCK
    dma = pltpu.SemaphoreType.DMA
    rows = pltpu.VMEM((blocks, BLOCK, width), BF)
    by_pair = pltpu.VMEM((pairs, length, PAIR), BF)
    whole_rows = pltpu.VMEM((length, width), BF)
    row = shape_of((width,), F32)
    loaded = (
        queries, keys, values, mixture, grad_mixture, query_more, ga_t, normed_t, wqkv, x
    )
    return pl.pallas_call(
        back_kernel,
        out_shape=[
            shape_of((length, width), BF),
            shape_of((length, width), BF),
            shape_of((3, depth, cols), F32),
            shape_of((depth, cols), F32),
            shape_of((depth, hidden), F32),
            shape_of((depth, hidden), F32),
            row, row, shape_of((2, cols), F32), row, row, row, shape_of((hidden,), F32), row,
        ],
        in_specs=[ANY_SPEC] * 10 + [VMEM_SPEC] * 4 + [ANY_SPEC] * 5,
        out_specs=[ANY_SPEC] * 2 + [VMEM_SPEC] * 12,
        scratch_shapes=[pltpu.VMEM(v.shape, BF) for v in loaded] + [
            whole_rows, whole_rows, pltpu.VMEM((PAIR, length), BF),
            pltpu.VMEM((length, PAIR), F32), pltpu.VMEM((length, PAIR), F32),
            by_pair, by_pair, by_pair,
            pltpu.VMEM((pairs, Z_SIZE, Y_SIZE, CORES, depth, CHUNK), BF),
            pltpu.VMEM((pairs, Z_SIZE, Y_SIZE, depth, CHUNK), BF),
            pltpu.VMEM((pairs, Z_SIZE, depth, CHUNK), BF),
            pltpu.VMEM((3, pairs, depth, CHUNK), BF),
            pltpu.VMEM((chunks, Z_SIZE, depth, CHUNK), BF),
            pltpu.VMEM((3, chunks, depth, CHUNK), BF),
            rows, rows, whole_rows,
            pltpu.VMEM((2, BLOCK, width), BF),
            pltpu.VMEM((2, GROUP, Z_SIZE, depth, CHUNK), BF),
            pltpu.VMEM((2, BLOCK, width), F32),
            pltpu.VMEM(small.shape, F32),
            pltpu.VMEM((Z_SIZE,) + small.shape, F32),
            pltpu.VMEM((2,) + small.shape, F32),
            pltpu.VMEM((2,) + small.shape, F32),
            pltpu.VMEM((2, 8, width), F32),
            dma((blocks,)), dma((blocks,)), dma((groups,)), dma((groups,)),
            dma((3 * groups,)), dma((3 * groups,)), dma((pairs,)), dma((pairs,)),
            dma((pairs,)), dma((pairs,)), dma((3 * pairs,)), dma((3 * pairs,)),
            dma((blocks,)), dma((blocks,)), dma((2,)), dma((6,)), dma((6,)), dma((2,)), dma((2,)),
            dma((6 * pairs,)), dma((4,)), dma((2 * blocks,)),
        ],
        compiler_params=pltpu.CompilerParams(
            collective_id=2, has_side_effects=True, vmem_limit_bytes=VMEM_LIMIT
        ),
    )(
        *loaded, key_more, gain, down_bias, small, middle, grad_middle, ff_part, branch,
        branch_first,
    )


def hand_over_kernel(*refs):
    *refs, sems = refs
    count = len(refs) // 3
    refs = refs[:count] + refs[2 * count:] + refs[count:2 * count]
    loads, stores = (
        [
            pltpu.make_async_copy(refs[a * count + n], refs[b * count + n], sems.at[a, n])
            for n in range(count)
        ]
        for a, b in ((0, 1), (1, 2))
    )
    for load in loads:
        load.start()
    for load, store in zip(loads, stores):
        load.wait()
        store.start()
    for store in stores:
        store.wait()


def hand_over(results):
    return pl.pallas_call(
        hand_over_kernel,
        out_shape=[shape_of(v.shape, v.dtype) for v in results],
        in_specs=[ANY_SPEC] * len(results),
        out_specs=[ANY_SPEC] * len(results),
        scratch_shapes=[pltpu.VMEM(v.shape, v.dtype) for v in results] + [
            pltpu.SemaphoreType.DMA((2, len(results)))
        ],
        compiler_params=pltpu.CompilerParams(vmem_limit_bytes=VMEM_LIMIT),
    )(*results)


def fast_body(
    tokens, segment_ids, context_flags, ln1_gain, ln1_bias, qkv_weight, qv_bias, out_weight,
    out_bias, ln2_gain, ln2_bias, up_weight, up_bias, down_weight, down_bias, cotangent,
):
    x, dy = tokens[0], cotangent[0]
    queries, keys, values, mixture, middle, normed_t, wff, key_more, query_more = run_fwd(
        x, segment_ids, context_flags, ln1_gain, ln1_bias, qv_bias, out_bias, qkv_weight,
        out_weight, up_weight, down_weight.T,
    )
    branch, branch_first, grad_middle, ga_t, grad_mixture, ff_part, small = run_ff(
        middle, dy, wff, ln2_gain, ln2_bias, up_bias, out_weight
    )
    (
        output, tokens_grad, qkv_grad, out_grad, up_grad, down_grad, gain_one, offset_one,
        qv_grad, out_bias_grad, gain_two, offset_two, up_bias_grad, down_bias_grad,
    ) = hand_over(run_back(
        queries, keys, values, mixture, grad_mixture, query_more, ga_t, normed_t, qkv_weight, x,
        key_more, ln1_gain, down_bias, small, middle, grad_middle, ff_part, branch,
        branch_first,
    ))
    return (
        output[None], tokens_grad[None], gain_one, offset_one, qkv_grad, qv_grad, out_grad.T,
        out_bias_grad, gain_two, offset_two, up_grad, up_bias_grad, down_grad.T, down_bias_grad,
    )


def solution(mesh):
    chosen = generic_body
    if mesh.shape["head"] == 2 and mesh.shape["seq"] == SEQ_SIZE:
        chosen = fast_body
    return jax.shard_map(
        chosen,
        mesh=mesh,
        in_specs=(
            P("seq", None, None),
            P("seq", None),
            P("seq", None),
            P(),
            P(),
            P(None, None, "head"),
            P(None, "head"),
            P("head", None),
            P(),
            P(),
            P(),
            P("seq", "head"),
            P("head"),
            P("head", "seq"),
            P(),
            P("seq", None, None),
        ),
        out_specs=(
            P("seq", None, None),
            P("seq", None, None),
            P(),
            P(),
            P(None, "seq", "head"),
            P(None, "head"),
            P("head", "seq"),
            P(),
            P(),
            P(),
            P("seq", "head"),
            P("head"),
            P("head", "seq"),
            P(),
        ),
        check_vma=False,
    )
```
